32 devices in a mesh: ens: 4 (over y, x), cols: 8 (over z, core).
Axes of the slice: x: 2, y: 2, z: 4, core: 2. Of those that a mesh axis runs over, the one named last changes fastest.
Arguments:
- static_control: float32 [16, 16, 4096], P(None, 'cols'), may hold values from -6 to 6
- ensemble_control: float32 [32, 16, 16, 4096], P('ens', None, 'cols'), may hold values from -6 to 6
- perturbations: bfloat16 [32, 16, 16, 4096], P('ens', None, 'cols'), may hold values from -6 to 6
- vertical_root: float32 [16, 16], replicated, may hold values from 0 to 1.5
- vertical_local: float32 [16, 16], replicated, may hold values from 0 to 1.5
- face_north: float32 [16, 4096], P('cols'), may hold values from 0.02 to 0.24
- face_east: float32 [16, 4096], P('cols'), may hold values from 0.02 to 0.24
- innovation: float32 [524288], P('cols'), may hold values from -6 to 6
- obs_weight: float32 [524288], P('cols'), may hold values from 0.5 to 4
- obs_slot: int32 [524288], P('cols'), may hold values from 0 to 8191
- send_index: int32 [64, 1024], P('cols'), may hold values from 0 to 131071
- send_count: int32 [64], P('cols'), may hold values from 256 to 1024, as said below
Outputs:
- static_grad: float32 [16, 16, 4096], P(None, 'cols')
- ensemble_grad: float32 [32, 16, 16, 4096], P('ens', None, 'cols')
The draws below stay inside these ranges and needn't reach their ends.
Inputs may be any that keep to these rules, and one draw needn't show every extreme that they name: `send_count`: in every draw one observation owner, drawn from the seed, receives full lists (count 1024) from every column owner; all other counts are drawn independently.
All inputs are finite; a program needn't handle non-finite values.
Results may differ from the reference program's by a relative error of at most 0.0003.
Values sent between devices are 32-bit elements; how exact they have to be, the bound alone decides.
No kernel may reach another device: no remote copies, remote signals or barrier semaphores. Data moves between devices by JAX's collectives and lax.ppermute only.
A program may use at most 128 MiB of HBM per device.

```python
import math
import jax
import jax.numpy as jnp
from jax import lax

LEV = 16
ROWS = 2
NL = 4096
NDIFF = 4
CAP = 1024
OBS_DEV = 65536
NR = 16
MEMBERS = 32
N_COLS = 8


def banded(key, width):
    level_ids = jnp.arange(LEV, dtype=jnp.int32)
    distance = jnp.abs(level_ids[:, None] - level_ids[None, :]).astype(jnp.float32)
    factor = jax.random.uniform(key, (LEV, LEV), jnp.float32, 0.5, 1.5)
    return factor * jnp.exp(-distance / width)


def draw_vertical_root(key, part):
    key = jax.random.fold_in(key, 11)
    return banded(key, 1.5)


def draw_vertical_local(key, part):
    key = jax.random.fold_in(key, 13)
    return banded(key, 3.0)


def draw_send_count(key, part):
    key = jax.random.fold_in(key, 17)
    counts = jax.random.randint(key, (N_COLS, N_COLS), CAP // 4, CAP + 1, dtype=jnp.int32)
    busiest = jax.random.randint(jax.random.fold_in(key, 1), (), 0, N_COLS, dtype=jnp.int32)
    column = jnp.arange(N_COLS, dtype=jnp.int32)[None, :]
    counts = jnp.where(column == busiest, CAP, counts)
    return counts.reshape(-1).astype(jnp.int32)


def draw_send_index(key, part):
    key = jax.random.fold_in(key, 19)
    cell_total = LEV * ROWS * NL
    indices = jax.random.randint(key, (N_COLS * N_COLS, CAP), 0, cell_total, dtype=jnp.int32)
    indices = indices.at[0, 0].set(0).at[0, 1].set(cell_total - 1)
    return indices


def draw_obs_slot(key, part):
    key = jax.random.fold_in(key, 23)
    indices = jax.random.randint(key, (N_COLS * OBS_DEV,), 0, N_COLS * CAP, dtype=jnp.int32)
    indices = indices.at[0].set(0).at[1].set(N_COLS * CAP - 1)
    return indices


def steps_of(rng, shape, split, smallest, largest):
    factor_of = 1.0
    for dim, parts in split:
        steps = jax.random.uniform(jax.random.fold_in(jax.random.fold_in(rng, 6), dim), (parts,), jnp.float32, smallest / len(split), largest / len(split))
        factor_of = factor_of * jnp.repeat(jnp.exp(steps), shape[dim] // parts).reshape((-1,) + (1,) * (len(shape) - 1 - dim))
    return factor_of


def noise(rng, extent, scale, reach, cuts=(), held_as=jnp.bfloat16):
    level = steps_of(rng, extent, cuts, -0.22, 0.18) if cuts else 1.0
    entries = jax.random.normal(rng, extent, jnp.float32) * scale * level
    return jnp.minimum(jnp.maximum(entries, -reach), reach).astype(held_as)


def setup_inputs(seed: int = 0) -> dict:
    seeds = jax.random.split(jax.random.key(seed), 13)
    static_control = noise(seeds[0], (LEV, NR, NL), 1.0, 6.0, ((1, 8),), jnp.float32)
    ensemble_control = noise(seeds[1], (MEMBERS, LEV, NR, NL), 1.0, 6.0, ((0, 4), (2, 8)), jnp.float32)
    perturbations = noise(seeds[2], (MEMBERS, LEV, NR, NL), 1.0, 6.0, ((0, 4), (2, 8)))
    vertical_root = draw_vertical_root(jax.random.fold_in(seeds[12], 71), 0)
    vertical_local = draw_vertical_local(jax.random.fold_in(seeds[12], 71), 0)
    face_north = jnp.clip(0.02 + 0.22 * jax.random.uniform(seeds[5], (NR, NL), jnp.float32) ** steps_of(seeds[5], (NR, NL), ((0, 8),), -0.2, 0.2), 0.02, 0.24)
    face_east = jnp.clip(0.02 + 0.22 * jax.random.uniform(seeds[6], (NR, NL), jnp.float32) ** steps_of(seeds[6], (NR, NL), ((0, 8),), -0.2, 0.2), 0.02, 0.24)
    innovation = noise(seeds[7], (N_COLS * OBS_DEV,), 1.0, 6.0, ((0, 8),), jnp.float32)
    obs_weight = jnp.clip(jnp.exp(math.log(4.0) - 2.0794415 * jax.random.uniform(seeds[8], (N_COLS * OBS_DEV,), jnp.float32) ** steps_of(seeds[8], (N_COLS * OBS_DEV,), ((0, 8),), -0.2, 0.2)), 0.5, 4.0)
    obs_slot = draw_obs_slot(jax.random.fold_in(seeds[12], 71), 0)
    send_index = draw_send_index(jax.random.fold_in(seeds[12], 71), 0)
    send_count = draw_send_count(jax.random.fold_in(seeds[12], 71), 0)
    return {"static_control": static_control, "ensemble_control": ensemble_control, "perturbations": perturbations, "vertical_root": vertical_root, "vertical_local": vertical_local, "face_north": face_north, "face_east": face_east, "innovation": innovation, "obs_weight": obs_weight, "obs_slot": obs_slot, "send_index": send_index, "send_count": send_count}


precise = lax.Precision.HIGHEST

def smooth(source, padded, k_north, k_south, k_east):
    upper_rows = padded[:, :-2]
    lower_rows = padded[:, 2:]
    eastern = jnp.roll(source, -1, axis=2)
    western = jnp.roll(source, 1, axis=2)
    k_west = jnp.roll(k_east, 1, axis=1)
    return source + k_north * (upper_rows - source) + k_south * (lower_rows - source) + k_east * (eastern - source) + k_west * (western - source)

def vertical(matrix, source):
    return jnp.einsum('lm,mrc->lrc', matrix, source, precision=precise)

def reference(static_control, ensemble_control, perturbations, vertical_root, vertical_local, face_north, face_east, innovation, obs_weight, obs_slot, send_index, send_count):
    k_south = jnp.concatenate([face_north[1:], jnp.zeros_like(face_north[:1])], axis=0)

    def diffuse(source):
        for repeat in range(NDIFF):
            padded = jnp.pad(source, ((0, 0), (1, 1), (0, 0)))
            source = smooth(source, padded, face_north, k_south, face_east)
        return source
    static_increment = diffuse(vertical(vertical_root, static_control))
    member_scale = 1.0 / math.sqrt(MEMBERS - 1)

    def add_member(running, members_pair):
        member_pert, member_alpha = members_pair
        localized = vertical(vertical_local, member_alpha)
        return (running + member_pert.astype(jnp.float32) * localized, None)
    ens_sum, unused = lax.scan(add_member, jnp.zeros(static_control.shape, jnp.float32), (perturbations, ensemble_control))
    increment = static_increment + member_scale * ens_sum
    flattened = increment.reshape(-1)
    tile_cells = ROWS * NL
    list_ids = jnp.arange(N_COLS * N_COLS, dtype=jnp.int32)
    column_dev = list_ids // N_COLS
    level_of = send_index // tile_cells
    within = send_index % tile_cells
    global_index = level_of * (N_COLS * tile_cells) + column_dev[:, None] * tile_cells + within
    live_mask = (jnp.arange(CAP, dtype=jnp.int32)[None, :] < send_count[:, None]).astype(jnp.float32)
    values = flattened[global_index] * live_mask
    owner_dev = jnp.arange(N_COLS * OBS_DEV, dtype=jnp.int32) // OBS_DEV
    source_dev = obs_slot // CAP
    position = (source_dev * N_COLS + owner_dev) * CAP + obs_slot % CAP
    model_eq = values.reshape(-1)[position]
    weighted = obs_weight * (model_eq - innovation)
    returned = jax.ops.segment_sum(weighted, position, num_segments=N_COLS * N_COLS * CAP).reshape(N_COLS * N_COLS, CAP) * live_mask
    adjoint = jnp.zeros(flattened.shape, jnp.float32).at[global_index.reshape(-1)].add(returned.reshape(-1)).reshape(increment.shape)
    static_grad = static_control + vertical(vertical_root.T, diffuse(adjoint))

    def member_grad(members_pair):
        member_pert, member_alpha = members_pair
        return member_alpha + member_scale * vertical(vertical_local.T, member_pert.astype(jnp.float32) * adjoint)
    ensemble_grad = lax.map(member_grad, (perturbations, ensemble_control))
    return (static_grad, ensemble_grad)
```

```python
import functools
import math

import jax
import jax.numpy as jnp
from jax import lax
from jax.experimental import pallas as pl
from jax.experimental.pallas import tpu as pltpu
from jax.sharding import PartitionSpec as P

NDIFF = 4
LANES = 128
FINE = 32
MIB = 1 << 20

f32 = jnp.float32
bf16 = jnp.bfloat16
SMEM = pl.BlockSpec(memory_space=pltpu.SMEM)
VMEM = pl.BlockSpec(memory_space=pltpu.VMEM)


def tiled(field):
    *lead, rows, lon = field.shape
    field = field.reshape(*lead, rows, lon // LANES, LANES)
    return jnp.swapaxes(field, -3, -2).reshape(*lead, rows * lon // LANES, LANES)


def untiled(field, rows):
    *lead, count, lanes = field.shape
    field = field.reshape(*lead, count // rows, rows, lanes)
    return jnp.swapaxes(field, -3, -2).reshape(*lead, rows, count // rows * lanes)


def params(limit, **more):
    return pltpu.CompilerParams(vmem_limit_bytes=limit * MIB, **more)


def halves(x):
    high = x.astype(bf16)
    return high, (x - high.astype(f32)).astype(bf16)


def one_hot(index, count):
    ids = lax.broadcasted_iota(jnp.int32, (count, index.shape[1]), 0)
    return jnp.where(ids == index, f32(1), f32(0)).astype(bf16)


def over(x, size):
    if size & (size - 1):
        return lax.div(x, jnp.int32(size)), lax.rem(x, jnp.int32(size))
    return lax.shift_right_logical(x, jnp.int32(size.bit_length() - 1)), x & (size - 1)


def prepare_kernel(lev_share, rows, where_ref, root_ref, count_ref, static_ref, north_ref, east_ref, index_ref, out_ref, row_ref, lane_ref):
    levels, per_level, _ = static_ref.shape
    first = where_ref[0] * lev_share
    for j in range(lev_share):
        total = root_ref[first + j, 0] * static_ref[0]
        for m in range(1, levels):
            total = total + root_ref[first + j, m] * static_ref[m]
        out_ref[j] = total
    out_ref[lev_share] = north_ref[...]
    out_ref[lev_share + 1] = east_ref[...]
    lists, capacity = index_ref.shape
    lon = per_level // rows * LANES
    pieces = capacity // LANES
    slot = lax.broadcasted_iota(jnp.int32, (1, capacity), 1)
    for q in range(lists):
        cell = index_ref[q : q + 1, :]
        rest, lane = over(cell, LANES)
        rest, block = over(rest, lon // LANES)
        level, row = over(rest, rows)
        grid_row = jnp.where(slot < count_ref[q], level * per_level + block * rows + row, -1)
        for c in range(pieces):
            row_ref[q * pieces + c : q * pieces + c + 1, :] = grid_row[:, c * LANES : (c + 1) * LANES]
            lane_ref[q * pieces + c : q * pieces + c + 1, :] = lane[:, c * LANES : (c + 1) * LANES]


def slots_kernel(n_cols, cap_rows, where_ref, slot_ref, weight_ref, innov_ref, out_ref, acc_ref, fold_ref):
    coarse = acc_ref.shape[0]
    obs_rows = slot_ref.shape[0]
    group = min(8, obs_rows)
    acc_ref[...] = jnp.zeros_like(acc_ref)

    def step(i, carry):
        at = pl.ds(pl.multiple_of(i * group, group), group)
        slot = slot_ref[at, :]
        weight = weight_ref[at, :]
        amount = weight * innov_ref[at, :]
        upper, lower = over(slot, FINE)
        terms = [t.astype(f32) for t in halves(weight) + halves(amount)]
        fine_ids = lax.broadcasted_iota(jnp.int32, (FINE, LANES), 0)
        left, right = [], []
        for r in range(group):
            left.append(one_hot(upper[r : r + 1, :], coarse))
            mask = fine_ids == lower[r : r + 1, :]
            right.append(
                jnp.concatenate([jnp.where(mask, t[r : r + 1, :], f32(0)).astype(bf16) for t in terms], axis=0)
            )
        acc_ref[...] += lax.dot_general(
            jnp.concatenate(left, axis=1),
            jnp.concatenate(right, axis=1),
            (((1,), (1,)), ((), ())),
            preferred_element_type=f32,
        )
        return carry

    lax.fori_loop(0, obs_rows // group, step, 0)
    acc = acc_ref[...]
    fold_ref[...] = acc + pltpu.roll(acc, LANES - FINE, 1)
    per_row = LANES // FINE
    lane = lax.broadcasted_iota(jnp.int32, (coarse // per_row, LANES), 1)
    weights = jnp.zeros((coarse // per_row, LANES), f32)
    amounts = jnp.zeros((coarse // per_row, LANES), f32)
    for c in range(per_row):
        piece = fold_ref[pl.ds(c, coarse // per_row, stride=per_row), :]
        here = lane // FINE == c
        weights = jnp.where(here, pltpu.roll(piece, c * FINE, 1) if c else piece, weights)
        shift = (c * FINE - 2 * FINE) % LANES
        amounts = jnp.where(here, pltpu.roll(piece, shift, 1) if shift else piece, amounts)
    for p in range(n_cols):
        out_ref[p, 0] = weights[p * cap_rows : (p + 1) * cap_rows]
        out_ref[p, 1] = amounts[p * cap_rows : (p + 1) * cap_rows]


def splat(matrix_ref, out_ref, scale, transpose):
    levels = matrix_ref.shape[0]
    for l in range(levels):
        for m in range(levels):
            entry = matrix_ref[m, l] if transpose else matrix_ref[l, m]
            out_ref[l, m] = jnp.full((8, LANES), entry * f32(scale), f32)


def forward_kernel(scale, local_ref, control_ref, pert_ref, out_ref, splat_ref):
    levels, per_level, _ = out_ref.shape

    @pl.when(pl.program_id(0) == 0)
    def _():
        splat(local_ref, splat_ref, scale, False)
        out_ref[...] = jnp.zeros_like(out_ref)

    def chunk(j, carry):
        at = pl.ds(pl.multiple_of(j * 16, 16), 16)
        control = [control_ref[0, m, at, :].reshape(2, 8, LANES) for m in range(levels)]
        for l in range(levels):
            total = splat_ref[l, 0][None] * control[0]
            for m in range(1, levels):
                total = total + splat_ref[l, m][None] * control[m]
            pert = pert_ref[0, l, at, :].astype(f32)
            out_ref[l, at, :] += pert * total.reshape(16, LANES)
        return carry

    lax.fori_loop(0, per_level // 16, chunk, 0)


def member_kernel(scale, local_ref, adjoint_ref, control_ref, pert_ref, out_ref, splat_ref):
    levels, per_level, _ = adjoint_ref.shape

    @pl.when(pl.program_id(0) == 0)
    def _():
        splat(local_ref, splat_ref, scale, True)

    def chunk(j, carry):
        at = pl.ds(pl.multiple_of(j * 16, 16), 16)
        weighted = [
            (pert_ref[0, l, at, :].astype(f32) * adjoint_ref[l, at, :]).reshape(2, 8, LANES) for l in range(levels)
        ]
        for m in range(levels):
            total = splat_ref[m, 0][None] * weighted[0]
            for l in range(1, levels):
                total = total + splat_ref[m, l][None] * weighted[l]
            out_ref[0, m, at, :] = control_ref[0, m, at, :] + total.reshape(16, LANES)
        return carry

    lax.fori_loop(0, per_level // 16, chunk, 0)


def eastern(x):
    lane = lax.broadcasted_iota(jnp.int32, x.shape, 1)
    near = pltpu.roll(x, LANES - 1, 1)
    return jnp.where(lane == LANES - 1, pltpu.roll(near, x.shape[0] - 1, 0), near)


def western(x):
    lane = lax.broadcasted_iota(jnp.int32, x.shape, 1)
    near = pltpu.roll(x, 1, 1)
    return jnp.where(lane == 0, pltpu.roll(near, 1, 0), near)


def diffuse_rows(tiles, level, coef_ref, rows):
    blocks = tiles[0].shape[1] // rows
    field = [t[level, pl.ds(r, blocks, stride=rows), :] for t in tiles for r in range(rows)]
    for step in range(NDIFF):
        field = [
            coef_ref[0, i + step] * field[i]
            + coef_ref[1, i + step] * field[i - 1]
            + coef_ref[2, i + step] * field[i + 1]
            + coef_ref[3, i + step] * eastern(field[i])
            + coef_ref[4, i + step] * western(field[i])
            for i in range(1, len(field) - 1)
        ]
        field = list(field)
    return field


def first_diffusion_kernel(lev_share, rows, where_ref, *refs):
    tiles, (out_ref, coef_ref) = refs[:-2], refs[-2:]
    blocks = tiles[0].shape[1] // rows
    side = len(tiles) // 2
    north = [t[lev_share, pl.ds(r, blocks, stride=rows), :] for t in tiles for r in range(rows)]
    east = [t[lev_share + 1, pl.ds(r, blocks, stride=rows), :] for t in tiles for r in range(rows)]
    for i in range(1, len(north) - 1):
        south = north[i + 1]
        if (i + 1) % rows == 0 and i < side * rows:
            south = south * jnp.where(where_ref[1] == side - (i + 1) // rows, f32(0), f32(1))
        west = western(east[i])
        coef_ref[0, i] = 1.0 - north[i] - south - east[i] - west
        coef_ref[1, i] = north[i]
        coef_ref[2, i] = south
        coef_ref[3, i] = east[i]
        coef_ref[4, i] = west
    for i in (0, len(north) - 1):
        for c in range(5):
            coef_ref[c, i] = jnp.zeros_like(north[0])

    def body(level, carry):
        final = diffuse_rows(tiles, level, coef_ref, rows)
        for r in range(rows):
            out_ref[level, pl.ds(r, blocks, stride=rows), :] = final[r]
        return carry

    lax.fori_loop(0, lev_share, body, 0)


def second_diffusion_kernel(rows, coef_ref, *refs):
    tiles, out_ref = refs[:-1], refs[-1]
    copies, lev_share = out_ref.shape[:2]
    blocks = tiles[0].shape[1] // rows

    def body(level, carry):
        final = diffuse_rows(tiles, level, coef_ref, rows)
        for copy in range(copies):
            for r in range(rows):
                out_ref[copy, level, pl.ds(r, blocks, stride=rows), :] = final[r]
        return carry

    lax.fori_loop(0, lev_share, body, 0)


def lookup_kernel(where_ref, part_ref, static_ref, row_ref, lane_ref, slots_ref, out_ref, field_ref, turned_ref):
    cells = part_ref.shape[0]
    own = static_ref.shape[0]
    n_lists, _, cap_rows, _ = slots_ref.shape
    field_ref[...] = part_ref[...]
    at = pl.ds(pl.multiple_of(where_ref[0] * own, own), own)
    field_ref[at, :] += static_ref[...]

    def turn(t, carry):
        at = pl.ds(pl.multiple_of(t * LANES, LANES), LANES)
        high, low = halves(field_ref[at, :].T)
        turned_ref[0:LANES, at] = high
        turned_ref[LANES : 2 * LANES, at] = low
        return carry

    lax.fori_loop(0, cells // LANES, turn, 0)
    lane_ids = lax.broadcasted_iota(jnp.int32, (LANES, LANES), 0)

    def look(q, carry):
        at = pl.ds(pl.multiple_of(q * cap_rows, cap_rows), cap_rows)
        rows = row_ref[at, :]
        lanes = lane_ref[at, :]
        found = []
        for c in range(cap_rows):
            got = jnp.dot(turned_ref[...], one_hot(rows[c : c + 1, :], cells), preferred_element_type=f32)
            got = got[:LANES] + got[LANES:]
            found.append(jnp.sum(jnp.where(lane_ids == lanes[c : c + 1, :], got, f32(0)), axis=0, keepdims=True))
        out_ref[0, at, :] = jnp.concatenate(found, axis=0)
        out_ref[1, at, :] = slots_ref[q, 0]
        out_ref[2, at, :] = slots_ref[q, 1]
        return carry

    lax.fori_loop(0, n_lists, look, 0)


def scatter_kernel(cap_rows, where_ref, row_ref, lane_ref, *refs):
    shares, (out_ref, own_ref, acc_ref) = refs[:-3], refs[-3:]
    cells = out_ref.shape[0]
    own = own_ref.shape[0]
    acc_ref[...] = jnp.zeros_like(acc_ref)
    lane_ids = lax.broadcasted_iota(jnp.int32, (LANES, LANES), 0)

    def put(q, carry):
        at = pl.ds(pl.multiple_of(q * cap_rows, cap_rows), cap_rows)
        value, weight, amount = (functools.reduce(jnp.add, [s[t, at, :] for s in shares]) for t in range(3))
        high, low = (h.astype(f32) for h in halves(value * weight - amount))
        rows = row_ref[at, :]
        lanes = lane_ref[at, :]
        left, right = [], []
        for c in range(cap_rows):
            left.append(one_hot(rows[c : c + 1, :], cells))
            mask = lane_ids == lanes[c : c + 1, :]
            right.append(
                jnp.concatenate(
                    [jnp.where(mask, h[c : c + 1, :], f32(0)).astype(bf16) for h in (high, low)], axis=0
                )
            )
        acc_ref[...] += lax.dot_general(
            jnp.concatenate(left, axis=1),
            jnp.concatenate(right, axis=1),
            (((1,), (1,)), ((), ())),
            preferred_element_type=f32,
        )
        return carry

    lax.fori_loop(0, row_ref.shape[0] // cap_rows, put, 0)
    out_ref[...] = acc_ref[:, :LANES] + acc_ref[:, LANES:]
    own_ref[...] = out_ref[pl.ds(pl.multiple_of(where_ref[0] * own, own), own), :]


def static_kernel(root_ref, static_ref, smooth_ref, out_ref):
    levels, per_level, _ = static_ref.shape

    def chunk(j, carry):
        at = pl.ds(pl.multiple_of(j * 16, 16), 16)
        smooth = [smooth_ref[l, at, :] for l in range(levels)]
        for m in range(levels):
            total = static_ref[m, at, :]
            for l in range(levels):
                total = total + root_ref[l, m] * smooth[l]
            out_ref[m, at, :] = total
        return carry

    lax.fori_loop(0, per_level // 16, chunk, 0)


def neighbours(x, axis):
    count = lax.axis_size(axis)
    by = (2, 1, -1, -2)
    return [lax.ppermute(x, axis, [(i, i + d) for i in range(count) if 0 <= i + d < count]) for d in by]


def local(
    static_control,
    ensemble_control,
    perturbations,
    vertical_root,
    vertical_local,
    face_north,
    face_east,
    innovation,
    obs_weight,
    obs_slot,
    send_index,
    send_count,
):
    n_ens = lax.axis_size("ens")
    n_cols = lax.axis_size("cols")
    members, levels, rows, lon = ensemble_control.shape
    per_level = rows * lon // LANES
    cells = levels * per_level
    lev_share = levels // n_ens
    own = lev_share * per_level
    lists, capacity = send_index.shape
    cap_rows = capacity // LANES
    entry_rows = lists * cap_rows
    member_scale = 1.0 / math.sqrt(members * n_ens - 1)
    where = jnp.stack([lax.axis_index("ens"), lax.axis_index("cols")]).astype(jnp.int32)

    static = tiled(static_control)
    control = tiled(ensemble_control)
    pert = tiled(perturbations)
    north = tiled(face_north)
    east = tiled(face_east)

    packed, entry_row, entry_lane = pl.pallas_call(
        functools.partial(prepare_kernel, lev_share, rows),
        in_specs=[SMEM, SMEM, SMEM, VMEM, VMEM, VMEM, VMEM],
        out_specs=[VMEM] * 3,
        out_shape=[
            jax.ShapeDtypeStruct((lev_share + 2, per_level, LANES), f32),
            jax.ShapeDtypeStruct((entry_rows, LANES), jnp.int32),
            jax.ShapeDtypeStruct((entry_rows, LANES), jnp.int32),
        ],
        compiler_params=params(16),
        name="prepare",
    )(where, vertical_root, send_count, static, north, east, send_index)
    packs = neighbours(packed, "cols")

    obs_rows = obs_slot.shape[0] // LANES
    share_rows = obs_rows // n_ens
    obs_spec = pl.BlockSpec((share_rows, LANES), lambda i, at: (at[0], 0))
    coarse = n_cols * capacity // FINE
    slots = pl.pallas_call(
        functools.partial(slots_kernel, n_cols, cap_rows),
        grid_spec=pltpu.PrefetchScalarGridSpec(
            num_scalar_prefetch=1,
            grid=(1,),
            in_specs=[obs_spec] * 3,
            out_specs=pl.BlockSpec((n_cols, 2, cap_rows, LANES), lambda i, at: (0, 0, 0, 0)),
            scratch_shapes=[pltpu.VMEM((coarse, LANES), f32), pltpu.VMEM((coarse, LANES), f32)],
        ),
        out_shape=jax.ShapeDtypeStruct((n_cols, 2, cap_rows, LANES), f32),
        compiler_params=params(32),
        cost_estimate=pl.CostEstimate(flops=2 * 128 * coarse * share_rows * LANES, bytes_accessed=12 * share_rows * LANES, transcendentals=0),
        name="slot_sums",
    )(
        where,
        obs_slot.reshape(obs_rows, LANES),
        obs_weight.reshape(obs_rows, LANES),
        innovation.reshape(obs_rows, LANES),
    )
    slots = lax.all_to_all(slots, "cols", split_axis=0, concat_axis=0, tiled=True)

    member_spec = pl.BlockSpec((1, levels, per_level, LANES), lambda k: (k, 0, 0, 0))
    whole_spec = pl.BlockSpec((levels, per_level, LANES), lambda k: (0, 0, 0))
    splat_shape = pltpu.VMEM((levels, levels, 8, LANES), f32)
    member_cost = pl.CostEstimate(flops=2 * members * levels * cells * LANES, bytes_accessed=members * cells * LANES * 6, transcendentals=0)
    part = pl.pallas_call(
        functools.partial(forward_kernel, member_scale),
        grid=(members,),
        in_specs=[SMEM, member_spec, member_spec],
        out_specs=whole_spec,
        out_shape=jax.ShapeDtypeStruct((levels, per_level, LANES), f32),
        scratch_shapes=[splat_shape],
        compiler_params=params(32),
        cost_estimate=member_cost,
        name="members_forward",
    )(vertical_local, control, pert)

    tiles = [packs[0], packs[1], packed, packs[2], packs[3]]
    blocks = per_level // rows
    increment, coefs = pl.pallas_call(
        functools.partial(first_diffusion_kernel, lev_share, rows),
        in_specs=[SMEM] + [VMEM] * 5,
        out_specs=[VMEM] * 2,
        out_shape=[
            jax.ShapeDtypeStruct((lev_share, per_level, LANES), f32),
            jax.ShapeDtypeStruct((5, 5 * rows, blocks, LANES), f32),
        ],
        compiler_params=params(32),
        name="diffuse_forward",
    )(where, *tiles)

    share = pl.pallas_call(
        lookup_kernel,
        in_specs=[SMEM] + [VMEM] * 5,
        out_specs=VMEM,
        out_shape=jax.ShapeDtypeStruct((3, entry_rows, LANES), f32),
        scratch_shapes=[pltpu.VMEM((cells, LANES), f32), pltpu.VMEM((2 * LANES, cells), bf16)],
        compiler_params=params(32),
        name="lookup",
    )(where, part.reshape(cells, LANES), increment.reshape(own, LANES), entry_row, entry_lane, slots)
    shares = [share] + [
        lax.ppermute(share, "ens", [((i + d) % n_ens, i) for i in range(n_ens)]) for d in range(1, n_ens)
    ]

    adjoint, adjoint_own = pl.pallas_call(
        functools.partial(scatter_kernel, cap_rows),
        in_specs=[SMEM] + [VMEM] * (2 + n_ens),
        out_specs=[VMEM] * 2,
        out_shape=[jax.ShapeDtypeStruct((cells, LANES), f32), jax.ShapeDtypeStruct((own, LANES), f32)],
        scratch_shapes=[pltpu.VMEM((cells, 2 * LANES), f32)],
        compiler_params=params(32),
        name="scatter",
    )(where, entry_row, entry_lane, *shares)
    adjoint_own = adjoint_own.reshape(lev_share, per_level, LANES)
    around = neighbours(adjoint_own, "cols")

    smooth = pl.pallas_call(
        functools.partial(second_diffusion_kernel, rows),
        in_specs=[VMEM] * 6,
        out_specs=VMEM,
        out_shape=jax.ShapeDtypeStruct((n_ens, lev_share, per_level, LANES), f32),
        compiler_params=params(32),
        name="diffuse_adjoint",
    )(coefs, around[0], around[1], adjoint_own, around[2], around[3])
    smooth = lax.all_to_all(smooth, "ens", split_axis=0, concat_axis=0, tiled=True)

    ensemble_grad = pl.pallas_call(
        functools.partial(member_kernel, member_scale),
        grid=(members,),
        in_specs=[SMEM, whole_spec, member_spec, member_spec],
        out_specs=member_spec,
        out_shape=jax.ShapeDtypeStruct((members, levels, per_level, LANES), f32),
        scratch_shapes=[splat_shape],
        compiler_params=params(32),
        cost_estimate=member_cost,
        name="members_gradient",
    )(vertical_local, adjoint.reshape(levels, per_level, LANES), control, pert)

    static_grad = pl.pallas_call(
        static_kernel,
        in_specs=[SMEM, VMEM, VMEM],
        out_specs=VMEM,
        out_shape=jax.ShapeDtypeStruct((levels, per_level, LANES), f32),
        compiler_params=params(16),
        name="static_gradient",
    )(vertical_root, static, smooth.reshape(levels, per_level, LANES))
    return (untiled(static_grad, rows), untiled(ensemble_grad, rows))


def solution(mesh):
    placed = (
        P(None, "cols", None),
        P("ens", None, "cols", None),
        P("ens", None, "cols", None),
        P(),
        P(),
        P("cols", None),
        P("cols", None),
        P("cols"),
        P("cols"),
        P("cols"),
        P("cols", None),
        P("cols"),
    )
    return jax.shard_map(
        local,
        mesh=mesh,
        in_specs=placed,
        out_specs=(P(None, "cols", None), P("ens", None, "cols", None)),
        check_vma=False,
    )
```

```python
import functools
import math

import jax
import jax.numpy as jnp
from jax import lax
from jax.experimental import pallas as pl
from jax.experimental.pallas import tpu as pltpu
from jax.sharding import PartitionSpec as P

NDIFF = 4
LANES = 128
FINE = 32
MIB = 1 << 20

f32 = jnp.float32
bf16 = jnp.bfloat16
SMEM = pl.BlockSpec(memory_space=pltpu.SMEM)
VMEM = pl.BlockSpec(memory_space=pltpu.VMEM)


def tiled(field):
    *lead, rows, lon = field.shape
    field = field.reshape(*lead, rows, lon // LANES, LANES)
    return jnp.swapaxes(field, -3, -2).reshape(*lead, rows * lon // LANES, LANES)


def untiled(field, rows):
    *lead, count, lanes = field.shape
    field = field.reshape(*lead, count // rows, rows, lanes)
    return jnp.swapaxes(field, -3, -2).reshape(*lead, rows, count // rows * lanes)


def params(limit, **more):
    return pltpu.CompilerParams(vmem_limit_bytes=limit * MIB, **more)


def halves(x):
    high = x.astype(bf16)
    return high, (x - high.astype(f32)).astype(bf16)


def in_hbm(x):
    return pltpu.with_memory_space_constraint(x, pltpu.HBM)


def spread(row, dtype):
    return jnp.broadcast_to(row, (16, row.shape[1])).astype(dtype)


def matches(index, count):
    ids = lax.broadcasted_iota(jnp.int32, (count, index.shape[1]), 0).astype(jnp.int16)
    return ids.reshape(count // 16, 16, index.shape[1]) == spread(index, jnp.int16)[None]


def placed_at(index, count, amount=None):
    where = matches(index, count)
    amount = bf16(1) if amount is None else spread(amount, bf16)[None]
    return jnp.where(where, amount, bf16(0)).reshape(count, index.shape[1])


def product_nt(left, right):
    return lax.dot_general(left, right, (((1,), (1,)), ((), ())), preferred_element_type=f32)


def over(x, size):
    if size & (size - 1):
        return lax.div(x, jnp.int32(size)), lax.rem(x, jnp.int32(size))
    return lax.shift_right_logical(x, jnp.int32(size.bit_length() - 1)), x & (size - 1)


def prepare_kernel(lev_share, rows, where_ref, root_ref, count_ref, static_ref, north_ref, east_ref, index_ref, out_ref, row_ref, lane_ref):
    levels, per_level, _ = static_ref.shape
    first = where_ref[0] * lev_share
    for j in range(lev_share):
        total = root_ref[first + j, 0] * static_ref[0]
        for m in range(1, levels):
            total = total + root_ref[first + j, m] * static_ref[m]
        out_ref[j] = total
    out_ref[lev_share] = north_ref[...]
    out_ref[lev_share + 1] = east_ref[...]
    lists, capacity = index_ref.shape
    lon = per_level // rows * LANES
    pieces = capacity // LANES
    slot = lax.broadcasted_iota(jnp.int32, (1, capacity), 1)
    for q in range(lists):
        cell = index_ref[q : q + 1, :]
        rest, lane = over(cell, LANES)
        rest, block = over(rest, lon // LANES)
        level, row = over(rest, rows)
        grid_row = jnp.where(slot < count_ref[q], level * per_level + block * rows + row, -1)
        code = (grid_row * LANES + lane).astype(f32)
        for c in range(pieces):
            at = q * pieces + c
            row_ref[at : at + 1, :] = grid_row[:, c * LANES : (c + 1) * LANES]
            lane_ref[at : at + 1, :] = lane[:, c * LANES : (c + 1) * LANES]
            plane = lev_share + 2 + at // per_level
            at = at % per_level
            out_ref[plane, at : at + 1, :] = code[:, c * LANES : (c + 1) * LANES]


def slots_kernel(n_cols, cap_rows, where_ref, slot_ref, weight_ref, innov_ref, out_ref, acc_ref, fold_ref):
    coarse = acc_ref.shape[0]
    obs_rows = slot_ref.shape[0]
    group = min(8, obs_rows)
    acc_ref[...] = jnp.zeros_like(acc_ref)

    def step(i, carry):
        at = pl.ds(pl.multiple_of(i * group, group), group)
        slot = slot_ref[at, :]
        weight = weight_ref[at, :]
        amount = weight * innov_ref[at, :]
        upper, lower = over(slot, FINE)
        terms = [t.astype(f32) for t in halves(weight) + halves(amount)]
        left, right = [], []
        for r in range(group):
            left.append(placed_at(upper[r : r + 1, :], coarse))
            mask = matches(lower[r : r + 1, :], FINE)
            right += [
                jnp.concatenate(
                    [
                        jnp.where(mask, spread(t[r : r + 1, :], bf16)[None], bf16(0)).reshape(FINE, LANES)
                        for t in terms
                    ],
                    axis=0,
                )
            ]
        acc_ref[...] += product_nt(jnp.concatenate(left, axis=1), jnp.concatenate(right, axis=1))
        return carry

    lax.fori_loop(0, obs_rows // group, step, 0)
    acc = acc_ref[...]
    fold_ref[...] = acc + pltpu.roll(acc, LANES - FINE, 1)
    per_row = LANES // FINE
    lane = lax.broadcasted_iota(jnp.int32, (coarse // per_row, LANES), 1)
    weights = jnp.zeros((coarse // per_row, LANES), f32)
    amounts = jnp.zeros((coarse // per_row, LANES), f32)
    for c in range(per_row):
        piece = fold_ref[pl.ds(c, coarse // per_row, stride=per_row), :]
        here = lane // FINE == c
        weights = jnp.where(here, pltpu.roll(piece, c * FINE, 1) if c else piece, weights)
        shift = (c * FINE - 2 * FINE) % LANES
        amounts = jnp.where(here, pltpu.roll(piece, shift, 1) if shift else piece, amounts)
    for p in range(n_cols):
        out_ref[p, 0] = weights[p * cap_rows : (p + 1) * cap_rows]
        out_ref[p, 1] = amounts[p * cap_rows : (p + 1) * cap_rows]


def splat(matrix_ref, out_ref, scale, transpose):
    levels = matrix_ref.shape[0]
    for l in range(levels):
        for m in range(levels):
            entry = matrix_ref[m, l] if transpose else matrix_ref[l, m]
            out_ref[l, m] = jnp.full((8, LANES), entry * f32(scale), f32)


def forward_kernel(scale, local_ref, control_ref, pert_ref, out_ref, splat_ref):
    levels, per_level, _ = out_ref.shape

    @pl.when(pl.program_id(0) == 0)
    def _():
        splat(local_ref, splat_ref, scale, False)
        out_ref[...] = jnp.zeros_like(out_ref)

    def chunk(j, carry):
        at = pl.ds(pl.multiple_of(j * 16, 16), 16)
        control = [control_ref[0, m, at, :].reshape(2, 8, LANES) for m in range(levels)]
        for l in range(levels):
            total = splat_ref[l, 0][None] * control[0]
            for m in range(1, levels):
                total = total + splat_ref[l, m][None] * control[m]
            pert = pert_ref[0, l, at, :].astype(f32)
            out_ref[l, at, :] += pert * total.reshape(16, LANES)
        return carry

    lax.fori_loop(0, per_level // 16, chunk, 0)


def member_kernel(scale, local_ref, adjoint_ref, control_ref, pert_ref, out_ref, splat_ref):
    levels, per_level, _ = adjoint_ref.shape

    @pl.when(pl.program_id(0) == 0)
    def _():
        splat(local_ref, splat_ref, scale, True)

    def chunk(j, carry):
        at = pl.ds(pl.multiple_of(j * 16, 16), 16)
        weighted = [
            (pert_ref[0, l, at, :].astype(f32) * adjoint_ref[l, at, :]).reshape(2, 8, LANES) for l in range(levels)
        ]
        for m in range(levels):
            total = splat_ref[m, 0][None] * weighted[0]
            for l in range(1, levels):
                total = total + splat_ref[m, l][None] * weighted[l]
            out_ref[0, m, at, :] = control_ref[0, m, at, :] + total.reshape(16, LANES)
        return carry

    lax.fori_loop(0, per_level // 16, chunk, 0)


def eastern(x):
    lane = lax.broadcasted_iota(jnp.int32, x.shape, 1)
    near = pltpu.roll(x, LANES - 1, 1)
    return jnp.where(lane == LANES - 1, pltpu.roll(near, x.shape[0] - 1, 0), near)


def western(x):
    lane = lax.broadcasted_iota(jnp.int32, x.shape, 1)
    near = pltpu.roll(x, 1, 1)
    return jnp.where(lane == 0, pltpu.roll(near, 1, 0), near)


def diffuse_rows(tiles, level, coef_ref, rows):
    blocks = tiles[0].shape[1] // rows
    field = [t[level, pl.ds(r, blocks, stride=rows), :] for t in tiles for r in range(rows)]
    for step in range(NDIFF):
        field = [
            coef_ref[0, i + step] * field[i]
            + coef_ref[1, i + step] * field[i - 1]
            + coef_ref[2, i + step] * field[i + 1]
            + coef_ref[3, i + step] * eastern(field[i])
            + coef_ref[4, i + step] * western(field[i])
            for i in range(1, len(field) - 1)
        ]
        field = list(field)
    return field


def first_diffusion_kernel(lev_share, rows, where_ref, *refs):
    tiles, (out_ref, coef_ref) = refs[:-2], refs[-2:]
    blocks = tiles[0].shape[1] // rows
    side = len(tiles) // 2
    north = [t[lev_share, pl.ds(r, blocks, stride=rows), :] for t in tiles for r in range(rows)]
    east = [t[lev_share + 1, pl.ds(r, blocks, stride=rows), :] for t in tiles for r in range(rows)]
    for i in range(1, len(north) - 1):
        south = north[i + 1]
        if (i + 1) % rows == 0 and i < side * rows:
            south = south * jnp.where(where_ref[1] == side - (i + 1) // rows, f32(0), f32(1))
        west = western(east[i])
        coef_ref[0, i] = 1.0 - north[i] - south - east[i] - west
        coef_ref[1, i] = north[i]
        coef_ref[2, i] = south
        coef_ref[3, i] = east[i]
        coef_ref[4, i] = west
    for i in (0, len(north) - 1):
        for c in range(5):
            coef_ref[c, i] = jnp.zeros_like(north[0])

    def body(level, carry):
        final = diffuse_rows(tiles, level, coef_ref, rows)
        for r in range(rows):
            out_ref[level, pl.ds(r, blocks, stride=rows), :] = final[r]
        return carry

    lax.fori_loop(0, lev_share, body, 0)


def second_diffusion_kernel(rows, cap_rows, where_ref, coef_ref, own_ref, *refs):
    sides, out_ref, acc_ref, tile_ref = refs[:-3], refs[-3], refs[-2], refs[-1]
    around = len(sides) // 2
    codes, amounts = sides[:around], sides[around:]
    copies, lev_share, per_level, _ = out_ref.shape
    own = lev_share * per_level
    entry_rows = amounts[0].shape[0]
    planes = entry_rows // per_level
    lists = entry_rows // cap_rows
    blocks = per_level // rows
    first = where_ref[0] * own

    for n in range(around):
        acc_ref[...] = jnp.zeros_like(acc_ref)

        def step(q, carry):
            at = pl.multiple_of(q * cap_rows, cap_rows)
            plane = lev_share + 2 + at // per_level
            code = codes[n][plane, pl.ds(pl.multiple_of(at % per_level, cap_rows), cap_rows), :].astype(jnp.int32)
            row = lax.shift_right_arithmetic(code, jnp.int32(LANES.bit_length() - 1)) - first
            put(acc_ref, row, code & (LANES - 1), amounts[n][pl.ds(at, cap_rows), :])
            return carry

        lax.fori_loop(0, lists, step, 0)
        tile_ref[n] = (acc_ref[:, :LANES] + acc_ref[:, LANES:]).reshape(lev_share, per_level, LANES)

    half = around // 2
    tiles = [tile_ref.at[n] for n in range(half)] + [own_ref] + [tile_ref.at[n] for n in range(half, around)]

    def body(level, carry):
        final = diffuse_rows(tiles, level, coef_ref, rows)
        for copy in range(copies):
            for r in range(rows):
                out_ref[copy, level, pl.ds(r, blocks, stride=rows), :] = final[r]
        return carry

    lax.fori_loop(0, lev_share, body, 0)


def lookup_kernel(where_ref, part_ref, static_ref, row_ref, lane_ref, slots_ref, out_ref, field_ref, terms_ref):
    cells = part_ref.shape[0]
    own = static_ref.shape[0]
    n_lists, _, cap_rows, _ = slots_ref.shape
    field_ref[...] = part_ref[...]
    at = pl.ds(pl.multiple_of(where_ref[0] * own, own), own)
    field_ref[at, :] += static_ref[...]
    high, low = halves(field_ref[...])
    terms_ref[:, :LANES] = high
    terms_ref[:, LANES:] = low
    ids16 = lax.broadcasted_iota(jnp.int32, (LANES, cells), 1).astype(jnp.int16)
    ids = lax.broadcasted_iota(jnp.int32, (LANES, LANES), 1)
    ones = jnp.ones((16, 2 * LANES), bf16)

    def look(q, carry):
        at = pl.ds(pl.multiple_of(q * cap_rows, cap_rows), cap_rows)
        rows = row_ref[at, :].astype(f32).T
        lanes = lane_ref[at, :].astype(f32).T
        picks = []
        for c in range(cap_rows):
            column = jnp.broadcast_to(rows[:, c : c + 1], (LANES, LANES)).astype(jnp.int32).astype(jnp.int16)
            column = jnp.concatenate([column] * (cells // LANES), axis=1)
            picks.append(jnp.where(ids16 == column, bf16(1), bf16(0)))
        got = jnp.dot(jnp.concatenate(picks, axis=0), terms_ref[...], preferred_element_type=f32)
        kept = []
        for c in range(cap_rows):
            mask = ids == jnp.broadcast_to(lanes[:, c : c + 1], (LANES, LANES)).astype(jnp.int32)
            mine = got[c * LANES : (c + 1) * LANES]
            kept.append(
                jnp.concatenate(
                    [jnp.where(mask, mine[:, :LANES], f32(0)), jnp.where(mask, mine[:, LANES:], f32(0))], axis=1
                ).astype(bf16)
            )
        total = product_nt(ones, jnp.concatenate(kept, axis=0))
        out_ref[0, at, :] = jnp.concatenate(
            [total[0:1, c * LANES : (c + 1) * LANES] for c in range(cap_rows)], axis=0
        )
        out_ref[1, at, :] = slots_ref[q, 0]
        out_ref[2, at, :] = slots_ref[q, 1]
        return carry

    lax.fori_loop(0, n_lists, look, 0)


def put(acc_ref, rows, lanes, amounts):
    high, low = (h.astype(f32) for h in halves(amounts))
    left, right = [], []
    for c in range(rows.shape[0]):
        piece = slice(c, c + 1)
        left.append(placed_at(rows[piece, :], acc_ref.shape[0]))
        mask = matches(lanes[piece, :], LANES)
        right.append(
            jnp.concatenate(
                [
                    jnp.where(mask, spread(h[piece, :], bf16)[None], bf16(0)).reshape(LANES, LANES)
                    for h in (high, low)
                ],
                axis=0,
            )
        )
    acc_ref[...] += product_nt(jnp.concatenate(left, axis=1), jnp.concatenate(right, axis=1))


def scatter_kernel(cap_rows, where_ref, row_ref, lane_ref, amount_ref, out_ref, own_ref, acc_ref):
    own = own_ref.shape[0]
    acc_ref[...] = jnp.zeros_like(acc_ref)

    def step(q, carry):
        at = pl.ds(pl.multiple_of(q * cap_rows, cap_rows), cap_rows)
        put(acc_ref, row_ref[at, :], lane_ref[at, :], amount_ref[at, :])
        return carry

    lax.fori_loop(0, row_ref.shape[0] // cap_rows, step, 0)
    out_ref[...] = acc_ref[:, :LANES] + acc_ref[:, LANES:]
    own_ref[...] = out_ref[pl.ds(pl.multiple_of(where_ref[0] * own, own), own), :]


def static_kernel(root_ref, static_ref, smooth_ref, out_ref):
    levels, per_level, _ = static_ref.shape

    def chunk(j, carry):
        at = pl.ds(pl.multiple_of(j * 16, 16), 16)
        smooth = [smooth_ref[l, at, :] for l in range(levels)]
        for m in range(levels):
            total = static_ref[m, at, :]
            for l in range(levels):
                total = total + root_ref[l, m] * smooth[l]
            out_ref[m, at, :] = total
        return carry

    lax.fori_loop(0, per_level // 16, chunk, 0)


def shifted(x, by):
    count = lax.axis_size("cols")
    return lax.ppermute(x, "cols", [(i, i + by) for i in range(count) if 0 <= i + by < count])


def local(
    static_control,
    ensemble_control,
    perturbations,
    vertical_root,
    vertical_local,
    face_north,
    face_east,
    innovation,
    obs_weight,
    obs_slot,
    send_index,
    send_count,
):
    n_ens = lax.axis_size("ens")
    n_cols = lax.axis_size("cols")
    members, levels, rows, lon = ensemble_control.shape
    per_level = rows * lon // LANES
    cells = levels * per_level
    lev_share = levels // n_ens
    own = lev_share * per_level
    lists, capacity = send_index.shape
    cap_rows = capacity // LANES
    entry_rows = lists * cap_rows
    member_scale = 1.0 / math.sqrt(members * n_ens - 1)
    where = jnp.stack([lax.axis_index("ens"), lax.axis_index("cols")]).astype(jnp.int32)

    static = in_hbm(tiled(static_control))
    control = in_hbm(tiled(ensemble_control))
    pert = in_hbm(tiled(perturbations))

    planes = lev_share + 2 + entry_rows // per_level
    whole = lambda *shape: pl.BlockSpec(shape, lambda i: (0,) * len(shape))
    packed, entry_row, entry_lane = pl.pallas_call(
        functools.partial(prepare_kernel, lev_share, rows),
        grid=(1,),
        in_specs=[
            SMEM,
            SMEM,
            SMEM,
            whole(levels, per_level, LANES),
            whole(per_level, LANES),
            whole(per_level, LANES),
            whole(lists, capacity),
        ],
        out_specs=[VMEM] * 3,
        out_shape=[
            pltpu.VMEM((planes, per_level, LANES), f32),
            pltpu.VMEM((entry_rows, LANES), jnp.int32),
            pltpu.VMEM((entry_rows, LANES), jnp.int32),
        ],
        compiler_params=params(8),
        name="prepare",
    )(
        where,
        in_hbm(vertical_root),
        in_hbm(send_count),
        static,
        in_hbm(tiled(face_north)),
        in_hbm(tiled(face_east)),
        in_hbm(send_index),
    )
    packs = {by: shifted(packed, by) for by in (2, -2)}

    obs_rows = obs_slot.shape[0] // LANES
    share_rows = obs_rows // n_ens
    obs_spec = pl.BlockSpec((share_rows, LANES), lambda i, at: (at[0], 0))
    coarse = n_cols * capacity // FINE
    slots = pl.pallas_call(
        functools.partial(slots_kernel, n_cols, cap_rows),
        grid_spec=pltpu.PrefetchScalarGridSpec(
            num_scalar_prefetch=1,
            grid=(1,),
            in_specs=[obs_spec] * 3,
            out_specs=VMEM,
            scratch_shapes=[pltpu.VMEM((coarse, LANES), f32), pltpu.VMEM((coarse, LANES), f32)],
        ),
        out_shape=pltpu.VMEM((n_cols, 2, cap_rows, LANES), f32),
        compiler_params=params(16),
        name="slot_sums",
    )(
        where,
        in_hbm(obs_slot.reshape(obs_rows, LANES)),
        in_hbm(obs_weight.reshape(obs_rows, LANES)),
        in_hbm(innovation.reshape(obs_rows, LANES)),
    )
    packed_again, slots = lax.optimization_barrier((packed, slots))
    packs |= {by: shifted(packed_again, by) for by in (1, -1)}
    slots = lax.all_to_all(slots, "cols", split_axis=0, concat_axis=0, tiled=True)

    member_spec = pl.BlockSpec((1, levels, per_level, LANES), lambda k: (k, 0, 0, 0))
    splat_shape = pltpu.VMEM((levels, levels, 8, LANES), f32)
    member_cost = pl.CostEstimate(
        flops=2 * members * levels * cells * LANES,
        bytes_accessed=members * cells * LANES * 6,
        transcendentals=0,
    )
    part = pl.pallas_call(
        functools.partial(forward_kernel, member_scale),
        grid=(members,),
        in_specs=[SMEM, member_spec, member_spec],
        out_specs=VMEM,
        out_shape=pltpu.VMEM((levels, per_level, LANES), f32),
        scratch_shapes=[splat_shape],
        compiler_params=params(8),
        cost_estimate=member_cost,
        name="members_forward",
    )(in_hbm(vertical_local), control, pert)

    blocks = per_level // rows
    increment, coefs = pl.pallas_call(
        functools.partial(first_diffusion_kernel, lev_share, rows),
        in_specs=[SMEM] + [VMEM] * 5,
        out_specs=[VMEM] * 2,
        out_shape=[
            pltpu.VMEM((lev_share, per_level, LANES), f32),
            pltpu.VMEM((5, 5 * rows, blocks, LANES), f32),
        ],
        compiler_params=params(8),
        name="diffuse_forward",
    )(where, packs[2], packs[1], packed, packs[-1], packs[-2])

    share = pl.pallas_call(
        lookup_kernel,
        in_specs=[SMEM] + [VMEM] * 5,
        out_specs=VMEM,
        out_shape=pltpu.VMEM((3, entry_rows, LANES), f32),
        scratch_shapes=[pltpu.VMEM((cells, LANES), f32), pltpu.VMEM((cells, 2 * LANES), bf16)],
        compiler_params=params(16),
        name="lookup",
    )(where, part.reshape(cells, LANES), increment.reshape(own, LANES), entry_row, entry_lane, slots)
    total = share
    for d in range(1, n_ens):
        total = total + lax.ppermute(share, "ens", [((i + d) % n_ens, i) for i in range(n_ens)])
    amounts = total[0] * total[1] - total[2]
    amounts_around = [shifted(amounts, by) for by in (2, 1, -1, -2)]

    adjoint, adjoint_own = pl.pallas_call(
        functools.partial(scatter_kernel, cap_rows),
        in_specs=[SMEM] + [VMEM] * 3,
        out_specs=[VMEM] * 2,
        out_shape=[pltpu.VMEM((cells, LANES), f32), pltpu.VMEM((own, LANES), f32)],
        scratch_shapes=[pltpu.VMEM((cells, 2 * LANES), f32)],
        compiler_params=params(16),
        name="scatter",
    )(where, entry_row, entry_lane, amounts)

    smooth = pl.pallas_call(
        functools.partial(second_diffusion_kernel, rows, cap_rows),
        in_specs=[SMEM] + [VMEM] * 10,
        out_specs=VMEM,
        out_shape=pltpu.VMEM((n_ens, lev_share, per_level, LANES), f32),
        scratch_shapes=[pltpu.VMEM((own, 2 * LANES), f32), pltpu.VMEM((4, lev_share, per_level, LANES), f32)],
        compiler_params=params(16),
        name="diffuse_adjoint",
    )(
        where,
        coefs,
        adjoint_own.reshape(lev_share, per_level, LANES),
        packs[2],
        packs[1],
        packs[-1],
        packs[-2],
        *amounts_around,
    )
    smooth = lax.all_to_all(smooth, "ens", split_axis=0, concat_axis=0, tiled=True)

    ensemble_grad = pl.pallas_call(
        functools.partial(member_kernel, member_scale),
        grid=(members,),
        in_specs=[SMEM, VMEM, member_spec, member_spec],
        out_specs=member_spec,
        out_shape=jax.ShapeDtypeStruct((members, levels, per_level, LANES), f32),
        scratch_shapes=[splat_shape],
        compiler_params=params(8),
        cost_estimate=member_cost,
        name="members_gradient",
    )(in_hbm(vertical_local), adjoint.reshape(levels, per_level, LANES), control, pert)

    static_grad = pl.pallas_call(
        static_kernel,
        grid=(1,),
        in_specs=[SMEM, whole(levels, per_level, LANES), VMEM],
        out_specs=whole(levels, per_level, LANES),
        out_shape=jax.ShapeDtypeStruct((levels, per_level, LANES), f32),
        compiler_params=params(8),
        name="static_gradient",
    )(in_hbm(vertical_root), static, smooth.reshape(levels, per_level, LANES))
    return (untiled(static_grad, rows), untiled(ensemble_grad, rows))


def solution(mesh):
    placed = (
        P(None, "cols", None),
        P("ens", None, "cols", None),
        P("ens", None, "cols", None),
        P(),
        P(),
        P("cols", None),
        P("cols", None),
        P("cols"),
        P("cols"),
        P("cols"),
        P("cols", None),
        P("cols"),
    )
    return jax.shard_map(
        local,
        mesh=mesh,
        in_specs=placed,
        out_specs=(P(None, "cols", None), P("ens", None, "cols", None)),
        check_vma=False,
    )
```

```python
import functools
import math

import jax
import jax.numpy as jnp
from jax import lax
from jax.experimental import pallas as pl
from jax.experimental.pallas import tpu as pltpu
from jax.sharding import PartitionSpec as P

NDIFF = 4
LANES = 128
FINE = 32
MIB = 1 << 20

f32 = jnp.float32
bf16 = jnp.bfloat16
SMEM = pl.BlockSpec(memory_space=pltpu.SMEM)
VMEM = pl.BlockSpec(memory_space=pltpu.VMEM)


def tiled(field):
    *lead, rows, lon = field.shape
    field = field.reshape(*lead, rows, lon // LANES, LANES)
    return jnp.swapaxes(field, -3, -2).reshape(*lead, rows * lon // LANES, LANES)


def untiled(field, rows):
    *lead, count, lanes = field.shape
    field = field.reshape(*lead, count // rows, rows, lanes)
    return jnp.swapaxes(field, -3, -2).reshape(*lead, rows, count // rows * lanes)


def params(limit, **more):
    return pltpu.CompilerParams(vmem_limit_bytes=limit * MIB, **more)


def halves(x):
    high = x.astype(bf16)
    return high, (x - high.astype(f32)).astype(bf16)


def in_hbm(x):
    return pltpu.with_memory_space_constraint(x, pltpu.HBM)


def spread(row, dtype):
    return jnp.broadcast_to(row, (16, row.shape[1])).astype(dtype)


def matches(index, count):
    ids = lax.broadcasted_iota(jnp.int32, (count, index.shape[1]), 0).astype(jnp.int16)
    return ids.reshape(count // 16, 16, index.shape[1]) == spread(index, jnp.int16)[None]


def placed_at(index, count, amount=None):
    where = matches(index, count)
    amount = bf16(1) if amount is None else spread(amount, bf16)[None]
    return jnp.where(where, amount, bf16(0)).reshape(count, index.shape[1])


def product_nt(left, right):
    return lax.dot_general(left, right, (((1,), (1,)), ((), ())), preferred_element_type=f32)


def over(x, size):
    if size & (size - 1):
        return lax.div(x, jnp.int32(size)), lax.rem(x, jnp.int32(size))
    return lax.shift_right_logical(x, jnp.int32(size.bit_length() - 1)), x & (size - 1)


def prepare_kernel(lev_share, rows, root_ref, count_ref, static_ref, north_ref, east_ref, index_ref, out_ref, row_ref, lane_ref):
    levels, per_level, _ = static_ref.shape
    first = lax.axis_index("ens") * lev_share
    for j in range(lev_share):
        total = root_ref[first + j, 0] * static_ref[0]
        for m in range(1, levels):
            total = total + root_ref[first + j, m] * static_ref[m]
        out_ref[j] = total
    out_ref[lev_share] = north_ref[...]
    out_ref[lev_share + 1] = east_ref[...]
    lists, capacity = index_ref.shape
    lon = per_level // rows * LANES
    pieces = capacity // LANES
    slot = lax.broadcasted_iota(jnp.int32, (1, capacity), 1)
    for q in range(lists):
        cell = index_ref[q : q + 1, :]
        rest, lane = over(cell, LANES)
        rest, block = over(rest, lon // LANES)
        level, row = over(rest, rows)
        grid_row = jnp.where(slot < count_ref[q], level * per_level + block * rows + row, -1)
        for c in range(pieces):
            at = q * pieces + c
            row_ref[at : at + 1, :] = grid_row[:, c * LANES : (c + 1) * LANES]
            lane_ref[at : at + 1, :] = lane[:, c * LANES : (c + 1) * LANES]


def level_product(matrix, transpose):
    levels = matrix.shape[0]
    size = levels * 16
    pick = lax.broadcasted_iota(jnp.int32, (size, levels), 0) // 16
    pick = jnp.where(pick == lax.broadcasted_iota(jnp.int32, (size, levels), 1), f32(1), f32(0)).astype(bf16)
    same = (
        lax.broadcasted_iota(jnp.int32, (size, size), 0) % 16 == lax.broadcasted_iota(jnp.int32, (size, size), 1) % 16
    )
    out = []
    for half in halves(matrix):
        if transpose:
            wide = product_nt(pick, half)
        else:
            wide = jnp.dot(pick, half, preferred_element_type=f32)
        wide = product_nt(wide.astype(bf16), pick)
        out.append(jnp.where(same, wide, f32(0)).astype(bf16))
    return jnp.concatenate([out[0], out[0], out[1]], axis=1)


def three_terms(x):
    high, low = halves(x)
    return jnp.concatenate([high, low, high], axis=0)


def slots_kernel(n_cols, cap_rows, scale, *refs):
    sources, (out_ref, *kept), matrices, (acc_ref, fold_ref, *landed), sems = (
        refs[:8],
        refs[8:12],
        refs[12:15],
        refs[15:22],
        refs[22],
    )
    coarse = acc_ref.shape[0]
    obs_rows = landed[0].shape[0]
    group = min(8, obs_rows)
    first = pl.multiple_of(lax.axis_index("ens") * obs_rows, obs_rows)
    copies = [
        pltpu.make_async_copy(sources[i].at[pl.ds(first, obs_rows), :], landed[i], sems.at[i]) for i in range(3)
    ]
    copies += [pltpu.make_async_copy(sources[3 + i], landed[3 + i], sems.at[3 + i]) for i in range(2)]
    copies += [pltpu.make_async_copy(sources[5 + i], kept[i], sems.at[5 + i]) for i in range(3)]
    for copy in copies:
        copy.start()
    acc_ref[...] = jnp.zeros_like(acc_ref)
    for copy in copies[:5]:
        copy.wait()
    slot_ref, weight_ref, innov_ref, local_ref, root_ref = landed

    def step(i, carry):
        at = pl.ds(pl.multiple_of(i * group, group), group)
        slot = slot_ref[at, :]
        weight = weight_ref[at, :]
        amount = weight * innov_ref[at, :]
        upper, lower = over(slot, FINE)
        terms = [t.astype(f32) for t in halves(weight) + halves(amount)]
        left, right = [], []
        for r in range(group):
            left.append(placed_at(upper[r : r + 1, :], coarse))
            mask = matches(lower[r : r + 1, :], FINE)
            right.append(
                jnp.concatenate(
                    [
                        jnp.where(mask, spread(t[r : r + 1, :], bf16)[None], bf16(0)).reshape(FINE, LANES)
                        for t in terms
                    ],
                    axis=0,
                )
            )
        acc_ref[...] += product_nt(jnp.concatenate(left, axis=1), jnp.concatenate(right, axis=1))
        return carry

    lax.fori_loop(0, obs_rows // group, step, 0)
    acc = acc_ref[...]
    fold_ref[...] = acc + pltpu.roll(acc, LANES - FINE, 1)
    per_row = LANES // FINE
    lane = lax.broadcasted_iota(jnp.int32, (coarse // per_row, LANES), 1)
    weights = jnp.zeros((coarse // per_row, LANES), f32)
    amounts = jnp.zeros((coarse // per_row, LANES), f32)
    for c in range(per_row):
        piece = fold_ref[pl.ds(c, coarse // per_row, stride=per_row), :]
        here = lane // FINE == c
        weights = jnp.where(here, pltpu.roll(piece, c * FINE, 1) if c else piece, weights)
        shift = (c * FINE - 2 * FINE) % LANES
        amounts = jnp.where(here, pltpu.roll(piece, shift, 1) if shift else piece, amounts)
    for p in range(n_cols):
        out_ref[p, 0] = weights[p * cap_rows : (p + 1) * cap_rows]
        out_ref[p, 1] = amounts[p * cap_rows : (p + 1) * cap_rows]
    matrices[0][...] = level_product(local_ref[...] * f32(scale), False)
    matrices[1][...] = level_product(local_ref[...] * f32(scale), True)
    matrices[2][...] = level_product(root_ref[...], True)
    for copy in copies[5:]:
        copy.wait()


def forward_kernel(matrix_ref, control_ref, pert_ref, out_ref):
    members, levels, per_level, _ = control_ref.shape
    pair = 2 - members % 2

    def chunk(j, carry):
        at = pl.ds(pl.multiple_of(j * 16, 16), 16)
        total = None
        for k in range(0, members, pair):
            terms = [three_terms(control_ref[k + i, :, at, :].reshape(levels * 16, LANES)) for i in range(pair)]
            local = jnp.dot(matrix_ref[...], jnp.concatenate(terms, axis=1), preferred_element_type=f32)
            for i in range(pair):
                pert = pert_ref[k + i, :, at, :].astype(f32).reshape(levels * 16, LANES)
                part = pert * local[:, i * LANES : (i + 1) * LANES]
                total = part if total is None else total + part
        out_ref[:, at, :] = total.reshape(levels, 16, LANES)
        return carry

    lax.fori_loop(0, per_level // 16, chunk, 0)


def member_kernel(matrix_ref, adjoint_ref, control_ref, pert_ref, out_ref):
    pair, levels, per_level, _ = out_ref.shape
    first = pl.program_id(0) * pair

    def chunk(j, carry):
        at = pl.ds(pl.multiple_of(j * 16, 16), 16)
        adjoint = adjoint_ref[:, at, :].reshape(levels * 16, LANES)
        terms = [
            three_terms(pert_ref[first + i, :, at, :].astype(f32).reshape(levels * 16, LANES) * adjoint)
            for i in range(pair)
        ]
        change = jnp.dot(matrix_ref[...], jnp.concatenate(terms, axis=1), preferred_element_type=f32)
        for i in range(pair):
            out_ref[i, :, at, :] = control_ref[first + i, :, at, :] + change[:, i * LANES : (i + 1) * LANES].reshape(
                levels, 16, LANES
            )
        return carry

    lax.fori_loop(0, per_level // 16, chunk, 0)


def eastern(x):
    lane = lax.broadcasted_iota(jnp.int32, x.shape, 1)
    near = pltpu.roll(x, LANES - 1, 1)
    return jnp.where(lane == LANES - 1, pltpu.roll(near, x.shape[0] - 1, 0), near)


def western(x):
    lane = lax.broadcasted_iota(jnp.int32, x.shape, 1)
    near = pltpu.roll(x, 1, 1)
    return jnp.where(lane == 0, pltpu.roll(near, 1, 0), near)


def diffuse_rows(tiles, level, coef_ref, rows):
    blocks = tiles[0].shape[1] // rows
    field = [t[level, pl.ds(r, blocks, stride=rows), :] for t in tiles for r in range(rows)]
    for step in range(NDIFF):
        field = [
            coef_ref[0, i + step] * field[i]
            + coef_ref[1, i + step] * field[i - 1]
            + coef_ref[2, i + step] * field[i + 1]
            + coef_ref[3, i + step] * eastern(field[i])
            + coef_ref[4, i + step] * western(field[i])
            for i in range(1, len(field) - 1)
        ]
        field = list(field)
    return field


def tiles_of(before_ref, own_ref, after_ref, other_ref):
    odd = lax.axis_index("cols") % 2
    return [before_ref, other_ref.at[1 - odd], own_ref, other_ref.at[2 * odd], after_ref]


def first_diffusion_kernel(lev_share, rows, before_ref, own_ref, after_ref, other_ref, out_ref, coef_ref):
    tiles = tiles_of(before_ref, own_ref, after_ref, other_ref)
    blocks = own_ref.shape[1] // rows
    side = len(tiles) // 2
    north = [t[lev_share, pl.ds(r, blocks, stride=rows), :] for t in tiles for r in range(rows)]
    east = [t[lev_share + 1, pl.ds(r, blocks, stride=rows), :] for t in tiles for r in range(rows)]
    for i in range(1, len(north) - 1):
        south = north[i + 1]
        if (i + 1) % rows == 0 and i < side * rows:
            south = south * jnp.where(lax.axis_index("cols") == side - (i + 1) // rows, f32(0), f32(1))
        west = western(east[i])
        coef_ref[0, i] = 1.0 - north[i] - south - east[i] - west
        coef_ref[1, i] = north[i]
        coef_ref[2, i] = south
        coef_ref[3, i] = east[i]
        coef_ref[4, i] = west
    for i in (0, len(north) - 1):
        for c in range(5):
            coef_ref[c, i] = jnp.zeros_like(north[0])

    def body(level, carry):
        final = diffuse_rows(tiles, level, coef_ref, rows)
        for r in range(rows):
            out_ref[level, pl.ds(r, blocks, stride=rows), :] = final[r]
        return carry

    lax.fori_loop(0, lev_share, body, 0)


def second_diffusion_kernel(rows, coef_ref, before_ref, own_ref, after_ref, other_ref, out_ref):
    tiles = tiles_of(before_ref, own_ref, after_ref, other_ref)
    copies, lev_share = out_ref.shape[:2]
    blocks = own_ref.shape[1] // rows

    def body(level, carry):
        final = diffuse_rows(tiles, level, coef_ref, rows)
        for copy in range(copies):
            for r in range(rows):
                out_ref[copy, level, pl.ds(r, blocks, stride=rows), :] = final[r]
        return carry

    lax.fori_loop(0, lev_share, body, 0)


def lookup_kernel(part_ref, static_ref, row_ref, lane_ref, slots_ref, out_ref, terms_ref):
    copies = out_ref.shape[0]
    cells = part_ref.shape[0]
    own = static_ref.shape[0]
    n_lists, _, cap_rows, _ = slots_ref.shape
    at = pl.ds(pl.multiple_of(lax.axis_index("ens") * own, own), own)
    for here, field in ((slice(None), part_ref[...]), (at, part_ref[at, :] + static_ref[...])):
        high, low = halves(field)
        terms_ref[here, :LANES] = high
        terms_ref[here, LANES:] = low
    ids16 = lax.broadcasted_iota(jnp.int32, (LANES, cells), 1).astype(jnp.int16)
    ids = lax.broadcasted_iota(jnp.int32, (LANES, LANES), 1)
    diagonal = ids == lax.broadcasted_iota(jnp.int32, (LANES, LANES), 0)

    def look(q, carry):
        at = pl.ds(pl.multiple_of(q * cap_rows, cap_rows), cap_rows)
        rows = row_ref[at, :].astype(f32).T
        lanes = lane_ref[at, :].astype(f32).T
        picks = []
        for c in range(cap_rows):
            column = jnp.broadcast_to(rows[:, c : c + 1], (LANES, LANES)).astype(jnp.int32).astype(jnp.int16)
            column = jnp.concatenate([column] * (cells // LANES), axis=1)
            picks.append(jnp.where(ids16 == column, bf16(1), bf16(0)))
        got = jnp.dot(jnp.concatenate(picks, axis=0), terms_ref[...], preferred_element_type=f32)
        values = []
        for c in range(cap_rows):
            mask = ids == jnp.broadcast_to(lanes[:, c : c + 1], (LANES, LANES)).astype(jnp.int32)
            mine = got[c * LANES : (c + 1) * LANES]
            found = jnp.sum(jnp.where(mask, mine[:, :LANES] + mine[:, LANES:], f32(0)), axis=1, keepdims=True)
            values.append(jnp.sum(jnp.where(diagonal, found, f32(0)), axis=0, keepdims=True))
        values = jnp.concatenate(values, axis=0)
        for copy in range(copies):
            out_ref[copy, 0, at, :] = values
            out_ref[copy, 1, at, :] = slots_ref[q, 0]
            out_ref[copy, 2, at, :] = slots_ref[q, 1]
        return carry

    lax.fori_loop(0, n_lists, look, 0)


def put(acc_ref, rows, lanes, amounts):
    high, low = (h.astype(f32) for h in halves(amounts))
    left, right = [], []
    for c in range(rows.shape[0]):
        piece = slice(c, c + 1)
        left.append(placed_at(rows[piece, :], acc_ref.shape[0]))
        mask = matches(lanes[piece, :], LANES)
        right.append(
            jnp.concatenate(
                [
                    jnp.where(mask, spread(h[piece, :], bf16)[None], bf16(0)).reshape(LANES, LANES)
                    for h in (high, low)
                ],
                axis=0,
            )
        )
    acc_ref[...] += product_nt(jnp.concatenate(left, axis=1), jnp.concatenate(right, axis=1))


def amounts_of(shares_ref, at):
    value, weight, amount = (
        functools.reduce(jnp.add, [shares_ref[e, t, at, :] for e in range(shares_ref.shape[0])]) for t in range(3)
    )
    return value * weight - amount


def scatter_own_kernel(cap_rows, row_ref, lane_ref, shares_ref, out_ref, amount_ref, acc_ref):
    own = out_ref.shape[0]
    first = lax.axis_index("ens") * own
    acc_ref[...] = jnp.zeros_like(acc_ref)

    def step(q, carry):
        at = pl.ds(pl.multiple_of(q * cap_rows, cap_rows), cap_rows)
        amounts = amounts_of(shares_ref, at)
        amount_ref[at, :] = amounts
        put(acc_ref, row_ref[at, :] - first, lane_ref[at, :], amounts)
        return carry

    lax.fori_loop(0, row_ref.shape[0] // cap_rows, step, 0)
    out_ref[...] = acc_ref[:, :LANES] + acc_ref[:, LANES:]


def scatter_rest_kernel(cap_rows, row_ref, lane_ref, amount_ref, own_ref, out_ref, acc_ref):
    cells = out_ref.shape[0]
    own = own_ref.shape[0]
    n_ens = cells // own
    me = lax.axis_index("ens")
    first = (me + 1) * own
    acc_ref[...] = jnp.zeros_like(acc_ref)

    def step(q, carry):
        at = pl.ds(pl.multiple_of(q * cap_rows, cap_rows), cap_rows)
        row = row_ref[at, :]
        turned = row - first
        turned = jnp.where(row < 0, -1, jnp.where(turned < 0, turned + cells, turned))
        put(acc_ref, turned, lane_ref[at, :], amount_ref[at, :])
        return carry

    lax.fori_loop(0, row_ref.shape[0] // cap_rows, step, 0)
    out_ref[pl.ds(pl.multiple_of(me * own, own), own), :] = own_ref[...]
    for t in range(1, n_ens):
        to = pl.ds(pl.multiple_of((me + t) % n_ens * own, own), own)
        piece = acc_ref[(t - 1) * own : t * own, :]
        out_ref[to, :] = piece[:, :LANES] + piece[:, LANES:]


def static_kernel(matrix_ref, static_ref, smooth_ref, out_ref):
    levels, per_level, _ = static_ref.shape
    for j in range(0, per_level, 32):
        terms = [
            three_terms(smooth_ref[:, j + i : j + i + 16, :].reshape(levels * 16, LANES)) for i in (0, 16)
        ]
        change = jnp.dot(matrix_ref[...], jnp.concatenate(terms, axis=1), preferred_element_type=f32)
        for i, part in ((0, change[:, :LANES]), (16, change[:, LANES:])):
            at = slice(j + i, j + i + 16)
            out_ref[:, at, :] = static_ref[:, at, :] + part.reshape(levels, 16, LANES)


def shifted(x, by):
    count = lax.axis_size("cols")
    return lax.ppermute(x, "cols", [(i, i + by) for i in range(count) if 0 <= i + by < count])


def swapped(x):
    count = lax.axis_size("cols")
    return lax.ppermute(x, "cols", [(i, i ^ 1) for i in range(count)])


def local(
    static_control,
    ensemble_control,
    perturbations,
    vertical_root,
    vertical_local,
    face_north,
    face_east,
    innovation,
    obs_weight,
    obs_slot,
    send_index,
    send_count,
):
    n_ens = lax.axis_size("ens")
    n_cols = lax.axis_size("cols")
    members, levels, rows, lon = ensemble_control.shape
    per_level = rows * lon // LANES
    cells = levels * per_level
    lev_share = levels // n_ens
    own = lev_share * per_level
    lists, capacity = send_index.shape
    cap_rows = capacity // LANES
    entry_rows = lists * cap_rows
    member_scale = 1.0 / math.sqrt(members * n_ens - 1)

    static = in_hbm(tiled(static_control))
    control = in_hbm(tiled(ensemble_control))
    pert = in_hbm(tiled(perturbations))

    def whole(*shape):
        return pl.BlockSpec(shape, lambda i: (0,) * len(shape))

    packed, entry_row, entry_lane = pl.pallas_call(
        functools.partial(prepare_kernel, lev_share, rows),
        grid=(1,),
        in_specs=[
            SMEM,
            SMEM,
            whole(levels, per_level, LANES),
            whole(per_level, LANES),
            whole(per_level, LANES),
            whole(lists, capacity),
        ],
        out_specs=[VMEM] * 3,
        out_shape=[
            pltpu.VMEM((lev_share + 2, per_level, LANES), f32),
            pltpu.VMEM((entry_rows, LANES), jnp.int32),
            pltpu.VMEM((entry_rows, LANES), jnp.int32),
        ],
        compiler_params=params(8),
        name="prepare",
    )(
        in_hbm(vertical_root),
        in_hbm(send_count),
        static,
        in_hbm(tiled(face_north)),
        in_hbm(tiled(face_east)),
        in_hbm(send_index),
    )
    before, after = shifted(packed, 2), shifted(packed, -2)

    obs_rows = obs_slot.shape[0] // LANES
    share_rows = obs_rows // n_ens
    coarse = n_cols * capacity // FINE
    size = levels * 16
    obs_slot, packed = lax.optimization_barrier((obs_slot, packed))
    slots, static_here, control_here, pert_here, to_local, from_local, from_root = pl.pallas_call(
        functools.partial(slots_kernel, n_cols, cap_rows, member_scale),
        in_specs=[pl.BlockSpec(memory_space=pl.ANY)] * 8,
        out_specs=[VMEM] * 7,
        out_shape=[
            pltpu.VMEM((n_cols, 2, cap_rows, LANES), f32),
            pltpu.VMEM(static.shape, f32),
            pltpu.VMEM(control.shape, f32),
            pltpu.VMEM(pert.shape, bf16),
        ]
        + [pltpu.VMEM((size, 3 * size), bf16)] * 3,
        scratch_shapes=[
            pltpu.VMEM((coarse, LANES), f32),
            pltpu.VMEM((coarse, LANES), f32),
            pltpu.VMEM((share_rows, LANES), jnp.int32),
            pltpu.VMEM((share_rows, LANES), f32),
            pltpu.VMEM((share_rows, LANES), f32),
            pltpu.VMEM((levels, levels), f32),
            pltpu.VMEM((levels, levels), f32),
            pltpu.SemaphoreType.DMA((8,)),
        ],
        compiler_params=params(16),
        name="slot_sums",
    )(
        in_hbm(obs_slot.reshape(obs_rows, LANES)),
        in_hbm(obs_weight.reshape(obs_rows, LANES)),
        in_hbm(innovation.reshape(obs_rows, LANES)),
        in_hbm(vertical_local),
        in_hbm(vertical_root),
        static,
        control,
        pert,
    )
    before, after, slots = lax.optimization_barrier((before, after, slots))
    other = swapped(jnp.stack([packed, before, after]))
    slots = lax.all_to_all(slots, "cols", split_axis=0, concat_axis=0, tiled=True)

    part = pl.pallas_call(
        forward_kernel,
        in_specs=[VMEM] * 3,
        out_specs=VMEM,
        out_shape=pltpu.VMEM((levels, per_level, LANES), f32),
        compiler_params=params(8),
        name="members_forward",
    )(to_local, control_here, pert_here)

    increment, coefs = pl.pallas_call(
        functools.partial(first_diffusion_kernel, lev_share, rows),
        in_specs=[VMEM] * 4,
        out_specs=[VMEM] * 2,
        out_shape=[
            pltpu.VMEM((lev_share, per_level, LANES), f32),
            pltpu.VMEM((5, 5 * rows, per_level // rows, LANES), f32),
        ],
        compiler_params=params(8),
        name="diffuse_forward",
    )(before, packed, after, other)

    shares = pl.pallas_call(
        lookup_kernel,
        in_specs=[VMEM] * 5,
        out_specs=VMEM,
        out_shape=pltpu.VMEM((n_ens, 3, entry_rows, LANES), f32),
        scratch_shapes=[pltpu.VMEM((cells, 2 * LANES), bf16)],
        compiler_params=params(16),
        name="lookup",
    )(part.reshape(cells, LANES), increment.reshape(own, LANES), entry_row, entry_lane, slots)
    shares = lax.all_to_all(shares, "ens", split_axis=0, concat_axis=0, tiled=True)

    adjoint_own, amounts = pl.pallas_call(
        functools.partial(scatter_own_kernel, cap_rows),
        in_specs=[VMEM] * 3,
        out_specs=[VMEM] * 2,
        out_shape=[pltpu.VMEM((own, LANES), f32), pltpu.VMEM((entry_rows, LANES), f32)],
        scratch_shapes=[pltpu.VMEM((own, 2 * LANES), f32)],
        compiler_params=params(16),
        name="scatter_own",
    )(entry_row, entry_lane, shares)
    tile = adjoint_own.reshape(lev_share, per_level, LANES)
    tile_before, tile_after = shifted(tile, 2), shifted(tile, -2)

    adjoint = pl.pallas_call(
        functools.partial(scatter_rest_kernel, cap_rows),
        in_specs=[VMEM] * 4,
        out_specs=VMEM,
        out_shape=pltpu.VMEM((cells, LANES), f32),
        scratch_shapes=[pltpu.VMEM((cells - own, 2 * LANES), f32)],
        compiler_params=params(16),
        name="scatter_rest",
    )(entry_row, entry_lane, amounts, adjoint_own)
    tile_before, tile_after, adjoint = lax.optimization_barrier((tile_before, tile_after, adjoint))
    tile_other = swapped(jnp.stack([tile, tile_before, tile_after]))

    smooth = pl.pallas_call(
        functools.partial(second_diffusion_kernel, rows),
        in_specs=[VMEM] * 5,
        out_specs=VMEM,
        out_shape=pltpu.VMEM((n_ens, lev_share, per_level, LANES), f32),
        compiler_params=params(8),
        name="diffuse_adjoint",
    )(coefs, tile_before, tile, tile_after, tile_other)
    smooth, adjoint = lax.optimization_barrier((smooth, adjoint))
    smooth = lax.all_to_all(smooth, "ens", split_axis=0, concat_axis=0, tiled=True)

    pair = 2 - members % 2
    ensemble_grad = pl.pallas_call(
        member_kernel,
        grid=(members // pair,),
        in_specs=[VMEM] * 4,
        out_specs=pl.BlockSpec((pair, levels, per_level, LANES), lambda k: (k, 0, 0, 0)),
        out_shape=jax.ShapeDtypeStruct((members, levels, per_level, LANES), f32),
        compiler_params=params(16),
        name="members_gradient",
    )(from_local, adjoint.reshape(levels, per_level, LANES), control_here, pert_here)

    static_grad = pl.pallas_call(
        static_kernel,
        grid=(1,),
        in_specs=[VMEM] * 3,
        out_specs=whole(levels, per_level, LANES),
        out_shape=jax.ShapeDtypeStruct((levels, per_level, LANES), f32),
        compiler_params=params(8),
        name="static_gradient",
    )(from_root, static_here, smooth.reshape(levels, per_level, LANES))
    return (untiled(static_grad, rows), untiled(ensemble_grad, rows))


def solution(mesh):
    placed = (
        P(None, "cols", None),
        P("ens", None, "cols", None),
        P("ens", None, "cols", None),
        P(),
        P(),
        P("cols", None),
        P("cols", None),
        P("cols"),
        P("cols"),
        P("cols"),
        P("cols", None),
        P("cols"),
    )
    return jax.shard_map(
        local,
        mesh=mesh,
        in_specs=placed,
        out_specs=(P(None, "cols", None), P("ens", None, "cols", None)),
        check_vma=False,
    )
```

```python
import functools
import math

import jax
import jax.numpy as jnp
from jax import lax
from jax.experimental import pallas as pl
from jax.experimental.pallas import tpu as pltpu
from jax.sharding import PartitionSpec as P

NDIFF = 4
LANES = 128
FINE = 32
MIB = 1 << 20

f32 = jnp.float32
bf16 = jnp.bfloat16
SMEM = pl.BlockSpec(memory_space=pltpu.SMEM)
VMEM = pl.BlockSpec(memory_space=pltpu.VMEM)


def tiled(field):
    *lead, rows, lon = field.shape
    field = field.reshape(*lead, rows, lon // LANES, LANES)
    return jnp.swapaxes(field, -3, -2).reshape(*lead, rows * lon // LANES, LANES)


def untiled(field, rows):
    *lead, count, lanes = field.shape
    field = field.reshape(*lead, count // rows, rows, lanes)
    return jnp.swapaxes(field, -3, -2).reshape(*lead, rows, count // rows * lanes)


def params(limit, **more):
    return pltpu.CompilerParams(vmem_limit_bytes=limit * MIB, **more)


def halves(x):
    high = x.astype(bf16)
    return high, (x - high.astype(f32)).astype(bf16)


def in_hbm(x):
    return pltpu.with_memory_space_constraint(x, pltpu.HBM)


def spread(row, dtype):
    return jnp.broadcast_to(row, (16, row.shape[1])).astype(dtype)


def matches(index, count):
    ids = lax.broadcasted_iota(jnp.int32, (count, index.shape[1]), 0).astype(jnp.int16)
    return ids.reshape(count // 16, 16, index.shape[1]) == spread(index, jnp.int16)[None]


def placed_at(index, count, amount=None):
    where = matches(index, count)
    amount = bf16(1) if amount is None else spread(amount, bf16)[None]
    return jnp.where(where, amount, bf16(0)).reshape(count, index.shape[1])


def product_nt(left, right):
    return lax.dot_general(left, right, (((1,), (1,)), ((), ())), preferred_element_type=f32)


def over(x, size):
    if size & (size - 1):
        return lax.div(x, jnp.int32(size)), lax.rem(x, jnp.int32(size))
    return lax.shift_right_logical(x, jnp.int32(size.bit_length() - 1)), x & (size - 1)


def prepare_kernel(lev_share, rows, root_ref, count_ref, static_ref, north_ref, east_ref, index_ref, out_ref, row_ref, lane_ref):
    levels, per_level, _ = static_ref.shape
    first = lax.axis_index("ens") * lev_share
    for j in range(lev_share):
        total = root_ref[first + j, 0] * static_ref[0]
        for m in range(1, levels):
            total = total + root_ref[first + j, m] * static_ref[m]
        out_ref[j] = total
    out_ref[lev_share] = north_ref[...]
    out_ref[lev_share + 1] = east_ref[...]
    lists, capacity = index_ref.shape
    lon = per_level // rows * LANES
    pieces = capacity // LANES
    slot = lax.broadcasted_iota(jnp.int32, (1, capacity), 1)
    for q in range(lists):
        cell = index_ref[q : q + 1, :]
        rest, lane = over(cell, LANES)
        rest, block = over(rest, lon // LANES)
        level, row = over(rest, rows)
        grid_row = jnp.where(slot < count_ref[q], level * per_level + block * rows + row, -1)
        for c in range(pieces):
            at = q * pieces + c
            row_ref[at : at + 1, :] = grid_row[:, c * LANES : (c + 1) * LANES]
            lane_ref[at : at + 1, :] = lane[:, c * LANES : (c + 1) * LANES]


def level_product(matrix, transpose):
    levels = matrix.shape[0]
    size = levels * 16
    pick = lax.broadcasted_iota(jnp.int32, (size, levels), 0) // 16
    pick = jnp.where(pick == lax.broadcasted_iota(jnp.int32, (size, levels), 1), f32(1), f32(0)).astype(bf16)
    same = (
        lax.broadcasted_iota(jnp.int32, (size, size), 0) % 16 == lax.broadcasted_iota(jnp.int32, (size, size), 1) % 16
    )
    out = []
    for half in halves(matrix):
        if transpose:
            wide = product_nt(pick, half)
        else:
            wide = jnp.dot(pick, half, preferred_element_type=f32)
        wide = product_nt(wide.astype(bf16), pick)
        out.append(jnp.where(same, wide, f32(0)).astype(bf16))
    return jnp.concatenate([out[0], out[0], out[1]], axis=1)


def three_terms(x):
    high, low = halves(x)
    return jnp.concatenate([high, low, high], axis=0)


def slots_kernel(n_cols, cap_rows, *refs):
    sources, out_ref, (acc_ref, fold_ref), landed, sems = refs[:3], refs[3], refs[4:6], refs[6:9], refs[9]
    coarse = acc_ref.shape[0]
    obs_rows = landed[0].shape[0]
    group = min(8, obs_rows)
    first = pl.multiple_of(lax.axis_index("ens") * obs_rows, obs_rows)
    copies = [
        pltpu.make_async_copy(sources[i].at[pl.ds(first, obs_rows), :], landed[i], sems.at[i]) for i in range(3)
    ]
    for copy in copies:
        copy.start()
    acc_ref[...] = jnp.zeros_like(acc_ref)
    for copy in copies:
        copy.wait()
    slot_ref, weight_ref, innov_ref = landed

    def step(i, carry):
        at = pl.ds(pl.multiple_of(i * group, group), group)
        slot = slot_ref[at, :]
        weight = weight_ref[at, :]
        amount = weight * innov_ref[at, :]
        upper, lower = over(slot, FINE)
        terms = [t.astype(f32) for t in halves(weight) + halves(amount)]
        left, right = [], []
        for r in range(group):
            left.append(placed_at(upper[r : r + 1, :], coarse))
            mask = matches(lower[r : r + 1, :], FINE)
            right.append(
                jnp.concatenate(
                    [
                        jnp.where(mask, spread(t[r : r + 1, :], bf16)[None], bf16(0)).reshape(FINE, LANES)
                        for t in terms
                    ],
                    axis=0,
                )
            )
        acc_ref[...] += product_nt(jnp.concatenate(left, axis=1), jnp.concatenate(right, axis=1))
        return carry

    lax.fori_loop(0, obs_rows // group, step, 0)
    acc = acc_ref[...]
    fold_ref[...] = acc + pltpu.roll(acc, LANES - FINE, 1)
    per_row = LANES // FINE
    lane = lax.broadcasted_iota(jnp.int32, (coarse // per_row, LANES), 1)
    weights = jnp.zeros((coarse // per_row, LANES), f32)
    amounts = jnp.zeros((coarse // per_row, LANES), f32)
    for c in range(per_row):
        piece = fold_ref[pl.ds(c, coarse // per_row, stride=per_row), :]
        here = lane // FINE == c
        weights = jnp.where(here, pltpu.roll(piece, c * FINE, 1) if c else piece, weights)
        shift = (c * FINE - 2 * FINE) % LANES
        amounts = jnp.where(here, pltpu.roll(piece, shift, 1) if shift else piece, amounts)
    for p in range(n_cols):
        out_ref[p, 0] = weights[p * cap_rows : (p + 1) * cap_rows]
        out_ref[p, 1] = amounts[p * cap_rows : (p + 1) * cap_rows]


def forward_kernel(scale, local_ref, control_ref, pert_ref, out_ref, matrix_ref):
    group, levels, per_level, _ = control_ref.shape

    @pl.when(pl.program_id(0) == 0)
    def _():
        matrix_ref[...] = level_product(local_ref[...] * f32(scale), False)
        out_ref[...] = jnp.zeros_like(out_ref)

    def chunk(j, carry):
        at = pl.ds(pl.multiple_of(j * 16, 16), 16)
        terms = [three_terms(control_ref[i, :, at, :].reshape(levels * 16, LANES)) for i in range(group)]
        local = jnp.dot(matrix_ref[...], jnp.concatenate(terms, axis=1), preferred_element_type=f32)
        total = out_ref[:, at, :]
        for i in range(group):
            part = local[:, i * LANES : (i + 1) * LANES].reshape(levels, 16, LANES)
            total = total + pert_ref[i, :, at, :].astype(f32) * part
        out_ref[:, at, :] = total
        return carry

    lax.fori_loop(0, per_level // 16, chunk, 0)


def member_kernel(scale, local_ref, adjoint_ref, control_ref, pert_ref, out_ref, matrix_ref):
    group, levels, per_level, _ = out_ref.shape

    @pl.when(pl.program_id(0) == 0)
    def _():
        matrix_ref[...] = level_product(local_ref[...] * f32(scale), True)

    def chunk(j, carry):
        at = pl.ds(pl.multiple_of(j * 16, 16), 16)
        adjoint = adjoint_ref[:, at, :]
        terms = [
            three_terms((pert_ref[i, :, at, :].astype(f32) * adjoint).reshape(levels * 16, LANES))
            for i in range(group)
        ]
        change = jnp.dot(matrix_ref[...], jnp.concatenate(terms, axis=1), preferred_element_type=f32)
        for i in range(group):
            part = change[:, i * LANES : (i + 1) * LANES].reshape(levels, 16, LANES)
            out_ref[i, :, at, :] = control_ref[i, :, at, :] + part
        return carry

    lax.fori_loop(0, per_level // 16, chunk, 0)


def eastern(x):
    lane = lax.broadcasted_iota(jnp.int32, x.shape, 1)
    near = pltpu.roll(x, LANES - 1, 1)
    return jnp.where(lane == LANES - 1, pltpu.roll(near, x.shape[0] - 1, 0), near)


def western(x):
    lane = lax.broadcasted_iota(jnp.int32, x.shape, 1)
    near = pltpu.roll(x, 1, 1)
    return jnp.where(lane == 0, pltpu.roll(near, 1, 0), near)


def diffuse_rows(tiles, level, coef_ref, rows):
    blocks = tiles[0].shape[1] // rows
    field = [t[level, pl.ds(r, blocks, stride=rows), :] for t in tiles for r in range(rows)]
    for step in range(NDIFF):
        field = [
            coef_ref[0, i + step] * field[i]
            + coef_ref[1, i + step] * field[i - 1]
            + coef_ref[2, i + step] * field[i + 1]
            + coef_ref[3, i + step] * eastern(field[i])
            + coef_ref[4, i + step] * western(field[i])
            for i in range(1, len(field) - 1)
        ]
        field = list(field)
    return field


def tiles_of(before_ref, own_ref, after_ref, other_ref):
    odd = lax.axis_index("cols") % 2
    return [before_ref, other_ref.at[1 - odd], own_ref, other_ref.at[odd], after_ref]


def first_diffusion_kernel(lev_share, rows, before_ref, own_ref, after_ref, other_ref, out_ref, coef_ref):
    tiles = tiles_of(before_ref, own_ref, after_ref, other_ref)
    blocks = own_ref.shape[1] // rows
    side = len(tiles) // 2
    north = [t[lev_share, pl.ds(r, blocks, stride=rows), :] for t in tiles for r in range(rows)]
    east = [t[lev_share + 1, pl.ds(r, blocks, stride=rows), :] for t in tiles for r in range(rows)]
    for i in range(1, len(north) - 1):
        south = north[i + 1]
        if (i + 1) % rows == 0 and i < side * rows:
            south = south * jnp.where(lax.axis_index("cols") == side - (i + 1) // rows, f32(0), f32(1))
        west = western(east[i])
        coef_ref[0, i] = 1.0 - north[i] - south - east[i] - west
        coef_ref[1, i] = north[i]
        coef_ref[2, i] = south
        coef_ref[3, i] = east[i]
        coef_ref[4, i] = west
    for i in (0, len(north) - 1):
        for c in range(5):
            coef_ref[c, i] = jnp.zeros_like(north[0])

    def body(level, carry):
        final = diffuse_rows(tiles, level, coef_ref, rows)
        for r in range(rows):
            out_ref[level, pl.ds(r, blocks, stride=rows), :] = final[r]
        return carry

    lax.fori_loop(0, lev_share, body, 0)


def second_diffusion_kernel(rows, coef_ref, before_ref, own_ref, after_ref, other_ref, out_ref):
    tiles = tiles_of(before_ref, own_ref, after_ref, other_ref)
    copies, lev_share = out_ref.shape[:2]
    blocks = own_ref.shape[1] // rows

    def body(level, carry):
        final = diffuse_rows(tiles, level, coef_ref, rows)
        for copy in range(copies):
            for r in range(rows):
                out_ref[copy, level, pl.ds(r, blocks, stride=rows), :] = final[r]
        return carry

    lax.fori_loop(0, lev_share, body, 0)


def lookup_kernel(part_ref, static_ref, row_ref, lane_ref, slots_ref, out_ref, terms_ref):
    cells = part_ref.shape[0]
    own = static_ref.shape[0]
    n_lists, _, cap_rows, _ = slots_ref.shape
    at = pl.ds(pl.multiple_of(lax.axis_index("ens") * own, own), own)
    for here, field in ((slice(None), part_ref[...]), (at, part_ref[at, :] + static_ref[...])):
        high, low = halves(field)
        terms_ref[here, :LANES] = high
        terms_ref[here, LANES:] = low
    ids16 = lax.broadcasted_iota(jnp.int32, (LANES, cells), 1).astype(jnp.int16)
    ids = lax.broadcasted_iota(jnp.int32, (LANES, LANES), 1)
    diagonal = ids == lax.broadcasted_iota(jnp.int32, (LANES, LANES), 0)

    def look(q, carry):
        at = pl.ds(pl.multiple_of(q * cap_rows, cap_rows), cap_rows)
        rows = row_ref[at, :].astype(f32).T
        lanes = lane_ref[at, :].astype(f32).T
        picks = []
        for c in range(cap_rows):
            column = jnp.broadcast_to(rows[:, c : c + 1], (LANES, LANES)).astype(jnp.int32).astype(jnp.int16)
            column = jnp.concatenate([column] * (cells // LANES), axis=1)
            picks.append(jnp.where(ids16 == column, bf16(1), bf16(0)))
        got = jnp.dot(jnp.concatenate(picks, axis=0), terms_ref[...], preferred_element_type=f32)
        values = []
        for c in range(cap_rows):
            mask = ids == jnp.broadcast_to(lanes[:, c : c + 1], (LANES, LANES)).astype(jnp.int32)
            mine = got[c * LANES : (c + 1) * LANES]
            found = jnp.sum(jnp.where(mask, mine[:, :LANES] + mine[:, LANES:], f32(0)), axis=1, keepdims=True)
            values.append(jnp.sum(jnp.where(diagonal, found, f32(0)), axis=0, keepdims=True))
        out_ref[0, at, :] = jnp.concatenate(values, axis=0)
        out_ref[1, at, :] = slots_ref[q, 0]
        out_ref[2, at, :] = slots_ref[q, 1]
        return carry

    lax.fori_loop(0, n_lists, look, 0)


def put(acc_ref, rows, lanes, amounts):
    high, low = (h.astype(f32) for h in halves(amounts))
    left, right = [], []
    for c in range(rows.shape[0]):
        piece = slice(c, c + 1)
        left.append(placed_at(rows[piece, :], acc_ref.shape[0]))
        mask = matches(lanes[piece, :], LANES)
        right.append(
            jnp.concatenate(
                [
                    jnp.where(mask, spread(h[piece, :], bf16)[None], bf16(0)).reshape(LANES, LANES)
                    for h in (high, low)
                ],
                axis=0,
            )
        )
    acc_ref[...] += product_nt(jnp.concatenate(left, axis=1), jnp.concatenate(right, axis=1))


def scatter_own_kernel(cap_rows, row_ref, lane_ref, *refs):
    shares, (out_ref, amount_ref, acc_ref) = refs[:-3], refs[-3:]
    own = out_ref.shape[0]
    first = lax.axis_index("ens") * own
    acc_ref[...] = jnp.zeros_like(acc_ref)

    def step(q, carry):
        at = pl.ds(pl.multiple_of(q * cap_rows, cap_rows), cap_rows)
        value, weight, amount = (functools.reduce(jnp.add, [s[t, at, :] for s in shares]) for t in range(3))
        amounts = value * weight - amount
        amount_ref[at, :] = amounts
        put(acc_ref, row_ref[at, :] - first, lane_ref[at, :], amounts)
        return carry

    lax.fori_loop(0, row_ref.shape[0] // cap_rows, step, 0)
    out_ref[...] = acc_ref[:, :LANES] + acc_ref[:, LANES:]


def scatter_rest_kernel(cap_rows, row_ref, lane_ref, amount_ref, own_ref, out_ref, acc_ref):
    cells = out_ref.shape[0]
    own = own_ref.shape[0]
    n_ens = cells // own
    me = lax.axis_index("ens")
    first = (me + 1) * own
    acc_ref[...] = jnp.zeros_like(acc_ref)

    def step(q, carry):
        at = pl.ds(pl.multiple_of(q * cap_rows, cap_rows), cap_rows)
        row = row_ref[at, :]
        turned = row - first
        turned = jnp.where(row < 0, -1, jnp.where(turned < 0, turned + cells, turned))
        put(acc_ref, turned, lane_ref[at, :], amount_ref[at, :])
        return carry

    lax.fori_loop(0, row_ref.shape[0] // cap_rows, step, 0)
    out_ref[pl.ds(pl.multiple_of(me * own, own), own), :] = own_ref[...]
    for t in range(1, n_ens):
        to = pl.ds(pl.multiple_of((me + t) % n_ens * own, own), own)
        piece = acc_ref[(t - 1) * own : t * own, :]
        out_ref[to, :] = piece[:, :LANES] + piece[:, LANES:]


def static_kernel(root_ref, static_ref, smooth_ref, out_ref):
    levels, per_level, _ = static_ref.shape
    matrix = level_product(root_ref[...], True)
    for j in range(0, per_level, 32):
        terms = [
            three_terms(smooth_ref[:, j + i : j + i + 16, :].reshape(levels * 16, LANES)) for i in (0, 16)
        ]
        change = jnp.dot(matrix, jnp.concatenate(terms, axis=1), preferred_element_type=f32)
        for i, part in ((0, change[:, :LANES]), (16, change[:, LANES:])):
            at = slice(j + i, j + i + 16)
            out_ref[:, at, :] = static_ref[:, at, :] + part.reshape(levels, 16, LANES)


def shifted(x, by):
    count = lax.axis_size("cols")
    return lax.ppermute(x, "cols", [(i, i + by) for i in range(count) if 0 <= i + by < count])


def swapped(own, before, after):
    odd = lax.axis_index("cols") % 2
    count = lax.axis_size("cols")
    pack = jnp.stack([own, jnp.where(odd == 1, before, after)])
    return lax.ppermute(pack, "cols", [(i, i ^ 1) for i in range(count)])


def local(
    static_control,
    ensemble_control,
    perturbations,
    vertical_root,
    vertical_local,
    face_north,
    face_east,
    innovation,
    obs_weight,
    obs_slot,
    send_index,
    send_count,
):
    n_ens = lax.axis_size("ens")
    n_cols = lax.axis_size("cols")
    members, levels, rows, lon = ensemble_control.shape
    per_level = rows * lon // LANES
    cells = levels * per_level
    lev_share = levels // n_ens
    own = lev_share * per_level
    lists, capacity = send_index.shape
    cap_rows = capacity // LANES
    entry_rows = lists * cap_rows
    member_scale = 1.0 / math.sqrt(members * n_ens - 1)

    static = in_hbm(tiled(static_control))
    control = in_hbm(tiled(ensemble_control))
    pert = in_hbm(tiled(perturbations))

    def whole(*shape):
        return pl.BlockSpec(shape, lambda i: (0,) * len(shape))

    packed, entry_row, entry_lane = pl.pallas_call(
        functools.partial(prepare_kernel, lev_share, rows),
        grid=(1,),
        in_specs=[
            SMEM,
            SMEM,
            whole(levels, per_level, LANES),
            whole(per_level, LANES),
            whole(per_level, LANES),
            whole(lists, capacity),
        ],
        out_specs=[VMEM] * 3,
        out_shape=[
            pltpu.VMEM((lev_share + 2, per_level, LANES), f32),
            pltpu.VMEM((entry_rows, LANES), jnp.int32),
            pltpu.VMEM((entry_rows, LANES), jnp.int32),
        ],
        compiler_params=params(8),
        name="prepare",
    )(
        in_hbm(vertical_root),
        in_hbm(send_count),
        static,
        in_hbm(tiled(face_north)),
        in_hbm(tiled(face_east)),
        in_hbm(send_index),
    )
    before, after = shifted(packed, 2), shifted(packed, -2)

    obs_rows = obs_slot.shape[0] // LANES
    share_rows = obs_rows // n_ens
    coarse = n_cols * capacity // FINE
    size = levels * 16
    obs_slot, packed = lax.optimization_barrier((obs_slot, packed))
    slots = pl.pallas_call(
        functools.partial(slots_kernel, n_cols, cap_rows),
        in_specs=[pl.BlockSpec(memory_space=pl.ANY)] * 3,
        out_specs=VMEM,
        out_shape=pltpu.VMEM((n_cols, 2, cap_rows, LANES), f32),
        scratch_shapes=[
            pltpu.VMEM((coarse, LANES), f32),
            pltpu.VMEM((coarse, LANES), f32),
            pltpu.VMEM((share_rows, LANES), jnp.int32),
            pltpu.VMEM((share_rows, LANES), f32),
            pltpu.VMEM((share_rows, LANES), f32),
            pltpu.SemaphoreType.DMA((3,)),
        ],
        compiler_params=params(16),
        name="slot_sums",
    )(
        in_hbm(obs_slot.reshape(obs_rows, LANES)),
        in_hbm(obs_weight.reshape(obs_rows, LANES)),
        in_hbm(innovation.reshape(obs_rows, LANES)),
    )
    before, after, slots = lax.optimization_barrier((before, after, slots))
    other = swapped(packed, before, after)
    slots = lax.all_to_all(slots, "cols", split_axis=0, concat_axis=0, tiled=True)

    group = 2 - members % 2
    member_spec = pl.BlockSpec((group, levels, per_level, LANES), lambda k: (k, 0, 0, 0))
    matrix_scratch = [pltpu.VMEM((size, 3 * size), bf16)]
    part = pl.pallas_call(
        functools.partial(forward_kernel, member_scale),
        grid=(members // group,),
        in_specs=[whole(levels, levels), member_spec, member_spec],
        out_specs=VMEM,
        out_shape=pltpu.VMEM((levels, per_level, LANES), f32),
        scratch_shapes=matrix_scratch,
        compiler_params=params(16),
        name="members_forward",
    )(in_hbm(vertical_local), control, pert)

    increment, coefs = pl.pallas_call(
        functools.partial(first_diffusion_kernel, lev_share, rows),
        in_specs=[VMEM] * 4,
        out_specs=[VMEM] * 2,
        out_shape=[
            pltpu.VMEM((lev_share, per_level, LANES), f32),
            pltpu.VMEM((5, 5 * rows, per_level // rows, LANES), f32),
        ],
        compiler_params=params(8),
        name="diffuse_forward",
    )(before, packed, after, other)

    share = pl.pallas_call(
        lookup_kernel,
        in_specs=[VMEM] * 5,
        out_specs=VMEM,
        out_shape=pltpu.VMEM((3, entry_rows, LANES), f32),
        scratch_shapes=[pltpu.VMEM((cells, 2 * LANES), bf16)],
        compiler_params=params(16),
        name="lookup",
    )(part.reshape(cells, LANES), increment.reshape(own, LANES), entry_row, entry_lane, slots)
    shares = [share] + [
        lax.ppermute(share, "ens", [((i + d) % n_ens, i) for i in range(n_ens)]) for d in range(1, n_ens)
    ]

    adjoint_own, amounts = pl.pallas_call(
        functools.partial(scatter_own_kernel, cap_rows),
        in_specs=[VMEM] * (2 + n_ens),
        out_specs=[VMEM] * 2,
        out_shape=[pltpu.VMEM((own, LANES), f32), pltpu.VMEM((entry_rows, LANES), f32)],
        scratch_shapes=[pltpu.VMEM((own, 2 * LANES), f32)],
        compiler_params=params(16),
        name="scatter_own",
    )(entry_row, entry_lane, *shares)
    tile = adjoint_own.reshape(lev_share, per_level, LANES)
    tile_before, tile_after = shifted(tile, 2), shifted(tile, -2)

    adjoint = pl.pallas_call(
        functools.partial(scatter_rest_kernel, cap_rows),
        in_specs=[VMEM] * 4,
        out_specs=VMEM,
        out_shape=pltpu.VMEM((cells, LANES), f32),
        scratch_shapes=[pltpu.VMEM((cells - own, 2 * LANES), f32)],
        compiler_params=params(16),
        name="scatter_rest",
    )(entry_row, entry_lane, amounts, adjoint_own)
    tile_before, tile_after, adjoint = lax.optimization_barrier((tile_before, tile_after, adjoint))
    tile_other = swapped(tile, tile_before, tile_after)

    smooth = pl.pallas_call(
        functools.partial(second_diffusion_kernel, rows),
        in_specs=[VMEM] * 5,
        out_specs=VMEM,
        out_shape=jax.ShapeDtypeStruct((n_ens, lev_share, per_level, LANES), f32),
        compiler_params=params(8),
        name="diffuse_adjoint",
    )(coefs, tile_before, tile, tile_after, tile_other)
    smooth, adjoint = lax.optimization_barrier((smooth, adjoint))
    smooth = lax.all_to_all(smooth, "ens", split_axis=0, concat_axis=0, tiled=True)

    ensemble_grad = pl.pallas_call(
        functools.partial(member_kernel, member_scale),
        grid=(members // group,),
        in_specs=[whole(levels, levels), VMEM, member_spec, member_spec],
        out_specs=member_spec,
        out_shape=jax.ShapeDtypeStruct((members, levels, per_level, LANES), f32),
        scratch_shapes=matrix_scratch,
        compiler_params=params(16),
        name="members_gradient",
    )(in_hbm(vertical_local), adjoint.reshape(levels, per_level, LANES), control, pert)

    static_grad = pl.pallas_call(
        static_kernel,
        grid=(1,),
        in_specs=[whole(levels, levels), whole(levels, per_level, LANES), VMEM],
        out_specs=whole(levels, per_level, LANES),
        out_shape=jax.ShapeDtypeStruct((levels, per_level, LANES), f32),
        compiler_params=params(8),
        name="static_gradient",
    )(in_hbm(vertical_root), static, smooth.reshape(levels, per_level, LANES))
    return (untiled(static_grad, rows), untiled(ensemble_grad, rows))


def solution(mesh):
    placed = (
        P(None, "cols", None),
        P("ens", None, "cols", None),
        P("ens", None, "cols", None),
        P(),
        P(),
        P("cols", None),
        P("cols", None),
        P("cols"),
        P("cols"),
        P("cols"),
        P("cols", None),
        P("cols"),
    )
    return jax.shard_map(
        local,
        mesh=mesh,
        in_specs=placed,
        out_specs=(P(None, "cols", None), P("ens", None, "cols", None)),
        check_vma=False,
    )
```

```python
import functools
import math

import jax
import jax.numpy as jnp
from jax import lax
from jax.experimental import pallas as pl
from jax.experimental.pallas import tpu as pltpu
from jax.sharding import PartitionSpec as P

NDIFF = 4
LANES = 128
FINE = 32
MIB = 1 << 20

f32 = jnp.float32
bf16 = jnp.bfloat16
SMEM = pl.BlockSpec(memory_space=pltpu.SMEM)
VMEM = pl.BlockSpec(memory_space=pltpu.VMEM)


def tiled(field):
    *lead, rows, lon = field.shape
    field = field.reshape(*lead, rows, lon // LANES, LANES)
    return jnp.swapaxes(field, -3, -2).reshape(*lead, rows * lon // LANES, LANES)


def untiled(field, rows):
    *lead, count, lanes = field.shape
    field = field.reshape(*lead, count // rows, rows, lanes)
    return jnp.swapaxes(field, -3, -2).reshape(*lead, rows, count // rows * lanes)


def params(limit, **more):
    return pltpu.CompilerParams(vmem_limit_bytes=limit * MIB, **more)


def halves(x):
    high = x.astype(bf16)
    return high, (x - high.astype(f32)).astype(bf16)


def in_hbm(x):
    return pltpu.with_memory_space_constraint(x, pltpu.HBM)


def spread(row, dtype):
    return jnp.broadcast_to(row, (16, row.shape[1])).astype(dtype)


def matches(index, count):
    ids = lax.broadcasted_iota(jnp.int32, (count, index.shape[1]), 0).astype(jnp.int16)
    return ids.reshape(count // 16, 16, index.shape[1]) == spread(index, jnp.int16)[None]


def placed_at(index, count, amount=None):
    where = matches(index, count)
    amount = bf16(1) if amount is None else spread(amount, bf16)[None]
    return jnp.where(where, amount, bf16(0)).reshape(count, index.shape[1])


def product_nt(left, right):
    return lax.dot_general(left, right, (((1,), (1,)), ((), ())), preferred_element_type=f32)


def over(x, size):
    if size & (size - 1):
        return lax.div(x, jnp.int32(size)), lax.rem(x, jnp.int32(size))
    return lax.shift_right_logical(x, jnp.int32(size.bit_length() - 1)), x & (size - 1)


def prepare_kernel(lev_share, rows, root_ref, count_ref, static_ref, north_ref, east_ref, index_ref, out_ref, row_ref, lane_ref):
    levels, per_level, _ = static_ref.shape
    first = lax.axis_index("ens") * lev_share
    for j in range(lev_share):
        total = root_ref[first + j, 0] * static_ref[0]
        for m in range(1, levels):
            total = total + root_ref[first + j, m] * static_ref[m]
        out_ref[j] = total
    out_ref[lev_share] = north_ref[...]
    out_ref[lev_share + 1] = east_ref[...]
    lists, capacity = index_ref.shape
    lon = per_level // rows * LANES
    pieces = capacity // LANES
    slot = lax.broadcasted_iota(jnp.int32, (1, capacity), 1)
    for q in range(lists):
        cell = index_ref[q : q + 1, :]
        rest, lane = over(cell, LANES)
        rest, block = over(rest, lon // LANES)
        level, row = over(rest, rows)
        grid_row = jnp.where(slot < count_ref[q], level * per_level + block * rows + row, -1)
        for c in range(pieces):
            at = q * pieces + c
            row_ref[at : at + 1, :] = grid_row[:, c * LANES : (c + 1) * LANES]
            lane_ref[at : at + 1, :] = lane[:, c * LANES : (c + 1) * LANES]


def level_product(matrix, transpose):
    levels = matrix.shape[0]
    size = levels * 16
    pick = lax.broadcasted_iota(jnp.int32, (size, levels), 0) // 16
    pick = jnp.where(pick == lax.broadcasted_iota(jnp.int32, (size, levels), 1), f32(1), f32(0)).astype(bf16)
    same = (
        lax.broadcasted_iota(jnp.int32, (size, size), 0) % 16 == lax.broadcasted_iota(jnp.int32, (size, size), 1) % 16
    )
    out = []
    for half in halves(matrix):
        if transpose:
            wide = product_nt(pick, half)
        else:
            wide = jnp.dot(pick, half, preferred_element_type=f32)
        wide = product_nt(wide.astype(bf16), pick)
        out.append(jnp.where(same, wide, f32(0)).astype(bf16))
    return jnp.concatenate([out[0], out[0], out[1]], axis=1)


def three_terms(x):
    high, low = halves(x)
    return jnp.concatenate([high, low, high], axis=0)


def observe_kernel(n_cols, cap_rows, scale, *refs):
    sources, (out_ref, part_ref), (acc_ref, fold_ref, matrix_ref), landed, sems = (
        refs[:6],
        refs[6:8],
        refs[8:11],
        refs[11:17],
        refs[17],
    )
    coarse = acc_ref.shape[0]
    obs_rows = landed[0].shape[0]
    group = min(8, obs_rows)
    first = pl.multiple_of(lax.axis_index("ens") * obs_rows, obs_rows)
    copies = [
        pltpu.make_async_copy(sources[i].at[pl.ds(first, obs_rows), :], landed[i], sems.at[i]) for i in range(3)
    ]
    copies += [pltpu.make_async_copy(sources[i], landed[i], sems.at[i]) for i in range(3, 6)]
    for copy in copies:
        copy.start()
    acc_ref[...] = jnp.zeros_like(acc_ref)
    for copy in copies[:3]:
        copy.wait()
    slot_ref, weight_ref, innov_ref, local_ref, control_ref, pert_ref = landed

    def step(i, carry):
        at = pl.ds(pl.multiple_of(i * group, group), group)
        slot = slot_ref[at, :]
        weight = weight_ref[at, :]
        amount = weight * innov_ref[at, :]
        upper, lower = over(slot, FINE)
        terms = [t.astype(f32) for t in halves(weight) + halves(amount)]
        left, right = [], []
        for r in range(group):
            left.append(placed_at(upper[r : r + 1, :], coarse))
            mask = matches(lower[r : r + 1, :], FINE)
            right.append(
                jnp.concatenate(
                    [
                        jnp.where(mask, spread(t[r : r + 1, :], bf16)[None], bf16(0)).reshape(FINE, LANES)
                        for t in terms
                    ],
                    axis=0,
                )
            )
        acc_ref[...] += product_nt(jnp.concatenate(left, axis=1), jnp.concatenate(right, axis=1))
        return carry

    lax.fori_loop(0, obs_rows // group, step, 0)
    acc = acc_ref[...]
    fold_ref[...] = acc + pltpu.roll(acc, LANES - FINE, 1)
    per_row = LANES // FINE
    lane = lax.broadcasted_iota(jnp.int32, (coarse // per_row, LANES), 1)
    weights = jnp.zeros((coarse // per_row, LANES), f32)
    amounts = jnp.zeros((coarse // per_row, LANES), f32)
    for c in range(per_row):
        piece = fold_ref[pl.ds(c, coarse // per_row, stride=per_row), :]
        here = lane // FINE == c
        weights = jnp.where(here, pltpu.roll(piece, c * FINE, 1) if c else piece, weights)
        shift = (c * FINE - 2 * FINE) % LANES
        amounts = jnp.where(here, pltpu.roll(piece, shift, 1) if shift else piece, amounts)
    for p in range(n_cols):
        out_ref[p, 0] = weights[p * cap_rows : (p + 1) * cap_rows]
        out_ref[p, 1] = amounts[p * cap_rows : (p + 1) * cap_rows]
    for copy in copies[3:]:
        copy.wait()
    matrix_ref[...] = level_product(local_ref[...] * f32(scale), False)
    sum_members(matrix_ref, control_ref, pert_ref, part_ref)


def sum_members(matrix_ref, control_ref, pert_ref, out_ref):
    members, levels, per_level, _ = control_ref.shape
    group = 2 - members % 2

    def chunk(j, carry):
        at = pl.ds(pl.multiple_of(j * 16, 16), 16)
        total = jnp.zeros((levels * 16, LANES), f32)
        for k in range(0, members, group):
            terms = [three_terms(control_ref[k + i, :, at, :].reshape(levels * 16, LANES)) for i in range(group)]
            local = jnp.dot(matrix_ref[...], jnp.concatenate(terms, axis=1), preferred_element_type=f32)
            for i in range(group):
                pert = pert_ref[k + i, :, at, :].astype(f32).reshape(levels * 16, LANES)
                total = total + pert * local[:, i * LANES : (i + 1) * LANES]
        out_ref[:, at, :] = total.reshape(levels, 16, LANES)
        return carry

    lax.fori_loop(0, per_level // 16, chunk, 0)


def member_kernel(matrix_ref, adjoint_ref, control_ref, pert_ref, out_ref):
    group, levels, per_level, _ = out_ref.shape
    first = pl.program_id(0) * group

    def chunk(j, carry):
        at = pl.ds(pl.multiple_of(j * 16, 16), 16)
        adjoint = adjoint_ref[:, at, :]
        terms = [
            three_terms((pert_ref[first + i, :, at, :].astype(f32) * adjoint).reshape(levels * 16, LANES))
            for i in range(group)
        ]
        change = jnp.dot(matrix_ref[...], jnp.concatenate(terms, axis=1), preferred_element_type=f32)
        for i in range(group):
            part = change[:, i * LANES : (i + 1) * LANES].reshape(levels, 16, LANES)
            out_ref[i, :, at, :] = control_ref[first + i, :, at, :] + part
        return carry

    lax.fori_loop(0, per_level // 16, chunk, 0)


def eastern(x):
    lane = lax.broadcasted_iota(jnp.int32, x.shape, 1)
    near = pltpu.roll(x, LANES - 1, 1)
    return jnp.where(lane == LANES - 1, pltpu.roll(near, x.shape[0] - 1, 0), near)


def western(x):
    lane = lax.broadcasted_iota(jnp.int32, x.shape, 1)
    near = pltpu.roll(x, 1, 1)
    return jnp.where(lane == 0, pltpu.roll(near, 1, 0), near)


def diffuse_rows(tiles, level, coef_ref, rows):
    blocks = tiles[0].shape[1] // rows
    field = [t[level, pl.ds(r, blocks, stride=rows), :] for t in tiles for r in range(rows)]
    for step in range(NDIFF):
        field = [
            coef_ref[0, i + step] * field[i]
            + coef_ref[1, i + step] * field[i - 1]
            + coef_ref[2, i + step] * field[i + 1]
            + coef_ref[3, i + step] * eastern(field[i])
            + coef_ref[4, i + step] * western(field[i])
            for i in range(1, len(field) - 1)
        ]
        field = list(field)
    return field


def tiles_of(before_ref, own_ref, after_ref, other_ref):
    odd = lax.axis_index("cols") % 2
    return [before_ref, other_ref.at[1 - odd], own_ref, other_ref.at[odd], after_ref]


def first_diffusion_kernel(lev_share, rows, before_ref, own_ref, after_ref, other_ref, out_ref, coef_ref):
    tiles = tiles_of(before_ref, own_ref, after_ref, other_ref)
    blocks = own_ref.shape[1] // rows
    side = len(tiles) // 2
    north = [t[lev_share, pl.ds(r, blocks, stride=rows), :] for t in tiles for r in range(rows)]
    east = [t[lev_share + 1, pl.ds(r, blocks, stride=rows), :] for t in tiles for r in range(rows)]
    for i in range(1, len(north) - 1):
        south = north[i + 1]
        if (i + 1) % rows == 0 and i < side * rows:
            south = south * jnp.where(lax.axis_index("cols") == side - (i + 1) // rows, f32(0), f32(1))
        west = western(east[i])
        coef_ref[0, i] = 1.0 - north[i] - south - east[i] - west
        coef_ref[1, i] = north[i]
        coef_ref[2, i] = south
        coef_ref[3, i] = east[i]
        coef_ref[4, i] = west
    for i in (0, len(north) - 1):
        for c in range(5):
            coef_ref[c, i] = jnp.zeros_like(north[0])

    def body(level, carry):
        final = diffuse_rows(tiles, level, coef_ref, rows)
        for r in range(rows):
            out_ref[level, pl.ds(r, blocks, stride=rows), :] = final[r]
        return carry

    lax.fori_loop(0, lev_share, body, 0)


def second_diffusion_kernel(rows, coef_ref, before_ref, own_ref, after_ref, other_ref, out_ref):
    tiles = tiles_of(before_ref, own_ref, after_ref, other_ref)
    lev_share = out_ref.shape[0]
    blocks = own_ref.shape[1] // rows

    def body(level, carry):
        final = diffuse_rows(tiles, level, coef_ref, rows)
        for r in range(rows):
            out_ref[level, pl.ds(r, blocks, stride=rows), :] = final[r]
        return carry

    lax.fori_loop(0, lev_share, body, 0)


def lookup_kernel(cap_rows, part_ref, static_ref, row_ref, lane_ref, out_ref, terms_ref):
    cells = part_ref.shape[0]
    own = static_ref.shape[0]
    n_lists = row_ref.shape[0] // cap_rows
    at = pl.ds(pl.multiple_of(lax.axis_index("ens") * own, own), own)
    for here, field in ((slice(None), part_ref[...]), (at, part_ref[at, :] + static_ref[...])):
        high, low = halves(field)
        terms_ref[here, :LANES] = high
        terms_ref[here, LANES:] = low
    ids16 = lax.broadcasted_iota(jnp.int32, (LANES, cells), 1).astype(jnp.int16)
    ids = lax.broadcasted_iota(jnp.int32, (LANES, LANES), 1)
    diagonal = ids == lax.broadcasted_iota(jnp.int32, (LANES, LANES), 0)

    def look(q, carry):
        at = pl.ds(pl.multiple_of(q * cap_rows, cap_rows), cap_rows)
        rows = row_ref[at, :].astype(f32).T
        lanes = lane_ref[at, :].astype(f32).T
        picks = []
        for c in range(cap_rows):
            column = jnp.broadcast_to(rows[:, c : c + 1], (LANES, LANES)).astype(jnp.int32).astype(jnp.int16)
            column = jnp.concatenate([column] * (cells // LANES), axis=1)
            picks.append(jnp.where(ids16 == column, bf16(1), bf16(0)))
        got = jnp.dot(jnp.concatenate(picks, axis=0), terms_ref[...], preferred_element_type=f32)
        values = []
        for c in range(cap_rows):
            mask = ids == jnp.broadcast_to(lanes[:, c : c + 1], (LANES, LANES)).astype(jnp.int32)
            mine = got[c * LANES : (c + 1) * LANES]
            found = jnp.sum(jnp.where(mask, mine[:, :LANES] + mine[:, LANES:], f32(0)), axis=1, keepdims=True)
            values.append(jnp.sum(jnp.where(diagonal, found, f32(0)), axis=0, keepdims=True))
        out_ref[at, :] = jnp.concatenate(values, axis=0)
        return carry

    lax.fori_loop(0, n_lists, look, 0)


def put(acc_ref, rows, lanes, amounts):
    high, low = (h.astype(f32) for h in halves(amounts))
    left, right = [], []
    for c in range(rows.shape[0]):
        piece = slice(c, c + 1)
        left.append(placed_at(rows[piece, :], acc_ref.shape[0]))
        mask = matches(lanes[piece, :], LANES)
        right.append(
            jnp.concatenate(
                [
                    jnp.where(mask, spread(h[piece, :], bf16)[None], bf16(0)).reshape(LANES, LANES)
                    for h in (high, low)
                ],
                axis=0,
            )
        )
    acc_ref[...] += product_nt(jnp.concatenate(left, axis=1), jnp.concatenate(right, axis=1))


def scatter_own_kernel(cap_rows, row_ref, lane_ref, *refs):
    shares, (out_ref, amount_ref, acc_ref) = refs[:-3], refs[-3:]
    own = out_ref.shape[0]
    first = lax.axis_index("ens") * own
    acc_ref[...] = jnp.zeros_like(acc_ref)

    def step(q, carry):
        at = pl.ds(pl.multiple_of(q * cap_rows, cap_rows), cap_rows)
        value, weight, amount = (functools.reduce(jnp.add, [s[t, at, :] for s in shares]) for t in range(3))
        amounts = value * weight - amount
        amount_ref[at, :] = amounts
        put(acc_ref, row_ref[at, :] - first, lane_ref[at, :], amounts)
        return carry

    lax.fori_loop(0, row_ref.shape[0] // cap_rows, step, 0)
    out_ref[...] = acc_ref[:, :LANES] + acc_ref[:, LANES:]


def scatter_rest_kernel(cap_rows, scale, row_ref, lane_ref, amount_ref, own_ref, *refs):
    sources, out_ref, kept, matrices, acc_ref, landed, sems = (
        refs[:5],
        refs[5],
        refs[6:9],
        refs[9:11],
        refs[11],
        refs[12:14],
        refs[14],
    )
    copies = [pltpu.make_async_copy(s, t, sems.at[i]) for i, (s, t) in enumerate(zip(sources, (*landed, *kept)))]
    for copy in copies:
        copy.start()
    cells = out_ref.shape[0]
    own = own_ref.shape[0]
    n_ens = cells // own
    me = lax.axis_index("ens")
    first = (me + 1) * own
    acc_ref[...] = jnp.zeros_like(acc_ref)

    def step(q, carry):
        at = pl.ds(pl.multiple_of(q * cap_rows, cap_rows), cap_rows)
        row = row_ref[at, :]
        turned = row - first
        turned = jnp.where(row < 0, -1, jnp.where(turned < 0, turned + cells, turned))
        put(acc_ref, turned, lane_ref[at, :], amount_ref[at, :])
        return carry

    lax.fori_loop(0, row_ref.shape[0] // cap_rows, step, 0)
    out_ref[pl.ds(pl.multiple_of(me * own, own), own), :] = own_ref[...]
    for t in range(1, n_ens):
        to = pl.ds(pl.multiple_of((me + t) % n_ens * own, own), own)
        piece = acc_ref[(t - 1) * own : t * own, :]
        out_ref[to, :] = piece[:, :LANES] + piece[:, LANES:]
    for copy in copies:
        copy.wait()
    matrices[0][...] = level_product(landed[0][...] * f32(scale), True)
    matrices[1][...] = level_product(landed[1][...], True)


def static_kernel(matrix_ref, static_ref, *refs):
    parts, (out_ref, smooth_ref) = refs[:-2], refs[-2:]
    levels, per_level, _ = static_ref.shape
    share = levels // len(parts)
    me = lax.axis_index("ens")
    for d, part in enumerate(parts):
        smooth_ref[pl.ds((me + d) % len(parts) * share, share)] = part[...]
    for j in range(0, per_level, 32):
        terms = [three_terms(smooth_ref[:, j + i : j + i + 16, :].reshape(levels * 16, LANES)) for i in (0, 16)]
        change = jnp.dot(matrix_ref[...], jnp.concatenate(terms, axis=1), preferred_element_type=f32)
        for i, part in ((0, change[:, :LANES]), (16, change[:, LANES:])):
            at = slice(j + i, j + i + 16)
            out_ref[:, at, :] = static_ref[:, at, :] + part.reshape(levels, 16, LANES)


def shifted(x, by):
    count = lax.axis_size("cols")
    return lax.ppermute(x, "cols", [(i, i + by) for i in range(count) if 0 <= i + by < count])


def from_peers(x):
    count = lax.axis_size("ens")
    return [lax.ppermute(x, "ens", [((i + d) % count, i) for i in range(count)]) for d in range(1, count)]


def swapped(own, before, after):
    odd = lax.axis_index("cols") % 2
    count = lax.axis_size("cols")
    pack = jnp.stack([own, jnp.where(odd == 1, before, after)])
    return lax.ppermute(pack, "cols", [(i, i ^ 1) for i in range(count)])


def local(
    static_control,
    ensemble_control,
    perturbations,
    vertical_root,
    vertical_local,
    face_north,
    face_east,
    innovation,
    obs_weight,
    obs_slot,
    send_index,
    send_count,
):
    n_ens = lax.axis_size("ens")
    n_cols = lax.axis_size("cols")
    members, levels, rows, lon = ensemble_control.shape
    per_level = rows * lon // LANES
    cells = levels * per_level
    lev_share = levels // n_ens
    own = lev_share * per_level
    lists, capacity = send_index.shape
    cap_rows = capacity // LANES
    entry_rows = lists * cap_rows
    member_scale = 1.0 / math.sqrt(members * n_ens - 1)

    static = in_hbm(tiled(static_control))
    control = in_hbm(tiled(ensemble_control))
    pert = in_hbm(tiled(perturbations))

    def whole(*shape):
        return pl.BlockSpec(shape, lambda i: (0,) * len(shape))

    packed, entry_row, entry_lane = pl.pallas_call(
        functools.partial(prepare_kernel, lev_share, rows),
        grid=(1,),
        in_specs=[
            SMEM,
            SMEM,
            whole(levels, per_level, LANES),
            whole(per_level, LANES),
            whole(per_level, LANES),
            whole(lists, capacity),
        ],
        out_specs=[VMEM] * 3,
        out_shape=[
            pltpu.VMEM((lev_share + 2, per_level, LANES), f32),
            pltpu.VMEM((entry_rows, LANES), jnp.int32),
            pltpu.VMEM((entry_rows, LANES), jnp.int32),
        ],
        compiler_params=params(8),
        name="prepare",
    )(
        in_hbm(vertical_root),
        in_hbm(send_count),
        static,
        in_hbm(tiled(face_north)),
        in_hbm(tiled(face_east)),
        in_hbm(send_index),
    )
    before, after = shifted(packed, 2), shifted(packed, -2)

    obs_rows = obs_slot.shape[0] // LANES
    share_rows = obs_rows // n_ens
    coarse = n_cols * capacity // FINE
    size = levels * 16
    obs_slot, packed = lax.optimization_barrier((obs_slot, packed))
    slots, part = pl.pallas_call(
        functools.partial(observe_kernel, n_cols, cap_rows, member_scale),
        in_specs=[pl.BlockSpec(memory_space=pl.ANY)] * 6,
        out_specs=[VMEM] * 2,
        out_shape=[
            pltpu.VMEM((n_cols, 2, cap_rows, LANES), f32),
            pltpu.VMEM((levels, per_level, LANES), f32),
        ],
        scratch_shapes=[
            pltpu.VMEM((coarse, LANES), f32),
            pltpu.VMEM((coarse, LANES), f32),
            pltpu.VMEM((size, 3 * size), bf16),
            pltpu.VMEM((share_rows, LANES), jnp.int32),
            pltpu.VMEM((share_rows, LANES), f32),
            pltpu.VMEM((share_rows, LANES), f32),
            pltpu.VMEM((levels, levels), f32),
            pltpu.VMEM(control.shape, f32),
            pltpu.VMEM(pert.shape, bf16),
            pltpu.SemaphoreType.DMA((6,)),
        ],
        compiler_params=params(24),
        name="slot_sums_and_members",
    )(
        in_hbm(obs_slot.reshape(obs_rows, LANES)),
        in_hbm(obs_weight.reshape(obs_rows, LANES)),
        in_hbm(innovation.reshape(obs_rows, LANES)),
        in_hbm(vertical_local),
        control,
        pert,
    )
    before, after, slots = lax.optimization_barrier((before, after, slots))
    other = swapped(packed, before, after)
    slots = lax.all_to_all(slots, "cols", split_axis=0, concat_axis=0, tiled=True)

    increment, coefs = pl.pallas_call(
        functools.partial(first_diffusion_kernel, lev_share, rows),
        in_specs=[VMEM] * 4,
        out_specs=[VMEM] * 2,
        out_shape=[
            pltpu.VMEM((lev_share, per_level, LANES), f32),
            pltpu.VMEM((5, 5 * rows, per_level // rows, LANES), f32),
        ],
        compiler_params=params(8),
        name="diffuse_forward",
    )(before, packed, after, other)

    values = pl.pallas_call(
        functools.partial(lookup_kernel, cap_rows),
        in_specs=[VMEM] * 4,
        out_specs=VMEM,
        out_shape=pltpu.VMEM((entry_rows, LANES), f32),
        scratch_shapes=[pltpu.VMEM((cells, 2 * LANES), bf16)],
        compiler_params=params(16),
        name="lookup",
    )(part.reshape(cells, LANES), increment.reshape(own, LANES), entry_row, entry_lane)
    slots = jnp.swapaxes(slots, 0, 1).reshape(2, entry_rows, LANES)
    share = jnp.concatenate([values[None], slots])
    shares = [share] + from_peers(share)

    adjoint_own, amounts = pl.pallas_call(
        functools.partial(scatter_own_kernel, cap_rows),
        in_specs=[VMEM] * (2 + n_ens),
        out_specs=[VMEM] * 2,
        out_shape=[pltpu.VMEM((own, LANES), f32), pltpu.VMEM((entry_rows, LANES), f32)],
        scratch_shapes=[pltpu.VMEM((own, 2 * LANES), f32)],
        compiler_params=params(16),
        name="scatter_own",
    )(entry_row, entry_lane, *shares)
    tile = adjoint_own.reshape(lev_share, per_level, LANES)
    tile_before, tile_after = shifted(tile, 2), shifted(tile, -2)

    adjoint, static_here, control_here, pert_here, from_local, from_root = pl.pallas_call(
        functools.partial(scatter_rest_kernel, cap_rows, member_scale),
        in_specs=[VMEM] * 4 + [pl.BlockSpec(memory_space=pl.ANY)] * 5,
        out_specs=[VMEM] * 6,
        out_shape=[
            pltpu.VMEM((cells, LANES), f32),
            pltpu.VMEM(static.shape, f32),
            pltpu.VMEM(control.shape, f32),
            pltpu.VMEM(pert.shape, bf16),
            pltpu.VMEM((size, 3 * size), bf16),
            pltpu.VMEM((size, 3 * size), bf16),
        ],
        scratch_shapes=[
            pltpu.VMEM((cells - own, 2 * LANES), f32),
            pltpu.VMEM((levels, levels), f32),
            pltpu.VMEM((levels, levels), f32),
            pltpu.SemaphoreType.DMA((5,)),
        ],
        compiler_params=params(16),
        name="scatter_rest",
    )(
        entry_row,
        entry_lane,
        amounts,
        adjoint_own,
        in_hbm(vertical_local),
        in_hbm(vertical_root),
        static,
        control,
        pert,
    )
    tile_before, tile_after, adjoint = lax.optimization_barrier((tile_before, tile_after, adjoint))
    tile_other = swapped(tile, tile_before, tile_after)

    smooth = pl.pallas_call(
        functools.partial(second_diffusion_kernel, rows),
        in_specs=[VMEM] * 5,
        out_specs=VMEM,
        out_shape=pltpu.VMEM((lev_share, per_level, LANES), f32),
        compiler_params=params(8),
        name="diffuse_adjoint",
    )(coefs, tile_before, tile, tile_after, tile_other)
    smooth, adjoint = lax.optimization_barrier((smooth, adjoint))
    smooths = [smooth] + from_peers(smooth)

    group = 2 - members % 2
    ensemble_grad = pl.pallas_call(
        member_kernel,
        grid=(members // group,),
        in_specs=[VMEM] * 4,
        out_specs=pl.BlockSpec((group, levels, per_level, LANES), lambda k: (k, 0, 0, 0)),
        out_shape=jax.ShapeDtypeStruct((members, levels, per_level, LANES), f32),
        compiler_params=params(16),
        name="members_gradient",
    )(from_local, adjoint.reshape(levels, per_level, LANES), control_here, pert_here)

    static_grad = pl.pallas_call(
        static_kernel,
        grid=(1,),
        in_specs=[VMEM] * (2 + n_ens),
        out_specs=whole(levels, per_level, LANES),
        out_shape=jax.ShapeDtypeStruct((levels, per_level, LANES), f32),
        scratch_shapes=[pltpu.VMEM((levels, per_level, LANES), f32)],
        compiler_params=params(8),
        name="static_gradient",
    )(from_root, static_here, *smooths)
    return (untiled(static_grad, rows), untiled(ensemble_grad, rows))


def solution(mesh):
    placed = (
        P(None, "cols", None),
        P("ens", None, "cols", None),
        P("ens", None, "cols", None),
        P(),
        P(),
        P("cols", None),
        P("cols", None),
        P("cols"),
        P("cols"),
        P("cols"),
        P("cols", None),
        P("cols"),
    )
    return jax.shard_map(
        local,
        mesh=mesh,
        in_specs=placed,
        out_specs=(P(None, "cols", None), P("ens", None, "cols", None)),
        check_vma=False,
    )
```

```python
import functools
import math

import jax
import jax.numpy as jnp
from jax import lax
from jax.experimental import pallas as pl
from jax.experimental.pallas import tpu as pltpu
from jax.sharding import PartitionSpec as P

NDIFF = 4
LANES = 128
FINE = 64
MIB = 1 << 20

f32 = jnp.float32
bf16 = jnp.bfloat16
SMEM = pl.BlockSpec(memory_space=pltpu.SMEM)
VMEM = pl.BlockSpec(memory_space=pltpu.VMEM)


def tiled(field):
    *lead, rows, lon = field.shape
    field = field.reshape(*lead, rows, lon // LANES, LANES)
    return jnp.swapaxes(field, -3, -2).reshape(*lead, rows * lon // LANES, LANES)


def untiled(field, rows):
    *lead, count, lanes = field.shape
    field = field.reshape(*lead, count // rows, rows, lanes)
    return jnp.swapaxes(field, -3, -2).reshape(*lead, rows, count // rows * lanes)


def params(limit, **more):
    return pltpu.CompilerParams(vmem_limit_bytes=limit * MIB, **more)


def halves(x):
    high = x.astype(bf16)
    return high, (x - high.astype(f32)).astype(bf16)


def in_hbm(x):
    return pltpu.with_memory_space_constraint(x, pltpu.HBM)


def spread(row, dtype):
    return jnp.broadcast_to(row, (16, row.shape[1])).astype(dtype)


def matches(index, count):
    ids = lax.broadcasted_iota(jnp.int32, (count, index.shape[1]), 0).astype(jnp.int16)
    return ids.reshape(count // 16, 16, index.shape[1]) == spread(index, jnp.int16)[None]


def placed_at(index, count, amount=None):
    where = matches(index, count)
    amount = bf16(1) if amount is None else spread(amount, bf16)[None]
    return jnp.where(where, amount, bf16(0)).reshape(count, index.shape[1])


def product_nt(left, right):
    return lax.dot_general(left, right, (((1,), (1,)), ((), ())), preferred_element_type=f32)


def over(x, size):
    if size & (size - 1):
        return lax.div(x, jnp.int32(size)), lax.rem(x, jnp.int32(size))
    return lax.shift_right_logical(x, jnp.int32(size.bit_length() - 1)), x & (size - 1)


def prepare_kernel(lev_share, rows, root_ref, count_ref, static_ref, north_ref, east_ref, index_ref, out_ref, row_ref, lane_ref):
    levels, per_level, _ = static_ref.shape
    first = lax.axis_index("ens") * lev_share
    for j in range(lev_share):
        total = root_ref[first + j, 0] * static_ref[0]
        for m in range(1, levels):
            total = total + root_ref[first + j, m] * static_ref[m]
        out_ref[j] = total
    out_ref[lev_share] = north_ref[...]
    out_ref[lev_share + 1] = east_ref[...]
    lists, capacity = index_ref.shape
    lon = per_level // rows * LANES
    pieces = capacity // LANES
    slot = lax.broadcasted_iota(jnp.int32, (1, capacity), 1)
    for q in range(lists):
        cell = index_ref[q : q + 1, :]
        rest, lane = over(cell, LANES)
        rest, block = over(rest, lon // LANES)
        level, row = over(rest, rows)
        grid_row = jnp.where(slot < count_ref[q], level * per_level + block * rows + row, -1)
        for c in range(pieces):
            at = q * pieces + c
            row_ref[at : at + 1, :] = grid_row[:, c * LANES : (c + 1) * LANES]
            lane_ref[at : at + 1, :] = lane[:, c * LANES : (c + 1) * LANES]


def level_product(matrix, transpose):
    levels = matrix.shape[0]
    size = levels * 16
    pick = lax.broadcasted_iota(jnp.int32, (size, levels), 0) // 16
    pick = jnp.where(pick == lax.broadcasted_iota(jnp.int32, (size, levels), 1), f32(1), f32(0)).astype(bf16)
    same = (
        lax.broadcasted_iota(jnp.int32, (size, size), 0) % 16 == lax.broadcasted_iota(jnp.int32, (size, size), 1) % 16
    )
    out = []
    for half in halves(matrix):
        if transpose:
            wide = product_nt(pick, half)
        else:
            wide = jnp.dot(pick, half, preferred_element_type=f32)
        wide = product_nt(wide.astype(bf16), pick)
        out.append(jnp.where(same, wide, f32(0)).astype(bf16))
    return jnp.concatenate([out[0], out[0], out[1]], axis=1)


def three_terms(x):
    high, low = halves(x)
    return jnp.concatenate([high, low, high], axis=0)


def observe_kernel(n_cols, cap_rows, scale, *refs):
    sources, (out_ref, part_ref), (acc_ref, fold_ref, matrix_ref), landed, sems = (
        refs[:6],
        refs[6:8],
        refs[8:11],
        refs[11:17],
        refs[17],
    )
    coarse = acc_ref.shape[0]
    obs_rows = landed[0].shape[0]
    group = min(8, obs_rows)
    first = pl.multiple_of(lax.axis_index("ens") * obs_rows, obs_rows)
    copies = [
        pltpu.make_async_copy(sources[i].at[pl.ds(first, obs_rows), :], landed[i], sems.at[i]) for i in range(3)
    ]
    copies += [pltpu.make_async_copy(sources[i], landed[i], sems.at[i]) for i in range(3, 6)]
    for copy in copies:
        copy.start()
    acc_ref[...] = jnp.zeros_like(acc_ref)
    for copy in copies[:3]:
        copy.wait()
    slot_ref, weight_ref, innov_ref, local_ref, control_ref, pert_ref = landed

    def step(i, carry):
        at = pl.ds(pl.multiple_of(i * group, group), group)
        slot = slot_ref[at, :]
        weight = weight_ref[at, :]
        amount = weight * innov_ref[at, :]
        upper, lower = over(slot, FINE)
        terms = [t.astype(f32) for t in halves(weight) + halves(amount)]
        left, right = [], []
        for r in range(group):
            left.append(placed_at(upper[r : r + 1, :], coarse))
            mask = matches(lower[r : r + 1, :], FINE)
            right.append(
                jnp.concatenate(
                    [
                        jnp.where(mask, spread(t[r : r + 1, :], bf16)[None], bf16(0)).reshape(FINE, LANES)
                        for t in terms
                    ],
                    axis=0,
                )
            )
        acc_ref[...] += product_nt(jnp.concatenate(left, axis=1), jnp.concatenate(right, axis=1))
        return carry

    lax.fori_loop(0, obs_rows // group, step, 0)
    for t in range(2):
        terms = acc_ref[:, t * LANES : (t + 1) * LANES]
        fold_ref[t] = terms + pltpu.roll(terms, FINE, 1)
    per_row = LANES // FINE
    lane = lax.broadcasted_iota(jnp.int32, (coarse // per_row, LANES), 1)
    weights, amounts = (
        jnp.where(
            lane < FINE,
            fold_ref[t, pl.ds(0, coarse // per_row, stride=per_row), :],
            fold_ref[t, pl.ds(1, coarse // per_row, stride=per_row), :],
        )
        for t in range(2)
    )
    for p in range(n_cols):
        out_ref[p, 0] = weights[p * cap_rows : (p + 1) * cap_rows]
        out_ref[p, 1] = amounts[p * cap_rows : (p + 1) * cap_rows]
    for copy in copies[3:]:
        copy.wait()
    matrix_ref[...] = level_product(local_ref[...] * f32(scale), False)
    sum_members(matrix_ref, control_ref, pert_ref, part_ref)


def sum_members(matrix_ref, control_ref, pert_ref, out_ref):
    members, levels, per_level, _ = control_ref.shape
    group = 2 - members % 2

    def chunk(j, carry):
        at = pl.ds(pl.multiple_of(j * 16, 16), 16)
        total = jnp.zeros((levels * 16, LANES), f32)
        for k in range(0, members, group):
            terms = [three_terms(control_ref[k + i, :, at, :].reshape(levels * 16, LANES)) for i in range(group)]
            local = jnp.dot(matrix_ref[...], jnp.concatenate(terms, axis=1), preferred_element_type=f32)
            for i in range(group):
                pert = pert_ref[k + i, :, at, :].astype(f32).reshape(levels * 16, LANES)
                total = total + pert * local[:, i * LANES : (i + 1) * LANES]
        out_ref[:, at, :] = total.reshape(levels, 16, LANES)
        return carry

    lax.fori_loop(0, per_level // 16, chunk, 0)


def member_kernel(matrix_ref, adjoint_ref, control_ref, pert_ref, out_ref):
    group, levels, per_level, _ = out_ref.shape
    first = pl.program_id(0) * group

    def chunk(j, carry):
        at = pl.ds(pl.multiple_of(j * 16, 16), 16)
        adjoint = adjoint_ref[:, at, :]
        terms = [
            three_terms((pert_ref[first + i, :, at, :].astype(f32) * adjoint).reshape(levels * 16, LANES))
            for i in range(group)
        ]
        change = jnp.dot(matrix_ref[...], jnp.concatenate(terms, axis=1), preferred_element_type=f32)
        for i in range(group):
            part = change[:, i * LANES : (i + 1) * LANES].reshape(levels, 16, LANES)
            out_ref[i, :, at, :] = control_ref[first + i, :, at, :] + part
        return carry

    lax.fori_loop(0, per_level // 16, chunk, 0)


def eastern(x):
    lane = lax.broadcasted_iota(jnp.int32, x.shape, 1)
    near = pltpu.roll(x, LANES - 1, 1)
    return jnp.where(lane == LANES - 1, pltpu.roll(near, x.shape[0] - 1, 0), near)


def western(x):
    lane = lax.broadcasted_iota(jnp.int32, x.shape, 1)
    near = pltpu.roll(x, 1, 1)
    return jnp.where(lane == 0, pltpu.roll(near, 1, 0), near)


def rows_of(tiles, plane, rows):
    at = lax.axis_index("cols")
    side = len(tiles) // 2
    out = []
    for i, tile in enumerate(tiles):
        for r in range(rows):
            row = tile[plane, pl.ds(r, tile.shape[1] // rows, stride=rows), :]
            if i != side:
                there = at + (i - side)
                row = jnp.where(jnp.logical_and(there >= 0, there < lax.axis_size("cols")), row, f32(0))
            out.append(row)
    return out


def diffuse_rows(tiles, level, coef_ref, rows):
    field = rows_of(tiles, level, rows)
    for step in range(NDIFF):
        field = [
            coef_ref[0, i + step] * field[i]
            + coef_ref[1, i + step] * field[i - 1]
            + coef_ref[2, i + step] * field[i + 1]
            + coef_ref[3, i + step] * eastern(field[i])
            + coef_ref[4, i + step] * western(field[i])
            for i in range(1, len(field) - 1)
        ]
        field = list(field)
    return field


def tiles_of(before_ref, own_ref, after_ref, other_ref):
    odd = lax.axis_index("cols") % 2
    return [before_ref, other_ref.at[1 - odd], own_ref, other_ref.at[odd], after_ref]


def first_diffusion_kernel(lev_share, rows, before_ref, own_ref, after_ref, other_ref, out_ref, coef_ref):
    tiles = tiles_of(before_ref, own_ref, after_ref, other_ref)
    blocks = own_ref.shape[1] // rows
    side = len(tiles) // 2
    north = rows_of(tiles, lev_share, rows)
    east = rows_of(tiles, lev_share + 1, rows)
    for i in range(1, len(north) - 1):
        south = north[i + 1]
        if (i + 1) % rows == 0 and i < side * rows:
            south = south * jnp.where(lax.axis_index("cols") == side - (i + 1) // rows, f32(0), f32(1))
        west = western(east[i])
        coef_ref[0, i] = 1.0 - north[i] - south - east[i] - west
        coef_ref[1, i] = north[i]
        coef_ref[2, i] = south
        coef_ref[3, i] = east[i]
        coef_ref[4, i] = west
    for i in (0, len(north) - 1):
        for c in range(5):
            coef_ref[c, i] = jnp.zeros_like(north[0])

    def body(level, carry):
        final = diffuse_rows(tiles, level, coef_ref, rows)
        for r in range(rows):
            out_ref[level, pl.ds(r, blocks, stride=rows), :] = final[r]
        return carry

    lax.fori_loop(0, lev_share, body, 0)


def second_diffusion_kernel(rows, coef_ref, before_ref, own_ref, after_ref, other_ref, out_ref):
    tiles = tiles_of(before_ref, own_ref, after_ref, other_ref)
    lev_share = out_ref.shape[0]
    blocks = own_ref.shape[1] // rows

    def body(level, carry):
        final = diffuse_rows(tiles, level, coef_ref, rows)
        for r in range(rows):
            out_ref[level, pl.ds(r, blocks, stride=rows), :] = final[r]
        return carry

    lax.fori_loop(0, lev_share, body, 0)


def lookup_kernel(cap_rows, part_ref, static_ref, row_ref, lane_ref, out_ref, terms_ref):
    cells = part_ref.shape[0]
    own = static_ref.shape[0]
    n_lists = row_ref.shape[0] // cap_rows
    at = pl.ds(pl.multiple_of(lax.axis_index("ens") * own, own), own)
    for here, field in ((slice(None), part_ref[...]), (at, part_ref[at, :] + static_ref[...])):
        high, low = halves(field)
        terms_ref[here, :LANES] = high
        terms_ref[here, LANES:] = low
    ids16 = lax.broadcasted_iota(jnp.int32, (LANES, cells), 1).astype(jnp.int16)
    ids = lax.broadcasted_iota(jnp.int32, (LANES, LANES), 1)
    diagonal = ids == lax.broadcasted_iota(jnp.int32, (LANES, LANES), 0)

    def look(q, carry):
        at = pl.ds(pl.multiple_of(q * cap_rows, cap_rows), cap_rows)
        rows = row_ref[at, :].astype(f32).T
        lanes = lane_ref[at, :].astype(f32).T
        picks = []
        for c in range(cap_rows):
            column = jnp.broadcast_to(rows[:, c : c + 1], (LANES, LANES)).astype(jnp.int32).astype(jnp.int16)
            column = jnp.concatenate([column] * (cells // LANES), axis=1)
            picks.append(jnp.where(ids16 == column, bf16(1), bf16(0)))
        got = jnp.dot(jnp.concatenate(picks, axis=0), terms_ref[...], preferred_element_type=f32)
        values = []
        for c in range(cap_rows):
            mask = ids == jnp.broadcast_to(lanes[:, c : c + 1], (LANES, LANES)).astype(jnp.int32)
            mine = got[c * LANES : (c + 1) * LANES]
            found = jnp.sum(jnp.where(mask, mine[:, :LANES] + mine[:, LANES:], f32(0)), axis=1, keepdims=True)
            values.append(jnp.sum(jnp.where(diagonal, found, f32(0)), axis=0, keepdims=True))
        out_ref[at, :] = jnp.concatenate(values, axis=0)
        return carry

    lax.fori_loop(0, n_lists, look, 0)


def put(acc_ref, rows, lanes, amounts):
    high, low = (h.astype(f32) for h in halves(amounts))
    left, right = [], []
    for c in range(rows.shape[0]):
        piece = slice(c, c + 1)
        left.append(placed_at(rows[piece, :], acc_ref.shape[0]))
        mask = matches(lanes[piece, :], LANES)
        right.append(
            jnp.concatenate(
                [
                    jnp.where(mask, spread(h[piece, :], bf16)[None], bf16(0)).reshape(LANES, LANES)
                    for h in (high, low)
                ],
                axis=0,
            )
        )
    acc_ref[...] += product_nt(jnp.concatenate(left, axis=1), jnp.concatenate(right, axis=1))


def scatter_own_kernel(cap_rows, row_ref, lane_ref, *refs):
    shares, (out_ref, amount_ref, acc_ref) = refs[:-3], refs[-3:]
    own = out_ref.shape[0]
    first = lax.axis_index("ens") * own
    acc_ref[...] = jnp.zeros_like(acc_ref)

    def step(q, carry):
        at = pl.ds(pl.multiple_of(q * cap_rows, cap_rows), cap_rows)
        value, weight, amount = (functools.reduce(jnp.add, [s[t, at, :] for s in shares]) for t in range(3))
        amounts = value * weight - amount
        amount_ref[at, :] = amounts
        put(acc_ref, row_ref[at, :] - first, lane_ref[at, :], amounts)
        return carry

    lax.fori_loop(0, row_ref.shape[0] // cap_rows, step, 0)
    out_ref[...] = acc_ref[:, :LANES] + acc_ref[:, LANES:]


def matrices_kernel(scale, local_ref, root_ref, to_members_ref, to_static_ref):
    to_members_ref[...] = level_product(local_ref[...] * f32(scale), True)
    to_static_ref[...] = level_product(root_ref[...], True)


def scatter_rest_kernel(cap_rows, row_ref, lane_ref, amount_ref, own_ref, *refs):
    sources, out_ref, kept, acc_ref, sems = refs[:3], refs[3], refs[4:7], refs[7], refs[8]
    copies = [pltpu.make_async_copy(s, t, sems.at[i]) for i, (s, t) in enumerate(zip(sources, kept))]
    for copy in copies:
        copy.start()
    cells = out_ref.shape[0]
    own = own_ref.shape[0]
    n_ens = cells // own
    me = lax.axis_index("ens")
    first = (me + 1) * own
    acc_ref[...] = jnp.zeros_like(acc_ref)

    def step(q, carry):
        at = pl.ds(pl.multiple_of(q * cap_rows, cap_rows), cap_rows)
        row = row_ref[at, :]
        turned = row - first
        turned = jnp.where(row < 0, -1, jnp.where(turned < 0, turned + cells, turned))
        put(acc_ref, turned, lane_ref[at, :], amount_ref[at, :])
        return carry

    lax.fori_loop(0, row_ref.shape[0] // cap_rows, step, 0)
    out_ref[pl.ds(pl.multiple_of(me * own, own), own), :] = own_ref[...]
    for t in range(1, n_ens):
        to = pl.ds(pl.multiple_of((me + t) % n_ens * own, own), own)
        piece = acc_ref[(t - 1) * own : t * own, :]
        out_ref[to, :] = piece[:, :LANES] + piece[:, LANES:]
    for copy in copies:
        copy.wait()


def static_kernel(matrix_ref, static_ref, *refs):
    parts, (out_ref, smooth_ref) = refs[:-2], refs[-2:]
    levels, per_level, _ = static_ref.shape
    share = levels // len(parts)
    me = lax.axis_index("ens")
    for d, part in enumerate(parts):
        smooth_ref[pl.ds((me + d) % len(parts) * share, share)] = part[...]
    for j in range(0, per_level, 32):
        terms = [three_terms(smooth_ref[:, j + i : j + i + 16, :].reshape(levels * 16, LANES)) for i in (0, 16)]
        change = jnp.dot(matrix_ref[...], jnp.concatenate(terms, axis=1), preferred_element_type=f32)
        for i, part in ((0, change[:, :LANES]), (16, change[:, LANES:])):
            at = slice(j + i, j + i + 16)
            out_ref[:, at, :] = static_ref[:, at, :] + part.reshape(levels, 16, LANES)


def shifted(x, by):
    count = lax.axis_size("cols")
    return lax.ppermute(x, "cols", [(i, (i + by) % count) for i in range(count)])


def from_peers(x):
    count = lax.axis_size("ens")
    return [lax.ppermute(x, "ens", [((i + d) % count, i) for i in range(count)]) for d in range(1, count)]


def swapped(own, before, after):
    odd = lax.axis_index("cols") % 2
    count = lax.axis_size("cols")
    pack = jnp.stack([own, jnp.where(odd == 1, before, after)])
    return lax.ppermute(pack, "cols", [(i, i ^ 1) for i in range(count)])


def local(
    static_control,
    ensemble_control,
    perturbations,
    vertical_root,
    vertical_local,
    face_north,
    face_east,
    innovation,
    obs_weight,
    obs_slot,
    send_index,
    send_count,
):
    n_ens = lax.axis_size("ens")
    n_cols = lax.axis_size("cols")
    members, levels, rows, lon = ensemble_control.shape
    per_level = rows * lon // LANES
    cells = levels * per_level
    lev_share = levels // n_ens
    own = lev_share * per_level
    lists, capacity = send_index.shape
    cap_rows = capacity // LANES
    entry_rows = lists * cap_rows
    member_scale = 1.0 / math.sqrt(members * n_ens - 1)

    static = in_hbm(tiled(static_control))
    control = in_hbm(tiled(ensemble_control))
    pert = in_hbm(tiled(perturbations))

    def whole(*shape):
        return pl.BlockSpec(shape, lambda i: (0,) * len(shape))

    packed, entry_row, entry_lane = pl.pallas_call(
        functools.partial(prepare_kernel, lev_share, rows),
        grid=(1,),
        in_specs=[
            SMEM,
            SMEM,
            whole(levels, per_level, LANES),
            whole(per_level, LANES),
            whole(per_level, LANES),
            whole(lists, capacity),
        ],
        out_specs=[VMEM] * 3,
        out_shape=[
            pltpu.VMEM((lev_share + 2, per_level, LANES), f32),
            pltpu.VMEM((entry_rows, LANES), jnp.int32),
            pltpu.VMEM((entry_rows, LANES), jnp.int32),
        ],
        compiler_params=params(8),
        name="prepare",
    )(
        in_hbm(vertical_root),
        in_hbm(send_count),
        static,
        in_hbm(tiled(face_north)),
        in_hbm(tiled(face_east)),
        in_hbm(send_index),
    )
    before, after = shifted(packed, 2), shifted(packed, -2)

    obs_rows = obs_slot.shape[0] // LANES
    share_rows = obs_rows // n_ens
    coarse = n_cols * capacity // FINE
    size = levels * 16
    obs_slot, packed = lax.optimization_barrier((obs_slot, packed))
    slots, part = pl.pallas_call(
        functools.partial(observe_kernel, n_cols, cap_rows, member_scale),
        in_specs=[pl.BlockSpec(memory_space=pl.ANY)] * 6,
        out_specs=[VMEM] * 2,
        out_shape=[
            pltpu.VMEM((n_cols, 2, cap_rows, LANES), f32),
            pltpu.VMEM((levels, per_level, LANES), f32),
        ],
        scratch_shapes=[
            pltpu.VMEM((coarse, 4 * FINE), f32),
            pltpu.VMEM((2, coarse, LANES), f32),
            pltpu.VMEM((size, 3 * size), bf16),
            pltpu.VMEM((share_rows, LANES), jnp.int32),
            pltpu.VMEM((share_rows, LANES), f32),
            pltpu.VMEM((share_rows, LANES), f32),
            pltpu.VMEM((levels, levels), f32),
            pltpu.VMEM(control.shape, f32),
            pltpu.VMEM(pert.shape, bf16),
            pltpu.SemaphoreType.DMA((6,)),
        ],
        compiler_params=params(24),
        name="slot_sums_and_members",
    )(
        in_hbm(obs_slot.reshape(obs_rows, LANES)),
        in_hbm(obs_weight.reshape(obs_rows, LANES)),
        in_hbm(innovation.reshape(obs_rows, LANES)),
        in_hbm(vertical_local),
        control,
        pert,
    )
    before, after, slots = lax.optimization_barrier((before, after, slots))
    other = swapped(packed, before, after)
    slots = lax.all_to_all(slots, "cols", split_axis=0, concat_axis=0, tiled=True)

    increment, coefs = pl.pallas_call(
        functools.partial(first_diffusion_kernel, lev_share, rows),
        in_specs=[VMEM] * 4,
        out_specs=[VMEM] * 2,
        out_shape=[
            pltpu.VMEM((lev_share, per_level, LANES), f32),
            pltpu.VMEM((5, 5 * rows, per_level // rows, LANES), f32),
        ],
        compiler_params=params(8),
        cost_estimate=pl.CostEstimate(flops=1 << 26, bytes_accessed=1 << 22, transcendentals=0),
        name="diffuse_forward",
    )(before, packed, after, other)

    values = pl.pallas_call(
        functools.partial(lookup_kernel, cap_rows),
        in_specs=[VMEM] * 4,
        out_specs=VMEM,
        out_shape=pltpu.VMEM((entry_rows, LANES), f32),
        scratch_shapes=[pltpu.VMEM((cells, 2 * LANES), bf16)],
        compiler_params=params(16),
        cost_estimate=pl.CostEstimate(
            flops=4 * cells * LANES * lists * capacity, bytes_accessed=8 * cells * lists * capacity // 4, transcendentals=0
        ),
        name="lookup",
    )(part.reshape(cells, LANES), increment.reshape(own, LANES), entry_row, entry_lane)
    slots = jnp.swapaxes(slots, 0, 1).reshape(2, entry_rows, LANES)
    share = jnp.concatenate([values[None], slots])
    shares = [share] + from_peers(share)

    adjoint_own, amounts = pl.pallas_call(
        functools.partial(scatter_own_kernel, cap_rows),
        in_specs=[VMEM] * (2 + n_ens),
        out_specs=[VMEM] * 2,
        out_shape=[pltpu.VMEM((own, LANES), f32), pltpu.VMEM((entry_rows, LANES), f32)],
        scratch_shapes=[pltpu.VMEM((own, 2 * LANES), f32)],
        compiler_params=params(16),
        name="scatter_own",
    )(entry_row, entry_lane, *shares)
    tile = adjoint_own.reshape(lev_share, per_level, LANES)
    tile_before, tile_after = shifted(tile, 2), shifted(tile, -2)

    adjoint, static_here, control_here, pert_here = pl.pallas_call(
        functools.partial(scatter_rest_kernel, cap_rows),
        in_specs=[VMEM] * 4 + [pl.BlockSpec(memory_space=pl.ANY)] * 3,
        out_specs=[VMEM] * 4,
        out_shape=[
            pltpu.VMEM((cells, LANES), f32),
            pltpu.VMEM(static.shape, f32),
            pltpu.VMEM(control.shape, f32),
            pltpu.VMEM(pert.shape, bf16),
        ],
        scratch_shapes=[pltpu.VMEM((cells - own, 2 * LANES), f32), pltpu.SemaphoreType.DMA((3,))],
        compiler_params=params(16),
        name="scatter_rest",
    )(entry_row, entry_lane, amounts, adjoint_own, static, control, pert)
    tile_before, tile_after, adjoint, vertical_local, vertical_root = lax.optimization_barrier(
        (tile_before, tile_after, adjoint, vertical_local, vertical_root)
    )
    tile_other = swapped(tile, tile_before, tile_after)
    from_local, from_root = pl.pallas_call(
        functools.partial(matrices_kernel, member_scale),
        grid=(1,),
        in_specs=[whole(levels, levels)] * 2,
        out_specs=[VMEM] * 2,
        out_shape=[pltpu.VMEM((size, 3 * size), bf16)] * 2,
        compiler_params=params(8),
        name="level_matrices",
    )(in_hbm(vertical_local), in_hbm(vertical_root))
    coefs, from_local, from_root = lax.optimization_barrier((coefs, from_local, from_root))

    smooth = pl.pallas_call(
        functools.partial(second_diffusion_kernel, rows),
        in_specs=[VMEM] * 5,
        out_specs=VMEM,
        out_shape=pltpu.VMEM((lev_share, per_level, LANES), f32),
        compiler_params=params(8),
        name="diffuse_adjoint",
    )(coefs, tile_before, tile, tile_after, tile_other)
    smooth, adjoint = lax.optimization_barrier((smooth, adjoint))
    smooths = [smooth] + from_peers(smooth)

    group = 2 - members % 2
    ensemble_grad = pl.pallas_call(
        member_kernel,
        grid=(members // group,),
        in_specs=[VMEM] * 4,
        out_specs=pl.BlockSpec((group, levels, per_level, LANES), lambda k: (k, 0, 0, 0)),
        out_shape=jax.ShapeDtypeStruct((members, levels, per_level, LANES), f32),
        compiler_params=params(16),
        name="members_gradient",
    )(from_local, adjoint.reshape(levels, per_level, LANES), control_here, pert_here)

    static_grad = pl.pallas_call(
        static_kernel,
        grid=(1,),
        in_specs=[VMEM] * (2 + n_ens),
        out_specs=whole(levels, per_level, LANES),
        out_shape=jax.ShapeDtypeStruct((levels, per_level, LANES), f32),
        scratch_shapes=[pltpu.VMEM((levels, per_level, LANES), f32)],
        compiler_params=params(8),
        name="static_gradient",
    )(from_root, static_here, *smooths)
    return (untiled(static_grad, rows), untiled(ensemble_grad, rows))


def solution(mesh):
    placed = (
        P(None, "cols", None),
        P("ens", None, "cols", None),
        P("ens", None, "cols", None),
        P(),
        P(),
        P("cols", None),
        P("cols", None),
        P("cols"),
        P("cols"),
        P("cols"),
        P("cols", None),
        P("cols"),
    )
    return jax.shard_map(
        local,
        mesh=mesh,
        in_specs=placed,
        out_specs=(P(None, "cols", None), P("ens", None, "cols", None)),
        check_vma=False,
    )
```

```python
import functools
import math

import jax
import jax.numpy as jnp
from jax import lax
from jax.experimental import pallas as pl
from jax.experimental.pallas import tpu as pltpu
from jax.sharding import PartitionSpec as P

NDIFF = 4
LANES = 128
FINE = 64
MIB = 1 << 20

f32 = jnp.float32
bf16 = jnp.bfloat16
SMEM = pl.BlockSpec(memory_space=pltpu.SMEM)
VMEM = pl.BlockSpec(memory_space=pltpu.VMEM)


def tiled(field):
    *lead, rows, lon = field.shape
    field = field.reshape(*lead, rows, lon // LANES, LANES)
    return jnp.swapaxes(field, -3, -2).reshape(*lead, rows * lon // LANES, LANES)


def untiled(field, rows):
    *lead, count, lanes = field.shape
    field = field.reshape(*lead, count // rows, rows, lanes)
    return jnp.swapaxes(field, -3, -2).reshape(*lead, rows, count // rows * lanes)


def params(limit, **more):
    return pltpu.CompilerParams(vmem_limit_bytes=limit * MIB, **more)


def halves(x):
    high = x.astype(bf16)
    return high, (x - high.astype(f32)).astype(bf16)


def in_hbm(x):
    return pltpu.with_memory_space_constraint(x, pltpu.HBM)


def spread(row, dtype):
    return jnp.broadcast_to(row, (16, row.shape[1])).astype(dtype)


def matches(index, count):
    ids = lax.broadcasted_iota(jnp.int32, (count, index.shape[1]), 0).astype(jnp.int16)
    return ids.reshape(count // 16, 16, index.shape[1]) == spread(index, jnp.int16)[None]


def placed_at(index, count, amount=None):
    where = matches(index, count)
    amount = bf16(1) if amount is None else spread(amount, bf16)[None]
    return jnp.where(where, amount, bf16(0)).reshape(count, index.shape[1])


def in_turns(count, build, use, slots):
    build(0, slots[0])

    def step(i, carry):
        use(2 * i, slots[0])
        build(2 * i + 1, slots[1])
        use(2 * i + 1, slots[1])
        build(jnp.minimum(2 * i + 2, count - 1), slots[0])
        return carry

    lax.fori_loop(0, count // 2, step, 0)
    if count % 2:
        use(count - 1, slots[0])


def product_nt(left, right):
    return lax.dot_general(left, right, (((1,), (1,)), ((), ())), preferred_element_type=f32)


def over(x, size):
    if size & (size - 1):
        return lax.div(x, jnp.int32(size)), lax.rem(x, jnp.int32(size))
    return lax.shift_right_logical(x, jnp.int32(size.bit_length() - 1)), x & (size - 1)


def prepare_kernel(lev_share, rows, root_ref, count_ref, static_ref, north_ref, east_ref, index_ref, out_ref, row_ref, lane_ref):
    levels, per_level, _ = static_ref.shape
    first = lax.axis_index("ens") * lev_share
    for j in range(lev_share):
        total = root_ref[first + j, 0] * static_ref[0]
        for m in range(1, levels):
            total = total + root_ref[first + j, m] * static_ref[m]
        out_ref[j] = total
    out_ref[lev_share] = north_ref[...]
    out_ref[lev_share + 1] = east_ref[...]
    lists, capacity = index_ref.shape
    lon = per_level // rows * LANES
    pieces = capacity // LANES
    slot = lax.broadcasted_iota(jnp.int32, (1, capacity), 1)
    for q in range(lists):
        cell = index_ref[q : q + 1, :]
        rest, lane = over(cell, LANES)
        rest, block = over(rest, lon // LANES)
        level, row = over(rest, rows)
        grid_row = jnp.where(slot < count_ref[q], level * per_level + block * rows + row, -1)
        for c in range(pieces):
            at = q * pieces + c
            row_ref[at : at + 1, :] = grid_row[:, c * LANES : (c + 1) * LANES]
            lane_ref[at : at + 1, :] = lane[:, c * LANES : (c + 1) * LANES]


def level_product(matrix, transpose):
    levels = matrix.shape[0]
    size = levels * 16
    pick = lax.broadcasted_iota(jnp.int32, (size, levels), 0) // 16
    pick = jnp.where(pick == lax.broadcasted_iota(jnp.int32, (size, levels), 1), f32(1), f32(0)).astype(bf16)
    same = (
        lax.broadcasted_iota(jnp.int32, (size, size), 0) % 16 == lax.broadcasted_iota(jnp.int32, (size, size), 1) % 16
    )
    out = []
    for half in halves(matrix):
        if transpose:
            wide = product_nt(pick, half)
        else:
            wide = jnp.dot(pick, half, preferred_element_type=f32)
        wide = product_nt(wide.astype(bf16), pick)
        out.append(jnp.where(same, wide, f32(0)).astype(bf16))
    return jnp.concatenate([out[0], out[0], out[1]], axis=1)


def three_terms(x):
    high, low = halves(x)
    return jnp.concatenate([high, low, high], axis=0)


def observe_kernel(n_cols, cap_rows, scale, *refs):
    sources, (out_ref, part_ref), (acc_ref, fold_ref, matrix_ref), landed, sems, slots = (
        refs[:6],
        refs[6:8],
        refs[8:11],
        refs[11:17],
        refs[17],
        (refs[18:20], refs[20:22]),
    )
    coarse = acc_ref.shape[0]
    obs_rows = landed[0].shape[0]
    group = min(8, obs_rows)
    first = pl.multiple_of(lax.axis_index("ens") * obs_rows, obs_rows)
    copies = [
        pltpu.make_async_copy(sources[i].at[pl.ds(first, obs_rows), :], landed[i], sems.at[i]) for i in range(3)
    ]
    copies += [pltpu.make_async_copy(sources[i], landed[i], sems.at[i]) for i in range(3, 6)]
    for copy in copies:
        copy.start()
    acc_ref[...] = jnp.zeros_like(acc_ref)
    for copy in copies[:3]:
        copy.wait()
    slot_ref, weight_ref, innov_ref, local_ref, control_ref, pert_ref = landed

    def build(i, to):
        at = pl.ds(pl.multiple_of(i * group, group), group)
        weight = weight_ref[at, :]
        amount = weight * innov_ref[at, :]
        upper, lower = over(slot_ref[at, :], FINE)
        terms = [t.astype(f32) for t in halves(weight) + halves(amount)]
        for r in range(group):
            here = slice(r * LANES, (r + 1) * LANES)
            to[0][:, here] = placed_at(upper[r : r + 1, :], coarse)
            mask = matches(lower[r : r + 1, :], FINE)
            for t, term in enumerate(terms):
                term = spread(term[r : r + 1, :], bf16)[None]
                to[1][t * FINE : (t + 1) * FINE, here] = jnp.where(mask, term, bf16(0)).reshape(FINE, LANES)

    def use(i, of):
        acc_ref[...] += product_nt(of[0][...], of[1][...])

    in_turns(obs_rows // group, build, use, slots)
    for t in range(2):
        terms = acc_ref[:, t * LANES : (t + 1) * LANES]
        fold_ref[t] = terms + pltpu.roll(terms, FINE, 1)
    per_row = LANES // FINE
    lane = lax.broadcasted_iota(jnp.int32, (coarse // per_row, LANES), 1)
    weights, amounts = (
        jnp.where(
            lane < FINE,
            fold_ref[t, pl.ds(0, coarse // per_row, stride=per_row), :],
            fold_ref[t, pl.ds(1, coarse // per_row, stride=per_row), :],
        )
        for t in range(2)
    )
    for e in range(out_ref.shape[0] // n_cols):
        for p in range(n_cols):
            out_ref[e * n_cols + p, 0] = weights[p * cap_rows : (p + 1) * cap_rows]
            out_ref[e * n_cols + p, 1] = amounts[p * cap_rows : (p + 1) * cap_rows]
    for copy in copies[3:]:
        copy.wait()
    matrix_ref[...] = level_product(local_ref[...] * f32(scale), False)
    sum_members(matrix_ref, control_ref, pert_ref, part_ref)


def sum_members(matrix_ref, control_ref, pert_ref, out_ref):
    members, levels, per_level, _ = control_ref.shape
    group = 2 - members % 2

    def chunk(j, carry):
        at = pl.ds(pl.multiple_of(j * 16, 16), 16)
        total = jnp.zeros((levels * 16, LANES), f32)
        for k in range(0, members, group):
            terms = [three_terms(control_ref[k + i, :, at, :].reshape(levels * 16, LANES)) for i in range(group)]
            local = jnp.dot(matrix_ref[...], jnp.concatenate(terms, axis=1), preferred_element_type=f32)
            for i in range(group):
                pert = pert_ref[k + i, :, at, :].astype(f32).reshape(levels * 16, LANES)
                total = total + pert * local[:, i * LANES : (i + 1) * LANES]
        out_ref[:, at, :] = total.reshape(levels, 16, LANES)
        return carry

    lax.fori_loop(0, per_level // 16, chunk, 0)


def member_kernel(matrix_ref, adjoint_ref, control_ref, pert_ref, out_ref):
    group, levels, per_level, _ = out_ref.shape
    first = pl.program_id(0) * group

    def chunk(j, carry):
        at = pl.ds(pl.multiple_of(j * 16, 16), 16)
        adjoint = adjoint_ref[:, at, :]
        terms = [
            three_terms((pert_ref[first + i, :, at, :].astype(f32) * adjoint).reshape(levels * 16, LANES))
            for i in range(group)
        ]
        change = jnp.dot(matrix_ref[...], jnp.concatenate(terms, axis=1), preferred_element_type=f32)
        for i in range(group):
            part = change[:, i * LANES : (i + 1) * LANES].reshape(levels, 16, LANES)
            out_ref[i, :, at, :] = control_ref[first + i, :, at, :] + part
        return carry

    lax.fori_loop(0, per_level // 16, chunk, 0)


def eastern(x):
    lane = lax.broadcasted_iota(jnp.int32, x.shape, 1)
    near = pltpu.roll(x, LANES - 1, 1)
    return jnp.where(lane == LANES - 1, pltpu.roll(near, x.shape[0] - 1, 0), near)


def western(x):
    lane = lax.broadcasted_iota(jnp.int32, x.shape, 1)
    near = pltpu.roll(x, 1, 1)
    return jnp.where(lane == 0, pltpu.roll(near, 1, 0), near)


def rows_of(tiles, plane, rows):
    at = lax.axis_index("cols")
    side = len(tiles) // 2
    out = []
    for i, tile in enumerate(tiles):
        for r in range(rows):
            row = tile[plane, pl.ds(r, tile.shape[1] // rows, stride=rows), :]
            if i != side:
                there = at + (i - side)
                row = jnp.where(jnp.logical_and(there >= 0, there < lax.axis_size("cols")), row, f32(0))
            out.append(row)
    return out


def diffuse_rows(tiles, level, coef_ref, rows):
    field = rows_of(tiles, level, rows)
    for step in range(NDIFF):
        field = [
            coef_ref[0, i + step] * field[i]
            + coef_ref[1, i + step] * field[i - 1]
            + coef_ref[2, i + step] * field[i + 1]
            + coef_ref[3, i + step] * eastern(field[i])
            + coef_ref[4, i + step] * western(field[i])
            for i in range(1, len(field) - 1)
        ]
        field = list(field)
    return field


def tiles_of(before_ref, own_ref, after_ref, other_ref):
    odd = lax.axis_index("cols") % 2
    return [before_ref, other_ref.at[1 - odd], own_ref, other_ref.at[odd], after_ref]


def first_diffusion_kernel(lev_share, rows, before_ref, own_ref, after_ref, other_ref, out_ref, coef_ref):
    tiles = tiles_of(before_ref, own_ref, after_ref, other_ref)
    blocks = own_ref.shape[1] // rows
    side = len(tiles) // 2
    north = rows_of(tiles, lev_share, rows)
    east = rows_of(tiles, lev_share + 1, rows)
    for i in range(1, len(north) - 1):
        south = north[i + 1]
        if (i + 1) % rows == 0 and i < side * rows:
            south = south * jnp.where(lax.axis_index("cols") == side - (i + 1) // rows, f32(0), f32(1))
        west = western(east[i])
        coef_ref[0, i] = 1.0 - north[i] - south - east[i] - west
        coef_ref[1, i] = north[i]
        coef_ref[2, i] = south
        coef_ref[3, i] = east[i]
        coef_ref[4, i] = west
    for i in (0, len(north) - 1):
        for c in range(5):
            coef_ref[c, i] = jnp.zeros_like(north[0])

    def body(level, carry):
        final = diffuse_rows(tiles, level, coef_ref, rows)
        for r in range(rows):
            out_ref[level, pl.ds(r, blocks, stride=rows), :] = final[r]
        return carry

    lax.fori_loop(0, lev_share, body, 0)


def second_diffusion_kernel(rows, coef_ref, before_ref, own_ref, after_ref, other_ref, out_ref):
    tiles = tiles_of(before_ref, own_ref, after_ref, other_ref)
    lev_share = out_ref.shape[0]
    blocks = own_ref.shape[1] // rows

    def body(level, carry):
        final = diffuse_rows(tiles, level, coef_ref, rows)
        for r in range(rows):
            out_ref[level, pl.ds(r, blocks, stride=rows), :] = final[r]
        return carry

    lax.fori_loop(0, lev_share, body, 0)


def lookup_kernel(cap_rows, part_ref, static_ref, row_ref, lane_ref, out_ref, terms_ref, *slots):
    cells = part_ref.shape[0]
    own = static_ref.shape[0]
    at = pl.ds(pl.multiple_of(lax.axis_index("ens") * own, own), own)
    for here, field in ((slice(None), part_ref[...]), (at, part_ref[at, :] + static_ref[...])):
        high, low = halves(field)
        terms_ref[here, :LANES] = high
        terms_ref[here, LANES:] = low
    ids16 = lax.broadcasted_iota(jnp.int32, (LANES, cells), 1).astype(jnp.int16)
    ids = lax.broadcasted_iota(jnp.int32, (LANES, LANES), 1)
    diagonal = ids == lax.broadcasted_iota(jnp.int32, (LANES, LANES), 0)

    def build(q, to):
        at = pl.ds(pl.multiple_of(q * cap_rows, cap_rows), cap_rows)
        rows = row_ref[at, :].astype(f32).T
        for c in range(cap_rows):
            column = jnp.broadcast_to(rows[:, c : c + 1], (LANES, LANES)).astype(jnp.int32).astype(jnp.int16)
            column = jnp.concatenate([column] * (cells // LANES), axis=1)
            to[c * LANES : (c + 1) * LANES, :] = jnp.where(ids16 == column, bf16(1), bf16(0))

    def use(q, of):
        at = pl.ds(pl.multiple_of(q * cap_rows, cap_rows), cap_rows)
        lanes = lane_ref[at, :].astype(f32).T
        got = jnp.dot(of[...], terms_ref[...], preferred_element_type=f32)
        values = []
        for c in range(cap_rows):
            mask = ids == jnp.broadcast_to(lanes[:, c : c + 1], (LANES, LANES)).astype(jnp.int32)
            mine = got[c * LANES : (c + 1) * LANES]
            found = jnp.sum(jnp.where(mask, mine[:, :LANES] + mine[:, LANES:], f32(0)), axis=1, keepdims=True)
            values.append(jnp.sum(jnp.where(diagonal, found, f32(0)), axis=0, keepdims=True))
        out_ref[at, :] = jnp.concatenate(values, axis=0)

    in_turns(row_ref.shape[0] // cap_rows, build, use, slots)


def put(to, rows, lanes, amounts):
    count = to[0].shape[0]
    terms = [h.astype(f32) for h in halves(amounts)]
    for c in range(rows.shape[0]):
        here = slice(c * LANES, (c + 1) * LANES)
        to[0][:, here] = placed_at(rows[c : c + 1, :], count)
        mask = matches(lanes[c : c + 1, :], LANES)
        for t, term in enumerate(terms):
            term = spread(term[c : c + 1, :], bf16)[None]
            to[1][t * LANES : (t + 1) * LANES, here] = jnp.where(mask, term, bf16(0)).reshape(LANES, LANES)


def scatter_own_kernel(cap_rows, row_ref, lane_ref, slots_ref, *refs):
    values, (out_ref, amount_ref, acc_ref), slots = refs[:-7], refs[-7:-4], (refs[-4:-2], refs[-2:])
    n_ens = len(values)
    own = out_ref.shape[0]
    lists = row_ref.shape[0] // cap_rows
    first = lax.axis_index("ens") * own
    acc_ref[...] = jnp.zeros_like(acc_ref)

    def build(q, to):
        at = pl.ds(pl.multiple_of(q * cap_rows, cap_rows), cap_rows)
        value = functools.reduce(jnp.add, [v[at, :] for v in values])
        weight, amount = (
            functools.reduce(jnp.add, [slots_ref[e * lists + q, t] for e in range(n_ens)]) for t in range(2)
        )
        amounts = value * weight - amount
        amount_ref[at, :] = amounts
        put(to, row_ref[at, :] - first, lane_ref[at, :], amounts)

    def use(q, of):
        acc_ref[...] += product_nt(of[0][...], of[1][...])

    in_turns(lists, build, use, slots)
    out_ref[...] = acc_ref[:, :LANES] + acc_ref[:, LANES:]


def matrices_kernel(scale, local_ref, root_ref, to_members_ref, to_static_ref):
    to_members_ref[...] = level_product(local_ref[...] * f32(scale), True)
    to_static_ref[...] = level_product(root_ref[...], True)


def scatter_rest_kernel(cap_rows, row_ref, lane_ref, amount_ref, own_ref, *refs):
    sources, out_ref, kept, acc_ref, sems, slots = (
        refs[:3],
        refs[3],
        refs[4:7],
        refs[7],
        refs[8],
        (refs[9:11], refs[11:13]),
    )
    copies = [pltpu.make_async_copy(s, t, sems.at[i]) for i, (s, t) in enumerate(zip(sources, kept))]
    for copy in copies:
        copy.start()
    cells = out_ref.shape[0]
    own = own_ref.shape[0]
    n_ens = cells // own
    me = lax.axis_index("ens")
    first = (me + 1) * own
    acc_ref[...] = jnp.zeros_like(acc_ref)

    def build(q, to):
        at = pl.ds(pl.multiple_of(q * cap_rows, cap_rows), cap_rows)
        row = row_ref[at, :]
        turned = row - first
        turned = jnp.where(row < 0, -1, jnp.where(turned < 0, turned + cells, turned))
        put(to, turned, lane_ref[at, :], amount_ref[at, :])

    def use(q, of):
        acc_ref[...] += product_nt(of[0][...], of[1][...])

    in_turns(row_ref.shape[0] // cap_rows, build, use, slots)
    out_ref[pl.ds(pl.multiple_of(me * own, own), own), :] = own_ref[...]
    for t in range(1, n_ens):
        to = pl.ds(pl.multiple_of((me + t) % n_ens * own, own), own)
        piece = acc_ref[(t - 1) * own : t * own, :]
        out_ref[to, :] = piece[:, :LANES] + piece[:, LANES:]
    for copy in copies:
        copy.wait()


def static_kernel(matrix_ref, static_ref, *refs):
    parts, (out_ref, smooth_ref) = refs[:-2], refs[-2:]
    levels, per_level, _ = static_ref.shape
    share = levels // len(parts)
    me = lax.axis_index("ens")
    for d, part in enumerate(parts):
        smooth_ref[pl.ds((me + d) % len(parts) * share, share)] = part[...]
    for j in range(0, per_level, 32):
        terms = [three_terms(smooth_ref[:, j + i : j + i + 16, :].reshape(levels * 16, LANES)) for i in (0, 16)]
        change = jnp.dot(matrix_ref[...], jnp.concatenate(terms, axis=1), preferred_element_type=f32)
        for i, part in ((0, change[:, :LANES]), (16, change[:, LANES:])):
            at = slice(j + i, j + i + 16)
            out_ref[:, at, :] = static_ref[:, at, :] + part.reshape(levels, 16, LANES)


def shifted(x, by):
    count = lax.axis_size("cols")
    return lax.ppermute(x, "cols", [(i, (i + by) % count) for i in range(count)])


def from_peers(x):
    count = lax.axis_size("ens")
    return [lax.ppermute(x, "ens", [((i + d) % count, i) for i in range(count)]) for d in range(1, count)]


def swapped(own, before, after):
    odd = lax.axis_index("cols") % 2
    count = lax.axis_size("cols")
    pack = jnp.stack([own, jnp.where(odd == 1, before, after)])
    return lax.ppermute(pack, "cols", [(i, i ^ 1) for i in range(count)])


def local(
    static_control,
    ensemble_control,
    perturbations,
    vertical_root,
    vertical_local,
    face_north,
    face_east,
    innovation,
    obs_weight,
    obs_slot,
    send_index,
    send_count,
):
    n_ens = lax.axis_size("ens")
    n_cols = lax.axis_size("cols")
    members, levels, rows, lon = ensemble_control.shape
    per_level = rows * lon // LANES
    cells = levels * per_level
    lev_share = levels // n_ens
    own = lev_share * per_level
    lists, capacity = send_index.shape
    cap_rows = capacity // LANES
    entry_rows = lists * cap_rows
    member_scale = 1.0 / math.sqrt(members * n_ens - 1)

    static = in_hbm(tiled(static_control))
    control = in_hbm(tiled(ensemble_control))
    pert = in_hbm(tiled(perturbations))

    def whole(*shape):
        return pl.BlockSpec(shape, lambda i: (0,) * len(shape))

    packed, entry_row, entry_lane = pl.pallas_call(
        functools.partial(prepare_kernel, lev_share, rows),
        grid=(1,),
        in_specs=[
            SMEM,
            SMEM,
            whole(levels, per_level, LANES),
            whole(per_level, LANES),
            whole(per_level, LANES),
            whole(lists, capacity),
        ],
        out_specs=[VMEM] * 3,
        out_shape=[
            pltpu.VMEM((lev_share + 2, per_level, LANES), f32),
            pltpu.VMEM((entry_rows, LANES), jnp.int32),
            pltpu.VMEM((entry_rows, LANES), jnp.int32),
        ],
        compiler_params=params(8),
        name="prepare",
    )(
        in_hbm(vertical_root),
        in_hbm(send_count),
        static,
        in_hbm(tiled(face_north)),
        in_hbm(tiled(face_east)),
        in_hbm(send_index),
    )
    before, after = shifted(packed, 2), shifted(packed, -2)

    obs_rows = obs_slot.shape[0] // LANES
    share_rows = obs_rows // n_ens
    coarse = n_cols * capacity // FINE
    size = levels * 16
    obs_slot, packed = lax.optimization_barrier((obs_slot, packed))
    slots, part = pl.pallas_call(
        functools.partial(observe_kernel, n_cols, cap_rows, member_scale),
        grid=(1,),
        in_specs=[pl.BlockSpec(memory_space=pl.ANY)] * 6,
        out_specs=[whole(n_ens * n_cols, 2, cap_rows, LANES), VMEM],
        out_shape=[
            pltpu.HBM((n_ens * n_cols, 2, cap_rows, LANES), f32),
            pltpu.VMEM((levels, per_level, LANES), f32),
        ],
        scratch_shapes=[
            pltpu.VMEM((coarse, 4 * FINE), f32),
            pltpu.VMEM((2, coarse, LANES), f32),
            pltpu.VMEM((size, 3 * size), bf16),
            pltpu.VMEM((share_rows, LANES), jnp.int32),
            pltpu.VMEM((share_rows, LANES), f32),
            pltpu.VMEM((share_rows, LANES), f32),
            pltpu.VMEM((levels, levels), f32),
            pltpu.VMEM(control.shape, f32),
            pltpu.VMEM(pert.shape, bf16),
            pltpu.SemaphoreType.DMA((6,)),
        ]
        + [pltpu.VMEM((coarse, 8 * LANES), bf16), pltpu.VMEM((4 * FINE, 8 * LANES), bf16)] * 2,
        compiler_params=params(24),
        name="slot_sums_and_members",
    )(
        in_hbm(obs_slot.reshape(obs_rows, LANES)),
        in_hbm(obs_weight.reshape(obs_rows, LANES)),
        in_hbm(innovation.reshape(obs_rows, LANES)),
        in_hbm(vertical_local),
        control,
        pert,
    )
    before, after, slots = lax.optimization_barrier((before, after, slots))
    other = swapped(packed, before, after)
    slots = lax.all_to_all(slots, ("ens", "cols"), split_axis=0, concat_axis=0, tiled=True)

    increment, coefs = pl.pallas_call(
        functools.partial(first_diffusion_kernel, lev_share, rows),
        in_specs=[VMEM] * 4,
        out_specs=[VMEM] * 2,
        out_shape=[
            pltpu.VMEM((lev_share, per_level, LANES), f32),
            pltpu.VMEM((5, 5 * rows, per_level // rows, LANES), f32),
        ],
        compiler_params=params(8),
        cost_estimate=pl.CostEstimate(flops=1 << 26, bytes_accessed=1 << 22, transcendentals=0),
        name="diffuse_forward",
    )(before, packed, after, other)

    values = pl.pallas_call(
        functools.partial(lookup_kernel, cap_rows),
        in_specs=[VMEM] * 4,
        out_specs=VMEM,
        out_shape=pltpu.VMEM((entry_rows, LANES), f32),
        scratch_shapes=[pltpu.VMEM((cells, 2 * LANES), bf16)] + [pltpu.VMEM((capacity, cells), bf16)] * 2,
        compiler_params=params(16),
        cost_estimate=pl.CostEstimate(
            flops=4 * cells * LANES * lists * capacity, bytes_accessed=8 * cells * lists * capacity // 4, transcendentals=0
        ),
        name="lookup",
    )(part.reshape(cells, LANES), increment.reshape(own, LANES), entry_row, entry_lane)
    values, slots = lax.optimization_barrier((values, slots))
    shares = [values] + from_peers(values)

    adjoint_own, amounts = pl.pallas_call(
        functools.partial(scatter_own_kernel, cap_rows),
        in_specs=[VMEM] * (3 + n_ens),
        out_specs=[VMEM] * 2,
        out_shape=[pltpu.VMEM((own, LANES), f32), pltpu.VMEM((entry_rows, LANES), f32)],
        scratch_shapes=[pltpu.VMEM((own, 2 * LANES), f32)]
        + [pltpu.VMEM((own, capacity), bf16), pltpu.VMEM((2 * LANES, capacity), bf16)] * 2,
        compiler_params=params(16),
        name="scatter_own",
    )(entry_row, entry_lane, slots, *shares)
    tile = adjoint_own.reshape(lev_share, per_level, LANES)
    tile_before, tile_after = shifted(tile, 2), shifted(tile, -2)

    adjoint, static_here, control_here, pert_here = pl.pallas_call(
        functools.partial(scatter_rest_kernel, cap_rows),
        in_specs=[VMEM] * 4 + [pl.BlockSpec(memory_space=pl.ANY)] * 3,
        out_specs=[VMEM] * 4,
        out_shape=[
            pltpu.VMEM((cells, LANES), f32),
            pltpu.VMEM(static.shape, f32),
            pltpu.VMEM(control.shape, f32),
            pltpu.VMEM(pert.shape, bf16),
        ],
        scratch_shapes=[pltpu.VMEM((cells - own, 2 * LANES), f32), pltpu.SemaphoreType.DMA((3,))]
        + [pltpu.VMEM((cells - own, capacity), bf16), pltpu.VMEM((2 * LANES, capacity), bf16)] * 2,
        compiler_params=params(16),
        name="scatter_rest",
    )(entry_row, entry_lane, amounts, adjoint_own, static, control, pert)
    tile_before, tile_after, adjoint, vertical_local, vertical_root = lax.optimization_barrier(
        (tile_before, tile_after, adjoint, vertical_local, vertical_root)
    )
    tile_other = swapped(tile, tile_before, tile_after)
    from_local, from_root = pl.pallas_call(
        functools.partial(matrices_kernel, member_scale),
        grid=(1,),
        in_specs=[whole(levels, levels)] * 2,
        out_specs=[VMEM] * 2,
        out_shape=[pltpu.VMEM((size, 3 * size), bf16)] * 2,
        compiler_params=params(8),
        name="level_matrices",
    )(in_hbm(vertical_local), in_hbm(vertical_root))
    coefs, from_local, from_root = lax.optimization_barrier((coefs, from_local, from_root))

    smooth = pl.pallas_call(
        functools.partial(second_diffusion_kernel, rows),
        in_specs=[VMEM] * 5,
        out_specs=VMEM,
        out_shape=pltpu.VMEM((lev_share, per_level, LANES), f32),
        compiler_params=params(8),
        name="diffuse_adjoint",
    )(coefs, tile_before, tile, tile_after, tile_other)
    smooth, adjoint = lax.optimization_barrier((smooth, adjoint))
    smooths = [smooth] + from_peers(smooth)

    group = 2 - members % 2
    ensemble_grad = pl.pallas_call(
        member_kernel,
        grid=(members // group,),
        in_specs=[VMEM] * 4,
        out_specs=pl.BlockSpec((group, levels, per_level, LANES), lambda k: (k, 0, 0, 0)),
        out_shape=jax.ShapeDtypeStruct((members, levels, per_level, LANES), f32),
        compiler_params=params(16),
        name="members_gradient",
    )(from_local, adjoint.reshape(levels, per_level, LANES), control_here, pert_here)

    static_grad = pl.pallas_call(
        static_kernel,
        grid=(1,),
        in_specs=[VMEM] * (2 + n_ens),
        out_specs=whole(levels, per_level, LANES),
        out_shape=jax.ShapeDtypeStruct((levels, per_level, LANES), f32),
        scratch_shapes=[pltpu.VMEM((levels, per_level, LANES), f32)],
        compiler_params=params(8),
        name="static_gradient",
    )(from_root, static_here, *smooths)
    return (untiled(static_grad, rows), untiled(ensemble_grad, rows))


def solution(mesh):
    placed = (
        P(None, "cols", None),
        P("ens", None, "cols", None),
        P("ens", None, "cols", None),
        P(),
        P(),
        P("cols", None),
        P("cols", None),
        P("cols"),
        P("cols"),
        P("cols"),
        P("cols", None),
        P("cols"),
    )
    return jax.shard_map(
        local,
        mesh=mesh,
        in_specs=placed,
        out_specs=(P(None, "cols", None), P("ens", None, "cols", None)),
        check_vma=False,
    )
```

```python
import functools
import math

import jax
import jax.numpy as jnp
from jax import lax
from jax.experimental import pallas as pl
from jax.experimental.pallas import tpu as pltpu
from jax.sharding import PartitionSpec as P

NDIFF = 4
LANES = 128
FINE = 64
MIB = 1 << 20

f32 = jnp.float32
bf16 = jnp.bfloat16
SMEM = pl.BlockSpec(memory_space=pltpu.SMEM)
VMEM = pl.BlockSpec(memory_space=pltpu.VMEM)


def tiled(field):
    *lead, rows, lon = field.shape
    field = field.reshape(*lead, rows, lon // LANES, LANES)
    return jnp.swapaxes(field, -3, -2).reshape(*lead, rows * lon // LANES, LANES)


def untiled(field, rows):
    *lead, count, lanes = field.shape
    field = field.reshape(*lead, count // rows, rows, lanes)
    return jnp.swapaxes(field, -3, -2).reshape(*lead, rows, count // rows * lanes)


def params(limit, **more):
    return pltpu.CompilerParams(vmem_limit_bytes=limit * MIB, **more)


def halves(x):
    high = x.astype(bf16)
    return high, (x - high.astype(f32)).astype(bf16)


def in_hbm(x):
    return pltpu.with_memory_space_constraint(x, pltpu.HBM)


def spread(row, dtype):
    return jnp.broadcast_to(row, (16, row.shape[1])).astype(dtype)


def matches(index, count):
    ids = lax.broadcasted_iota(jnp.int32, (count, index.shape[1]), 0).astype(jnp.int16)
    return ids.reshape(count // 16, 16, index.shape[1]) == spread(index, jnp.int16)[None]


def placed_at(index, count, amount=None):
    where = matches(index, count)
    amount = bf16(1) if amount is None else spread(amount, bf16)[None]
    return jnp.where(where, amount, bf16(0)).reshape(count, index.shape[1])


def in_turns(count, build, use, slots):
    build(0, slots[0])

    def step(i, carry):
        use(2 * i, slots[0])
        build(2 * i + 1, slots[1])
        use(2 * i + 1, slots[1])
        build(jnp.minimum(2 * i + 2, count - 1), slots[0])
        return carry

    lax.fori_loop(0, count // 2, step, 0)
    if count % 2:
        use(count - 1, slots[0])


def product_nt(left, right):
    return lax.dot_general(left, right, (((1,), (1,)), ((), ())), preferred_element_type=f32)


def over(x, size):
    if size & (size - 1):
        return lax.div(x, jnp.int32(size)), lax.rem(x, jnp.int32(size))
    return lax.shift_right_logical(x, jnp.int32(size.bit_length() - 1)), x & (size - 1)


def prepare_kernel(lev_share, rows, root_ref, count_ref, static_ref, north_ref, east_ref, index_ref, out_ref, row_ref, lane_ref):
    levels, per_level, _ = static_ref.shape
    first = lax.axis_index("ens") * lev_share
    for j in range(lev_share):
        total = root_ref[first + j, 0] * static_ref[0]
        for m in range(1, levels):
            total = total + root_ref[first + j, m] * static_ref[m]
        out_ref[j] = total
    out_ref[lev_share] = north_ref[...]
    out_ref[lev_share + 1] = east_ref[...]
    lists, capacity = index_ref.shape
    lon = per_level // rows * LANES
    pieces = capacity // LANES
    slot = lax.broadcasted_iota(jnp.int32, (1, capacity), 1)
    for q in range(lists):
        cell = index_ref[q : q + 1, :]
        rest, lane = over(cell, LANES)
        rest, block = over(rest, lon // LANES)
        level, row = over(rest, rows)
        grid_row = jnp.where(slot < count_ref[q], level * per_level + block * rows + row, -1)
        for c in range(pieces):
            at = q * pieces + c
            row_ref[at : at + 1, :] = grid_row[:, c * LANES : (c + 1) * LANES]
            lane_ref[at : at + 1, :] = lane[:, c * LANES : (c + 1) * LANES]


def level_product(matrix, transpose):
    levels = matrix.shape[0]
    size = levels * 16
    pick = lax.broadcasted_iota(jnp.int32, (size, levels), 0) // 16
    pick = jnp.where(pick == lax.broadcasted_iota(jnp.int32, (size, levels), 1), f32(1), f32(0)).astype(bf16)
    same = (
        lax.broadcasted_iota(jnp.int32, (size, size), 0) % 16 == lax.broadcasted_iota(jnp.int32, (size, size), 1) % 16
    )
    out = []
    for half in halves(matrix):
        if transpose:
            wide = product_nt(pick, half)
        else:
            wide = jnp.dot(pick, half, preferred_element_type=f32)
        wide = product_nt(wide.astype(bf16), pick)
        out.append(jnp.where(same, wide, f32(0)).astype(bf16))
    return jnp.concatenate([out[0], out[0], out[1]], axis=1)


def three_terms(x):
    high, low = halves(x)
    return jnp.concatenate([high, low, high], axis=0)


def observe_kernel(n_cols, cap_rows, scale, *refs):
    sources, (out_ref, part_ref), (acc_ref, fold_ref, matrix_ref), landed, sems, slots = (
        refs[:6],
        refs[6:8],
        refs[8:11],
        refs[11:17],
        refs[17],
        (refs[18:20], refs[20:22]),
    )
    coarse = acc_ref.shape[0]
    obs_rows = landed[0].shape[0]
    group = min(8, obs_rows)
    first = pl.multiple_of(lax.axis_index("ens") * obs_rows, obs_rows)
    copies = [
        pltpu.make_async_copy(sources[i].at[pl.ds(first, obs_rows), :], landed[i], sems.at[i]) for i in range(3)
    ]
    copies += [pltpu.make_async_copy(sources[i], landed[i], sems.at[i]) for i in range(3, 6)]
    for copy in copies:
        copy.start()
    acc_ref[...] = jnp.zeros_like(acc_ref)
    for copy in copies[:3]:
        copy.wait()
    slot_ref, weight_ref, innov_ref, local_ref, control_ref, pert_ref = landed

    def build(i, to):
        at = pl.ds(pl.multiple_of(i * group, group), group)
        weight = weight_ref[at, :]
        amount = weight * innov_ref[at, :]
        upper, lower = over(slot_ref[at, :], FINE)
        terms = [t.astype(f32) for t in halves(weight) + halves(amount)]
        for r in range(group):
            here = slice(r * LANES, (r + 1) * LANES)
            to[0][:, here] = placed_at(upper[r : r + 1, :], coarse)
            mask = matches(lower[r : r + 1, :], FINE)
            for t, term in enumerate(terms):
                term = spread(term[r : r + 1, :], bf16)[None]
                to[1][t * FINE : (t + 1) * FINE, here] = jnp.where(mask, term, bf16(0)).reshape(FINE, LANES)

    def use(i, of):
        acc_ref[...] += product_nt(of[0][...], of[1][...])

    in_turns(obs_rows // group, build, use, slots)
    for t in range(2):
        terms = acc_ref[:, t * LANES : (t + 1) * LANES]
        fold_ref[t] = terms + pltpu.roll(terms, FINE, 1)
    per_row = LANES // FINE
    lane = lax.broadcasted_iota(jnp.int32, (coarse // per_row, LANES), 1)
    weights, amounts = (
        jnp.where(
            lane < FINE,
            fold_ref[t, pl.ds(0, coarse // per_row, stride=per_row), :],
            fold_ref[t, pl.ds(1, coarse // per_row, stride=per_row), :],
        )
        for t in range(2)
    )
    for e in range(out_ref.shape[0] // n_cols):
        for p in range(n_cols):
            out_ref[e * n_cols + p, 0] = weights[p * cap_rows : (p + 1) * cap_rows]
            out_ref[e * n_cols + p, 1] = amounts[p * cap_rows : (p + 1) * cap_rows]
    for copy in copies[3:]:
        copy.wait()
    matrix_ref[...] = level_product(local_ref[...] * f32(scale), False)
    sum_members(matrix_ref, control_ref, pert_ref, part_ref)


def sum_members(matrix_ref, control_ref, pert_ref, out_ref):
    members, levels, per_level, _ = control_ref.shape
    group = 2 - members % 2

    def chunk(j, carry):
        at = pl.ds(pl.multiple_of(j * 16, 16), 16)
        total = jnp.zeros((levels * 16, LANES), f32)
        for k in range(0, members, group):
            terms = [three_terms(control_ref[k + i, :, at, :].reshape(levels * 16, LANES)) for i in range(group)]
            local = jnp.dot(matrix_ref[...], jnp.concatenate(terms, axis=1), preferred_element_type=f32)
            for i in range(group):
                pert = pert_ref[k + i, :, at, :].astype(f32).reshape(levels * 16, LANES)
                total = total + pert * local[:, i * LANES : (i + 1) * LANES]
        out_ref[:, at, :] = total.reshape(levels, 16, LANES)
        return carry

    lax.fori_loop(0, per_level // 16, chunk, 0)


def member_kernel(matrix_ref, adjoint_ref, control_ref, pert_ref, out_ref):
    group, levels, per_level, _ = out_ref.shape
    first = pl.program_id(0) * group

    def chunk(j, carry):
        at = pl.ds(pl.multiple_of(j * 16, 16), 16)
        adjoint = adjoint_ref[:, at, :]
        terms = [
            three_terms((pert_ref[first + i, :, at, :].astype(f32) * adjoint).reshape(levels * 16, LANES))
            for i in range(group)
        ]
        change = jnp.dot(matrix_ref[...], jnp.concatenate(terms, axis=1), preferred_element_type=f32)
        for i in range(group):
            part = change[:, i * LANES : (i + 1) * LANES].reshape(levels, 16, LANES)
            out_ref[i, :, at, :] = control_ref[first + i, :, at, :] + part
        return carry

    lax.fori_loop(0, per_level // 16, chunk, 0)


def eastern(x):
    lane = lax.broadcasted_iota(jnp.int32, x.shape, 1)
    near = pltpu.roll(x, LANES - 1, 1)
    return jnp.where(lane == LANES - 1, pltpu.roll(near, x.shape[0] - 1, 0), near)


def western(x):
    lane = lax.broadcasted_iota(jnp.int32, x.shape, 1)
    near = pltpu.roll(x, 1, 1)
    return jnp.where(lane == 0, pltpu.roll(near, 1, 0), near)


def rows_of(tiles, plane, rows):
    at = lax.axis_index("cols")
    side = len(tiles) // 2
    out = []
    for i, tile in enumerate(tiles):
        for r in range(rows):
            row = tile[plane, pl.ds(r, tile.shape[1] // rows, stride=rows), :]
            if i != side:
                there = at + (i - side)
                row = jnp.where(jnp.logical_and(there >= 0, there < lax.axis_size("cols")), row, f32(0))
            out.append(row)
    return out


def diffuse_rows(tiles, level, coef_ref, rows):
    field = rows_of(tiles, level, rows)
    for step in range(NDIFF):
        field = [
            coef_ref[0, i + step] * field[i]
            + coef_ref[1, i + step] * field[i - 1]
            + coef_ref[2, i + step] * field[i + 1]
            + coef_ref[3, i + step] * eastern(field[i])
            + coef_ref[4, i + step] * western(field[i])
            for i in range(1, len(field) - 1)
        ]
        field = list(field)
    return field


def tiles_of(before_ref, own_ref, after_ref, other_ref):
    odd = lax.axis_index("cols") % 2
    return [before_ref, other_ref.at[1 - odd], own_ref, other_ref.at[odd], after_ref]


def first_diffusion_kernel(lev_share, rows, before_ref, own_ref, after_ref, other_ref, out_ref, coef_ref):
    tiles = tiles_of(before_ref, own_ref, after_ref, other_ref)
    blocks = own_ref.shape[1] // rows
    side = len(tiles) // 2
    north = rows_of(tiles, lev_share, rows)
    east = rows_of(tiles, lev_share + 1, rows)
    for i in range(1, len(north) - 1):
        south = north[i + 1]
        if (i + 1) % rows == 0 and i < side * rows:
            south = south * jnp.where(lax.axis_index("cols") == side - (i + 1) // rows, f32(0), f32(1))
        west = western(east[i])
        coef_ref[0, i] = 1.0 - north[i] - south - east[i] - west
        coef_ref[1, i] = north[i]
        coef_ref[2, i] = south
        coef_ref[3, i] = east[i]
        coef_ref[4, i] = west
    for i in (0, len(north) - 1):
        for c in range(5):
            coef_ref[c, i] = jnp.zeros_like(north[0])

    def body(level, carry):
        final = diffuse_rows(tiles, level, coef_ref, rows)
        for r in range(rows):
            out_ref[level, pl.ds(r, blocks, stride=rows), :] = final[r]
        return carry

    lax.fori_loop(0, lev_share, body, 0)


def second_diffusion_kernel(rows, coef_ref, before_ref, own_ref, after_ref, other_ref, out_ref):
    tiles = tiles_of(before_ref, own_ref, after_ref, other_ref)
    lev_share = out_ref.shape[0]
    blocks = own_ref.shape[1] // rows

    def body(level, carry):
        final = diffuse_rows(tiles, level, coef_ref, rows)
        for r in range(rows):
            out_ref[level, pl.ds(r, blocks, stride=rows), :] = final[r]
        return carry

    lax.fori_loop(0, lev_share, body, 0)


def lookup_kernel(cap_rows, part_ref, static_ref, row_ref, lane_ref, out_ref, field_ref, terms_ref):
    cells = part_ref.shape[0]
    own = static_ref.shape[0]
    at = pl.ds(pl.multiple_of(lax.axis_index("ens") * own, own), own)
    field_ref[...] = part_ref[...]
    field_ref[at, :] += static_ref[...]
    for c in range(0, cells, LANES):
        high, low = halves(field_ref[c : c + LANES, :].T)
        terms_ref[:LANES, c : c + LANES] = high
        terms_ref[LANES:, c : c + LANES] = low
    ids = lax.broadcasted_iota(jnp.int32, (LANES, LANES), 0)

    def look(q, carry):
        at = pl.ds(pl.multiple_of(q * cap_rows, cap_rows), cap_rows)
        rows = row_ref[at, :]
        lanes = lane_ref[at, :]
        picks = [placed_at(rows[c : c + 1, :], cells) for c in range(cap_rows)]
        got = jnp.dot(terms_ref[...], jnp.concatenate(picks, axis=1), preferred_element_type=f32)
        values = []
        for c in range(cap_rows):
            here = slice(c * LANES, (c + 1) * LANES)
            mine = got[:LANES, here] + got[LANES:, here]
            values.append(jnp.sum(jnp.where(ids == lanes[c : c + 1, :], mine, f32(0)), axis=0, keepdims=True))
        out_ref[at, :] = jnp.concatenate(values, axis=0)
        return carry

    lax.fori_loop(0, row_ref.shape[0] // cap_rows, look, 0)


def put(acc_ref, rows, lanes, amounts):
    terms = [h.astype(f32) for h in halves(amounts)]
    left, right = [], []
    for c in range(rows.shape[0]):
        left.append(placed_at(rows[c : c + 1, :], acc_ref.shape[0]))
        mask = matches(lanes[c : c + 1, :], LANES)
        right.append(
            jnp.concatenate(
                [
                    jnp.where(mask, spread(t[c : c + 1, :], bf16)[None], bf16(0)).reshape(LANES, LANES)
                    for t in terms
                ],
                axis=0,
            )
        )
    acc_ref[...] += product_nt(jnp.concatenate(left, axis=1), jnp.concatenate(right, axis=1))


def scatter_own_kernel(cap_rows, row_ref, lane_ref, slots_ref, *refs):
    values, (out_ref, amount_ref, acc_ref) = refs[:-3], refs[-3:]
    own = out_ref.shape[0]
    lists = row_ref.shape[0] // cap_rows
    first = lax.axis_index("ens") * own
    acc_ref[...] = jnp.zeros_like(acc_ref)

    def step(q, carry):
        at = pl.ds(pl.multiple_of(q * cap_rows, cap_rows), cap_rows)
        value = functools.reduce(jnp.add, [v[at, :] for v in values])
        weight, amount = (
            functools.reduce(jnp.add, [slots_ref[e * lists + q, t] for e in range(slots_ref.shape[0] // lists)])
            for t in range(2)
        )
        amounts = value * weight - amount
        amount_ref[at, :] = amounts
        put(acc_ref, row_ref[at, :] - first, lane_ref[at, :], amounts)
        return carry

    lax.fori_loop(0, lists, step, 0)
    out_ref[...] = acc_ref[:, :LANES] + acc_ref[:, LANES:]


def matrices_kernel(scale, local_ref, root_ref, to_members_ref, to_static_ref):
    to_members_ref[...] = level_product(local_ref[...] * f32(scale), True)
    to_static_ref[...] = level_product(root_ref[...], True)


def scatter_rest_kernel(cap_rows, row_ref, lane_ref, amount_ref, own_ref, *refs):
    sources, out_ref, kept, acc_ref, sems = refs[:3], refs[3], refs[4:7], refs[7], refs[8]
    copies = [pltpu.make_async_copy(s, t, sems.at[i]) for i, (s, t) in enumerate(zip(sources, kept))]
    for copy in copies:
        copy.start()
    cells = out_ref.shape[0]
    own = own_ref.shape[0]
    n_ens = cells // own
    me = lax.axis_index("ens")
    first = (me + 1) * own
    acc_ref[...] = jnp.zeros_like(acc_ref)

    def step(q, carry):
        at = pl.ds(pl.multiple_of(q * cap_rows, cap_rows), cap_rows)
        row = row_ref[at, :]
        turned = row - first
        turned = jnp.where(row < 0, -1, jnp.where(turned < 0, turned + cells, turned))
        put(acc_ref, turned, lane_ref[at, :], amount_ref[at, :])
        return carry

    lax.fori_loop(0, row_ref.shape[0] // cap_rows, step, 0)
    out_ref[pl.ds(pl.multiple_of(me * own, own), own), :] = own_ref[...]
    for t in range(1, n_ens):
        to = pl.ds(pl.multiple_of((me + t) % n_ens * own, own), own)
        piece = acc_ref[(t - 1) * own : t * own, :]
        out_ref[to, :] = piece[:, :LANES] + piece[:, LANES:]
    for copy in copies:
        copy.wait()


def static_kernel(matrix_ref, static_ref, *refs):
    parts, (out_ref, smooth_ref) = refs[:-2], refs[-2:]
    levels, per_level, _ = static_ref.shape
    share = levels // len(parts)
    me = lax.axis_index("ens")
    for d, part in enumerate(parts):
        smooth_ref[pl.ds((me + d) % len(parts) * share, share)] = part[...]
    for j in range(0, per_level, 32):
        terms = [three_terms(smooth_ref[:, j + i : j + i + 16, :].reshape(levels * 16, LANES)) for i in (0, 16)]
        change = jnp.dot(matrix_ref[...], jnp.concatenate(terms, axis=1), preferred_element_type=f32)
        for i, part in ((0, change[:, :LANES]), (16, change[:, LANES:])):
            at = slice(j + i, j + i + 16)
            out_ref[:, at, :] = static_ref[:, at, :] + part.reshape(levels, 16, LANES)


def shifted(x, by):
    count = lax.axis_size("cols")
    return lax.ppermute(x, "cols", [(i, (i + by) % count) for i in range(count)])


def from_peers(x):
    count = lax.axis_size("ens")
    return [lax.ppermute(x, "ens", [((i + d) % count, i) for i in range(count)]) for d in range(1, count)]


def over_ens(x):
    count = lax.axis_size("ens")
    if count < 2 or count & (count - 1):
        return [x] + from_peers(x)
    by = 1
    while True:
        other = lax.ppermute(x, "ens", [(i, i ^ by) for i in range(count)])
        by *= 2
        if by == count:
            return [x, other]
        x = x + other


def swapped(own, before, after):
    odd = lax.axis_index("cols") % 2
    count = lax.axis_size("cols")
    pack = jnp.stack([own, jnp.where(odd == 1, before, after)])
    return lax.ppermute(pack, "cols", [(i, i ^ 1) for i in range(count)])


def local(
    static_control,
    ensemble_control,
    perturbations,
    vertical_root,
    vertical_local,
    face_north,
    face_east,
    innovation,
    obs_weight,
    obs_slot,
    send_index,
    send_count,
):
    n_ens = lax.axis_size("ens")
    n_cols = lax.axis_size("cols")
    members, levels, rows, lon = ensemble_control.shape
    per_level = rows * lon // LANES
    cells = levels * per_level
    lev_share = levels // n_ens
    own = lev_share * per_level
    lists, capacity = send_index.shape
    cap_rows = capacity // LANES
    entry_rows = lists * cap_rows
    member_scale = 1.0 / math.sqrt(members * n_ens - 1)

    static = in_hbm(tiled(static_control))
    control = in_hbm(tiled(ensemble_control))
    pert = in_hbm(tiled(perturbations))

    def whole(*shape):
        return pl.BlockSpec(shape, lambda i: (0,) * len(shape))

    packed, entry_row, entry_lane = pl.pallas_call(
        functools.partial(prepare_kernel, lev_share, rows),
        grid=(1,),
        in_specs=[
            SMEM,
            SMEM,
            whole(levels, per_level, LANES),
            whole(per_level, LANES),
            whole(per_level, LANES),
            whole(lists, capacity),
        ],
        out_specs=[VMEM] * 3,
        out_shape=[
            pltpu.VMEM((lev_share + 2, per_level, LANES), f32),
            pltpu.VMEM((entry_rows, LANES), jnp.int32),
            pltpu.VMEM((entry_rows, LANES), jnp.int32),
        ],
        compiler_params=params(8),
        name="prepare",
    )(
        in_hbm(vertical_root),
        in_hbm(send_count),
        static,
        in_hbm(tiled(face_north)),
        in_hbm(tiled(face_east)),
        in_hbm(send_index),
    )
    before, after = shifted(packed, 2), shifted(packed, -2)

    obs_rows = obs_slot.shape[0] // LANES
    share_rows = obs_rows // n_ens
    coarse = n_cols * capacity // FINE
    size = levels * 16
    obs_slot, packed = lax.optimization_barrier((obs_slot, packed))
    slots, part = pl.pallas_call(
        functools.partial(observe_kernel, n_cols, cap_rows, member_scale),
        grid=(1,),
        in_specs=[pl.BlockSpec(memory_space=pl.ANY)] * 6,
        out_specs=[whole(n_ens * n_cols, 2, cap_rows, LANES), VMEM],
        out_shape=[
            pltpu.HBM((n_ens * n_cols, 2, cap_rows, LANES), f32),
            pltpu.VMEM((levels, per_level, LANES), f32),
        ],
        scratch_shapes=[
            pltpu.VMEM((coarse, 4 * FINE), f32),
            pltpu.VMEM((2, coarse, LANES), f32),
            pltpu.VMEM((size, 3 * size), bf16),
            pltpu.VMEM((share_rows, LANES), jnp.int32),
            pltpu.VMEM((share_rows, LANES), f32),
            pltpu.VMEM((share_rows, LANES), f32),
            pltpu.VMEM((levels, levels), f32),
            pltpu.VMEM(control.shape, f32),
            pltpu.VMEM(pert.shape, bf16),
            pltpu.SemaphoreType.DMA((6,)),
        ]
        + [pltpu.VMEM((coarse, 8 * LANES), bf16), pltpu.VMEM((4 * FINE, 8 * LANES), bf16)] * 2,
        compiler_params=params(24),
        name="slot_sums_and_members",
    )(
        in_hbm(obs_slot.reshape(obs_rows, LANES)),
        in_hbm(obs_weight.reshape(obs_rows, LANES)),
        in_hbm(innovation.reshape(obs_rows, LANES)),
        in_hbm(vertical_local),
        control,
        pert,
    )
    before, after, slots = lax.optimization_barrier((before, after, slots))
    other = swapped(packed, before, after)
    slots = lax.all_to_all(slots, ("ens", "cols"), split_axis=0, concat_axis=0, tiled=True)

    increment, coefs = pl.pallas_call(
        functools.partial(first_diffusion_kernel, lev_share, rows),
        in_specs=[VMEM] * 4,
        out_specs=[VMEM] * 2,
        out_shape=[
            pltpu.VMEM((lev_share, per_level, LANES), f32),
            pltpu.VMEM((5, 5 * rows, per_level // rows, LANES), f32),
        ],
        compiler_params=params(8),
        cost_estimate=pl.CostEstimate(flops=1 << 26, bytes_accessed=1 << 22, transcendentals=0),
        name="diffuse_forward",
    )(before, packed, after, other)

    values = pl.pallas_call(
        functools.partial(lookup_kernel, cap_rows),
        in_specs=[VMEM] * 4,
        out_specs=VMEM,
        out_shape=pltpu.VMEM((entry_rows, LANES), f32),
        scratch_shapes=[pltpu.VMEM((cells, LANES), f32), pltpu.VMEM((2 * LANES, cells), bf16)],
        compiler_params=params(16),
        cost_estimate=pl.CostEstimate(
            flops=4 * cells * LANES * lists * capacity, bytes_accessed=8 * cells * lists * capacity // 4, transcendentals=0
        ),
        name="lookup",
    )(part.reshape(cells, LANES), increment.reshape(own, LANES), entry_row, entry_lane)
    values, slots = lax.optimization_barrier((values, slots))
    shares = over_ens(values)

    adjoint_own, amounts = pl.pallas_call(
        functools.partial(scatter_own_kernel, cap_rows),
        in_specs=[VMEM] * (3 + len(shares)),
        out_specs=[VMEM] * 2,
        out_shape=[pltpu.VMEM((own, LANES), f32), pltpu.VMEM((entry_rows, LANES), f32)],
        scratch_shapes=[pltpu.VMEM((own, 2 * LANES), f32)],
        compiler_params=params(16),
        name="scatter_own",
    )(entry_row, entry_lane, slots, *shares)
    tile = adjoint_own.reshape(lev_share, per_level, LANES)
    tile_before, tile_after = shifted(tile, 2), shifted(tile, -2)

    adjoint, static_here, control_here, pert_here = pl.pallas_call(
        functools.partial(scatter_rest_kernel, cap_rows),
        in_specs=[VMEM] * 4 + [pl.BlockSpec(memory_space=pl.ANY)] * 3,
        out_specs=[VMEM] * 4,
        out_shape=[
            pltpu.VMEM((cells, LANES), f32),
            pltpu.VMEM(static.shape, f32),
            pltpu.VMEM(control.shape, f32),
            pltpu.VMEM(pert.shape, bf16),
        ],
        scratch_shapes=[pltpu.VMEM((cells - own, 2 * LANES), f32), pltpu.SemaphoreType.DMA((3,))],
        compiler_params=params(16),
        name="scatter_rest",
    )(entry_row, entry_lane, amounts, adjoint_own, static, control, pert)
    tile_before, tile_after, adjoint, vertical_local, vertical_root = lax.optimization_barrier(
        (tile_before, tile_after, adjoint, vertical_local, vertical_root)
    )
    tile_other = swapped(tile, tile_before, tile_after)
    from_local, from_root = pl.pallas_call(
        functools.partial(matrices_kernel, member_scale),
        grid=(1,),
        in_specs=[whole(levels, levels)] * 2,
        out_specs=[VMEM] * 2,
        out_shape=[pltpu.VMEM((size, 3 * size), bf16)] * 2,
        compiler_params=params(8),
        name="level_matrices",
    )(in_hbm(vertical_local), in_hbm(vertical_root))
    coefs, from_local, from_root = lax.optimization_barrier((coefs, from_local, from_root))

    smooth = pl.pallas_call(
        functools.partial(second_diffusion_kernel, rows),
        in_specs=[VMEM] * 5,
        out_specs=VMEM,
        out_shape=pltpu.VMEM((lev_share, per_level, LANES), f32),
        compiler_params=params(8),
        name="diffuse_adjoint",
    )(coefs, tile_before, tile, tile_after, tile_other)
    smooth, adjoint = lax.optimization_barrier((smooth, adjoint))
    smooths = [smooth] + from_peers(smooth)

    group = 2 - members % 2
    ensemble_grad = pl.pallas_call(
        member_kernel,
        grid=(members // group,),
        in_specs=[VMEM] * 4,
        out_specs=pl.BlockSpec((group, levels, per_level, LANES), lambda k: (k, 0, 0, 0)),
        out_shape=jax.ShapeDtypeStruct((members, levels, per_level, LANES), f32),
        compiler_params=params(16),
        name="members_gradient",
    )(from_local, adjoint.reshape(levels, per_level, LANES), control_here, pert_here)

    static_grad = pl.pallas_call(
        static_kernel,
        grid=(1,),
        in_specs=[VMEM] * (2 + n_ens),
        out_specs=whole(levels, per_level, LANES),
        out_shape=jax.ShapeDtypeStruct((levels, per_level, LANES), f32),
        scratch_shapes=[pltpu.VMEM((levels, per_level, LANES), f32)],
        compiler_params=params(8),
        name="static_gradient",
    )(from_root, static_here, *smooths)
    return (untiled(static_grad, rows), untiled(ensemble_grad, rows))


def solution(mesh):
    placed = (
        P(None, "cols", None),
        P("ens", None, "cols", None),
        P("ens", None, "cols", None),
        P(),
        P(),
        P("cols", None),
        P("cols", None),
        P("cols"),
        P("cols"),
        P("cols"),
        P("cols", None),
        P("cols"),
    )
    return jax.shard_map(
        local,
        mesh=mesh,
        in_specs=placed,
        out_specs=(P(None, "cols", None), P("ens", None, "cols", None)),
        check_vma=False,
    )
```

```python
import functools
import math

import jax
import jax.numpy as jnp
from jax import lax
from jax.experimental import pallas as pl
from jax.experimental.pallas import tpu as pltpu
from jax.sharding import PartitionSpec as P

NDIFF = 4
LANES = 128
FINE = 64
MIB = 1 << 20

f32 = jnp.float32
bf16 = jnp.bfloat16
SMEM = pl.BlockSpec(memory_space=pltpu.SMEM)
VMEM = pl.BlockSpec(memory_space=pltpu.VMEM)


def tiled(field):
    *lead, rows, lon = field.shape
    field = field.reshape(*lead, rows, lon // LANES, LANES)
    return jnp.swapaxes(field, -3, -2).reshape(*lead, rows * lon // LANES, LANES)


def untiled(field, rows):
    *lead, count, lanes = field.shape
    field = field.reshape(*lead, count // rows, rows, lanes)
    return jnp.swapaxes(field, -3, -2).reshape(*lead, rows, count // rows * lanes)


def params(limit, **more):
    return pltpu.CompilerParams(vmem_limit_bytes=limit * MIB, **more)


def halves(x):
    high = x.astype(bf16)
    return high, (x - high.astype(f32)).astype(bf16)


def in_hbm(x):
    return pltpu.with_memory_space_constraint(x, pltpu.HBM)


def spread(row, dtype):
    return jnp.broadcast_to(row, (16, row.shape[1])).astype(dtype)


def matches(index, count):
    ids = lax.broadcasted_iota(jnp.int32, (count, index.shape[1]), 0).astype(jnp.int16)
    return ids.reshape(count // 16, 16, index.shape[1]) == spread(index, jnp.int16)[None]


def placed_at(index, count, amount=None):
    where = matches(index, count)
    amount = bf16(1) if amount is None else spread(amount, bf16)[None]
    return jnp.where(where, amount, bf16(0)).reshape(count, index.shape[1])


def in_turns(count, build, use, slots):
    build(0, slots[0])

    def step(i, carry):
        use(2 * i, slots[0])
        build(2 * i + 1, slots[1])
        use(2 * i + 1, slots[1])
        build(jnp.minimum(2 * i + 2, count - 1), slots[0])
        return carry

    lax.fori_loop(0, count // 2, step, 0)
    if count % 2:
        use(count - 1, slots[0])


def product_nt(left, right):
    return lax.dot_general(left, right, (((1,), (1,)), ((), ())), preferred_element_type=f32)


def over(x, size):
    if size & (size - 1):
        return lax.div(x, jnp.int32(size)), lax.rem(x, jnp.int32(size))
    return lax.shift_right_logical(x, jnp.int32(size.bit_length() - 1)), x & (size - 1)


def peer(i, d, count):
    return (i + d) % count if count & (count - 1) else i ^ d


def prepare_kernel(lev_share, rows, root_ref, count_ref, static_ref, north_ref, east_ref, index_ref, out_ref, row_ref, lane_ref):
    levels, per_level, _ = static_ref.shape
    first = lax.axis_index("ens") * lev_share
    for j in range(lev_share):
        total = root_ref[first + j, 0] * static_ref[0]
        for m in range(1, levels):
            total = total + root_ref[first + j, m] * static_ref[m]
        out_ref[j] = total
    out_ref[lev_share] = north_ref[...]
    out_ref[lev_share + 1] = east_ref[...]
    lists, capacity = index_ref.shape
    lon = per_level // rows * LANES
    pieces = capacity // LANES
    slot = lax.broadcasted_iota(jnp.int32, (1, capacity), 1)
    for q in range(lists):
        cell = index_ref[q : q + 1, :]
        rest, lane = over(cell, LANES)
        rest, block = over(rest, lon // LANES)
        level, row = over(rest, rows)
        grid_row = jnp.where(slot < count_ref[q], level * per_level + block * rows + row, -1)
        for c in range(pieces):
            at = q * pieces + c
            row_ref[at : at + 1, :] = grid_row[:, c * LANES : (c + 1) * LANES]
            lane_ref[at : at + 1, :] = lane[:, c * LANES : (c + 1) * LANES]


def level_product(matrix, transpose):
    levels = matrix.shape[0]
    size = levels * 16
    pick = lax.broadcasted_iota(jnp.int32, (size, levels), 0) // 16
    pick = jnp.where(pick == lax.broadcasted_iota(jnp.int32, (size, levels), 1), f32(1), f32(0)).astype(bf16)
    same = (
        lax.broadcasted_iota(jnp.int32, (size, size), 0) % 16 == lax.broadcasted_iota(jnp.int32, (size, size), 1) % 16
    )
    out = []
    for half in halves(matrix):
        if transpose:
            wide = product_nt(pick, half)
        else:
            wide = jnp.dot(pick, half, preferred_element_type=f32)
        wide = product_nt(wide.astype(bf16), pick)
        out.append(jnp.where(same, wide, f32(0)).astype(bf16))
    return jnp.concatenate([out[0], out[0], out[1]], axis=1)


def three_terms(x):
    high, low = halves(x)
    return jnp.concatenate([high, low, high], axis=0)


def observe_kernel(n_cols, cap_rows, scale, *refs):
    sources, (out_ref, part_ref), (acc_ref, fold_ref, matrix_ref), landed, sems, slots = (
        refs[:6],
        refs[6:8],
        refs[8:11],
        refs[11:17],
        refs[17],
        (refs[18:20], refs[20:22]),
    )
    coarse = acc_ref.shape[0]
    obs_rows = landed[0].shape[0]
    group = min(8, obs_rows)
    first = pl.multiple_of(lax.axis_index("ens") * obs_rows, obs_rows)
    copies = [
        pltpu.make_async_copy(sources[i].at[pl.ds(first, obs_rows), :], landed[i], sems.at[i]) for i in range(3)
    ]
    copies += [pltpu.make_async_copy(sources[i], landed[i], sems.at[i]) for i in range(3, 6)]
    for copy in copies:
        copy.start()
    acc_ref[...] = jnp.zeros_like(acc_ref)
    for copy in copies[:3]:
        copy.wait()
    slot_ref, weight_ref, innov_ref, local_ref, control_ref, pert_ref = landed

    def build(i, to):
        at = pl.ds(pl.multiple_of(i * group, group), group)
        weight = weight_ref[at, :]
        amount = weight * innov_ref[at, :]
        upper, lower = over(slot_ref[at, :], FINE)
        terms = [t.astype(f32) for t in halves(weight) + halves(amount)]
        for r in range(group):
            here = slice(r * LANES, (r + 1) * LANES)
            to[0][:, here] = placed_at(upper[r : r + 1, :], coarse)
            mask = matches(lower[r : r + 1, :], FINE)
            for t, term in enumerate(terms):
                term = spread(term[r : r + 1, :], bf16)[None]
                to[1][t * FINE : (t + 1) * FINE, here] = jnp.where(mask, term, bf16(0)).reshape(FINE, LANES)

    def use(i, of):
        acc_ref[...] += product_nt(of[0][...], of[1][...])

    in_turns(obs_rows // group, build, use, slots)
    for t in range(2):
        terms = acc_ref[:, t * LANES : (t + 1) * LANES]
        fold_ref[t] = terms + pltpu.roll(terms, FINE, 1)
    per_row = LANES // FINE
    lane = lax.broadcasted_iota(jnp.int32, (coarse // per_row, LANES), 1)
    weights, amounts = (
        jnp.where(
            lane < FINE,
            fold_ref[t, pl.ds(0, coarse // per_row, stride=per_row), :],
            fold_ref[t, pl.ds(1, coarse // per_row, stride=per_row), :],
        )
        for t in range(2)
    )
    for p in range(n_cols):
        out_ref[p, 0] = weights[p * cap_rows : (p + 1) * cap_rows]
        out_ref[p, 1] = amounts[p * cap_rows : (p + 1) * cap_rows]
    for copy in copies[3:]:
        copy.wait()
    matrix_ref[...] = level_product(local_ref[...] * f32(scale), False)
    sum_members(matrix_ref, control_ref, pert_ref, part_ref)


def sum_members(matrix_ref, control_ref, pert_ref, out_ref):
    members, levels, per_level, _ = control_ref.shape
    group = 2 - members % 2

    def chunk(j, carry):
        at = pl.ds(pl.multiple_of(j * 16, 16), 16)
        total = jnp.zeros((levels * 16, LANES), f32)
        for k in range(0, members, group):
            terms = [three_terms(control_ref[k + i, :, at, :].reshape(levels * 16, LANES)) for i in range(group)]
            local = jnp.dot(matrix_ref[...], jnp.concatenate(terms, axis=1), preferred_element_type=f32)
            for i in range(group):
                pert = pert_ref[k + i, :, at, :].astype(f32).reshape(levels * 16, LANES)
                total = total + pert * local[:, i * LANES : (i + 1) * LANES]
        out_ref[:, at, :] = total.reshape(levels, 16, LANES)
        return carry

    lax.fori_loop(0, per_level // 16, chunk, 0)


def member_kernel(matrix_ref, adjoint_ref, control_ref, pert_ref, out_ref):
    group, levels, per_level, _ = out_ref.shape
    first = pl.program_id(0) * group

    def chunk(j, carry):
        at = pl.ds(pl.multiple_of(j * 16, 16), 16)
        adjoint = adjoint_ref[:, at, :]
        terms = [
            three_terms((pert_ref[first + i, :, at, :].astype(f32) * adjoint).reshape(levels * 16, LANES))
            for i in range(group)
        ]
        change = jnp.dot(matrix_ref[...], jnp.concatenate(terms, axis=1), preferred_element_type=f32)
        for i in range(group):
            part = change[:, i * LANES : (i + 1) * LANES].reshape(levels, 16, LANES)
            out_ref[i, :, at, :] = control_ref[first + i, :, at, :] + part
        return carry

    lax.fori_loop(0, per_level // 16, chunk, 0)


def eastern(x):
    lane = lax.broadcasted_iota(jnp.int32, x.shape, 1)
    near = pltpu.roll(x, LANES - 1, 1)
    return jnp.where(lane == LANES - 1, pltpu.roll(near, x.shape[0] - 1, 0), near)


def western(x):
    lane = lax.broadcasted_iota(jnp.int32, x.shape, 1)
    near = pltpu.roll(x, 1, 1)
    return jnp.where(lane == 0, pltpu.roll(near, 1, 0), near)


def rows_of(first_ref, second_ref, own_ref, other_ref, plane, rows):
    at = lax.axis_index("cols")
    count = lax.axis_size("cols")
    core, chip = at % 2, at // 2 % 2
    reads = [pl.ds(r, own_ref.shape[1] // rows, stride=rows) for r in range(rows)]
    first = [first_ref[plane, r, :] for r in reads]
    second = [second_ref[plane, r, :] for r in reads]
    out = [jnp.where(jnp.logical_and(chip == 1, at >= 2), f, f32(0)) for f in first]
    out = [jnp.where(jnp.logical_and(chip == 0, at >= 2), s, o) for s, o in zip(second, out)]
    out += [jnp.where(at >= 1, other_ref[1 - core, plane, r, :], f32(0)) for r in reads]
    out += [own_ref[plane, r, :] for r in reads]
    out += [jnp.where(at < count - 1, other_ref[core, plane, r, :], f32(0)) for r in reads]
    last = [jnp.where(jnp.logical_and(chip == 0, at < count - 2), f, f32(0)) for f in first]
    return out + [jnp.where(jnp.logical_and(chip == 1, at < count - 2), s, o) for s, o in zip(second, last)]


def diffuse_rows(tiles, level, coef_ref, rows):
    field = rows_of(*tiles, level, rows)
    for step in range(NDIFF):
        field = [
            coef_ref[0, i + step] * field[i]
            + coef_ref[1, i + step] * field[i - 1]
            + coef_ref[2, i + step] * field[i + 1]
            + coef_ref[3, i + step] * eastern(field[i])
            + coef_ref[4, i + step] * western(field[i])
            for i in range(1, len(field) - 1)
        ]
        field = list(field)
    return field


def first_diffusion_kernel(lev_share, rows, first_ref, second_ref, own_ref, other_ref, out_ref, coef_ref):
    tiles = (first_ref, second_ref, own_ref, other_ref)
    blocks = own_ref.shape[1] // rows
    side = 2
    north = rows_of(*tiles, lev_share, rows)
    east = rows_of(*tiles, lev_share + 1, rows)
    for i in range(1, len(north) - 1):
        south = north[i + 1]
        if (i + 1) % rows == 0 and i < side * rows:
            south = south * jnp.where(lax.axis_index("cols") == side - (i + 1) // rows, f32(0), f32(1))
        west = western(east[i])
        coef_ref[0, i] = 1.0 - north[i] - south - east[i] - west
        coef_ref[1, i] = north[i]
        coef_ref[2, i] = south
        coef_ref[3, i] = east[i]
        coef_ref[4, i] = west
    for i in (0, len(north) - 1):
        for c in range(5):
            coef_ref[c, i] = jnp.zeros_like(north[0])

    def body(level, carry):
        final = diffuse_rows(tiles, level, coef_ref, rows)
        for r in range(rows):
            out_ref[level, pl.ds(r, blocks, stride=rows), :] = final[r]
        return carry

    lax.fori_loop(0, lev_share, body, 0)


def second_diffusion_kernel(rows, coef_ref, first_ref, second_ref, own_ref, other_ref, out_ref):
    tiles = (first_ref, second_ref, own_ref, other_ref)
    lev_share = out_ref.shape[0]
    blocks = own_ref.shape[1] // rows

    def body(level, carry):
        final = diffuse_rows(tiles, level, coef_ref, rows)
        for r in range(rows):
            out_ref[level, pl.ds(r, blocks, stride=rows), :] = final[r]
        return carry

    lax.fori_loop(0, lev_share, body, 0)


def lookup_kernel(cap_rows, part_ref, static_ref, row_ref, lane_ref, out_ref, field_ref, terms_ref):
    cells = part_ref.shape[0]
    own = static_ref.shape[0]
    at = pl.ds(pl.multiple_of(lax.axis_index("ens") * own, own), own)
    field_ref[...] = part_ref[...]
    field_ref[at, :] += static_ref[...]
    for c in range(0, cells, LANES):
        high, low = halves(field_ref[c : c + LANES, :].T)
        terms_ref[:LANES, c : c + LANES] = high
        terms_ref[LANES:, c : c + LANES] = low
    ids = lax.broadcasted_iota(jnp.int32, (LANES, LANES), 0)

    def look(q, carry):
        at = pl.ds(pl.multiple_of(q * cap_rows, cap_rows), cap_rows)
        rows = row_ref[at, :]
        lanes = lane_ref[at, :]
        picks = [placed_at(rows[c : c + 1, :], cells) for c in range(cap_rows)]
        got = jnp.dot(terms_ref[...], jnp.concatenate(picks, axis=1), preferred_element_type=f32)
        values = []
        for c in range(cap_rows):
            here = slice(c * LANES, (c + 1) * LANES)
            mine = got[:LANES, here] + got[LANES:, here]
            values.append(jnp.sum(jnp.where(ids == lanes[c : c + 1, :], mine, f32(0)), axis=0, keepdims=True))
        out_ref[at, :] = jnp.concatenate(values, axis=0)
        return carry

    lax.fori_loop(0, row_ref.shape[0] // cap_rows, look, 0)


def put(acc_ref, rows, lanes, amounts):
    terms = [h.astype(f32) for h in halves(amounts)]
    left, right = [], []
    for c in range(rows.shape[0]):
        left.append(placed_at(rows[c : c + 1, :], acc_ref.shape[0]))
        mask = matches(lanes[c : c + 1, :], LANES)
        right.append(
            jnp.concatenate(
                [
                    jnp.where(mask, spread(t[c : c + 1, :], bf16)[None], bf16(0)).reshape(LANES, LANES)
                    for t in terms
                ],
                axis=0,
            )
        )
    acc_ref[...] += product_nt(jnp.concatenate(left, axis=1), jnp.concatenate(right, axis=1))


def scatter_own_kernel(cap_rows, row_ref, lane_ref, *refs):
    shares, (out_ref, amount_ref, acc_ref) = refs[:-3], refs[-3:]
    own = out_ref.shape[0]
    lists = row_ref.shape[0] // cap_rows
    first = lax.axis_index("ens") * own
    acc_ref[...] = jnp.zeros_like(acc_ref)

    def step(q, carry):
        at = pl.ds(pl.multiple_of(q * cap_rows, cap_rows), cap_rows)
        value, weight, amount = (functools.reduce(jnp.add, [s[t, at, :] for s in shares]) for t in range(3))
        amounts = value * weight - amount
        amount_ref[at, :] = amounts
        put(acc_ref, row_ref[at, :] - first, lane_ref[at, :], amounts)
        return carry

    lax.fori_loop(0, lists, step, 0)
    out_ref[...] = acc_ref[:, :LANES] + acc_ref[:, LANES:]


def matrices_kernel(scale, local_ref, root_ref, to_members_ref, to_static_ref):
    to_members_ref[...] = level_product(local_ref[...] * f32(scale), True)
    to_static_ref[...] = level_product(root_ref[...], True)


def scatter_rest_kernel(cap_rows, row_ref, lane_ref, amount_ref, own_ref, *refs):
    sources, out_ref, kept, acc_ref, sems = refs[:3], refs[3], refs[4:7], refs[7], refs[8]
    copies = [pltpu.make_async_copy(s, t, sems.at[i]) for i, (s, t) in enumerate(zip(sources, kept))]
    for copy in copies:
        copy.start()
    cells = out_ref.shape[0]
    own = own_ref.shape[0]
    n_ens = cells // own
    me = lax.axis_index("ens")
    first = (me + 1) * own
    acc_ref[...] = jnp.zeros_like(acc_ref)

    def step(q, carry):
        at = pl.ds(pl.multiple_of(q * cap_rows, cap_rows), cap_rows)
        row = row_ref[at, :]
        turned = row - first
        turned = jnp.where(row < 0, -1, jnp.where(turned < 0, turned + cells, turned))
        put(acc_ref, turned, lane_ref[at, :], amount_ref[at, :])
        return carry

    lax.fori_loop(0, row_ref.shape[0] // cap_rows, step, 0)
    out_ref[pl.ds(pl.multiple_of(me * own, own), own), :] = own_ref[...]
    for t in range(1, n_ens):
        to = pl.ds(pl.multiple_of((me + t) % n_ens * own, own), own)
        piece = acc_ref[(t - 1) * own : t * own, :]
        out_ref[to, :] = piece[:, :LANES] + piece[:, LANES:]
    for copy in copies:
        copy.wait()


def static_kernel(matrix_ref, static_ref, *refs):
    parts, (out_ref, smooth_ref) = refs[:-2], refs[-2:]
    levels, per_level, _ = static_ref.shape
    share = levels // len(parts)
    me = lax.axis_index("ens")
    for d, part in enumerate(parts):
        smooth_ref[pl.ds(peer(me, d, len(parts)) * share, share)] = part[...]
    for j in range(0, per_level, 32):
        terms = [three_terms(smooth_ref[:, j + i : j + i + 16, :].reshape(levels * 16, LANES)) for i in (0, 16)]
        change = jnp.dot(matrix_ref[...], jnp.concatenate(terms, axis=1), preferred_element_type=f32)
        for i, part in ((0, change[:, :LANES]), (16, change[:, LANES:])):
            at = slice(j + i, j + i + 16)
            out_ref[:, at, :] = static_ref[:, at, :] + part.reshape(levels, 16, LANES)


def exchanged(x):
    count = lax.axis_size("cols")
    out = []
    for start in (0, 1):
        pairs = []
        for i in range(count):
            chip, core = divmod(i, 2)
            partner = (chip + start ^ 1) - start
            pairs.append((i, 2 * partner + core if 0 <= 2 * partner + core < count else i))
        out.append(lax.ppermute(x, "cols", pairs))
    return out


def from_peers(x):
    count = lax.axis_size("ens")
    return [lax.ppermute(x, "ens", [(peer(i, d, count), i) for i in range(count)]) for d in range(1, count)]


def swapped(own, first, second):
    at = lax.axis_index("cols")
    pack = jnp.stack([own, jnp.where(at % 2 == at // 2 % 2, first, second)])
    return lax.ppermute(pack, "cols", [(i, i ^ 1) for i in range(lax.axis_size("cols"))])


def local(
    static_control,
    ensemble_control,
    perturbations,
    vertical_root,
    vertical_local,
    face_north,
    face_east,
    innovation,
    obs_weight,
    obs_slot,
    send_index,
    send_count,
):
    n_ens = lax.axis_size("ens")
    n_cols = lax.axis_size("cols")
    members, levels, rows, lon = ensemble_control.shape
    per_level = rows * lon // LANES
    cells = levels * per_level
    lev_share = levels // n_ens
    own = lev_share * per_level
    lists, capacity = send_index.shape
    cap_rows = capacity // LANES
    entry_rows = lists * cap_rows
    member_scale = 1.0 / math.sqrt(members * n_ens - 1)

    static = in_hbm(tiled(static_control))
    control = in_hbm(tiled(ensemble_control))
    pert = in_hbm(tiled(perturbations))

    def whole(*shape):
        return pl.BlockSpec(shape, lambda i: (0,) * len(shape))

    packed, entry_row, entry_lane = pl.pallas_call(
        functools.partial(prepare_kernel, lev_share, rows),
        grid=(1,),
        in_specs=[
            SMEM,
            SMEM,
            whole(levels, per_level, LANES),
            whole(per_level, LANES),
            whole(per_level, LANES),
            whole(lists, capacity),
        ],
        out_specs=[VMEM] * 3,
        out_shape=[
            pltpu.VMEM((lev_share + 2, per_level, LANES), f32),
            pltpu.VMEM((entry_rows, LANES), jnp.int32),
            pltpu.VMEM((entry_rows, LANES), jnp.int32),
        ],
        compiler_params=params(8),
        name="prepare",
    )(
        in_hbm(vertical_root),
        in_hbm(send_count),
        static,
        in_hbm(tiled(face_north)),
        in_hbm(tiled(face_east)),
        in_hbm(send_index),
    )
    first, second = exchanged(packed)

    obs_rows = obs_slot.shape[0] // LANES
    share_rows = obs_rows // n_ens
    coarse = n_cols * capacity // FINE
    size = levels * 16
    obs_slot, packed = lax.optimization_barrier((obs_slot, packed))
    slots, part = pl.pallas_call(
        functools.partial(observe_kernel, n_cols, cap_rows, member_scale),
        grid=(1,),
        in_specs=[pl.BlockSpec(memory_space=pl.ANY)] * 6,
        out_specs=[whole(n_cols, 2, cap_rows, LANES), VMEM],
        out_shape=[
            pltpu.HBM((n_cols, 2, cap_rows, LANES), f32),
            pltpu.VMEM((levels, per_level, LANES), f32),
        ],
        scratch_shapes=[
            pltpu.VMEM((coarse, 4 * FINE), f32),
            pltpu.VMEM((2, coarse, LANES), f32),
            pltpu.VMEM((size, 3 * size), bf16),
            pltpu.VMEM((share_rows, LANES), jnp.int32),
            pltpu.VMEM((share_rows, LANES), f32),
            pltpu.VMEM((share_rows, LANES), f32),
            pltpu.VMEM((levels, levels), f32),
            pltpu.VMEM(control.shape, f32),
            pltpu.VMEM(pert.shape, bf16),
            pltpu.SemaphoreType.DMA((6,)),
        ]
        + [pltpu.VMEM((coarse, 8 * LANES), bf16), pltpu.VMEM((4 * FINE, 8 * LANES), bf16)] * 2,
        compiler_params=params(24),
        name="slot_sums_and_members",
    )(
        in_hbm(obs_slot.reshape(obs_rows, LANES)),
        in_hbm(obs_weight.reshape(obs_rows, LANES)),
        in_hbm(innovation.reshape(obs_rows, LANES)),
        in_hbm(vertical_local),
        control,
        pert,
    )
    first, second, slots = lax.optimization_barrier((first, second, slots))
    other = swapped(packed, first, second)
    slots = lax.all_to_all(slots, "cols", split_axis=0, concat_axis=0, tiled=True)

    increment, coefs = pl.pallas_call(
        functools.partial(first_diffusion_kernel, lev_share, rows),
        in_specs=[VMEM] * 4,
        out_specs=[VMEM] * 2,
        out_shape=[
            pltpu.VMEM((lev_share, per_level, LANES), f32),
            pltpu.VMEM((5, 5 * rows, per_level // rows, LANES), f32),
        ],
        compiler_params=params(8),
        cost_estimate=pl.CostEstimate(flops=1 << 26, bytes_accessed=1 << 22, transcendentals=0),
        name="diffuse_forward",
    )(first, second, packed, other)

    values = pl.pallas_call(
        functools.partial(lookup_kernel, cap_rows),
        in_specs=[VMEM] * 4,
        out_specs=VMEM,
        out_shape=pltpu.VMEM((entry_rows, LANES), f32),
        scratch_shapes=[pltpu.VMEM((cells, LANES), f32), pltpu.VMEM((2 * LANES, cells), bf16)],
        compiler_params=params(16),
        cost_estimate=pl.CostEstimate(
            flops=4 * cells * LANES * lists * capacity, bytes_accessed=8 * cells * lists * capacity // 4, transcendentals=0
        ),
        name="lookup",
    )(part.reshape(cells, LANES), increment.reshape(own, LANES), entry_row, entry_lane)
    values, slots = lax.optimization_barrier((values, slots))
    slots = jnp.swapaxes(slots, 0, 1).reshape(2, entry_rows, LANES)
    share = jnp.concatenate([values[None], slots])
    shares = [share] + from_peers(share)

    adjoint_own, amounts = pl.pallas_call(
        functools.partial(scatter_own_kernel, cap_rows),
        in_specs=[VMEM] * (2 + n_ens),
        out_specs=[VMEM] * 2,
        out_shape=[pltpu.VMEM((own, LANES), f32), pltpu.VMEM((entry_rows, LANES), f32)],
        scratch_shapes=[pltpu.VMEM((own, 2 * LANES), f32)],
        compiler_params=params(16),
        name="scatter_own",
    )(entry_row, entry_lane, *shares)
    tile = adjoint_own.reshape(lev_share, per_level, LANES)
    tile_first, tile_second = exchanged(tile)

    adjoint, static_here, control_here, pert_here = pl.pallas_call(
        functools.partial(scatter_rest_kernel, cap_rows),
        in_specs=[VMEM] * 4 + [pl.BlockSpec(memory_space=pl.ANY)] * 3,
        out_specs=[VMEM] * 4,
        out_shape=[
            pltpu.VMEM((cells, LANES), f32),
            pltpu.VMEM(static.shape, f32),
            pltpu.VMEM(control.shape, f32),
            pltpu.VMEM(pert.shape, bf16),
        ],
        scratch_shapes=[pltpu.VMEM((cells - own, 2 * LANES), f32), pltpu.SemaphoreType.DMA((3,))],
        compiler_params=params(16),
        name="scatter_rest",
    )(entry_row, entry_lane, amounts, adjoint_own, static, control, pert)
    tile_first, tile_second, adjoint, vertical_local, vertical_root = lax.optimization_barrier(
        (tile_first, tile_second, adjoint, vertical_local, vertical_root)
    )
    tile_other = swapped(tile, tile_first, tile_second)
    from_local, from_root = pl.pallas_call(
        functools.partial(matrices_kernel, member_scale),
        grid=(1,),
        in_specs=[whole(levels, levels)] * 2,
        out_specs=[VMEM] * 2,
        out_shape=[pltpu.VMEM((size, 3 * size), bf16)] * 2,
        compiler_params=params(8),
        name="level_matrices",
    )(in_hbm(vertical_local), in_hbm(vertical_root))
    coefs, from_local, from_root = lax.optimization_barrier((coefs, from_local, from_root))

    smooth = pl.pallas_call(
        functools.partial(second_diffusion_kernel, rows),
        in_specs=[VMEM] * 5,
        out_specs=VMEM,
        out_shape=pltpu.VMEM((lev_share, per_level, LANES), f32),
        compiler_params=params(8),
        name="diffuse_adjoint",
    )(coefs, tile_first, tile_second, tile, tile_other)
    smooth, adjoint = lax.optimization_barrier((smooth, adjoint))
    smooths = [smooth] + from_peers(smooth)

    group = 2 - members % 2
    ensemble_grad = pl.pallas_call(
        member_kernel,
        grid=(members // group,),
        in_specs=[VMEM] * 4,
        out_specs=pl.BlockSpec((group, levels, per_level, LANES), lambda k: (k, 0, 0, 0)),
        out_shape=jax.ShapeDtypeStruct((members, levels, per_level, LANES), f32),
        compiler_params=params(16),
        name="members_gradient",
    )(from_local, adjoint.reshape(levels, per_level, LANES), control_here, pert_here)

    static_grad = pl.pallas_call(
        static_kernel,
        grid=(1,),
        in_specs=[VMEM] * (2 + n_ens),
        out_specs=whole(levels, per_level, LANES),
        out_shape=jax.ShapeDtypeStruct((levels, per_level, LANES), f32),
        scratch_shapes=[pltpu.VMEM((levels, per_level, LANES), f32)],
        compiler_params=params(8),
        name="static_gradient",
    )(from_root, static_here, *smooths)
    return (untiled(static_grad, rows), untiled(ensemble_grad, rows))


def solution(mesh):
    placed = (
        P(None, "cols", None),
        P("ens", None, "cols", None),
        P("ens", None, "cols", None),
        P(),
        P(),
        P("cols", None),
        P("cols", None),
        P("cols"),
        P("cols"),
        P("cols"),
        P("cols", None),
        P("cols"),
    )
    return jax.shard_map(
        local,
        mesh=mesh,
        in_specs=placed,
        out_specs=(P(None, "cols", None), P("ens", None, "cols", None)),
        check_vma=False,
    )
```

```python
import functools
import math

import jax
import jax.numpy as jnp
from jax import lax
from jax.experimental import pallas as pl
from jax.experimental.pallas import tpu as pltpu
from jax.sharding import PartitionSpec as P

NDIFF = 4
LANES = 128
FINE = 64
MIB = 1 << 20

f32 = jnp.float32
bf16 = jnp.bfloat16
SMEM = pl.BlockSpec(memory_space=pltpu.SMEM)
VMEM = pl.BlockSpec(memory_space=pltpu.VMEM)


def tiled(field):
    *lead, rows, lon = field.shape
    field = field.reshape(*lead, rows, lon // LANES, LANES)
    return jnp.swapaxes(field, -3, -2).reshape(*lead, rows * lon // LANES, LANES)


def untiled(field, rows):
    *lead, count, lanes = field.shape
    field = field.reshape(*lead, count // rows, rows, lanes)
    return jnp.swapaxes(field, -3, -2).reshape(*lead, rows, count // rows * lanes)


def params(limit, **more):
    return pltpu.CompilerParams(vmem_limit_bytes=limit * MIB, **more)


def halves(x):
    high = x.astype(bf16)
    return high, (x - high.astype(f32)).astype(bf16)


def in_hbm(x):
    return pltpu.with_memory_space_constraint(x, pltpu.HBM)


def spread(row, dtype):
    return jnp.broadcast_to(row, (16, row.shape[1])).astype(dtype)


def matches(index, count):
    ids = lax.broadcasted_iota(jnp.int32, (count, index.shape[1]), 0).astype(jnp.int16)
    return ids.reshape(count // 16, 16, index.shape[1]) == spread(index, jnp.int16)[None]


def placed_at(index, count, amount=None):
    where = matches(index, count)
    amount = bf16(1) if amount is None else spread(amount, bf16)[None]
    return jnp.where(where, amount, bf16(0)).reshape(count, index.shape[1])


def in_turns(count, build, use, slots):
    build(0, slots[0])

    def step(i, carry):
        use(2 * i, slots[0])
        build(2 * i + 1, slots[1])
        use(2 * i + 1, slots[1])
        build(jnp.minimum(2 * i + 2, count - 1), slots[0])
        return carry

    lax.fori_loop(0, count // 2, step, 0)
    if count % 2:
        use(count - 1, slots[0])


def product_nt(left, right):
    return lax.dot_general(left, right, (((1,), (1,)), ((), ())), preferred_element_type=f32)


def over(x, size):
    if size & (size - 1):
        return lax.div(x, jnp.int32(size)), lax.rem(x, jnp.int32(size))
    return lax.shift_right_logical(x, jnp.int32(size.bit_length() - 1)), x & (size - 1)


def peer(i, d, count):
    return (i + d) % count if count & (count - 1) else i ^ d


def prepare_kernel(lev_share, rows, *refs):
    (root_ref, count_ref, static_ref, north_ref, east_ref, index_ref), sources = refs[:6], refs[6:9]
    (out_ref, row_ref, lane_ref), landed, sems = refs[9:12], refs[12:15], refs[15]
    obs_rows = landed[0].shape[0]
    here = pl.ds(pl.multiple_of(lax.axis_index("ens") * obs_rows, obs_rows), obs_rows)
    copies = [pltpu.make_async_copy(s.at[here, :], t, sems.at[i]) for i, (s, t) in enumerate(zip(sources, landed))]
    for copy in copies:
        copy.start()
    levels, per_level, _ = static_ref.shape
    first = lax.axis_index("ens") * lev_share
    for j in range(lev_share):
        total = root_ref[first + j, 0] * static_ref[0]
        for m in range(1, levels):
            total = total + root_ref[first + j, m] * static_ref[m]
        out_ref[j] = total
    out_ref[lev_share] = north_ref[...]
    out_ref[lev_share + 1] = east_ref[...]
    lists, capacity = index_ref.shape
    lon = per_level // rows * LANES
    pieces = capacity // LANES
    slot = lax.broadcasted_iota(jnp.int32, (1, capacity), 1)
    for q in range(lists):
        cell = index_ref[q : q + 1, :]
        rest, lane = over(cell, LANES)
        rest, block = over(rest, lon // LANES)
        level, row = over(rest, rows)
        grid_row = jnp.where(slot < count_ref[q], level * per_level + block * rows + row, -1)
        for c in range(pieces):
            at = q * pieces + c
            row_ref[at : at + 1, :] = grid_row[:, c * LANES : (c + 1) * LANES]
            lane_ref[at : at + 1, :] = lane[:, c * LANES : (c + 1) * LANES]
    for copy in copies:
        copy.wait()


def level_product(matrix, transpose):
    levels = matrix.shape[0]
    size = levels * 16
    pick = lax.broadcasted_iota(jnp.int32, (size, levels), 0) // 16
    pick = jnp.where(pick == lax.broadcasted_iota(jnp.int32, (size, levels), 1), f32(1), f32(0)).astype(bf16)
    same = (
        lax.broadcasted_iota(jnp.int32, (size, size), 0) % 16 == lax.broadcasted_iota(jnp.int32, (size, size), 1) % 16
    )
    out = []
    for half in halves(matrix):
        if transpose:
            wide = product_nt(pick, half)
        else:
            wide = jnp.dot(pick, half, preferred_element_type=f32)
        wide = product_nt(wide.astype(bf16), pick)
        out.append(jnp.where(same, wide, f32(0)).astype(bf16))
    return jnp.concatenate([out[0], out[0], out[1]], axis=1)


def three_terms(x):
    high, low = halves(x)
    return jnp.concatenate([high, low, high], axis=0)


def observe_kernel(n_cols, cap_rows, scale, *refs):
    (slot_ref, weight_ref, innov_ref), sources, (out_ref, part_ref) = refs[:3], refs[3:6], refs[6:8]
    (acc_ref, fold_ref, matrix_ref), landed, sems, slots = (
        refs[8:11],
        refs[11:14],
        refs[14],
        (refs[15:17], refs[17:19]),
    )
    coarse = acc_ref.shape[1]
    obs_rows = slot_ref.shape[0]
    group = min(8, obs_rows)
    copies = [pltpu.make_async_copy(s, t, sems.at[i]) for i, (s, t) in enumerate(zip(sources, landed))]
    for copy in copies:
        copy.start()
    acc_ref[...] = jnp.zeros_like(acc_ref)
    local_ref, control_ref, pert_ref = landed

    def build(i, to):
        at = pl.ds(pl.multiple_of(i * group, group), group)
        weight = weight_ref[at, :]
        amount = weight * innov_ref[at, :]
        upper, lower = over(slot_ref[at, :], FINE)
        terms = [t.astype(f32) for t in halves(weight) + halves(amount)]
        for r in range(group):
            here = slice(r * LANES, (r + 1) * LANES)
            to[0][:, here] = placed_at(upper[r : r + 1, :], coarse)
            mask = matches(lower[r : r + 1, :], FINE)
            for t, term in enumerate(terms):
                term = spread(term[r : r + 1, :], bf16)[None]
                to[1][t * FINE : (t + 1) * FINE, here] = jnp.where(mask, term, bf16(0)).reshape(FINE, LANES)

    def use(i, of):
        acc_ref[...] += product_nt(of[1][...], of[0][...])

    in_turns(obs_rows // group, build, use, slots)
    for t in range(2):
        at = 2 * t * FINE
        terms = acc_ref[at : at + FINE, :] + acc_ref[at + FINE : at + 2 * FINE, :]
        fold_ref[t] = jnp.concatenate([terms] * (LANES // FINE), axis=0).T
    per_row = LANES // FINE
    lane = lax.broadcasted_iota(jnp.int32, (coarse // per_row, LANES), 1)
    weights, amounts = (
        jnp.where(
            lane < FINE,
            fold_ref[t, pl.ds(0, coarse // per_row, stride=per_row), :],
            fold_ref[t, pl.ds(1, coarse // per_row, stride=per_row), :],
        )
        for t in range(2)
    )
    for p in range(n_cols):
        out_ref[p, 0] = weights[p * cap_rows : (p + 1) * cap_rows]
        out_ref[p, 1] = amounts[p * cap_rows : (p + 1) * cap_rows]
    for copy in copies:
        copy.wait()
    matrix_ref[...] = level_product(local_ref[...] * f32(scale), False)
    sum_members(matrix_ref, control_ref, pert_ref, part_ref)


def sum_members(matrix_ref, control_ref, pert_ref, out_ref):
    members, levels, per_level, _ = control_ref.shape
    group = 2 - members % 2

    def chunk(j, carry):
        at = pl.ds(pl.multiple_of(j * 16, 16), 16)
        total = jnp.zeros((levels * 16, LANES), f32)
        for k in range(0, members, group):
            terms = [three_terms(control_ref[k + i, :, at, :].reshape(levels * 16, LANES)) for i in range(group)]
            local = jnp.dot(matrix_ref[...], jnp.concatenate(terms, axis=1), preferred_element_type=f32)
            for i in range(group):
                pert = pert_ref[k + i, :, at, :].astype(f32).reshape(levels * 16, LANES)
                total = total + pert * local[:, i * LANES : (i + 1) * LANES]
        out_ref[:, at, :] = total.reshape(levels, 16, LANES)
        return carry

    lax.fori_loop(0, per_level // 16, chunk, 0)


def member_kernel(matrix_ref, adjoint_ref, control_ref, pert_ref, out_ref):
    group, levels, per_level, _ = out_ref.shape
    first = pl.program_id(0) * group

    def chunk(j, carry):
        at = pl.ds(pl.multiple_of(j * 16, 16), 16)
        adjoint = adjoint_ref[:, at, :]
        terms = [
            three_terms((pert_ref[first + i, :, at, :].astype(f32) * adjoint).reshape(levels * 16, LANES))
            for i in range(group)
        ]
        change = jnp.dot(matrix_ref[...], jnp.concatenate(terms, axis=1), preferred_element_type=f32)
        for i in range(group):
            part = change[:, i * LANES : (i + 1) * LANES].reshape(levels, 16, LANES)
            out_ref[i, :, at, :] = control_ref[first + i, :, at, :] + part
        return carry

    lax.fori_loop(0, per_level // 16, chunk, 0)


def eastern(x):
    lane = lax.broadcasted_iota(jnp.int32, x.shape, 1)
    near = pltpu.roll(x, LANES - 1, 1)
    return jnp.where(lane == LANES - 1, pltpu.roll(near, x.shape[0] - 1, 0), near)


def western(x):
    lane = lax.broadcasted_iota(jnp.int32, x.shape, 1)
    near = pltpu.roll(x, 1, 1)
    return jnp.where(lane == 0, pltpu.roll(near, 1, 0), near)


def rows_of(first_ref, second_ref, own_ref, other_ref, plane, rows):
    at = lax.axis_index("cols")
    count = lax.axis_size("cols")
    core, chip = at % 2, at // 2 % 2
    reads = [pl.ds(r, own_ref.shape[1] // rows, stride=rows) for r in range(rows)]
    first = [first_ref[plane, r, :] for r in reads]
    second = [second_ref[plane, r, :] for r in reads]
    out = [jnp.where(jnp.logical_and(chip == 1, at >= 2), f, f32(0)) for f in first]
    out = [jnp.where(jnp.logical_and(chip == 0, at >= 2), s, o) for s, o in zip(second, out)]
    out += [jnp.where(at >= 1, other_ref[1 - core, plane, r, :], f32(0)) for r in reads]
    out += [own_ref[plane, r, :] for r in reads]
    out += [jnp.where(at < count - 1, other_ref[core, plane, r, :], f32(0)) for r in reads]
    last = [jnp.where(jnp.logical_and(chip == 0, at < count - 2), f, f32(0)) for f in first]
    return out + [jnp.where(jnp.logical_and(chip == 1, at < count - 2), s, o) for s, o in zip(second, last)]


def diffuse_rows(tiles, level, coef_ref, rows):
    field = rows_of(*tiles, level, rows)
    for step in range(NDIFF):
        field = [
            coef_ref[0, i + step] * field[i]
            + coef_ref[1, i + step] * field[i - 1]
            + coef_ref[2, i + step] * field[i + 1]
            + coef_ref[3, i + step] * eastern(field[i])
            + coef_ref[4, i + step] * western(field[i])
            for i in range(1, len(field) - 1)
        ]
        field = list(field)
    return field


def first_diffusion_kernel(lev_share, rows, first_ref, second_ref, own_ref, other_ref, out_ref, coef_ref):
    tiles = (first_ref, second_ref, own_ref, other_ref)
    blocks = own_ref.shape[1] // rows
    side = 2
    north = rows_of(*tiles, lev_share, rows)
    east = rows_of(*tiles, lev_share + 1, rows)
    for i in range(1, len(north) - 1):
        south = north[i + 1]
        if (i + 1) % rows == 0 and i < side * rows:
            south = south * jnp.where(lax.axis_index("cols") == side - (i + 1) // rows, f32(0), f32(1))
        west = western(east[i])
        coef_ref[0, i] = 1.0 - north[i] - south - east[i] - west
        coef_ref[1, i] = north[i]
        coef_ref[2, i] = south
        coef_ref[3, i] = east[i]
        coef_ref[4, i] = west
    for i in (0, len(north) - 1):
        for c in range(5):
            coef_ref[c, i] = jnp.zeros_like(north[0])

    def body(level, carry):
        final = diffuse_rows(tiles, level, coef_ref, rows)
        for r in range(rows):
            out_ref[level, pl.ds(r, blocks, stride=rows), :] = final[r]
        return carry

    lax.fori_loop(0, lev_share, body, 0)


def second_diffusion_kernel(rows, coef_ref, first_ref, second_ref, own_ref, other_ref, out_ref):
    tiles = (first_ref, second_ref, own_ref, other_ref)
    lev_share = out_ref.shape[0]
    blocks = own_ref.shape[1] // rows

    def body(level, carry):
        final = diffuse_rows(tiles, level, coef_ref, rows)
        for r in range(rows):
            out_ref[level, pl.ds(r, blocks, stride=rows), :] = final[r]
        return carry

    lax.fori_loop(0, lev_share, body, 0)


def lookup_kernel(cap_rows, part_ref, static_ref, row_ref, lane_ref, out_ref, field_ref, terms_ref):
    cells = part_ref.shape[0]
    own = static_ref.shape[0]
    at = pl.ds(pl.multiple_of(lax.axis_index("ens") * own, own), own)
    field_ref[...] = part_ref[...]
    field_ref[at, :] += static_ref[...]
    for c in range(0, cells, LANES):
        high, low = halves(field_ref[c : c + LANES, :].T)
        terms_ref[:LANES, c : c + LANES] = high
        terms_ref[LANES:, c : c + LANES] = low
    ids = lax.broadcasted_iota(jnp.int32, (LANES, LANES), 0)

    def look(q, carry):
        at = pl.ds(pl.multiple_of(q * cap_rows, cap_rows), cap_rows)
        rows = row_ref[at, :]
        lanes = lane_ref[at, :]
        picks = [placed_at(rows[c : c + 1, :], cells) for c in range(cap_rows)]
        got = jnp.dot(terms_ref[...], jnp.concatenate(picks, axis=1), preferred_element_type=f32)
        values = []
        for c in range(cap_rows):
            here = slice(c * LANES, (c + 1) * LANES)
            mine = got[:LANES, here] + got[LANES:, here]
            values.append(jnp.sum(jnp.where(ids == lanes[c : c + 1, :], mine, f32(0)), axis=0, keepdims=True))
        out_ref[at, :] = jnp.concatenate(values, axis=0)
        return carry

    lax.fori_loop(0, row_ref.shape[0] // cap_rows, look, 0)


def put(acc_ref, rows, lanes, amounts):
    terms = [h.astype(f32) for h in halves(amounts)]
    left, right = [], []
    for c in range(rows.shape[0]):
        left.append(placed_at(rows[c : c + 1, :], acc_ref.shape[0]))
        mask = matches(lanes[c : c + 1, :], LANES)
        right.append(
            jnp.concatenate(
                [
                    jnp.where(mask, spread(t[c : c + 1, :], bf16)[None], bf16(0)).reshape(LANES, LANES)
                    for t in terms
                ],
                axis=0,
            )
        )
    acc_ref[...] += product_nt(jnp.concatenate(left, axis=1), jnp.concatenate(right, axis=1))


def scatter_own_kernel(cap_rows, row_ref, lane_ref, *refs):
    shares, (out_ref, amount_ref, acc_ref) = refs[:-3], refs[-3:]
    own = out_ref.shape[0]
    lists = row_ref.shape[0] // cap_rows
    first = lax.axis_index("ens") * own
    acc_ref[...] = jnp.zeros_like(acc_ref)

    def step(q, carry):
        at = pl.ds(pl.multiple_of(q * cap_rows, cap_rows), cap_rows)
        value, weight, amount = (functools.reduce(jnp.add, [s[t, at, :] for s in shares]) for t in range(3))
        amounts = value * weight - amount
        amount_ref[at, :] = amounts
        put(acc_ref, row_ref[at, :] - first, lane_ref[at, :], amounts)
        return carry

    lax.fori_loop(0, lists, step, 0)
    out_ref[...] = acc_ref[:, :LANES] + acc_ref[:, LANES:]


def matrices_kernel(scale, local_ref, root_ref, to_members_ref, to_static_ref):
    to_members_ref[...] = level_product(local_ref[...] * f32(scale), True)
    to_static_ref[...] = level_product(root_ref[...], True)


def scatter_rest_kernel(cap_rows, row_ref, lane_ref, amount_ref, own_ref, *refs):
    sources, out_ref, kept, acc_ref, sems = refs[:3], refs[3], refs[4:7], refs[7], refs[8]
    copies = [pltpu.make_async_copy(s, t, sems.at[i]) for i, (s, t) in enumerate(zip(sources, kept))]
    for copy in copies:
        copy.start()
    cells = out_ref.shape[0]
    own = own_ref.shape[0]
    n_ens = cells // own
    me = lax.axis_index("ens")
    first = (me + 1) * own
    acc_ref[...] = jnp.zeros_like(acc_ref)

    def step(q, carry):
        at = pl.ds(pl.multiple_of(q * cap_rows, cap_rows), cap_rows)
        row = row_ref[at, :]
        turned = row - first
        turned = jnp.where(row < 0, -1, jnp.where(turned < 0, turned + cells, turned))
        put(acc_ref, turned, lane_ref[at, :], amount_ref[at, :])
        return carry

    lax.fori_loop(0, row_ref.shape[0] // cap_rows, step, 0)
    out_ref[pl.ds(pl.multiple_of(me * own, own), own), :] = own_ref[...]
    for t in range(1, n_ens):
        to = pl.ds(pl.multiple_of((me + t) % n_ens * own, own), own)
        piece = acc_ref[(t - 1) * own : t * own, :]
        out_ref[to, :] = piece[:, :LANES] + piece[:, LANES:]
    for copy in copies:
        copy.wait()


def static_kernel(matrix_ref, static_ref, *refs):
    parts, (out_ref, smooth_ref) = refs[:-2], refs[-2:]
    levels, per_level, _ = static_ref.shape
    share = levels // len(parts)
    me = lax.axis_index("ens")
    for d, part in enumerate(parts):
        smooth_ref[pl.ds(peer(me, d, len(parts)) * share, share)] = part[...]
    for j in range(0, per_level, 32):
        terms = [three_terms(smooth_ref[:, j + i : j + i + 16, :].reshape(levels * 16, LANES)) for i in (0, 16)]
        change = jnp.dot(matrix_ref[...], jnp.concatenate(terms, axis=1), preferred_element_type=f32)
        for i, part in ((0, change[:, :LANES]), (16, change[:, LANES:])):
            at = slice(j + i, j + i + 16)
            out_ref[:, at, :] = static_ref[:, at, :] + part.reshape(levels, 16, LANES)


def exchanged(x, starts):
    count = lax.axis_size("cols")
    out = []
    for start in starts:
        pairs = []
        for i in range(count):
            chip, core = divmod(i, 2)
            partner = (chip + start ^ 1) - start
            pairs.append((i, 2 * partner + core if 0 <= 2 * partner + core < count else i))
        out.append(lax.ppermute(x, "cols", pairs))
    return out


def from_peers(x):
    count = lax.axis_size("ens")
    return [lax.ppermute(x, "ens", [(peer(i, d, count), i) for i in range(count)]) for d in range(1, count)]


def swapped(own, first, second):
    at = lax.axis_index("cols")
    pack = jnp.stack([own, jnp.where(at % 2 == at // 2 % 2, first, second)])
    return lax.ppermute(pack, "cols", [(i, i ^ 1) for i in range(lax.axis_size("cols"))])


def local(
    static_control,
    ensemble_control,
    perturbations,
    vertical_root,
    vertical_local,
    face_north,
    face_east,
    innovation,
    obs_weight,
    obs_slot,
    send_index,
    send_count,
):
    n_ens = lax.axis_size("ens")
    n_cols = lax.axis_size("cols")
    members, levels, rows, lon = ensemble_control.shape
    per_level = rows * lon // LANES
    cells = levels * per_level
    lev_share = levels // n_ens
    own = lev_share * per_level
    lists, capacity = send_index.shape
    cap_rows = capacity // LANES
    entry_rows = lists * cap_rows
    member_scale = 1.0 / math.sqrt(members * n_ens - 1)

    static = in_hbm(tiled(static_control))
    control = in_hbm(tiled(ensemble_control))
    pert = in_hbm(tiled(perturbations))

    def whole(*shape):
        return pl.BlockSpec(shape, lambda i: (0,) * len(shape))

    obs_rows = obs_slot.shape[0] // LANES
    share_rows = obs_rows // n_ens
    packed, entry_row, entry_lane, *observed = pl.pallas_call(
        functools.partial(prepare_kernel, lev_share, rows),
        grid=(1,),
        in_specs=[
            SMEM,
            SMEM,
            whole(levels, per_level, LANES),
            whole(per_level, LANES),
            whole(per_level, LANES),
            whole(lists, capacity),
            pl.BlockSpec(memory_space=pl.ANY),
            pl.BlockSpec(memory_space=pl.ANY),
            pl.BlockSpec(memory_space=pl.ANY),
        ],
        out_specs=[VMEM] * 6,
        out_shape=[
            pltpu.VMEM((lev_share + 2, per_level, LANES), f32),
            pltpu.VMEM((entry_rows, LANES), jnp.int32),
            pltpu.VMEM((entry_rows, LANES), jnp.int32),
            pltpu.VMEM((share_rows, LANES), jnp.int32),
            pltpu.VMEM((share_rows, LANES), f32),
            pltpu.VMEM((share_rows, LANES), f32),
        ],
        scratch_shapes=[pltpu.SemaphoreType.DMA((3,))],
        compiler_params=params(8),
        name="prepare",
    )(
        in_hbm(vertical_root),
        in_hbm(send_count),
        static,
        in_hbm(tiled(face_north)),
        in_hbm(tiled(face_east)),
        in_hbm(send_index),
        in_hbm(obs_slot.reshape(obs_rows, LANES)),
        in_hbm(obs_weight.reshape(obs_rows, LANES)),
        in_hbm(innovation.reshape(obs_rows, LANES)),
    )
    second, first = exchanged(packed, (1, 0))

    coarse = n_cols * capacity // FINE
    size = levels * 16
    slots, part = pl.pallas_call(
        functools.partial(observe_kernel, n_cols, cap_rows, member_scale),
        grid=(1,),
        in_specs=[VMEM] * 3 + [pl.BlockSpec(memory_space=pl.ANY)] * 3,
        out_specs=[whole(n_cols, 2, cap_rows, LANES), VMEM],
        out_shape=[
            pltpu.HBM((n_cols, 2, cap_rows, LANES), f32),
            pltpu.VMEM((levels, per_level, LANES), f32),
        ],
        scratch_shapes=[
            pltpu.VMEM((4 * FINE, coarse), f32),
            pltpu.VMEM((2, coarse, LANES), f32),
            pltpu.VMEM((size, 3 * size), bf16),
            pltpu.VMEM((levels, levels), f32),
            pltpu.VMEM(control.shape, f32),
            pltpu.VMEM(pert.shape, bf16),
            pltpu.SemaphoreType.DMA((3,)),
        ]
        + [pltpu.VMEM((coarse, 8 * LANES), bf16), pltpu.VMEM((4 * FINE, 8 * LANES), bf16)] * 2,
        compiler_params=params(24),
        name="slot_sums_and_members",
    )(*observed, in_hbm(vertical_local), control, pert)
    first, second, slots = lax.optimization_barrier((first, second, slots))
    other = swapped(packed, first, second)
    slots = lax.all_to_all(slots, "cols", split_axis=0, concat_axis=0, tiled=True)

    increment, coefs = pl.pallas_call(
        functools.partial(first_diffusion_kernel, lev_share, rows),
        in_specs=[VMEM] * 4,
        out_specs=[VMEM] * 2,
        out_shape=[
            pltpu.VMEM((lev_share, per_level, LANES), f32),
            pltpu.VMEM((5, 5 * rows, per_level // rows, LANES), f32),
        ],
        compiler_params=params(8),
        cost_estimate=pl.CostEstimate(flops=1 << 26, bytes_accessed=1 << 22, transcendentals=0),
        name="diffuse_forward",
    )(first, second, packed, other)

    values = pl.pallas_call(
        functools.partial(lookup_kernel, cap_rows),
        in_specs=[VMEM] * 4,
        out_specs=VMEM,
        out_shape=pltpu.VMEM((entry_rows, LANES), f32),
        scratch_shapes=[pltpu.VMEM((cells, LANES), f32), pltpu.VMEM((2 * LANES, cells), bf16)],
        compiler_params=params(16),
        cost_estimate=pl.CostEstimate(
            flops=4 * cells * LANES * lists * capacity, bytes_accessed=8 * cells * lists * capacity // 4, transcendentals=0
        ),
        name="lookup",
    )(part.reshape(cells, LANES), increment.reshape(own, LANES), entry_row, entry_lane)
    values, slots = lax.optimization_barrier((values, slots))
    slots = jnp.swapaxes(slots, 0, 1).reshape(2, entry_rows, LANES)
    share = jnp.concatenate([values[None], slots])
    shares = [share] + from_peers(share)

    adjoint_own, amounts = pl.pallas_call(
        functools.partial(scatter_own_kernel, cap_rows),
        in_specs=[VMEM] * (2 + n_ens),
        out_specs=[VMEM] * 2,
        out_shape=[pltpu.VMEM((own, LANES), f32), pltpu.VMEM((entry_rows, LANES), f32)],
        scratch_shapes=[pltpu.VMEM((own, 2 * LANES), f32)],
        compiler_params=params(16),
        name="scatter_own",
    )(entry_row, entry_lane, *shares)
    tile = adjoint_own.reshape(lev_share, per_level, LANES)
    tile_first, tile_second = exchanged(tile, (0, 1))

    adjoint, static_here, control_here, pert_here = pl.pallas_call(
        functools.partial(scatter_rest_kernel, cap_rows),
        in_specs=[VMEM] * 4 + [pl.BlockSpec(memory_space=pl.ANY)] * 3,
        out_specs=[VMEM] * 4,
        out_shape=[
            pltpu.VMEM((cells, LANES), f32),
            pltpu.VMEM(static.shape, f32),
            pltpu.VMEM(control.shape, f32),
            pltpu.VMEM(pert.shape, bf16),
        ],
        scratch_shapes=[pltpu.VMEM((cells - own, 2 * LANES), f32), pltpu.SemaphoreType.DMA((3,))],
        compiler_params=params(16),
        name="scatter_rest",
    )(entry_row, entry_lane, amounts, adjoint_own, static, control, pert)
    tile_first, tile_second, adjoint, vertical_local, vertical_root = lax.optimization_barrier(
        (tile_first, tile_second, adjoint, vertical_local, vertical_root)
    )
    tile_other = swapped(tile, tile_first, tile_second)
    from_local, from_root = pl.pallas_call(
        functools.partial(matrices_kernel, member_scale),
        grid=(1,),
        in_specs=[whole(levels, levels)] * 2,
        out_specs=[VMEM] * 2,
        out_shape=[pltpu.VMEM((size, 3 * size), bf16)] * 2,
        compiler_params=params(8),
        name="level_matrices",
    )(in_hbm(vertical_local), in_hbm(vertical_root))
    coefs, from_local, from_root = lax.optimization_barrier((coefs, from_local, from_root))

    smooth = pl.pallas_call(
        functools.partial(second_diffusion_kernel, rows),
        in_specs=[VMEM] * 5,
        out_specs=VMEM,
        out_shape=pltpu.VMEM((lev_share, per_level, LANES), f32),
        compiler_params=params(8),
        name="diffuse_adjoint",
    )(coefs, tile_first, tile_second, tile, tile_other)
    smooth, adjoint = lax.optimization_barrier((smooth, adjoint))
    smooths = [smooth] + from_peers(smooth)

    group = 2 - members % 2
    ensemble_grad = pl.pallas_call(
        member_kernel,
        grid=(members // group,),
        in_specs=[VMEM] * 4,
        out_specs=pl.BlockSpec((group, levels, per_level, LANES), lambda k: (k, 0, 0, 0)),
        out_shape=jax.ShapeDtypeStruct((members, levels, per_level, LANES), f32),
        compiler_params=params(16),
        name="members_gradient",
    )(from_local, adjoint.reshape(levels, per_level, LANES), control_here, pert_here)

    static_grad = pl.pallas_call(
        static_kernel,
        grid=(1,),
        in_specs=[VMEM] * (2 + n_ens),
        out_specs=whole(levels, per_level, LANES),
        out_shape=jax.ShapeDtypeStruct((levels, per_level, LANES), f32),
        scratch_shapes=[pltpu.VMEM((levels, per_level, LANES), f32)],
        compiler_params=params(8),
        name="static_gradient",
    )(from_root, static_here, *smooths)
    return (untiled(static_grad, rows), untiled(ensemble_grad, rows))


def solution(mesh):
    placed = (
        P(None, "cols", None),
        P("ens", None, "cols", None),
        P("ens", None, "cols", None),
        P(),
        P(),
        P("cols", None),
        P("cols", None),
        P("cols"),
        P("cols"),
        P("cols"),
        P("cols", None),
        P("cols"),
    )
    return jax.shard_map(
        local,
        mesh=mesh,
        in_specs=placed,
        out_specs=(P(None, "cols", None), P("ens", None, "cols", None)),
        check_vma=False,
    )
```

```python
import functools
import math

import jax
import jax.numpy as jnp
from jax import lax
from jax.experimental import pallas as pl
from jax.experimental.pallas import tpu as pltpu
from jax.sharding import PartitionSpec as P

NDIFF = 4
LANES = 128
FINE = 64
MIB = 1 << 20

f32 = jnp.float32
bf16 = jnp.bfloat16
SMEM = pl.BlockSpec(memory_space=pltpu.SMEM)
VMEM = pl.BlockSpec(memory_space=pltpu.VMEM)


def tiled(field):
    *lead, rows, lon = field.shape
    field = field.reshape(*lead, rows, lon // LANES, LANES)
    return jnp.swapaxes(field, -3, -2).reshape(*lead, rows * lon // LANES, LANES)


def untiled(field, rows):
    *lead, count, lanes = field.shape
    field = field.reshape(*lead, count // rows, rows, lanes)
    return jnp.swapaxes(field, -3, -2).reshape(*lead, rows, count // rows * lanes)


def params(limit, **more):
    return pltpu.CompilerParams(vmem_limit_bytes=limit * MIB, **more)


def halves(x):
    high = x.astype(bf16)
    return high, (x - high.astype(f32)).astype(bf16)


def in_hbm(x):
    return pltpu.with_memory_space_constraint(x, pltpu.HBM)


def spread(row, dtype):
    return jnp.broadcast_to(row, (16, row.shape[1])).astype(dtype)


def matches(index, count):
    ids = lax.broadcasted_iota(jnp.int32, (count, index.shape[1]), 0).astype(jnp.int16)
    return ids.reshape(count // 16, 16, index.shape[1]) == spread(index, jnp.int16)[None]


def placed_at(index, count, amount=None):
    where = matches(index, count)
    amount = bf16(1) if amount is None else spread(amount, bf16)[None]
    return jnp.where(where, amount, bf16(0)).reshape(count, index.shape[1])


def in_turns(count, build, use, slots):
    build(0, slots[0])

    def step(i, carry):
        use(2 * i, slots[0])
        build(2 * i + 1, slots[1])
        use(2 * i + 1, slots[1])
        build(jnp.minimum(2 * i + 2, count - 1), slots[0])
        return carry

    lax.fori_loop(0, count // 2, step, 0)
    if count % 2:
        use(count - 1, slots[0])


def product_nt(left, right):
    return lax.dot_general(left, right, (((1,), (1,)), ((), ())), preferred_element_type=f32)


def over(x, size):
    if size & (size - 1):
        return lax.div(x, jnp.int32(size)), lax.rem(x, jnp.int32(size))
    return lax.shift_right_logical(x, jnp.int32(size.bit_length() - 1)), x & (size - 1)


def peer(i, d, count):
    return (i + d) % count if count & (count - 1) else i ^ d


def prepare_kernel(lev_share, rows, *refs):
    (root_ref, count_ref, static_ref, north_ref, east_ref, index_ref), sources = refs[:6], refs[6:9]
    (out_ref, row_ref, lane_ref), landed, sems = refs[9:12], refs[12:15], refs[15]
    obs_rows = landed[0].shape[0]
    here = pl.ds(pl.multiple_of(lax.axis_index("ens") * obs_rows, obs_rows), obs_rows)
    copies = [pltpu.make_async_copy(s.at[here, :], t, sems.at[i]) for i, (s, t) in enumerate(zip(sources, landed))]
    for copy in copies:
        copy.start()
    levels, per_level, _ = static_ref.shape
    first = lax.axis_index("ens") * lev_share
    for j in range(lev_share):
        total = root_ref[first + j, 0] * static_ref[0]
        for m in range(1, levels):
            total = total + root_ref[first + j, m] * static_ref[m]
        out_ref[j] = total
    out_ref[lev_share] = north_ref[...]
    out_ref[lev_share + 1] = east_ref[...]
    lists, capacity = index_ref.shape
    lon = per_level // rows * LANES
    pieces = capacity // LANES
    slot = lax.broadcasted_iota(jnp.int32, (1, capacity), 1)
    for q in range(lists):
        cell = index_ref[q : q + 1, :]
        rest, lane = over(cell, LANES)
        rest, block = over(rest, lon // LANES)
        level, row = over(rest, rows)
        grid_row = jnp.where(slot < count_ref[q], level * per_level + block * rows + row, -1)
        for c in range(pieces):
            at = q * pieces + c
            row_ref[at : at + 1, :] = grid_row[:, c * LANES : (c + 1) * LANES]
            lane_ref[at : at + 1, :] = lane[:, c * LANES : (c + 1) * LANES]
    for copy in copies:
        copy.wait()


def level_product(matrix, transpose):
    levels = matrix.shape[0]
    size = levels * 16
    pick = lax.broadcasted_iota(jnp.int32, (size, levels), 0) // 16
    pick = jnp.where(pick == lax.broadcasted_iota(jnp.int32, (size, levels), 1), f32(1), f32(0)).astype(bf16)
    same = (
        lax.broadcasted_iota(jnp.int32, (size, size), 0) % 16 == lax.broadcasted_iota(jnp.int32, (size, size), 1) % 16
    )
    out = []
    for half in halves(matrix):
        if transpose:
            wide = product_nt(pick, half)
        else:
            wide = jnp.dot(pick, half, preferred_element_type=f32)
        wide = product_nt(wide.astype(bf16), pick)
        out.append(jnp.where(same, wide, f32(0)).astype(bf16))
    return jnp.concatenate([out[0], out[0], out[1]], axis=1)


def three_terms(x):
    high, low = halves(x)
    return jnp.concatenate([high, low, high], axis=0)


def observe_kernel(n_cols, cap_rows, scale, *refs):
    (slot_ref, weight_ref, innov_ref), sources, (out_ref, part_ref) = refs[:3], refs[3:6], refs[6:8]
    (acc_ref, fold_ref, matrix_ref), landed, sems, slots = (
        refs[8:11],
        refs[11:14],
        refs[14],
        (refs[15:17], refs[17:19]),
    )
    coarse = acc_ref.shape[1]
    obs_rows = slot_ref.shape[0]
    group = min(8, obs_rows)
    copies = [pltpu.make_async_copy(s, t, sems.at[i]) for i, (s, t) in enumerate(zip(sources, landed))]
    for copy in copies:
        copy.start()
    acc_ref[...] = jnp.zeros_like(acc_ref)
    local_ref, control_ref, pert_ref = landed

    def build(i, to):
        at = pl.ds(pl.multiple_of(i * group, group), group)
        weight = weight_ref[at, :]
        amount = weight * innov_ref[at, :]
        upper, lower = over(slot_ref[at, :], FINE)
        terms = [t.astype(f32) for t in halves(weight) + halves(amount)]
        for r in range(group):
            here = slice(r * LANES, (r + 1) * LANES)
            to[0][:, here] = placed_at(upper[r : r + 1, :], coarse)
            mask = matches(lower[r : r + 1, :], FINE)
            for t, term in enumerate(terms):
                term = spread(term[r : r + 1, :], bf16)[None]
                to[1][t * FINE : (t + 1) * FINE, here] = jnp.where(mask, term, bf16(0)).reshape(FINE, LANES)

    def use(i, of):
        acc_ref[...] += product_nt(of[1][...], of[0][...])

    in_turns(obs_rows // group, build, use, slots)
    for t in range(2):
        at = 2 * t * FINE
        terms = acc_ref[at : at + FINE, :] + acc_ref[at + FINE : at + 2 * FINE, :]
        fold_ref[t] = jnp.concatenate([terms] * (LANES // FINE), axis=0).T
    per_row = LANES // FINE
    lane = lax.broadcasted_iota(jnp.int32, (coarse // per_row, LANES), 1)
    weights, amounts = (
        jnp.where(
            lane < FINE,
            fold_ref[t, pl.ds(0, coarse // per_row, stride=per_row), :],
            fold_ref[t, pl.ds(1, coarse // per_row, stride=per_row), :],
        )
        for t in range(2)
    )
    for p in range(n_cols):
        out_ref[p, 0] = weights[p * cap_rows : (p + 1) * cap_rows]
        out_ref[p, 1] = amounts[p * cap_rows : (p + 1) * cap_rows]
    for copy in copies:
        copy.wait()
    matrix_ref[...] = level_product(local_ref[...] * f32(scale), False)
    sum_members(matrix_ref, control_ref, pert_ref, part_ref)


def sum_members(matrix_ref, control_ref, pert_ref, out_ref):
    members, levels, per_level, _ = control_ref.shape
    group = 2 - members % 2

    def chunk(j, carry):
        at = pl.ds(pl.multiple_of(j * 16, 16), 16)
        total = jnp.zeros((levels * 16, LANES), f32)
        for k in range(0, members, group):
            terms = [three_terms(control_ref[k + i, :, at, :].reshape(levels * 16, LANES)) for i in range(group)]
            local = jnp.dot(matrix_ref[...], jnp.concatenate(terms, axis=1), preferred_element_type=f32)
            for i in range(group):
                pert = pert_ref[k + i, :, at, :].astype(f32).reshape(levels * 16, LANES)
                total = total + pert * local[:, i * LANES : (i + 1) * LANES]
        out_ref[:, at, :] = total.reshape(levels, 16, LANES)
        return carry

    lax.fori_loop(0, per_level // 16, chunk, 0)


def member_kernel(matrix_ref, adjoint_ref, control_ref, pert_ref, out_ref):
    group, levels, height, _ = out_ref.shape
    first = pl.program_id(0) * group
    top = pl.program_id(1) * height

    def chunk(j, carry):
        to = pl.ds(pl.multiple_of(j * 16, 16), 16)
        at = pl.ds(pl.multiple_of(top + j * 16, 16), 16)
        adjoint = adjoint_ref[:, at, :]
        terms = [
            three_terms((pert_ref[first + i, :, at, :].astype(f32) * adjoint).reshape(levels * 16, LANES))
            for i in range(group)
        ]
        change = jnp.dot(matrix_ref[...], jnp.concatenate(terms, axis=1), preferred_element_type=f32)
        for i in range(group):
            part = change[:, i * LANES : (i + 1) * LANES].reshape(levels, 16, LANES)
            out_ref[i, :, to, :] = control_ref[first + i, :, at, :] + part
        return carry

    lax.fori_loop(0, height // 16, chunk, 0)


def eastern(x):
    lane = lax.broadcasted_iota(jnp.int32, x.shape, 1)
    near = pltpu.roll(x, LANES - 1, 1)
    return jnp.where(lane == LANES - 1, pltpu.roll(near, x.shape[0] - 1, 0), near)


def western(x):
    lane = lax.broadcasted_iota(jnp.int32, x.shape, 1)
    near = pltpu.roll(x, 1, 1)
    return jnp.where(lane == 0, pltpu.roll(near, 1, 0), near)


def rows_of(second_ref, first_ref, own_ref, other_ref, plane, rows):
    at = lax.axis_index("cols")
    count = lax.axis_size("cols")
    core, chip = at % 2, at // 2 % 2
    reads = [pl.ds(r, own_ref.shape[1] // rows, stride=rows) for r in range(rows)]
    first = [first_ref[plane, r, :] for r in reads]
    second = [second_ref[plane, r, :] for r in reads]
    out = [jnp.where(jnp.logical_and(chip == 1, at >= 2), f, f32(0)) for f in first]
    out = [jnp.where(jnp.logical_and(chip == 0, at >= 2), s, o) for s, o in zip(second, out)]
    out += [jnp.where(at >= 1, other_ref[1 - core, plane, r, :], f32(0)) for r in reads]
    out += [own_ref[plane, r, :] for r in reads]
    out += [jnp.where(at < count - 1, other_ref[core, plane, r, :], f32(0)) for r in reads]
    last = [jnp.where(jnp.logical_and(chip == 0, at < count - 2), f, f32(0)) for f in first]
    return out + [jnp.where(jnp.logical_and(chip == 1, at < count - 2), s, o) for s, o in zip(second, last)]


def diffuse_rows(tiles, level, coef_ref, rows):
    field = rows_of(*tiles, level, rows)
    for step in range(NDIFF):
        field = [
            coef_ref[0, i + step] * field[i]
            + coef_ref[1, i + step] * field[i - 1]
            + coef_ref[2, i + step] * field[i + 1]
            + coef_ref[3, i + step] * eastern(field[i])
            + coef_ref[4, i + step] * western(field[i])
            for i in range(1, len(field) - 1)
        ]
        field = list(field)
    return field


def first_diffusion_kernel(lev_share, rows, second_ref, first_ref, own_ref, other_ref, out_ref, coef_ref):
    tiles = (second_ref, first_ref, own_ref, other_ref)
    blocks = own_ref.shape[1] // rows
    side = 2
    north = rows_of(*tiles, lev_share, rows)
    east = rows_of(*tiles, lev_share + 1, rows)
    for i in range(1, len(north) - 1):
        south = north[i + 1]
        if (i + 1) % rows == 0 and i < side * rows:
            south = south * jnp.where(lax.axis_index("cols") == side - (i + 1) // rows, f32(0), f32(1))
        west = western(east[i])
        coef_ref[0, i] = 1.0 - north[i] - south - east[i] - west
        coef_ref[1, i] = north[i]
        coef_ref[2, i] = south
        coef_ref[3, i] = east[i]
        coef_ref[4, i] = west
    for i in (0, len(north) - 1):
        for c in range(5):
            coef_ref[c, i] = jnp.zeros_like(north[0])

    def body(level, carry):
        final = diffuse_rows(tiles, level, coef_ref, rows)
        for r in range(rows):
            out_ref[level, pl.ds(r, blocks, stride=rows), :] = final[r]
        return carry

    lax.fori_loop(0, lev_share, body, 0)


def second_diffusion_kernel(rows, coef_ref, second_ref, first_ref, own_ref, other_ref, out_ref):
    tiles = (second_ref, first_ref, own_ref, other_ref)
    lev_share = out_ref.shape[0]
    blocks = own_ref.shape[1] // rows

    def body(level, carry):
        final = diffuse_rows(tiles, level, coef_ref, rows)
        for r in range(rows):
            out_ref[level, pl.ds(r, blocks, stride=rows), :] = final[r]
        return carry

    lax.fori_loop(0, lev_share, body, 0)


def lookup_kernel(cap_rows, part_ref, static_ref, row_ref, lane_ref, out_ref, field_ref, terms_ref):
    cells = part_ref.shape[0]
    own = static_ref.shape[0]
    at = pl.ds(pl.multiple_of(lax.axis_index("ens") * own, own), own)
    field_ref[...] = part_ref[...]
    field_ref[at, :] += static_ref[...]
    for c in range(0, cells, LANES):
        high, low = halves(field_ref[c : c + LANES, :].T)
        terms_ref[:LANES, c : c + LANES] = high
        terms_ref[LANES:, c : c + LANES] = low
    ids = lax.broadcasted_iota(jnp.int32, (LANES, LANES), 0)

    def look(q, carry):
        at = pl.ds(pl.multiple_of(q * cap_rows, cap_rows), cap_rows)
        rows = row_ref[at, :]
        lanes = lane_ref[at, :]
        picks = [placed_at(rows[c : c + 1, :], cells) for c in range(cap_rows)]
        got = jnp.dot(terms_ref[...], jnp.concatenate(picks, axis=1), preferred_element_type=f32)
        values = []
        for c in range(cap_rows):
            here = slice(c * LANES, (c + 1) * LANES)
            mine = got[:LANES, here] + got[LANES:, here]
            values.append(jnp.sum(jnp.where(ids == lanes[c : c + 1, :], mine, f32(0)), axis=0, keepdims=True))
        out_ref[at, :] = jnp.concatenate(values, axis=0)
        return carry

    lax.fori_loop(0, row_ref.shape[0] // cap_rows, look, 0)


def put(acc_ref, rows, lanes, amounts):
    terms = [h.astype(f32) for h in halves(amounts)]
    left, right = [], []
    for c in range(rows.shape[0]):
        left.append(placed_at(rows[c : c + 1, :], acc_ref.shape[0]))
        mask = matches(lanes[c : c + 1, :], LANES)
        right.append(
            jnp.concatenate(
                [
                    jnp.where(mask, spread(t[c : c + 1, :], bf16)[None], bf16(0)).reshape(LANES, LANES)
                    for t in terms
                ],
                axis=0,
            )
        )
    acc_ref[...] += product_nt(jnp.concatenate(left, axis=1), jnp.concatenate(right, axis=1))


def scatter_own_kernel(cap_rows, row_ref, lane_ref, *refs):
    shares, (out_ref, amount_ref, acc_ref) = refs[:-3], refs[-3:]
    own = out_ref.shape[0]
    lists = row_ref.shape[0] // cap_rows
    first = lax.axis_index("ens") * own
    acc_ref[...] = jnp.zeros_like(acc_ref)

    def step(q, carry):
        at = pl.ds(pl.multiple_of(q * cap_rows, cap_rows), cap_rows)
        value, weight, amount = (functools.reduce(jnp.add, [s[t, at, :] for s in shares]) for t in range(3))
        amounts = value * weight - amount
        amount_ref[at, :] = amounts
        put(acc_ref, row_ref[at, :] - first, lane_ref[at, :], amounts)
        return carry

    lax.fori_loop(0, lists, step, 0)
    out_ref[...] = acc_ref[:, :LANES] + acc_ref[:, LANES:]


def matrices_kernel(scale, local_ref, root_ref, to_members_ref, to_static_ref):
    to_members_ref[...] = level_product(local_ref[...] * f32(scale), True)
    to_static_ref[...] = level_product(root_ref[...], True)


def scatter_rest_kernel(cap_rows, row_ref, lane_ref, amount_ref, own_ref, *refs):
    sources, out_ref, kept, acc_ref, sems = refs[:3], refs[3], refs[4:7], refs[7], refs[8]
    copies = [pltpu.make_async_copy(s, t, sems.at[i]) for i, (s, t) in enumerate(zip(sources, kept))]
    for copy in copies:
        copy.start()
    cells = out_ref.shape[0]
    own = own_ref.shape[0]
    n_ens = cells // own
    me = lax.axis_index("ens")
    first = (me + 1) * own
    acc_ref[...] = jnp.zeros_like(acc_ref)

    def step(q, carry):
        at = pl.ds(pl.multiple_of(q * cap_rows, cap_rows), cap_rows)
        row = row_ref[at, :]
        turned = row - first
        turned = jnp.where(row < 0, -1, jnp.where(turned < 0, turned + cells, turned))
        put(acc_ref, turned, lane_ref[at, :], amount_ref[at, :])
        return carry

    lax.fori_loop(0, row_ref.shape[0] // cap_rows, step, 0)
    out_ref[pl.ds(pl.multiple_of(me * own, own), own), :] = own_ref[...]
    for t in range(1, n_ens):
        to = pl.ds(pl.multiple_of((me + t) % n_ens * own, own), own)
        piece = acc_ref[(t - 1) * own : t * own, :]
        out_ref[to, :] = piece[:, :LANES] + piece[:, LANES:]
    for copy in copies:
        copy.wait()


def static_kernel(matrix_ref, static_ref, *refs):
    parts, (out_ref, smooth_ref) = refs[:-2], refs[-2:]
    levels, per_level, _ = static_ref.shape
    share = levels // len(parts)
    me = lax.axis_index("ens")
    for i, part in enumerate(parts):
        at = peer(me, (len(parts) - i) % len(parts), len(parts))
        smooth_ref[pl.ds(at * share, share)] = part[...]
    for j in range(0, per_level, 32):
        terms = [three_terms(smooth_ref[:, j + i : j + i + 16, :].reshape(levels * 16, LANES)) for i in (0, 16)]
        change = jnp.dot(matrix_ref[...], jnp.concatenate(terms, axis=1), preferred_element_type=f32)
        for i, part in ((0, change[:, :LANES]), (16, change[:, LANES:])):
            at = slice(j + i, j + i + 16)
            out_ref[:, at, :] = static_ref[:, at, :] + part.reshape(levels, 16, LANES)


def exchanged(x, starts):
    count = lax.axis_size("cols")
    out = []
    for start in starts:
        pairs = []
        for i in range(count):
            chip, core = divmod(i, 2)
            partner = (chip + start ^ 1) - start
            pairs.append((i, 2 * partner + core if 0 <= 2 * partner + core < count else i))
        out.append(lax.ppermute(x, "cols", pairs))
    return out


def from_peers(x):
    count = lax.axis_size("ens")
    return [lax.ppermute(x, "ens", [(peer(i, d, count), i) for i in range(count)]) for d in range(count - 1, 0, -1)]


def swapped(own, first, second):
    at = lax.axis_index("cols")
    pack = jnp.stack([own, jnp.where(at % 2 == at // 2 % 2, first, second)])
    return lax.ppermute(pack, "cols", [(i, i ^ 1) for i in range(lax.axis_size("cols"))])


def local(
    static_control,
    ensemble_control,
    perturbations,
    vertical_root,
    vertical_local,
    face_north,
    face_east,
    innovation,
    obs_weight,
    obs_slot,
    send_index,
    send_count,
):
    n_ens = lax.axis_size("ens")
    n_cols = lax.axis_size("cols")
    members, levels, rows, lon = ensemble_control.shape
    per_level = rows * lon // LANES
    cells = levels * per_level
    lev_share = levels // n_ens
    own = lev_share * per_level
    lists, capacity = send_index.shape
    cap_rows = capacity // LANES
    entry_rows = lists * cap_rows
    member_scale = 1.0 / math.sqrt(members * n_ens - 1)

    static = in_hbm(tiled(static_control))
    control = in_hbm(tiled(ensemble_control))
    pert = in_hbm(tiled(perturbations))

    def whole(*shape):
        return pl.BlockSpec(shape, lambda i: (0,) * len(shape))

    obs_rows = obs_slot.shape[0] // LANES
    share_rows = obs_rows // n_ens
    packed, entry_row, entry_lane, *observed = pl.pallas_call(
        functools.partial(prepare_kernel, lev_share, rows),
        grid=(1,),
        in_specs=[
            SMEM,
            SMEM,
            whole(levels, per_level, LANES),
            whole(per_level, LANES),
            whole(per_level, LANES),
            whole(lists, capacity),
            pl.BlockSpec(memory_space=pl.ANY),
            pl.BlockSpec(memory_space=pl.ANY),
            pl.BlockSpec(memory_space=pl.ANY),
        ],
        out_specs=[VMEM] * 6,
        out_shape=[
            pltpu.VMEM((lev_share + 2, per_level, LANES), f32),
            pltpu.VMEM((entry_rows, LANES), jnp.int32),
            pltpu.VMEM((entry_rows, LANES), jnp.int32),
            pltpu.VMEM((share_rows, LANES), jnp.int32),
            pltpu.VMEM((share_rows, LANES), f32),
            pltpu.VMEM((share_rows, LANES), f32),
        ],
        scratch_shapes=[pltpu.SemaphoreType.DMA((3,))],
        compiler_params=params(8),
        name="prepare",
    )(
        in_hbm(vertical_root),
        in_hbm(send_count),
        static,
        in_hbm(tiled(face_north)),
        in_hbm(tiled(face_east)),
        in_hbm(send_index),
        in_hbm(obs_slot.reshape(obs_rows, LANES)),
        in_hbm(obs_weight.reshape(obs_rows, LANES)),
        in_hbm(innovation.reshape(obs_rows, LANES)),
    )
    second, first = exchanged(packed, (1, 0))

    coarse = n_cols * capacity // FINE
    size = levels * 16
    slots, part = pl.pallas_call(
        functools.partial(observe_kernel, n_cols, cap_rows, member_scale),
        grid=(1,),
        in_specs=[VMEM] * 3 + [pl.BlockSpec(memory_space=pl.ANY)] * 3,
        out_specs=[whole(n_cols, 2, cap_rows, LANES), VMEM],
        out_shape=[
            pltpu.HBM((n_cols, 2, cap_rows, LANES), f32),
            pltpu.VMEM((levels, per_level, LANES), f32),
        ],
        scratch_shapes=[
            pltpu.VMEM((4 * FINE, coarse), f32),
            pltpu.VMEM((2, coarse, LANES), f32),
            pltpu.VMEM((size, 3 * size), bf16),
            pltpu.VMEM((levels, levels), f32),
            pltpu.VMEM(control.shape, f32),
            pltpu.VMEM(pert.shape, bf16),
            pltpu.SemaphoreType.DMA((3,)),
        ]
        + [pltpu.VMEM((coarse, 8 * LANES), bf16), pltpu.VMEM((4 * FINE, 8 * LANES), bf16)] * 2,
        compiler_params=params(24),
        name="slot_sums_and_members",
    )(*observed, in_hbm(vertical_local), control, pert)
    second, first, slots = lax.optimization_barrier((second, first, slots))
    other = swapped(packed, first, second)
    slots = lax.all_to_all(slots, "cols", split_axis=0, concat_axis=0, tiled=True)

    increment, coefs = pl.pallas_call(
        functools.partial(first_diffusion_kernel, lev_share, rows),
        in_specs=[VMEM] * 4,
        out_specs=[VMEM] * 2,
        out_shape=[
            pltpu.VMEM((lev_share, per_level, LANES), f32),
            pltpu.VMEM((5, 5 * rows, per_level // rows, LANES), f32),
        ],
        compiler_params=params(8),
        cost_estimate=pl.CostEstimate(flops=1 << 26, bytes_accessed=1 << 22, transcendentals=0),
        name="diffuse_forward",
    )(second, first, packed, other)

    values = pl.pallas_call(
        functools.partial(lookup_kernel, cap_rows),
        in_specs=[VMEM] * 4,
        out_specs=VMEM,
        out_shape=pltpu.VMEM((entry_rows, LANES), f32),
        scratch_shapes=[pltpu.VMEM((cells, LANES), f32), pltpu.VMEM((2 * LANES, cells), bf16)],
        compiler_params=params(16),
        cost_estimate=pl.CostEstimate(
            flops=4 * cells * LANES * lists * capacity, bytes_accessed=8 * cells * lists * capacity // 4, transcendentals=0
        ),
        name="lookup",
    )(part.reshape(cells, LANES), increment.reshape(own, LANES), entry_row, entry_lane)
    values, slots = lax.optimization_barrier((values, slots))
    slots = jnp.swapaxes(slots, 0, 1).reshape(2, entry_rows, LANES)
    share = jnp.concatenate([values[None], slots])
    shares = [share] + from_peers(share)

    adjoint_own, amounts = pl.pallas_call(
        functools.partial(scatter_own_kernel, cap_rows),
        in_specs=[VMEM] * (2 + n_ens),
        out_specs=[VMEM] * 2,
        out_shape=[pltpu.VMEM((own, LANES), f32), pltpu.VMEM((entry_rows, LANES), f32)],
        scratch_shapes=[pltpu.VMEM((own, 2 * LANES), f32)],
        compiler_params=params(16),
        name="scatter_own",
    )(entry_row, entry_lane, *shares)
    tile = adjoint_own.reshape(lev_share, per_level, LANES)
    tile_first, tile_second = exchanged(tile, (0, 1))

    adjoint, static_here, control_here, pert_here = pl.pallas_call(
        functools.partial(scatter_rest_kernel, cap_rows),
        in_specs=[VMEM] * 4 + [pl.BlockSpec(memory_space=pl.ANY)] * 3,
        out_specs=[VMEM] * 4,
        out_shape=[
            pltpu.VMEM((cells, LANES), f32),
            pltpu.VMEM(static.shape, f32),
            pltpu.VMEM(control.shape, f32),
            pltpu.VMEM(pert.shape, bf16),
        ],
        scratch_shapes=[pltpu.VMEM((cells - own, 2 * LANES), f32), pltpu.SemaphoreType.DMA((3,))],
        compiler_params=params(16),
        name="scatter_rest",
    )(entry_row, entry_lane, amounts, adjoint_own, static, control, pert)
    tile_first, tile_second, adjoint, vertical_local, vertical_root = lax.optimization_barrier(
        (tile_first, tile_second, adjoint, vertical_local, vertical_root)
    )
    tile_other = swapped(tile, tile_first, tile_second)
    from_local, from_root = pl.pallas_call(
        functools.partial(matrices_kernel, member_scale),
        grid=(1,),
        in_specs=[whole(levels, levels)] * 2,
        out_specs=[VMEM] * 2,
        out_shape=[pltpu.VMEM((size, 3 * size), bf16)] * 2,
        compiler_params=params(8),
        name="level_matrices",
    )(in_hbm(vertical_local), in_hbm(vertical_root))
    coefs, from_local, from_root = lax.optimization_barrier((coefs, from_local, from_root))

    smooth = pl.pallas_call(
        functools.partial(second_diffusion_kernel, rows),
        in_specs=[VMEM] * 5,
        out_specs=VMEM,
        out_shape=pltpu.VMEM((lev_share, per_level, LANES), f32),
        compiler_params=params(8),
        name="diffuse_adjoint",
    )(coefs, tile_second, tile_first, tile, tile_other)
    smooth, adjoint = lax.optimization_barrier((smooth, adjoint))
    smooths = [smooth] + from_peers(smooth)

    group = 2 - members % 2
    ensemble_grad = pl.pallas_call(
        member_kernel,
        grid=(members // group, 2),
        in_specs=[VMEM] * 4,
        out_specs=pl.BlockSpec((group, levels, per_level // 2, LANES), lambda k, h: (k, 0, h, 0)),
        out_shape=jax.ShapeDtypeStruct((members, levels, per_level, LANES), f32),
        compiler_params=params(16),
        name="members_gradient",
    )(from_local, adjoint.reshape(levels, per_level, LANES), control_here, pert_here)

    static_grad = pl.pallas_call(
        static_kernel,
        grid=(1,),
        in_specs=[VMEM] * (2 + n_ens),
        out_specs=whole(levels, per_level, LANES),
        out_shape=jax.ShapeDtypeStruct((levels, per_level, LANES), f32),
        scratch_shapes=[pltpu.VMEM((levels, per_level, LANES), f32)],
        compiler_params=params(8),
        name="static_gradient",
    )(from_root, static_here, *smooths)
    return (untiled(static_grad, rows), untiled(ensemble_grad, rows))


def solution(mesh):
    placed = (
        P(None, "cols", None),
        P("ens", None, "cols", None),
        P("ens", None, "cols", None),
        P(),
        P(),
        P("cols", None),
        P("cols", None),
        P("cols"),
        P("cols"),
        P("cols"),
        P("cols", None),
        P("cols"),
    )
    return jax.shard_map(
        local,
        mesh=mesh,
        in_specs=placed,
        out_specs=(P(None, "cols", None), P("ens", None, "cols", None)),
        check_vma=False,
    )
```

```python
import functools
import math

import jax
import jax.numpy as jnp
from jax import lax
from jax.experimental import pallas as pl
from jax.experimental.pallas import tpu as pltpu
from jax.sharding import PartitionSpec as P

NDIFF = 4
LANES = 128
FINE = 64
MIB = 1 << 20

f32 = jnp.float32
bf16 = jnp.bfloat16
SMEM = pl.BlockSpec(memory_space=pltpu.SMEM)
VMEM = pl.BlockSpec(memory_space=pltpu.VMEM)


def tiled(field):
    *lead, rows, lon = field.shape
    field = field.reshape(*lead, rows, lon // LANES, LANES)
    return jnp.swapaxes(field, -3, -2).reshape(*lead, rows * lon // LANES, LANES)


def untiled(field, rows):
    *lead, count, lanes = field.shape
    field = field.reshape(*lead, count // rows, rows, lanes)
    return jnp.swapaxes(field, -3, -2).reshape(*lead, rows, count // rows * lanes)


def params(limit, **more):
    return pltpu.CompilerParams(vmem_limit_bytes=limit * MIB, **more)


def halves(x):
    high = x.astype(bf16)
    return high, (x - high.astype(f32)).astype(bf16)


def in_hbm(x):
    return pltpu.with_memory_space_constraint(x, pltpu.HBM)


def spread(row, dtype):
    return jnp.broadcast_to(row, (16, row.shape[1])).astype(dtype)


def matches(index, count):
    ids = lax.broadcasted_iota(jnp.int32, (count, index.shape[1]), 0).astype(jnp.int16)
    return ids.reshape(count // 16, 16, index.shape[1]) == spread(index, jnp.int16)[None]


def placed_at(index, count, amount=None):
    where = matches(index, count)
    amount = bf16(1) if amount is None else spread(amount, bf16)[None]
    return jnp.where(where, amount, bf16(0)).reshape(count, index.shape[1])


def in_turns(count, build, use, slots):
    build(0, slots[0])

    def step(i, carry):
        use(2 * i, slots[0])
        build(2 * i + 1, slots[1])
        use(2 * i + 1, slots[1])
        build(jnp.minimum(2 * i + 2, count - 1), slots[0])
        return carry

    lax.fori_loop(0, count // 2, step, 0)
    if count % 2:
        use(count - 1, slots[0])


def product_nt(left, right):
    return lax.dot_general(left, right, (((1,), (1,)), ((), ())), preferred_element_type=f32)


def over(x, size):
    if size & (size - 1):
        return lax.div(x, jnp.int32(size)), lax.rem(x, jnp.int32(size))
    return lax.shift_right_logical(x, jnp.int32(size.bit_length() - 1)), x & (size - 1)


def peer(i, d, count):
    return (i + d) % count if count & (count - 1) else i ^ d


def back(d, count):
    return count - d if count & (count - 1) else d


def prepare_kernel(lev_share, rows, *refs):
    (root_ref, count_ref, static_ref, north_ref, east_ref, index_ref), sources = refs[:6], refs[6:9]
    (out_ref, row_ref, lane_ref), landed, sems = refs[9:12], refs[12:15], refs[15]
    obs_rows = landed[0].shape[0]
    here = pl.ds(pl.multiple_of(lax.axis_index("ens") * obs_rows, obs_rows), obs_rows)
    copies = [pltpu.make_async_copy(s.at[here, :], t, sems.at[i]) for i, (s, t) in enumerate(zip(sources, landed))]
    for copy in copies:
        copy.start()
    levels, per_level, _ = static_ref.shape
    first = lax.axis_index("ens") * lev_share
    for j in range(lev_share):
        total = root_ref[first + j, 0] * static_ref[0]
        for m in range(1, levels):
            total = total + root_ref[first + j, m] * static_ref[m]
        out_ref[j] = total
    out_ref[lev_share] = north_ref[...]
    out_ref[lev_share + 1] = east_ref[...]
    lists, capacity = index_ref.shape
    lon = per_level // rows * LANES
    pieces = capacity // LANES
    slot = lax.broadcasted_iota(jnp.int32, (1, capacity), 1)
    for q in range(lists):
        cell = index_ref[q : q + 1, :]
        rest, lane = over(cell, LANES)
        rest, block = over(rest, lon // LANES)
        level, row = over(rest, rows)
        grid_row = jnp.where(slot < count_ref[q], level * per_level + block * rows + row, -1)
        for c in range(pieces):
            at = q * pieces + c
            row_ref[at : at + 1, :] = grid_row[:, c * LANES : (c + 1) * LANES]
            lane_ref[at : at + 1, :] = lane[:, c * LANES : (c + 1) * LANES]
    for copy in copies:
        copy.wait()


def level_product(matrix, transpose):
    levels = matrix.shape[0]
    size = levels * 16
    pick = lax.broadcasted_iota(jnp.int32, (size, levels), 0) // 16
    pick = jnp.where(pick == lax.broadcasted_iota(jnp.int32, (size, levels), 1), f32(1), f32(0)).astype(bf16)
    same = (
        lax.broadcasted_iota(jnp.int32, (size, size), 0) % 16 == lax.broadcasted_iota(jnp.int32, (size, size), 1) % 16
    )
    out = []
    for half in halves(matrix):
        if transpose:
            wide = product_nt(pick, half)
        else:
            wide = jnp.dot(pick, half, preferred_element_type=f32)
        wide = product_nt(wide.astype(bf16), pick)
        out.append(jnp.where(same, wide, f32(0)).astype(bf16))
    return jnp.concatenate([out[0], out[0], out[1]], axis=1)


def three_terms(x):
    high, low = halves(x)
    return jnp.concatenate([high, low, high], axis=0)


def observe_kernel(n_cols, cap_rows, scale, *refs):
    n_ens = len(refs) - 19
    (slot_ref, weight_ref, innov_ref), sources, out_ref, parts = refs[:3], refs[3:6], refs[6], refs[7 : 7 + n_ens]
    refs = refs[7 + n_ens :]
    (acc_ref, fold_ref, matrix_ref, part_ref), landed, sems, slots = (
        refs[:4],
        refs[4:7],
        refs[7],
        (refs[8:10], refs[10:12]),
    )
    coarse = acc_ref.shape[1]
    obs_rows = slot_ref.shape[0]
    group = min(8, obs_rows)
    copies = [pltpu.make_async_copy(s, t, sems.at[i]) for i, (s, t) in enumerate(zip(sources, landed))]
    for copy in copies:
        copy.start()
    acc_ref[...] = jnp.zeros_like(acc_ref)
    local_ref, control_ref, pert_ref = landed

    def build(i, to):
        at = pl.ds(pl.multiple_of(i * group, group), group)
        weight = weight_ref[at, :]
        amount = weight * innov_ref[at, :]
        upper, lower = over(slot_ref[at, :], FINE)
        terms = [t.astype(f32) for t in halves(weight) + halves(amount)]
        for r in range(group):
            here = slice(r * LANES, (r + 1) * LANES)
            to[0][:, here] = placed_at(upper[r : r + 1, :], coarse)
            mask = matches(lower[r : r + 1, :], FINE)
            for t, term in enumerate(terms):
                term = spread(term[r : r + 1, :], bf16)[None]
                to[1][t * FINE : (t + 1) * FINE, here] = jnp.where(mask, term, bf16(0)).reshape(FINE, LANES)

    def use(i, of):
        acc_ref[...] += product_nt(of[1][...], of[0][...])

    in_turns(obs_rows // group, build, use, slots)
    for t in range(2):
        at = 2 * t * FINE
        terms = acc_ref[at : at + FINE, :] + acc_ref[at + FINE : at + 2 * FINE, :]
        fold_ref[t] = jnp.concatenate([terms] * (LANES // FINE), axis=0).T
    per_row = LANES // FINE
    lane = lax.broadcasted_iota(jnp.int32, (coarse // per_row, LANES), 1)
    weights, amounts = (
        jnp.where(
            lane < FINE,
            fold_ref[t, pl.ds(0, coarse // per_row, stride=per_row), :],
            fold_ref[t, pl.ds(1, coarse // per_row, stride=per_row), :],
        )
        for t in range(2)
    )
    for e in range(n_ens):
        for p in range(n_cols):
            out_ref[e * n_cols + p, 0] = weights[p * cap_rows : (p + 1) * cap_rows]
            out_ref[e * n_cols + p, 1] = amounts[p * cap_rows : (p + 1) * cap_rows]
    for copy in copies:
        copy.wait()
    matrix_ref[...] = level_product(local_ref[...] * f32(scale), False)
    sum_members(matrix_ref, control_ref, pert_ref, part_ref)
    share = part_ref.shape[0] // n_ens
    for d, part in enumerate(parts):
        at = peer(lax.axis_index("ens"), d, n_ens) * share
        part[...] = part_ref[pl.ds(at, share)]


def sum_members(matrix_ref, control_ref, pert_ref, out_ref):
    members, levels, per_level, _ = control_ref.shape
    group = 2 - members % 2

    def chunk(j, carry):
        at = pl.ds(pl.multiple_of(j * 16, 16), 16)
        total = jnp.zeros((levels * 16, LANES), f32)
        for k in range(0, members, group):
            terms = [three_terms(control_ref[k + i, :, at, :].reshape(levels * 16, LANES)) for i in range(group)]
            local = jnp.dot(matrix_ref[...], jnp.concatenate(terms, axis=1), preferred_element_type=f32)
            for i in range(group):
                pert = pert_ref[k + i, :, at, :].astype(f32).reshape(levels * 16, LANES)
                total = total + pert * local[:, i * LANES : (i + 1) * LANES]
        out_ref[:, at, :] = total.reshape(levels, 16, LANES)
        return carry

    lax.fori_loop(0, per_level // 16, chunk, 0)


def gather_levels(parts, to_ref):
    share = to_ref.shape[0] // len(parts)
    for i, part in enumerate(parts):
        at = peer(lax.axis_index("ens"), (len(parts) - i) % len(parts), len(parts))
        to_ref[pl.ds(at * share, share)] = part[...]


def member_kernel(matrix_ref, control_ref, pert_ref, *refs):
    parts, out_ref, adjoint_ref = refs[:-2], refs[-2], refs[-1]
    group, levels, per_level, _ = out_ref.shape
    first = pl.program_id(0) * group

    @pl.when(pl.program_id(0) == 0)
    def _():
        gather_levels(parts, adjoint_ref)

    def chunk(j, carry):
        at = pl.ds(pl.multiple_of(j * 16, 16), 16)
        adjoint = adjoint_ref[:, at, :]
        terms = [
            three_terms((pert_ref[first + i, :, at, :].astype(f32) * adjoint).reshape(levels * 16, LANES))
            for i in range(group)
        ]
        change = jnp.dot(matrix_ref[...], jnp.concatenate(terms, axis=1), preferred_element_type=f32)
        for i in range(group):
            part = change[:, i * LANES : (i + 1) * LANES].reshape(levels, 16, LANES)
            out_ref[i, :, at, :] = control_ref[first + i, :, at, :] + part
        return carry

    lax.fori_loop(0, per_level // 16, chunk, 0)


def eastern(x):
    lane = lax.broadcasted_iota(jnp.int32, x.shape, 1)
    near = pltpu.roll(x, LANES - 1, 1)
    return jnp.where(lane == LANES - 1, pltpu.roll(near, x.shape[0] - 1, 0), near)


def western(x):
    lane = lax.broadcasted_iota(jnp.int32, x.shape, 1)
    near = pltpu.roll(x, 1, 1)
    return jnp.where(lane == 0, pltpu.roll(near, 1, 0), near)


def rows_of(second_ref, first_ref, own_ref, other_ref, plane, rows):
    at = lax.axis_index("cols")
    count = lax.axis_size("cols")
    core, chip = at % 2, at // 2 % 2
    reads = [pl.ds(r, own_ref.shape[1] // rows, stride=rows) for r in range(rows)]
    first = [first_ref[plane, r, :] for r in reads]
    second = [second_ref[plane, r, :] for r in reads]
    out = [jnp.where(jnp.logical_and(chip == 1, at >= 2), f, f32(0)) for f in first]
    out = [jnp.where(jnp.logical_and(chip == 0, at >= 2), s, o) for s, o in zip(second, out)]
    out += [jnp.where(at >= 1, other_ref[1 - core, plane, r, :], f32(0)) for r in reads]
    out += [own_ref[plane, r, :] for r in reads]
    out += [jnp.where(at < count - 1, other_ref[core, plane, r, :], f32(0)) for r in reads]
    last = [jnp.where(jnp.logical_and(chip == 0, at < count - 2), f, f32(0)) for f in first]
    return out + [jnp.where(jnp.logical_and(chip == 1, at < count - 2), s, o) for s, o in zip(second, last)]


def diffuse_rows(tiles, level, coef_ref, rows):
    field = rows_of(*tiles, level, rows)
    for step in range(NDIFF):
        field = [
            coef_ref[0, i + step] * field[i]
            + coef_ref[1, i + step] * field[i - 1]
            + coef_ref[1, i + step + 1] * field[i + 1]
            + coef_ref[2, i + step] * eastern(field[i])
            + western(coef_ref[2, i + step] * field[i])
            for i in range(1, len(field) - 1)
        ]
    return field


def first_diffusion_kernel(lev_share, rows, second_ref, first_ref, own_ref, other_ref, out_ref, coef_ref):
    tiles = (second_ref, first_ref, own_ref, other_ref)
    blocks = own_ref.shape[1] // rows
    side = 2
    north = rows_of(*tiles, lev_share, rows)
    east = rows_of(*tiles, lev_share + 1, rows)
    faces = [
        jnp.where(lax.axis_index("cols") == side - i // rows, f32(0), n) if i % rows == 0 and i <= side * rows else n
        for i, n in enumerate(north)
    ]
    for i in range(len(north)):
        inner = 0 < i < len(north) - 1
        coef_ref[0, i] = 1.0 - north[i] - faces[i + 1] - east[i] - western(east[i]) if inner else jnp.zeros_like(east[i])
        coef_ref[1, i] = faces[i]
        coef_ref[2, i] = east[i]

    def body(level, carry):
        final = diffuse_rows(tiles, level, coef_ref, rows)
        for r in range(rows):
            out_ref[level, pl.ds(r, blocks, stride=rows), :] = final[r]
        return carry

    lax.fori_loop(0, lev_share, body, 0)


def second_diffusion_kernel(rows, coef_ref, second_ref, first_ref, own_ref, other_ref, out_ref):
    tiles = (second_ref, first_ref, own_ref, other_ref)
    lev_share = out_ref.shape[0]
    blocks = own_ref.shape[1] // rows

    def body(level, carry):
        final = diffuse_rows(tiles, level, coef_ref, rows)
        for r in range(rows):
            out_ref[level, pl.ds(r, blocks, stride=rows), :] = final[r]
        return carry

    lax.fori_loop(0, lev_share, body, 0)


def scatter_kernel(cap_rows, row_ref, lane_ref, slots_ref, *refs):
    sources, out_ref, kept, acc_ref, sems = refs[:3], refs[3], refs[4:7], refs[7], refs[8]
    copies = [pltpu.make_async_copy(s, t, sems.at[i]) for i, (s, t) in enumerate(zip(sources, kept))]
    for copy in copies:
        copy.start()
    own = out_ref.shape[1]
    lists = row_ref.shape[0] // cap_rows
    first = lax.axis_index("ens") * own
    acc_ref[...] = jnp.zeros_like(acc_ref)

    def step(q, carry):
        at = pl.ds(pl.multiple_of(q * cap_rows, cap_rows), cap_rows)
        rows = row_ref[at, :] - first
        lanes = lane_ref[at, :]
        terms = []
        for t in range(2):
            total = functools.reduce(
                jnp.add, [slots_ref[e * lists + q, t] for e in range(slots_ref.shape[0] // lists)]
            )
            terms += [h.astype(f32) for h in halves(total)]
        left, right = [], []
        for c in range(cap_rows):
            left.append(placed_at(rows[c : c + 1, :], own))
            mask = matches(lanes[c : c + 1, :], LANES)
            right.append(
                jnp.concatenate(
                    [
                        jnp.where(mask, spread(t[c : c + 1, :], bf16)[None], bf16(0)).reshape(LANES, LANES)
                        for t in terms
                    ],
                    axis=0,
                )
            )
        acc_ref[...] += product_nt(jnp.concatenate(right, axis=1), jnp.concatenate(left, axis=1))
        return carry

    lax.fori_loop(0, lists, step, 0)
    for t in range(2):
        at = 2 * t * LANES
        out_ref[t] = (acc_ref[at : at + LANES, :] + acc_ref[at + LANES : at + 2 * LANES, :]).T
    for copy in copies:
        copy.wait()


def matrices_kernel(scale, local_ref, root_ref, to_members_ref, to_static_ref):
    to_members_ref[...] = level_product(local_ref[...] * f32(scale), True)
    to_static_ref[...] = level_product(root_ref[...], True)


def static_kernel(matrix_ref, static_ref, *refs):
    parts, (out_ref, smooth_ref) = refs[:-2], refs[-2:]
    levels, per_level, _ = static_ref.shape
    gather_levels(parts, smooth_ref)
    for j in range(0, per_level, 32):
        terms = [three_terms(smooth_ref[:, j + i : j + i + 16, :].reshape(levels * 16, LANES)) for i in (0, 16)]
        change = jnp.dot(matrix_ref[...], jnp.concatenate(terms, axis=1), preferred_element_type=f32)
        for i, part in ((0, change[:, :LANES]), (16, change[:, LANES:])):
            at = slice(j + i, j + i + 16)
            out_ref[:, at, :] = static_ref[:, at, :] + part.reshape(levels, 16, LANES)


def exchanged(x, starts):
    count = lax.axis_size("cols")
    out = []
    for start in starts:
        pairs = []
        for i in range(count):
            chip, core = divmod(i, 2)
            partner = (chip + start ^ 1) - start
            pairs.append((i, 2 * partner + core if 0 <= 2 * partner + core < count else i))
        out.append(lax.ppermute(x, "cols", pairs))
    return out


def from_peers(x):
    count = lax.axis_size("ens")
    return [lax.ppermute(x, "ens", [(peer(i, d, count), i) for i in range(count)]) for d in range(count - 1, 0, -1)]


def swapped(own, first, second):
    at = lax.axis_index("cols")
    pack = jnp.stack([own, jnp.where(at % 2 == at // 2 % 2, first, second)])
    return lax.ppermute(pack, "cols", [(i, i ^ 1) for i in range(lax.axis_size("cols"))])


def local(
    static_control,
    ensemble_control,
    perturbations,
    vertical_root,
    vertical_local,
    face_north,
    face_east,
    innovation,
    obs_weight,
    obs_slot,
    send_index,
    send_count,
):
    n_ens = lax.axis_size("ens")
    n_cols = lax.axis_size("cols")
    members, levels, rows, lon = ensemble_control.shape
    per_level = rows * lon // LANES
    cells = levels * per_level
    lev_share = levels // n_ens
    own = lev_share * per_level
    lists, capacity = send_index.shape
    cap_rows = capacity // LANES
    entry_rows = lists * cap_rows
    member_scale = 1.0 / math.sqrt(members * n_ens - 1)

    static = in_hbm(tiled(static_control))
    control = in_hbm(tiled(ensemble_control))
    pert = in_hbm(tiled(perturbations))

    def whole(*shape):
        return pl.BlockSpec(shape, lambda i: (0,) * len(shape))

    obs_rows = obs_slot.shape[0] // LANES
    share_rows = obs_rows // n_ens
    packed, entry_row, entry_lane, *observed = pl.pallas_call(
        functools.partial(prepare_kernel, lev_share, rows),
        grid=(1,),
        in_specs=[
            SMEM,
            SMEM,
            whole(levels, per_level, LANES),
            whole(per_level, LANES),
            whole(per_level, LANES),
            whole(lists, capacity),
            pl.BlockSpec(memory_space=pl.ANY),
            pl.BlockSpec(memory_space=pl.ANY),
            pl.BlockSpec(memory_space=pl.ANY),
        ],
        out_specs=[VMEM] * 6,
        out_shape=[
            pltpu.VMEM((lev_share + 2, per_level, LANES), f32),
            pltpu.VMEM((entry_rows, LANES), jnp.int32),
            pltpu.VMEM((entry_rows, LANES), jnp.int32),
            pltpu.VMEM((share_rows, LANES), jnp.int32),
            pltpu.VMEM((share_rows, LANES), f32),
            pltpu.VMEM((share_rows, LANES), f32),
        ],
        scratch_shapes=[pltpu.SemaphoreType.DMA((3,))],
        compiler_params=params(8),
        name="prepare",
    )(
        in_hbm(vertical_root),
        in_hbm(send_count),
        static,
        in_hbm(tiled(face_north)),
        in_hbm(tiled(face_east)),
        in_hbm(send_index),
        in_hbm(obs_slot.reshape(obs_rows, LANES)),
        in_hbm(obs_weight.reshape(obs_rows, LANES)),
        in_hbm(innovation.reshape(obs_rows, LANES)),
    )
    coarse = n_cols * capacity // FINE
    size = levels * 16
    slots, *parts = pl.pallas_call(
        functools.partial(observe_kernel, n_cols, cap_rows, member_scale),
        grid=(1,),
        in_specs=[VMEM] * 3 + [pl.BlockSpec(memory_space=pl.ANY)] * 3,
        out_specs=[whole(n_ens * n_cols, 2, cap_rows, LANES)] + [VMEM] * n_ens,
        out_shape=[
            pltpu.HBM((n_ens * n_cols, 2, cap_rows, LANES), f32),
        ]
        + [pltpu.VMEM((lev_share, per_level, LANES), f32)] * n_ens,
        scratch_shapes=[
            pltpu.VMEM((4 * FINE, coarse), f32),
            pltpu.VMEM((2, coarse, LANES), f32),
            pltpu.VMEM((size, 3 * size), bf16),
            pltpu.VMEM((levels, per_level, LANES), f32),
            pltpu.VMEM((levels, levels), f32),
            pltpu.VMEM(control.shape, f32),
            pltpu.VMEM(pert.shape, bf16),
            pltpu.SemaphoreType.DMA((3,)),
        ]
        + [pltpu.VMEM((coarse, 8 * LANES), bf16), pltpu.VMEM((4 * FINE, 8 * LANES), bf16)] * 2,
        compiler_params=params(24),
        name="slot_sums_and_members",
    )(*observed, in_hbm(vertical_local), control, pert)
    slots, packed = lax.optimization_barrier((slots, packed))
    slots = lax.all_to_all(slots, ("ens", "cols"), split_axis=0, concat_axis=0, tiled=True)
    second, first = exchanged(packed, (1, 0))
    sums = [parts[0]] + [
        lax.ppermute(parts[back(d, n_ens)], "ens", [(peer(i, d, n_ens), i) for i in range(n_ens)])
        for d in range(n_ens - 1, 0, -1)
    ]
    other = swapped(packed, first, second)

    increment, coefs = pl.pallas_call(
        functools.partial(first_diffusion_kernel, lev_share, rows),
        in_specs=[VMEM] * 4,
        out_specs=[VMEM] * 2,
        out_shape=[
            pltpu.VMEM((lev_share, per_level, LANES), f32),
            pltpu.VMEM((3, 5 * rows, per_level // rows, LANES), f32),
        ],
        compiler_params=params(8),
        cost_estimate=pl.CostEstimate(flops=1 << 26, bytes_accessed=1 << 22, transcendentals=0),
        name="diffuse_forward",
    )(second, first, packed, other)

    slot_sums, static_here, control_here, pert_here = pl.pallas_call(
        functools.partial(scatter_kernel, cap_rows),
        in_specs=[VMEM] * 3 + [pl.BlockSpec(memory_space=pl.ANY)] * 3,
        out_specs=[VMEM] * 4,
        out_shape=[
            pltpu.VMEM((2, own, LANES), f32),
            pltpu.VMEM(static.shape, f32),
            pltpu.VMEM(control.shape, f32),
            pltpu.VMEM(pert.shape, bf16),
        ],
        scratch_shapes=[pltpu.VMEM((4 * LANES, own), f32), pltpu.SemaphoreType.DMA((3,))],
        compiler_params=params(16),
        cost_estimate=pl.CostEstimate(flops=8 * own * LANES * lists * capacity, bytes_accessed=1 << 23, transcendentals=0),
        name="scatter",
    )(entry_row, entry_lane, slots, static, control, pert)

    slot_sums = slot_sums.reshape(2, lev_share, per_level, LANES)
    tile = functools.reduce(jnp.add, sums) + increment
    tile = tile * slot_sums[0] - slot_sums[1]
    tile_first, tile_second = exchanged(tile, (0, 1))
    adjoints = [tile] + from_peers(tile)
    tile_first, tile_second, vertical_local, vertical_root = lax.optimization_barrier(
        (tile_first, tile_second, vertical_local, vertical_root)
    )
    tile_other = swapped(tile, tile_first, tile_second)
    from_local, from_root = pl.pallas_call(
        functools.partial(matrices_kernel, member_scale),
        grid=(1,),
        in_specs=[whole(levels, levels)] * 2,
        out_specs=[VMEM] * 2,
        out_shape=[pltpu.VMEM((size, 3 * size), bf16)] * 2,
        compiler_params=params(8),
        name="level_matrices",
    )(in_hbm(vertical_local), in_hbm(vertical_root))
    coefs, from_local, from_root = lax.optimization_barrier((coefs, from_local, from_root))

    smooth = pl.pallas_call(
        functools.partial(second_diffusion_kernel, rows),
        in_specs=[VMEM] * 5,
        out_specs=VMEM,
        out_shape=pltpu.VMEM((lev_share, per_level, LANES), f32),
        compiler_params=params(8),
        name="diffuse_adjoint",
    )(coefs, tile_second, tile_first, tile, tile_other)
    smooth, from_local = lax.optimization_barrier((smooth, from_local))
    smooths = [smooth] + from_peers(smooth)

    group = 2 - members % 2
    ensemble_grad = pl.pallas_call(
        member_kernel,
        grid=(members // group,),
        in_specs=[VMEM] * (3 + n_ens),
        out_specs=pl.BlockSpec((group, levels, per_level, LANES), lambda k: (k, 0, 0, 0)),
        out_shape=jax.ShapeDtypeStruct((members, levels, per_level, LANES), f32),
        scratch_shapes=[pltpu.VMEM((levels, per_level, LANES), f32)],
        compiler_params=params(16),
        name="members_gradient",
    )(from_local, control_here, pert_here, *adjoints)

    static_grad = pl.pallas_call(
        static_kernel,
        grid=(1,),
        in_specs=[VMEM] * (2 + n_ens),
        out_specs=whole(levels, per_level, LANES),
        out_shape=jax.ShapeDtypeStruct((levels, per_level, LANES), f32),
        scratch_shapes=[pltpu.VMEM((levels, per_level, LANES), f32)],
        compiler_params=params(8),
        name="static_gradient",
    )(from_root, static_here, *smooths)
    return (untiled(static_grad, rows), untiled(ensemble_grad, rows))


def solution(mesh):
    placed = (
        P(None, "cols", None),
        P("ens", None, "cols", None),
        P("ens", None, "cols", None),
        P(),
        P(),
        P("cols", None),
        P("cols", None),
        P("cols"),
        P("cols"),
        P("cols"),
        P("cols", None),
        P("cols"),
    )
    return jax.shard_map(
        local,
        mesh=mesh,
        in_specs=placed,
        out_specs=(P(None, "cols", None), P("ens", None, "cols", None)),
        check_vma=False,
    )
```

```python
import functools
import math

import jax
import jax.numpy as jnp
from jax import lax
from jax.experimental import pallas as pl
from jax.experimental.pallas import tpu as pltpu
from jax.sharding import PartitionSpec as P

NDIFF = 4
LANES = 128
FINE = 64
MIB = 1 << 20

f32 = jnp.float32
bf16 = jnp.bfloat16
SMEM = pl.BlockSpec(memory_space=pltpu.SMEM)
VMEM = pl.BlockSpec(memory_space=pltpu.VMEM)


def tiled(field):
    *lead, rows, lon = field.shape
    field = field.reshape(*lead, rows, lon // LANES, LANES)
    return jnp.swapaxes(field, -3, -2).reshape(*lead, rows * lon // LANES, LANES)


def untiled(field, rows):
    *lead, count, lanes = field.shape
    field = field.reshape(*lead, count // rows, rows, lanes)
    return jnp.swapaxes(field, -3, -2).reshape(*lead, rows, count // rows * lanes)


def params(limit, **more):
    return pltpu.CompilerParams(vmem_limit_bytes=limit * MIB, **more)


def halves(x):
    high = x.astype(bf16)
    return high, (x - high.astype(f32)).astype(bf16)


def in_hbm(x):
    return pltpu.with_memory_space_constraint(x, pltpu.HBM)


def spread(row, dtype):
    return jnp.broadcast_to(row, (16, row.shape[1])).astype(dtype)


def matches(index, count):
    ids = lax.broadcasted_iota(jnp.int32, (count, index.shape[1]), 0).astype(jnp.int16)
    return ids.reshape(count // 16, 16, index.shape[1]) == spread(index, jnp.int16)[None]


def placed_at(index, count, amount=None):
    where = matches(index, count)
    amount = bf16(1) if amount is None else spread(amount, bf16)[None]
    return jnp.where(where, amount, bf16(0)).reshape(count, index.shape[1])


def in_turns(count, build, use, slots):
    build(0, slots[0])

    def step(i, carry):
        use(2 * i, slots[0])
        build(2 * i + 1, slots[1])
        use(2 * i + 1, slots[1])
        build(jnp.minimum(2 * i + 2, count - 1), slots[0])
        return carry

    lax.fori_loop(0, count // 2, step, 0)
    if count % 2:
        use(count - 1, slots[0])


def product_nt(left, right):
    return lax.dot_general(left, right, (((1,), (1,)), ((), ())), preferred_element_type=f32)


def over(x, size):
    if size & (size - 1):
        return lax.div(x, jnp.int32(size)), lax.rem(x, jnp.int32(size))
    return lax.shift_right_logical(x, jnp.int32(size.bit_length() - 1)), x & (size - 1)


def peer(i, d, count):
    return (i + d) % count if count & (count - 1) else i ^ d


def back(d, count):
    return count - d if count & (count - 1) else d


def prepare_kernel(lev_share, rows, *refs):
    (root_ref, count_ref, static_ref, north_ref, east_ref, index_ref), sources = refs[:6], refs[6:9]
    (out_ref, row_ref, lane_ref), landed, sems = refs[9:12], refs[12:15], refs[15]
    obs_rows = landed[0].shape[0]
    here = pl.ds(pl.multiple_of(lax.axis_index("ens") * obs_rows, obs_rows), obs_rows)
    copies = [pltpu.make_async_copy(s.at[here, :], t, sems.at[i]) for i, (s, t) in enumerate(zip(sources, landed))]
    for copy in copies:
        copy.start()
    levels, per_level, _ = static_ref.shape
    first = lax.axis_index("ens") * lev_share
    for j in range(lev_share):
        total = root_ref[first + j, 0] * static_ref[0]
        for m in range(1, levels):
            total = total + root_ref[first + j, m] * static_ref[m]
        out_ref[j] = total
    out_ref[lev_share] = north_ref[...]
    out_ref[lev_share + 1] = east_ref[...]
    lists, capacity = index_ref.shape
    lon = per_level // rows * LANES
    pieces = capacity // LANES
    slot = lax.broadcasted_iota(jnp.int32, (1, capacity), 1)
    for q in range(lists):
        cell = index_ref[q : q + 1, :]
        rest, lane = over(cell, LANES)
        rest, block = over(rest, lon // LANES)
        level, row = over(rest, rows)
        grid_row = jnp.where(slot < count_ref[q], level * per_level + block * rows + row, -1)
        for c in range(pieces):
            at = q * pieces + c
            row_ref[at : at + 1, :] = grid_row[:, c * LANES : (c + 1) * LANES]
            lane_ref[at : at + 1, :] = lane[:, c * LANES : (c + 1) * LANES]
    for copy in copies:
        copy.wait()


def level_product(matrix, transpose):
    levels = matrix.shape[0]
    size = levels * 16
    pick = lax.broadcasted_iota(jnp.int32, (size, levels), 0) // 16
    pick = jnp.where(pick == lax.broadcasted_iota(jnp.int32, (size, levels), 1), f32(1), f32(0)).astype(bf16)
    same = (
        lax.broadcasted_iota(jnp.int32, (size, size), 0) % 16 == lax.broadcasted_iota(jnp.int32, (size, size), 1) % 16
    )
    out = []
    for half in halves(matrix):
        if transpose:
            wide = product_nt(pick, half)
        else:
            wide = jnp.dot(pick, half, preferred_element_type=f32)
        wide = product_nt(wide.astype(bf16), pick)
        out.append(jnp.where(same, wide, f32(0)).astype(bf16))
    return jnp.concatenate([out[0], out[0], out[1]], axis=1)


def three_terms(x):
    high, low = halves(x)
    return jnp.concatenate([high, low, high], axis=0)


def slots_kernel(n_cols, cap_rows, slot_ref, weight_ref, innov_ref, out_ref, acc_ref, fold_ref, *slots):
    slots = (slots[:2], slots[2:])
    coarse = acc_ref.shape[1]
    obs_rows = slot_ref.shape[0]
    group = min(8, obs_rows)
    acc_ref[...] = jnp.zeros_like(acc_ref)

    def build(i, to):
        at = pl.ds(pl.multiple_of(i * group, group), group)
        weight = weight_ref[at, :]
        amount = weight * innov_ref[at, :]
        upper, lower = over(slot_ref[at, :], FINE)
        terms = [t.astype(f32) for t in halves(weight) + halves(amount)]
        for r in range(group):
            here = slice(r * LANES, (r + 1) * LANES)
            to[0][:, here] = placed_at(upper[r : r + 1, :], coarse)
            mask = matches(lower[r : r + 1, :], FINE)
            for t, term in enumerate(terms):
                term = spread(term[r : r + 1, :], bf16)[None]
                to[1][t * FINE : (t + 1) * FINE, here] = jnp.where(mask, term, bf16(0)).reshape(FINE, LANES)

    def use(i, of):
        acc_ref[...] += product_nt(of[1][...], of[0][...])

    in_turns(obs_rows // group, build, use, slots)
    for t in range(2):
        at = 2 * t * FINE
        terms = acc_ref[at : at + FINE, :] + acc_ref[at + FINE : at + 2 * FINE, :]
        fold_ref[t] = jnp.concatenate([terms] * (LANES // FINE), axis=0).T
    per_row = LANES // FINE
    lane = lax.broadcasted_iota(jnp.int32, (coarse // per_row, LANES), 1)
    weights, amounts = (
        jnp.where(
            lane < FINE,
            fold_ref[t, pl.ds(0, coarse // per_row, stride=per_row), :],
            fold_ref[t, pl.ds(1, coarse // per_row, stride=per_row), :],
        )
        for t in range(2)
    )
    for e in range(out_ref.shape[0] // n_cols):
        for p in range(n_cols):
            out_ref[e * n_cols + p, 0] = weights[p * cap_rows : (p + 1) * cap_rows]
            out_ref[e * n_cols + p, 1] = amounts[p * cap_rows : (p + 1) * cap_rows]


def forward_kernel(scale, local_ref, *refs):
    sources, parts = refs[:2], refs[2:-5]
    matrix_ref, part_ref, control_ref, pert_ref, sems = refs[-5:]
    members, levels, per_level, _ = control_ref.shape
    group = 2 - members % 2
    copies = [
        [
            pltpu.make_async_copy(s.at[pl.ds(k, group)], t.at[pl.ds(k, group)], sems.at[i, k // group])
            for i, (s, t) in enumerate(zip(sources, (control_ref, pert_ref)))
        ]
        for k in range(0, members, group)
    ]
    for pair in copies:
        for copy in pair:
            copy.start()
    matrix_ref[...] = level_product(local_ref[...] * f32(scale), False)
    for k, pair in zip(range(0, members, group), copies):
        for copy in pair:
            copy.wait()

        def chunk(j, carry):
            at = pl.ds(pl.multiple_of(j * 16, 16), 16)
            terms = [three_terms(control_ref[k + i, :, at, :].reshape(levels * 16, LANES)) for i in range(group)]
            local = jnp.dot(matrix_ref[...], jnp.concatenate(terms, axis=1), preferred_element_type=f32)
            total = part_ref[:, at, :] if k else jnp.zeros((levels, 16, LANES), f32)
            for i in range(group):
                part = local[:, i * LANES : (i + 1) * LANES].reshape(levels, 16, LANES)
                total = total + pert_ref[k + i, :, at, :].astype(f32) * part
            part_ref[:, at, :] = total
            return carry

        lax.fori_loop(0, per_level // 16, chunk, 0)
    share = levels // len(parts)
    for d, part in enumerate(parts):
        at = peer(lax.axis_index("ens"), d, len(parts)) * share
        part[...] = part_ref[pl.ds(at, share)]


def gather_levels(parts, to_ref):
    share = to_ref.shape[0] // len(parts)
    for i, part in enumerate(parts):
        at = peer(lax.axis_index("ens"), (len(parts) - i) % len(parts), len(parts))
        to_ref[pl.ds(at * share, share)] = part[...]


def member_kernel(matrix_ref, control_ref, pert_ref, *refs):
    parts, out_ref, adjoint_ref = refs[:-2], refs[-2], refs[-1]
    group, levels, per_level, _ = out_ref.shape
    first = pl.program_id(0) * group

    @pl.when(pl.program_id(0) == 0)
    def _():
        gather_levels(parts, adjoint_ref)

    def chunk(j, carry):
        at = pl.ds(pl.multiple_of(j * 16, 16), 16)
        adjoint = adjoint_ref[:, at, :]
        terms = [
            three_terms((pert_ref[first + i, :, at, :].astype(f32) * adjoint).reshape(levels * 16, LANES))
            for i in range(group)
        ]
        change = jnp.dot(matrix_ref[...], jnp.concatenate(terms, axis=1), preferred_element_type=f32)
        for i in range(group):
            part = change[:, i * LANES : (i + 1) * LANES].reshape(levels, 16, LANES)
            out_ref[i, :, at, :] = control_ref[first + i, :, at, :] + part
        return carry

    lax.fori_loop(0, per_level // 16, chunk, 0)


def eastern(x):
    lane = lax.broadcasted_iota(jnp.int32, x.shape, 1)
    near = pltpu.roll(x, LANES - 1, 1)
    return jnp.where(lane == LANES - 1, pltpu.roll(near, x.shape[0] - 1, 0), near)


def western(x):
    lane = lax.broadcasted_iota(jnp.int32, x.shape, 1)
    near = pltpu.roll(x, 1, 1)
    return jnp.where(lane == 0, pltpu.roll(near, 1, 0), near)


def rows_of(second_ref, first_ref, own_ref, other_ref, plane, rows):
    at = lax.axis_index("cols")
    count = lax.axis_size("cols")
    core, chip = at % 2, at // 2 % 2
    reads = [pl.ds(r, own_ref.shape[1] // rows, stride=rows) for r in range(rows)]
    first = [first_ref[plane, r, :] for r in reads]
    second = [second_ref[plane, r, :] for r in reads]
    out = [jnp.where(jnp.logical_and(chip == 1, at >= 2), f, f32(0)) for f in first]
    out = [jnp.where(jnp.logical_and(chip == 0, at >= 2), s, o) for s, o in zip(second, out)]
    out += [jnp.where(at >= 1, other_ref[1 - core, plane, r, :], f32(0)) for r in reads]
    out += [own_ref[plane, r, :] for r in reads]
    out += [jnp.where(at < count - 1, other_ref[core, plane, r, :], f32(0)) for r in reads]
    last = [jnp.where(jnp.logical_and(chip == 0, at < count - 2), f, f32(0)) for f in first]
    return out + [jnp.where(jnp.logical_and(chip == 1, at < count - 2), s, o) for s, o in zip(second, last)]


def diffuse_rows(tiles, level, coef_ref, rows):
    field = rows_of(*tiles, level, rows)
    for step in range(NDIFF):
        field = [
            coef_ref[0, i + step] * field[i]
            + coef_ref[1, i + step] * field[i - 1]
            + coef_ref[1, i + step + 1] * field[i + 1]
            + coef_ref[2, i + step] * eastern(field[i])
            + western(coef_ref[2, i + step] * field[i])
            for i in range(1, len(field) - 1)
        ]
    return field


def first_diffusion_kernel(lev_share, rows, second_ref, first_ref, own_ref, other_ref, out_ref, coef_ref):
    tiles = (second_ref, first_ref, own_ref, other_ref)
    blocks = own_ref.shape[1] // rows
    side = 2
    north = rows_of(*tiles, lev_share, rows)
    east = rows_of(*tiles, lev_share + 1, rows)
    faces = [
        jnp.where(lax.axis_index("cols") == side - i // rows, f32(0), n) if i % rows == 0 and i <= side * rows else n
        for i, n in enumerate(north)
    ]
    for i in range(len(north)):
        inner = 0 < i < len(north) - 1
        coef_ref[0, i] = 1.0 - north[i] - faces[i + 1] - east[i] - western(east[i]) if inner else jnp.zeros_like(east[i])
        coef_ref[1, i] = faces[i]
        coef_ref[2, i] = east[i]

    def body(level, carry):
        final = diffuse_rows(tiles, level, coef_ref, rows)
        for r in range(rows):
            out_ref[level, pl.ds(r, blocks, stride=rows), :] = final[r]
        return carry

    lax.fori_loop(0, lev_share, body, 0)


def second_diffusion_kernel(rows, coef_ref, second_ref, first_ref, own_ref, other_ref, out_ref):
    tiles = (second_ref, first_ref, own_ref, other_ref)
    lev_share = out_ref.shape[0]
    blocks = own_ref.shape[1] // rows

    def body(level, carry):
        final = diffuse_rows(tiles, level, coef_ref, rows)
        for r in range(rows):
            out_ref[level, pl.ds(r, blocks, stride=rows), :] = final[r]
        return carry

    lax.fori_loop(0, lev_share, body, 0)


def scatter_kernel(cap_rows, row_ref, lane_ref, slots_ref, *refs):
    sources, out_ref, kept, acc_ref, sems = refs[:3], refs[3], refs[4:7], refs[7], refs[8]
    copies = [pltpu.make_async_copy(s, t, sems.at[i]) for i, (s, t) in enumerate(zip(sources, kept))]
    for copy in copies:
        copy.start()
    own = out_ref.shape[1]
    lists = row_ref.shape[0] // cap_rows
    first = lax.axis_index("ens") * own
    acc_ref[...] = jnp.zeros_like(acc_ref)

    def step(q, carry):
        at = pl.ds(pl.multiple_of(q * cap_rows, cap_rows), cap_rows)
        rows = row_ref[at, :] - first
        lanes = lane_ref[at, :]
        terms = []
        for t in range(2):
            total = functools.reduce(
                jnp.add, [slots_ref[e * lists + q, t] for e in range(slots_ref.shape[0] // lists)]
            )
            terms += [h.astype(f32) for h in halves(total)]
        left, right = [], []
        for c in range(cap_rows):
            left.append(placed_at(rows[c : c + 1, :], own))
            mask = matches(lanes[c : c + 1, :], LANES)
            right.append(
                jnp.concatenate(
                    [
                        jnp.where(mask, spread(t[c : c + 1, :], bf16)[None], bf16(0)).reshape(LANES, LANES)
                        for t in terms
                    ],
                    axis=0,
                )
            )
        acc_ref[...] += product_nt(jnp.concatenate(right, axis=1), jnp.concatenate(left, axis=1))
        return carry

    lax.fori_loop(0, lists, step, 0)
    for t in range(2):
        at = 2 * t * LANES
        out_ref[t] = (acc_ref[at : at + LANES, :] + acc_ref[at + LANES : at + 2 * LANES, :]).T
    for copy in copies:
        copy.wait()


def matrices_kernel(scale, local_ref, root_ref, to_members_ref, to_static_ref):
    to_members_ref[...] = level_product(local_ref[...] * f32(scale), True)
    to_static_ref[...] = level_product(root_ref[...], True)


def static_kernel(matrix_ref, static_ref, *refs):
    parts, (out_ref, smooth_ref) = refs[:-2], refs[-2:]
    levels, per_level, _ = static_ref.shape
    gather_levels(parts, smooth_ref)
    for j in range(0, per_level, 32):
        terms = [three_terms(smooth_ref[:, j + i : j + i + 16, :].reshape(levels * 16, LANES)) for i in (0, 16)]
        change = jnp.dot(matrix_ref[...], jnp.concatenate(terms, axis=1), preferred_element_type=f32)
        for i, part in ((0, change[:, :LANES]), (16, change[:, LANES:])):
            at = slice(j + i, j + i + 16)
            out_ref[:, at, :] = static_ref[:, at, :] + part.reshape(levels, 16, LANES)


def exchanged(x, starts):
    count = lax.axis_size("cols")
    out = []
    for start in starts:
        pairs = []
        for i in range(count):
            chip, core = divmod(i, 2)
            partner = (chip + start ^ 1) - start
            pairs.append((i, 2 * partner + core if 0 <= 2 * partner + core < count else i))
        out.append(lax.ppermute(x, "cols", pairs))
    return out


def from_peers(x):
    count = lax.axis_size("ens")
    return [lax.ppermute(x, "ens", [(peer(i, d, count), i) for i in range(count)]) for d in range(count - 1, 0, -1)]


def swapped(own, first, second):
    at = lax.axis_index("cols")
    pack = jnp.stack([own, jnp.where(at % 2 == at // 2 % 2, first, second)])
    return lax.ppermute(pack, "cols", [(i, i ^ 1) for i in range(lax.axis_size("cols"))])


def local(
    static_control,
    ensemble_control,
    perturbations,
    vertical_root,
    vertical_local,
    face_north,
    face_east,
    innovation,
    obs_weight,
    obs_slot,
    send_index,
    send_count,
):
    n_ens = lax.axis_size("ens")
    n_cols = lax.axis_size("cols")
    members, levels, rows, lon = ensemble_control.shape
    per_level = rows * lon // LANES
    cells = levels * per_level
    lev_share = levels // n_ens
    own = lev_share * per_level
    lists, capacity = send_index.shape
    cap_rows = capacity // LANES
    entry_rows = lists * cap_rows
    member_scale = 1.0 / math.sqrt(members * n_ens - 1)

    static = in_hbm(tiled(static_control))
    control = in_hbm(tiled(ensemble_control))
    pert = in_hbm(tiled(perturbations))

    def whole(*shape):
        return pl.BlockSpec(shape, lambda i: (0,) * len(shape))

    obs_rows = obs_slot.shape[0] // LANES
    share_rows = obs_rows // n_ens
    packed, entry_row, entry_lane, *observed = pl.pallas_call(
        functools.partial(prepare_kernel, lev_share, rows),
        grid=(1,),
        in_specs=[
            SMEM,
            SMEM,
            whole(levels, per_level, LANES),
            whole(per_level, LANES),
            whole(per_level, LANES),
            whole(lists, capacity),
            pl.BlockSpec(memory_space=pl.ANY),
            pl.BlockSpec(memory_space=pl.ANY),
            pl.BlockSpec(memory_space=pl.ANY),
        ],
        out_specs=[VMEM] * 6,
        out_shape=[
            pltpu.VMEM((lev_share + 2, per_level, LANES), f32),
            pltpu.VMEM((entry_rows, LANES), jnp.int32),
            pltpu.VMEM((entry_rows, LANES), jnp.int32),
            pltpu.VMEM((share_rows, LANES), jnp.int32),
            pltpu.VMEM((share_rows, LANES), f32),
            pltpu.VMEM((share_rows, LANES), f32),
        ],
        scratch_shapes=[pltpu.SemaphoreType.DMA((3,))],
        compiler_params=params(8),
        name="prepare",
    )(
        in_hbm(vertical_root),
        in_hbm(send_count),
        static,
        in_hbm(tiled(face_north)),
        in_hbm(tiled(face_east)),
        in_hbm(send_index),
        in_hbm(obs_slot.reshape(obs_rows, LANES)),
        in_hbm(obs_weight.reshape(obs_rows, LANES)),
        in_hbm(innovation.reshape(obs_rows, LANES)),
    )
    coarse = n_cols * capacity // FINE
    size = levels * 16
    slots = pl.pallas_call(
        functools.partial(slots_kernel, n_cols, cap_rows),
        grid=(1,),
        in_specs=[VMEM] * 3,
        out_specs=whole(n_ens * n_cols, 2, cap_rows, LANES),
        out_shape=pltpu.HBM((n_ens * n_cols, 2, cap_rows, LANES), f32),
        scratch_shapes=[
            pltpu.VMEM((4 * FINE, coarse), f32),
            pltpu.VMEM((2, coarse, LANES), f32),
        ]
        + [pltpu.VMEM((coarse, 8 * LANES), bf16), pltpu.VMEM((4 * FINE, 8 * LANES), bf16)] * 2,
        compiler_params=params(16),
        name="slot_sums",
    )(*observed)
    slots, packed, vertical_local = lax.optimization_barrier((slots, packed, vertical_local))
    groups = members // (2 - members % 2)
    parts = pl.pallas_call(
        functools.partial(forward_kernel, member_scale),
        grid=(1,),
        in_specs=[whole(levels, levels)] + [pl.BlockSpec(memory_space=pl.ANY)] * 2,
        out_specs=[VMEM] * n_ens,
        out_shape=[pltpu.VMEM((lev_share, per_level, LANES), f32)] * n_ens,
        scratch_shapes=[
            pltpu.VMEM((size, 3 * size), bf16),
            pltpu.VMEM((levels, per_level, LANES), f32),
            pltpu.VMEM(control.shape, f32),
            pltpu.VMEM(pert.shape, bf16),
            pltpu.SemaphoreType.DMA((2, groups)),
        ],
        compiler_params=params(24),
        cost_estimate=pl.CostEstimate(flops=1 << 31, bytes_accessed=1 << 24, transcendentals=0),
        name="members_forward",
    )(in_hbm(vertical_local), control, pert)
    slots = lax.all_to_all(slots, ("ens", "cols"), split_axis=0, concat_axis=0, tiled=True)
    second, first = exchanged(packed, (1, 0))
    sums = [parts[0]] + [
        lax.ppermute(parts[back(d, n_ens)], "ens", [(peer(i, d, n_ens), i) for i in range(n_ens)])
        for d in range(n_ens - 1, 0, -1)
    ]
    other = swapped(packed, first, second)

    increment, coefs = pl.pallas_call(
        functools.partial(first_diffusion_kernel, lev_share, rows),
        in_specs=[VMEM] * 4,
        out_specs=[VMEM] * 2,
        out_shape=[
            pltpu.VMEM((lev_share, per_level, LANES), f32),
            pltpu.VMEM((3, 5 * rows, per_level // rows, LANES), f32),
        ],
        compiler_params=params(8),
        cost_estimate=pl.CostEstimate(flops=1 << 26, bytes_accessed=1 << 22, transcendentals=0),
        name="diffuse_forward",
    )(second, first, packed, other)

    increment, coefs, slots = lax.optimization_barrier((increment, coefs, slots))
    slot_sums, static_here, control_here, pert_here = pl.pallas_call(
        functools.partial(scatter_kernel, cap_rows),
        in_specs=[VMEM] * 3 + [pl.BlockSpec(memory_space=pl.ANY)] * 3,
        out_specs=[VMEM] * 4,
        out_shape=[
            pltpu.VMEM((2, own, LANES), f32),
            pltpu.VMEM(static.shape, f32),
            pltpu.VMEM(control.shape, f32),
            pltpu.VMEM(pert.shape, bf16),
        ],
        scratch_shapes=[pltpu.VMEM((4 * LANES, own), f32), pltpu.SemaphoreType.DMA((3,))],
        compiler_params=params(16),
        cost_estimate=pl.CostEstimate(flops=8 * own * LANES * lists * capacity, bytes_accessed=1 << 23, transcendentals=0),
        name="scatter",
    )(entry_row, entry_lane, slots, static, control, pert)

    slot_sums = slot_sums.reshape(2, lev_share, per_level, LANES)
    tile = functools.reduce(jnp.add, sums) + increment
    tile = tile * slot_sums[0] - slot_sums[1]
    tile_first, tile_second = exchanged(tile, (0, 1))
    adjoints = [tile] + from_peers(tile)
    tile, vertical_local, vertical_root = lax.optimization_barrier((tile, vertical_local, vertical_root))
    from_local, from_root = pl.pallas_call(
        functools.partial(matrices_kernel, member_scale),
        grid=(1,),
        in_specs=[whole(levels, levels)] * 2,
        out_specs=[VMEM] * 2,
        out_shape=[pltpu.VMEM((size, 3 * size), bf16)] * 2,
        compiler_params=params(8),
        name="level_matrices",
    )(in_hbm(vertical_local), in_hbm(vertical_root))
    tile_first, tile_second, from_local, from_root = lax.optimization_barrier(
        (tile_first, tile_second, from_local, from_root)
    )
    tile_other = swapped(tile, tile_first, tile_second)

    smooth = pl.pallas_call(
        functools.partial(second_diffusion_kernel, rows),
        in_specs=[VMEM] * 5,
        out_specs=VMEM,
        out_shape=pltpu.VMEM((lev_share, per_level, LANES), f32),
        compiler_params=params(8),
        name="diffuse_adjoint",
    )(coefs, tile_second, tile_first, tile, tile_other)
    smooth, from_local = lax.optimization_barrier((smooth, from_local))
    smooths = [smooth] + from_peers(smooth)

    group = 2 - members % 2
    ensemble_grad = pl.pallas_call(
        member_kernel,
        grid=(members // group,),
        in_specs=[VMEM] * (3 + n_ens),
        out_specs=pl.BlockSpec((group, levels, per_level, LANES), lambda k: (k, 0, 0, 0)),
        out_shape=jax.ShapeDtypeStruct((members, levels, per_level, LANES), f32),
        scratch_shapes=[pltpu.VMEM((levels, per_level, LANES), f32)],
        compiler_params=params(16),
        name="members_gradient",
    )(from_local, control_here, pert_here, *adjoints)

    static_grad = pl.pallas_call(
        static_kernel,
        grid=(1,),
        in_specs=[VMEM] * (2 + n_ens),
        out_specs=whole(levels, per_level, LANES),
        out_shape=jax.ShapeDtypeStruct((levels, per_level, LANES), f32),
        scratch_shapes=[pltpu.VMEM((levels, per_level, LANES), f32)],
        compiler_params=params(8),
        name="static_gradient",
    )(from_root, static_here, *smooths)
    return (untiled(static_grad, rows), untiled(ensemble_grad, rows))


def solution(mesh):
    placed = (
        P(None, "cols", None),
        P("ens", None, "cols", None),
        P("ens", None, "cols", None),
        P(),
        P(),
        P("cols", None),
        P("cols", None),
        P("cols"),
        P("cols"),
        P("cols"),
        P("cols", None),
        P("cols"),
    )
    return jax.shard_map(
        local,
        mesh=mesh,
        in_specs=placed,
        out_specs=(P(None, "cols", None), P("ens", None, "cols", None)),
        check_vma=False,
    )
```

```python
import functools
import math

import jax
import jax.numpy as jnp
from jax import lax
from jax.experimental import pallas as pl
from jax.experimental.pallas import tpu as pltpu
from jax.sharding import PartitionSpec as P

NDIFF = 4
LANES = 128
FINE = 64
MIB = 1 << 20

f32 = jnp.float32
bf16 = jnp.bfloat16
SMEM = pl.BlockSpec(memory_space=pltpu.SMEM)
VMEM = pl.BlockSpec(memory_space=pltpu.VMEM)


def tiled(field):
    *lead, rows, lon = field.shape
    field = field.reshape(*lead, rows, lon // LANES, LANES)
    return jnp.swapaxes(field, -3, -2).reshape(*lead, rows * lon // LANES, LANES)


def untiled(field, rows):
    *lead, count, lanes = field.shape
    field = field.reshape(*lead, count // rows, rows, lanes)
    return jnp.swapaxes(field, -3, -2).reshape(*lead, rows, count // rows * lanes)


def params(limit, **more):
    return pltpu.CompilerParams(vmem_limit_bytes=limit * MIB, **more)


def halves(x):
    high = x.astype(bf16)
    return high, (x - high.astype(f32)).astype(bf16)


def in_hbm(x):
    return pltpu.with_memory_space_constraint(x, pltpu.HBM)


def spread(row, dtype):
    return jnp.broadcast_to(row, (16, row.shape[1])).astype(dtype)


def matches(index, count):
    ids = lax.broadcasted_iota(jnp.int32, (count, index.shape[1]), 0).astype(jnp.int16)
    return ids.reshape(count // 16, 16, index.shape[1]) == spread(index, jnp.int16)[None]


def placed_at(index, count, amount=None):
    where = matches(index, count)
    amount = bf16(1) if amount is None else spread(amount, bf16)[None]
    return jnp.where(where, amount, bf16(0)).reshape(count, index.shape[1])


def in_turns(count, build, use, slots):
    build(0, slots[0])

    def step(i, carry):
        use(2 * i, slots[0])
        build(2 * i + 1, slots[1])
        use(2 * i + 1, slots[1])
        build(jnp.minimum(2 * i + 2, count - 1), slots[0])
        return carry

    lax.fori_loop(0, count // 2, step, 0)
    if count % 2:
        use(count - 1, slots[0])


def product_nt(left, right):
    return lax.dot_general(left, right, (((1,), (1,)), ((), ())), preferred_element_type=f32)


def over(x, size):
    if size & (size - 1):
        return lax.div(x, jnp.int32(size)), lax.rem(x, jnp.int32(size))
    return lax.shift_right_logical(x, jnp.int32(size.bit_length() - 1)), x & (size - 1)


def peer(i, d, count):
    return (i + d) % count if count & (count - 1) else i ^ d


def back(d, count):
    return count - d if count & (count - 1) else d


def prepare_kernel(lev_share, root_ref, static_ref, north_ref, east_ref, out_ref):
    levels = static_ref.shape[0]
    first = lax.axis_index("ens") * lev_share
    for j in range(lev_share):
        total = root_ref[first + j, 0] * static_ref[0]
        for m in range(1, levels):
            total = total + root_ref[first + j, m] * static_ref[m]
        out_ref[j] = total
    out_ref[lev_share] = north_ref[...]
    out_ref[lev_share + 1] = east_ref[...]


def list_cells(rows, lon, index_ref, count_ref, row_ref, lane_ref):
    lists, capacity = index_ref.shape
    pieces = capacity // LANES
    slot = lax.broadcasted_iota(jnp.int32, (1, capacity), 1)
    for q in range(lists):
        rest, lane = over(index_ref[q : q + 1, :], LANES)
        rest, block = over(rest, lon // LANES)
        level, row = over(rest, rows)
        grid_row = (level * (lon // LANES) + block) * rows + row
        grid_row = jnp.where(slot < count_ref[q], grid_row, -1)
        for c in range(pieces):
            at = q * pieces + c
            row_ref[at : at + 1, :] = grid_row[:, c * LANES : (c + 1) * LANES]
            lane_ref[at : at + 1, :] = lane[:, c * LANES : (c + 1) * LANES]


def level_product(matrix, transpose):
    levels = matrix.shape[0]
    size = levels * 16
    pick = lax.broadcasted_iota(jnp.int32, (size, levels), 0) // 16
    pick = jnp.where(pick == lax.broadcasted_iota(jnp.int32, (size, levels), 1), f32(1), f32(0)).astype(bf16)
    same = (
        lax.broadcasted_iota(jnp.int32, (size, size), 0) % 16 == lax.broadcasted_iota(jnp.int32, (size, size), 1) % 16
    )
    out = []
    for half in halves(matrix):
        if transpose:
            wide = product_nt(pick, half)
        else:
            wide = jnp.dot(pick, half, preferred_element_type=f32)
        wide = product_nt(wide.astype(bf16), pick)
        out.append(jnp.where(same, wide, f32(0)).astype(bf16))
    return jnp.concatenate([out[0], out[0], out[1]], axis=1)


def three_terms(x):
    high, low = halves(x)
    return jnp.concatenate([high, low, high], axis=0)


def observe_kernel(n_cols, cap_rows, rows, lon, scale, *refs):
    n_ens = len(refs) - 28
    sources, (out_ref, row_ref, lane_ref), parts = refs[:8], refs[8:11], refs[11 : 11 + n_ens]
    refs = refs[11 + n_ens :]
    (acc_ref, fold_ref, matrix_ref, part_ref), landed, sems, slots = (
        refs[:4],
        refs[4:12],
        refs[12],
        (refs[13:15], refs[15:17]),
    )
    slot_ref, weight_ref, innov_ref, index_ref, count_ref, local_ref, control_ref, pert_ref = landed
    coarse = acc_ref.shape[1]
    obs_rows = slot_ref.shape[0]
    group = min(8, obs_rows)
    here = pl.ds(pl.multiple_of(lax.axis_index("ens") * obs_rows, obs_rows), obs_rows)
    copies = [
        pltpu.make_async_copy(s.at[here, :] if i < 3 else s, t, sems.at[i])
        for i, (s, t) in enumerate(zip(sources, landed))
    ]
    for copy in copies:
        copy.start()
    acc_ref[...] = jnp.zeros_like(acc_ref)
    for copy in copies[:3]:
        copy.wait()

    def build(i, to):
        at = pl.ds(pl.multiple_of(i * group, group), group)
        weight = weight_ref[at, :]
        amount = weight * innov_ref[at, :]
        upper, lower = over(slot_ref[at, :], FINE)
        terms = [t.astype(f32) for t in halves(weight) + halves(amount)]
        for r in range(group):
            here = slice(r * LANES, (r + 1) * LANES)
            to[0][:, here] = placed_at(upper[r : r + 1, :], coarse)
            mask = matches(lower[r : r + 1, :], FINE)
            for t, term in enumerate(terms):
                term = spread(term[r : r + 1, :], bf16)[None]
                to[1][t * FINE : (t + 1) * FINE, here] = jnp.where(mask, term, bf16(0)).reshape(FINE, LANES)

    def use(i, of):
        acc_ref[...] += product_nt(of[1][...], of[0][...])

    in_turns(obs_rows // group, build, use, slots)
    for t in range(2):
        at = 2 * t * FINE
        terms = acc_ref[at : at + FINE, :] + acc_ref[at + FINE : at + 2 * FINE, :]
        fold_ref[t] = jnp.concatenate([terms] * (LANES // FINE), axis=0).T
    per_row = LANES // FINE
    lane = lax.broadcasted_iota(jnp.int32, (coarse // per_row, LANES), 1)
    weights, amounts = (
        jnp.where(
            lane < FINE,
            fold_ref[t, pl.ds(0, coarse // per_row, stride=per_row), :],
            fold_ref[t, pl.ds(1, coarse // per_row, stride=per_row), :],
        )
        for t in range(2)
    )
    for e in range(n_ens):
        for p in range(n_cols):
            out_ref[e * n_cols + p, 0] = weights[p * cap_rows : (p + 1) * cap_rows]
            out_ref[e * n_cols + p, 1] = amounts[p * cap_rows : (p + 1) * cap_rows]
    for copy in copies[3:]:
        copy.wait()
    list_cells(rows, lon, index_ref, count_ref, row_ref, lane_ref)
    matrix_ref[...] = level_product(local_ref[...] * f32(scale), False)
    sum_members(matrix_ref, control_ref, pert_ref, part_ref)
    share = part_ref.shape[0] // n_ens
    for d, part in enumerate(parts):
        at = peer(lax.axis_index("ens"), d, n_ens) * share
        part[...] = part_ref[pl.ds(at, share)]


def sum_members(matrix_ref, control_ref, pert_ref, out_ref):
    members, levels, per_level, _ = control_ref.shape
    group = 2 - members % 2

    def chunk(j, carry):
        at = pl.ds(pl.multiple_of(j * 16, 16), 16)
        total = jnp.zeros((levels * 16, LANES), f32)
        for k in range(0, members, group):
            terms = [three_terms(control_ref[k + i, :, at, :].reshape(levels * 16, LANES)) for i in range(group)]
            local = jnp.dot(matrix_ref[...], jnp.concatenate(terms, axis=1), preferred_element_type=f32)
            for i in range(group):
                pert = pert_ref[k + i, :, at, :].astype(f32).reshape(levels * 16, LANES)
                total = total + pert * local[:, i * LANES : (i + 1) * LANES]
        out_ref[:, at, :] = total.reshape(levels, 16, LANES)
        return carry

    lax.fori_loop(0, per_level // 16, chunk, 0)


def gather_levels(parts, to_ref):
    share = to_ref.shape[0] // len(parts)
    for i, part in enumerate(parts):
        at = peer(lax.axis_index("ens"), (len(parts) - i) % len(parts), len(parts))
        to_ref[pl.ds(at * share, share)] = part[...]


def member_kernel(matrix_ref, control_ref, pert_ref, *refs):
    parts, out_ref, adjoint_ref = refs[:-2], refs[-2], refs[-1]
    group, levels, per_level, _ = out_ref.shape
    first = pl.program_id(0) * group

    @pl.when(pl.program_id(0) == 0)
    def _():
        gather_levels(parts, adjoint_ref)

    def chunk(j, carry):
        at = pl.ds(pl.multiple_of(j * 16, 16), 16)
        adjoint = adjoint_ref[:, at, :]
        terms = [
            three_terms((pert_ref[first + i, :, at, :].astype(f32) * adjoint).reshape(levels * 16, LANES))
            for i in range(group)
        ]
        change = jnp.dot(matrix_ref[...], jnp.concatenate(terms, axis=1), preferred_element_type=f32)
        for i in range(group):
            part = change[:, i * LANES : (i + 1) * LANES].reshape(levels, 16, LANES)
            out_ref[i, :, at, :] = control_ref[first + i, :, at, :] + part
        return carry

    lax.fori_loop(0, per_level // 16, chunk, 0)


def eastern(x):
    lane = lax.broadcasted_iota(jnp.int32, x.shape, 1)
    near = pltpu.roll(x, LANES - 1, 1)
    return jnp.where(lane == LANES - 1, pltpu.roll(near, x.shape[0] - 1, 0), near)


def western(x):
    lane = lax.broadcasted_iota(jnp.int32, x.shape, 1)
    near = pltpu.roll(x, 1, 1)
    return jnp.where(lane == 0, pltpu.roll(near, 1, 0), near)


def rows_of(second_ref, first_ref, own_ref, other_ref, plane, rows):
    at = lax.axis_index("cols")
    count = lax.axis_size("cols")
    core, chip = at % 2, at // 2 % 2
    reads = [pl.ds(r, own_ref.shape[1] // rows, stride=rows) for r in range(rows)]
    first = [first_ref[plane, r, :] for r in reads]
    second = [second_ref[plane, r, :] for r in reads]
    out = [jnp.where(jnp.logical_and(chip == 1, at >= 2), f, f32(0)) for f in first]
    out = [jnp.where(jnp.logical_and(chip == 0, at >= 2), s, o) for s, o in zip(second, out)]
    out += [jnp.where(at >= 1, other_ref[1 - core, plane, r, :], f32(0)) for r in reads]
    out += [own_ref[plane, r, :] for r in reads]
    out += [jnp.where(at < count - 1, other_ref[core, plane, r, :], f32(0)) for r in reads]
    last = [jnp.where(jnp.logical_and(chip == 0, at < count - 2), f, f32(0)) for f in first]
    return out + [jnp.where(jnp.logical_and(chip == 1, at < count - 2), s, o) for s, o in zip(second, last)]


def diffuse_rows(tiles, level, coef_ref, rows):
    field = rows_of(*tiles, level, rows)
    for step in range(NDIFF):
        field = [
            coef_ref[0, i + step] * field[i]
            + coef_ref[1, i + step] * field[i - 1]
            + coef_ref[1, i + step + 1] * field[i + 1]
            + coef_ref[2, i + step] * eastern(field[i])
            + western(coef_ref[2, i + step] * field[i])
            for i in range(1, len(field) - 1)
        ]
    return field


def first_diffusion_kernel(lev_share, rows, second_ref, first_ref, own_ref, other_ref, out_ref, coef_ref):
    tiles = (second_ref, first_ref, own_ref, other_ref)
    blocks = own_ref.shape[1] // rows
    side = 2
    north = rows_of(*tiles, lev_share, rows)
    east = rows_of(*tiles, lev_share + 1, rows)
    faces = [
        jnp.where(lax.axis_index("cols") == side - i // rows, f32(0), n) if i % rows == 0 and i <= side * rows else n
        for i, n in enumerate(north)
    ]
    for i in range(len(north)):
        inner = 0 < i < len(north) - 1
        coef_ref[0, i] = 1.0 - north[i] - faces[i + 1] - east[i] - western(east[i]) if inner else jnp.zeros_like(east[i])
        coef_ref[1, i] = faces[i]
        coef_ref[2, i] = east[i]

    def body(level, carry):
        final = diffuse_rows(tiles, level, coef_ref, rows)
        for r in range(rows):
            out_ref[level, pl.ds(r, blocks, stride=rows), :] = final[r]
        return carry

    lax.fori_loop(0, lev_share, body, 0)


def second_diffusion_kernel(rows, coef_ref, second_ref, first_ref, own_ref, other_ref, out_ref):
    tiles = (second_ref, first_ref, own_ref, other_ref)
    lev_share = out_ref.shape[0]
    blocks = own_ref.shape[1] // rows

    def body(level, carry):
        final = diffuse_rows(tiles, level, coef_ref, rows)
        for r in range(rows):
            out_ref[level, pl.ds(r, blocks, stride=rows), :] = final[r]
        return carry

    lax.fori_loop(0, lev_share, body, 0)


def scatter_kernel(cap_rows, row_ref, lane_ref, slots_ref, *refs):
    sources, out_ref, kept, acc_ref, sems = refs[:3], refs[3], refs[4:7], refs[7], refs[8]
    copies = [pltpu.make_async_copy(s, t, sems.at[i]) for i, (s, t) in enumerate(zip(sources, kept))]
    for copy in copies:
        copy.start()
    own = out_ref.shape[1]
    lists = row_ref.shape[0] // cap_rows
    first = lax.axis_index("ens") * own
    acc_ref[...] = jnp.zeros_like(acc_ref)

    def step(q, carry):
        at = pl.ds(pl.multiple_of(q * cap_rows, cap_rows), cap_rows)
        rows = row_ref[at, :] - first
        lanes = lane_ref[at, :]
        terms = []
        for t in range(2):
            total = functools.reduce(
                jnp.add, [slots_ref[e * lists + q, t] for e in range(slots_ref.shape[0] // lists)]
            )
            terms += [h.astype(f32) for h in halves(total)]
        left, right = [], []
        for c in range(cap_rows):
            left.append(placed_at(rows[c : c + 1, :], own))
            mask = matches(lanes[c : c + 1, :], LANES)
            right.append(
                jnp.concatenate(
                    [
                        jnp.where(mask, spread(t[c : c + 1, :], bf16)[None], bf16(0)).reshape(LANES, LANES)
                        for t in terms
                    ],
                    axis=0,
                )
            )
        acc_ref[...] += product_nt(jnp.concatenate(right, axis=1), jnp.concatenate(left, axis=1))
        return carry

    lax.fori_loop(0, lists, step, 0)
    for t in range(2):
        at = 2 * t * LANES
        out_ref[t] = (acc_ref[at : at + LANES, :] + acc_ref[at + LANES : at + 2 * LANES, :]).T
    for copy in copies:
        copy.wait()


def matrices_kernel(scale, local_ref, root_ref, to_members_ref, to_static_ref):
    to_members_ref[...] = level_product(local_ref[...] * f32(scale), True)
    to_static_ref[...] = level_product(root_ref[...], True)


def static_kernel(matrix_ref, static_ref, *refs):
    parts, (out_ref, smooth_ref) = refs[:-2], refs[-2:]
    levels, per_level, _ = static_ref.shape
    gather_levels(parts, smooth_ref)
    for j in range(0, per_level, 32):
        terms = [three_terms(smooth_ref[:, j + i : j + i + 16, :].reshape(levels * 16, LANES)) for i in (0, 16)]
        change = jnp.dot(matrix_ref[...], jnp.concatenate(terms, axis=1), preferred_element_type=f32)
        for i, part in ((0, change[:, :LANES]), (16, change[:, LANES:])):
            at = slice(j + i, j + i + 16)
            out_ref[:, at, :] = static_ref[:, at, :] + part.reshape(levels, 16, LANES)


def exchanged(x, starts):
    count = lax.axis_size("cols")
    out = []
    for start in starts:
        pairs = []
        for i in range(count):
            chip, core = divmod(i, 2)
            partner = (chip + start ^ 1) - start
            pairs.append((i, 2 * partner + core if 0 <= 2 * partner + core < count else i))
        out.append(lax.ppermute(x, "cols", pairs))
    return out


def from_peers(x):
    count = lax.axis_size("ens")
    return [lax.ppermute(x, "ens", [(peer(i, d, count), i) for i in range(count)]) for d in range(count - 1, 0, -1)]


def swapped(own, first, second):
    at = lax.axis_index("cols")
    pack = jnp.stack([own, jnp.where(at % 2 == at // 2 % 2, first, second)])
    return lax.ppermute(pack, "cols", [(i, i ^ 1) for i in range(lax.axis_size("cols"))])


def local(
    static_control,
    ensemble_control,
    perturbations,
    vertical_root,
    vertical_local,
    face_north,
    face_east,
    innovation,
    obs_weight,
    obs_slot,
    send_index,
    send_count,
):
    n_ens = lax.axis_size("ens")
    n_cols = lax.axis_size("cols")
    members, levels, rows, lon = ensemble_control.shape
    per_level = rows * lon // LANES
    cells = levels * per_level
    lev_share = levels // n_ens
    own = lev_share * per_level
    lists, capacity = send_index.shape
    cap_rows = capacity // LANES
    entry_rows = lists * cap_rows
    member_scale = 1.0 / math.sqrt(members * n_ens - 1)

    static = in_hbm(tiled(static_control))
    control = in_hbm(tiled(ensemble_control))
    pert = in_hbm(tiled(perturbations))

    def whole(*shape):
        return pl.BlockSpec(shape, lambda i: (0,) * len(shape))

    obs_rows = obs_slot.shape[0] // LANES
    share_rows = obs_rows // n_ens
    coarse = n_cols * capacity // FINE
    size = levels * 16
    slots, entry_row, entry_lane, *parts = pl.pallas_call(
        functools.partial(observe_kernel, n_cols, cap_rows, rows, lon, member_scale),
        grid=(1,),
        in_specs=[pl.BlockSpec(memory_space=pl.ANY)] * 8,
        out_specs=[whole(n_ens * n_cols, 2, cap_rows, LANES)] + [VMEM] * (2 + n_ens),
        out_shape=[
            pltpu.HBM((n_ens * n_cols, 2, cap_rows, LANES), f32),
            pltpu.VMEM((entry_rows, LANES), jnp.int32),
            pltpu.VMEM((entry_rows, LANES), jnp.int32),
        ]
        + [pltpu.VMEM((lev_share, per_level, LANES), f32)] * n_ens,
        scratch_shapes=[
            pltpu.VMEM((4 * FINE, coarse), f32),
            pltpu.VMEM((2, coarse, LANES), f32),
            pltpu.VMEM((size, 3 * size), bf16),
            pltpu.VMEM((levels, per_level, LANES), f32),
            pltpu.VMEM((share_rows, LANES), jnp.int32),
            pltpu.VMEM((share_rows, LANES), f32),
            pltpu.VMEM((share_rows, LANES), f32),
            pltpu.VMEM((lists, capacity), jnp.int32),
            pltpu.SMEM((lists,), jnp.int32),
            pltpu.VMEM((levels, levels), f32),
            pltpu.VMEM(control.shape, f32),
            pltpu.VMEM(pert.shape, bf16),
            pltpu.SemaphoreType.DMA((8,)),
        ]
        + [pltpu.VMEM((coarse, 8 * LANES), bf16), pltpu.VMEM((4 * FINE, 8 * LANES), bf16)] * 2,
        compiler_params=params(24),
        name="slot_sums_and_members",
    )(
        in_hbm(obs_slot.reshape(obs_rows, LANES)),
        in_hbm(obs_weight.reshape(obs_rows, LANES)),
        in_hbm(innovation.reshape(obs_rows, LANES)),
        in_hbm(send_index),
        in_hbm(send_count),
        in_hbm(vertical_local),
        control,
        pert,
    )
    slots, face_north, face_east = lax.optimization_barrier((slots, face_north, face_east))
    packed = pl.pallas_call(
        functools.partial(prepare_kernel, lev_share),
        grid=(1,),
        in_specs=[SMEM, whole(levels, per_level, LANES), whole(per_level, LANES), whole(per_level, LANES)],
        out_specs=VMEM,
        out_shape=pltpu.VMEM((lev_share + 2, per_level, LANES), f32),
        compiler_params=params(8),
        cost_estimate=pl.CostEstimate(flops=1 << 31, bytes_accessed=1 << 25, transcendentals=0),
        name="prepare",
    )(in_hbm(vertical_root), static, in_hbm(tiled(face_north)), in_hbm(tiled(face_east)))
    slots = lax.all_to_all(slots, ("ens", "cols"), split_axis=0, concat_axis=0, tiled=True)
    second, first = exchanged(packed, (1, 0))
    sums = [parts[0]] + [
        lax.ppermute(parts[back(d, n_ens)], "ens", [(peer(i, d, n_ens), i) for i in range(n_ens)])
        for d in range(n_ens - 1, 0, -1)
    ]
    other = swapped(packed, first, second)

    increment, coefs = pl.pallas_call(
        functools.partial(first_diffusion_kernel, lev_share, rows),
        in_specs=[VMEM] * 4,
        out_specs=[VMEM] * 2,
        out_shape=[
            pltpu.VMEM((lev_share, per_level, LANES), f32),
            pltpu.VMEM((3, 5 * rows, per_level // rows, LANES), f32),
        ],
        compiler_params=params(8),
        cost_estimate=pl.CostEstimate(flops=1 << 26, bytes_accessed=1 << 22, transcendentals=0),
        name="diffuse_forward",
    )(second, first, packed, other)

    increment, coefs, slots = lax.optimization_barrier((increment, coefs, slots))
    slot_sums, static_here, control_here, pert_here = pl.pallas_call(
        functools.partial(scatter_kernel, cap_rows),
        in_specs=[VMEM] * 3 + [pl.BlockSpec(memory_space=pl.ANY)] * 3,
        out_specs=[VMEM] * 4,
        out_shape=[
            pltpu.VMEM((2, own, LANES), f32),
            pltpu.VMEM(static.shape, f32),
            pltpu.VMEM(control.shape, f32),
            pltpu.VMEM(pert.shape, bf16),
        ],
        scratch_shapes=[pltpu.VMEM((4 * LANES, own), f32), pltpu.SemaphoreType.DMA((3,))],
        compiler_params=params(16),
        cost_estimate=pl.CostEstimate(flops=8 * own * LANES * lists * capacity, bytes_accessed=1 << 23, transcendentals=0),
        name="scatter",
    )(entry_row, entry_lane, slots, static, control, pert)

    slot_sums = slot_sums.reshape(2, lev_share, per_level, LANES)
    tile = functools.reduce(jnp.add, sums) + increment
    tile = tile * slot_sums[0] - slot_sums[1]
    tile_first, tile_second = exchanged(tile, (0, 1))
    adjoints = [tile] + from_peers(tile)
    tile, vertical_local, vertical_root = lax.optimization_barrier((tile, vertical_local, vertical_root))
    from_local, from_root = pl.pallas_call(
        functools.partial(matrices_kernel, member_scale),
        grid=(1,),
        in_specs=[whole(levels, levels)] * 2,
        out_specs=[VMEM] * 2,
        out_shape=[pltpu.VMEM((size, 3 * size), bf16)] * 2,
        compiler_params=params(8),
        name="level_matrices",
    )(in_hbm(vertical_local), in_hbm(vertical_root))
    tile_first, tile_second, from_local, from_root = lax.optimization_barrier(
        (tile_first, tile_second, from_local, from_root)
    )
    tile_other = swapped(tile, tile_first, tile_second)

    smooth = pl.pallas_call(
        functools.partial(second_diffusion_kernel, rows),
        in_specs=[VMEM] * 5,
        out_specs=VMEM,
        out_shape=pltpu.VMEM((lev_share, per_level, LANES), f32),
        compiler_params=params(8),
        name="diffuse_adjoint",
    )(coefs, tile_second, tile_first, tile, tile_other)
    smooth, from_local = lax.optimization_barrier((smooth, from_local))
    smooths = [smooth] + from_peers(smooth)

    group = 2 - members % 2
    ensemble_grad = pl.pallas_call(
        member_kernel,
        grid=(members // group,),
        in_specs=[VMEM] * (3 + n_ens),
        out_specs=pl.BlockSpec((group, levels, per_level, LANES), lambda k: (k, 0, 0, 0)),
        out_shape=jax.ShapeDtypeStruct((members, levels, per_level, LANES), f32),
        scratch_shapes=[pltpu.VMEM((levels, per_level, LANES), f32)],
        compiler_params=params(16),
        name="members_gradient",
    )(from_local, control_here, pert_here, *adjoints)

    static_grad = pl.pallas_call(
        static_kernel,
        grid=(1,),
        in_specs=[VMEM] * (2 + n_ens),
        out_specs=whole(levels, per_level, LANES),
        out_shape=jax.ShapeDtypeStruct((levels, per_level, LANES), f32),
        scratch_shapes=[pltpu.VMEM((levels, per_level, LANES), f32)],
        compiler_params=params(8),
        name="static_gradient",
    )(from_root, static_here, *smooths)
    return (untiled(static_grad, rows), untiled(ensemble_grad, rows))


def solution(mesh):
    placed = (
        P(None, "cols", None),
        P("ens", None, "cols", None),
        P("ens", None, "cols", None),
        P(),
        P(),
        P("cols", None),
        P("cols", None),
        P("cols"),
        P("cols"),
        P("cols"),
        P("cols", None),
        P("cols"),
    )
    return jax.shard_map(
        local,
        mesh=mesh,
        in_specs=placed,
        out_specs=(P(None, "cols", None), P("ens", None, "cols", None)),
        check_vma=False,
    )
```

```python
import functools
import math

import jax
import jax.numpy as jnp
from jax import lax
from jax.experimental import pallas as pl
from jax.experimental.pallas import tpu as pltpu
from jax.sharding import PartitionSpec as P

NDIFF = 4
LANES = 128
FINE = 64
MIB = 1 << 20

f32 = jnp.float32
bf16 = jnp.bfloat16
SMEM = pl.BlockSpec(memory_space=pltpu.SMEM)
VMEM = pl.BlockSpec(memory_space=pltpu.VMEM)


def tiled(field):
    *lead, rows, lon = field.shape
    field = field.reshape(*lead, rows, lon // LANES, LANES)
    return jnp.swapaxes(field, -3, -2).reshape(*lead, rows * lon // LANES, LANES)


def untiled(field, rows):
    *lead, count, lanes = field.shape
    field = field.reshape(*lead, count // rows, rows, lanes)
    return jnp.swapaxes(field, -3, -2).reshape(*lead, rows, count // rows * lanes)


def params(limit, **more):
    return pltpu.CompilerParams(vmem_limit_bytes=limit * MIB, **more)


def halves(x):
    high = x.astype(bf16)
    return high, (x - high.astype(f32)).astype(bf16)


def in_hbm(x):
    return pltpu.with_memory_space_constraint(x, pltpu.HBM)


def spread(row, dtype):
    return jnp.broadcast_to(row, (16, row.shape[1])).astype(dtype)


def matches(index, count):
    ids = lax.broadcasted_iota(jnp.int32, (count, index.shape[1]), 0).astype(jnp.int16)
    return ids.reshape(count // 16, 16, index.shape[1]) == spread(index, jnp.int16)[None]


def placed_at(index, count, amount=None):
    where = matches(index, count)
    amount = bf16(1) if amount is None else spread(amount, bf16)[None]
    return jnp.where(where, amount, bf16(0)).reshape(count, index.shape[1])


def in_turns(count, build, use, slots):
    build(0, slots[0])

    def step(i, carry):
        use(2 * i, slots[0])
        build(2 * i + 1, slots[1])
        use(2 * i + 1, slots[1])
        build(jnp.minimum(2 * i + 2, count - 1), slots[0])
        return carry

    lax.fori_loop(0, count // 2, step, 0)
    if count % 2:
        use(count - 1, slots[0])


def product_nt(left, right):
    return lax.dot_general(left, right, (((1,), (1,)), ((), ())), preferred_element_type=f32)


def over(x, size):
    if size & (size - 1):
        return lax.div(x, jnp.int32(size)), lax.rem(x, jnp.int32(size))
    return lax.shift_right_logical(x, jnp.int32(size.bit_length() - 1)), x & (size - 1)


def peer(i, d, count):
    return (i + d) % count if count & (count - 1) else i ^ d


def back(d, count):
    return count - d if count & (count - 1) else d


def prepare(root_ref, static_ref, north_ref, east_ref, out_ref):
    levels = static_ref.shape[0]
    lev_share = out_ref.shape[0] - 2
    first = lax.axis_index("ens") * lev_share
    for j in range(lev_share):
        total = root_ref[first + j, 0] * static_ref[0]
        for m in range(1, levels):
            total = total + root_ref[first + j, m] * static_ref[m]
        out_ref[j] = total
    out_ref[lev_share] = north_ref[...]
    out_ref[lev_share + 1] = east_ref[...]


def list_cells(rows, lon, index_ref, count_ref, row_ref, lane_ref):
    lists, capacity = index_ref.shape
    pieces = capacity // LANES
    slot = lax.broadcasted_iota(jnp.int32, (1, capacity), 1)
    for q in range(lists):
        rest, lane = over(index_ref[q : q + 1, :], LANES)
        rest, block = over(rest, lon // LANES)
        level, row = over(rest, rows)
        grid_row = (level * (lon // LANES) + block) * rows + row
        grid_row = jnp.where(slot < count_ref[q], grid_row, -1)
        for c in range(pieces):
            at = q * pieces + c
            row_ref[at : at + 1, :] = grid_row[:, c * LANES : (c + 1) * LANES]
            lane_ref[at : at + 1, :] = lane[:, c * LANES : (c + 1) * LANES]


def level_product(matrix, transpose):
    levels = matrix.shape[0]
    size = levels * 16
    pick = lax.broadcasted_iota(jnp.int32, (size, levels), 0) // 16
    pick = jnp.where(pick == lax.broadcasted_iota(jnp.int32, (size, levels), 1), f32(1), f32(0)).astype(bf16)
    same = (
        lax.broadcasted_iota(jnp.int32, (size, size), 0) % 16 == lax.broadcasted_iota(jnp.int32, (size, size), 1) % 16
    )
    out = []
    for half in halves(matrix):
        if transpose:
            wide = product_nt(pick, half)
        else:
            wide = jnp.dot(pick, half, preferred_element_type=f32)
        wide = product_nt(wide.astype(bf16), pick)
        out.append(jnp.where(same, wide, f32(0)).astype(bf16))
    return jnp.concatenate([out[0], out[0], out[1]], axis=1)


def three_terms(x):
    high, low = halves(x)
    return jnp.concatenate([high, low, high], axis=0)


def observe_kernel(n_cols, cap_rows, scale, *refs):
    n_ens = len(refs) - 31
    sources, (out_ref, packed_ref), parts = refs[:10], refs[10:12], refs[12 : 12 + n_ens]
    refs = refs[12 + n_ens :]
    (acc_ref, fold_ref, matrix_ref, part_ref), landed, sems, slots = (
        refs[:4],
        refs[4:14],
        refs[14],
        (refs[15:17], refs[17:19]),
    )
    slot_ref, weight_ref, innov_ref, local_ref, control_ref, pert_ref, *static_refs = landed
    coarse = acc_ref.shape[1]
    obs_rows = slot_ref.shape[0]
    group = min(8, obs_rows)
    here = pl.ds(pl.multiple_of(lax.axis_index("ens") * obs_rows, obs_rows), obs_rows)
    copies = [
        pltpu.make_async_copy(s.at[here, :] if i < 3 else s, t, sems.at[i])
        for i, (s, t) in enumerate(zip(sources, landed))
    ]
    for copy in copies:
        copy.start()
    acc_ref[...] = jnp.zeros_like(acc_ref)
    for copy in copies[:3]:
        copy.wait()

    def build(i, to):
        at = pl.ds(pl.multiple_of(i * group, group), group)
        weight = weight_ref[at, :]
        amount = weight * innov_ref[at, :]
        upper, lower = over(slot_ref[at, :], FINE)
        terms = [t.astype(f32) for t in halves(weight) + halves(amount)]
        for r in range(group):
            here = slice(r * LANES, (r + 1) * LANES)
            to[0][:, here] = placed_at(upper[r : r + 1, :], coarse)
            mask = matches(lower[r : r + 1, :], FINE)
            for t, term in enumerate(terms):
                term = spread(term[r : r + 1, :], bf16)[None]
                to[1][t * FINE : (t + 1) * FINE, here] = jnp.where(mask, term, bf16(0)).reshape(FINE, LANES)

    def use(i, of):
        acc_ref[...] += product_nt(of[1][...], of[0][...])

    in_turns(obs_rows // group, build, use, slots)
    for t in range(2):
        at = 2 * t * FINE
        terms = acc_ref[at : at + FINE, :] + acc_ref[at + FINE : at + 2 * FINE, :]
        fold_ref[t] = jnp.concatenate([terms] * (LANES // FINE), axis=0).T
    per_row = LANES // FINE
    lane = lax.broadcasted_iota(jnp.int32, (coarse // per_row, LANES), 1)
    weights, amounts = (
        jnp.where(
            lane < FINE,
            fold_ref[t, pl.ds(0, coarse // per_row, stride=per_row), :],
            fold_ref[t, pl.ds(1, coarse // per_row, stride=per_row), :],
        )
        for t in range(2)
    )
    for e in range(n_ens):
        for p in range(n_cols):
            out_ref[e * n_cols + p, 0] = weights[p * cap_rows : (p + 1) * cap_rows]
            out_ref[e * n_cols + p, 1] = amounts[p * cap_rows : (p + 1) * cap_rows]
    for copy in copies[3:]:
        copy.wait()
    prepare(*static_refs, packed_ref)
    matrix_ref[...] = level_product(local_ref[...] * f32(scale), False)
    sum_members(matrix_ref, control_ref, pert_ref, part_ref)
    share = part_ref.shape[0] // n_ens
    for d, part in enumerate(parts):
        at = peer(lax.axis_index("ens"), d, n_ens) * share
        part[...] = part_ref[pl.ds(at, share)]


def sum_members(matrix_ref, control_ref, pert_ref, out_ref):
    members, levels, per_level, _ = control_ref.shape
    group = 2 - members % 2

    def chunk(j, carry):
        at = pl.ds(pl.multiple_of(j * 16, 16), 16)
        total = jnp.zeros((levels * 16, LANES), f32)
        for k in range(0, members, group):
            terms = [three_terms(control_ref[k + i, :, at, :].reshape(levels * 16, LANES)) for i in range(group)]
            local = jnp.dot(matrix_ref[...], jnp.concatenate(terms, axis=1), preferred_element_type=f32)
            for i in range(group):
                pert = pert_ref[k + i, :, at, :].astype(f32).reshape(levels * 16, LANES)
                total = total + pert * local[:, i * LANES : (i + 1) * LANES]
        out_ref[:, at, :] = total.reshape(levels, 16, LANES)
        return carry

    lax.fori_loop(0, per_level // 16, chunk, 0)


def gather_levels(parts, to_ref):
    share = to_ref.shape[0] // len(parts)
    for i, part in enumerate(parts):
        at = peer(lax.axis_index("ens"), (len(parts) - i) % len(parts), len(parts))
        to_ref[pl.ds(at * share, share)] = part[...]


def member_kernel(matrix_ref, control_ref, pert_ref, *refs):
    parts, out_ref, adjoint_ref = refs[:-2], refs[-2], refs[-1]
    group, levels, per_level, _ = out_ref.shape
    first = pl.program_id(0) * group

    @pl.when(pl.program_id(0) == 0)
    def _():
        gather_levels(parts, adjoint_ref)

    def chunk(j, carry):
        at = pl.ds(pl.multiple_of(j * 16, 16), 16)
        adjoint = adjoint_ref[:, at, :]
        terms = [
            three_terms((pert_ref[first + i, :, at, :].astype(f32) * adjoint).reshape(levels * 16, LANES))
            for i in range(group)
        ]
        change = jnp.dot(matrix_ref[...], jnp.concatenate(terms, axis=1), preferred_element_type=f32)
        for i in range(group):
            part = change[:, i * LANES : (i + 1) * LANES].reshape(levels, 16, LANES)
            out_ref[i, :, at, :] = control_ref[first + i, :, at, :] + part
        return carry

    lax.fori_loop(0, per_level // 16, chunk, 0)


def eastern(x):
    lane = lax.broadcasted_iota(jnp.int32, x.shape, 1)
    near = pltpu.roll(x, LANES - 1, 1)
    return jnp.where(lane == LANES - 1, pltpu.roll(near, x.shape[0] - 1, 0), near)


def western(x):
    lane = lax.broadcasted_iota(jnp.int32, x.shape, 1)
    near = pltpu.roll(x, 1, 1)
    return jnp.where(lane == 0, pltpu.roll(near, 1, 0), near)


def rows_of(before_ref, after_ref, own_ref, other_ref, plane, rows):
    at = lax.axis_index("cols")
    count = lax.axis_size("cols")
    core = at % 2
    reads = [pl.ds(r, own_ref.shape[1] // rows, stride=rows) for r in range(rows)]
    out = [jnp.where(at >= 2, before_ref[plane, r, :], f32(0)) for r in reads]
    out += [jnp.where(at >= 1, other_ref[1 - core, plane, r, :], f32(0)) for r in reads]
    out += [own_ref[plane, r, :] for r in reads]
    out += [jnp.where(at < count - 1, other_ref[core, plane, r, :], f32(0)) for r in reads]
    return out + [jnp.where(at < count - 2, after_ref[plane, r, :], f32(0)) for r in reads]


def diffuse_rows(tiles, level, coef_ref, rows):
    field = rows_of(*tiles, level, rows)
    for step in range(NDIFF):
        field = [
            coef_ref[0, i + step] * field[i]
            + coef_ref[1, i + step] * field[i - 1]
            + coef_ref[1, i + step + 1] * field[i + 1]
            + coef_ref[2, i + step] * eastern(field[i])
            + western(coef_ref[2, i + step] * field[i])
            for i in range(1, len(field) - 1)
        ]
    return field


def first_diffusion_kernel(lev_share, rows, *refs):
    before_ref, after_ref, own_ref, other_ref, *sources = refs[:6]
    out_ref, coef_ref, row_ref, lane_ref, *landed, sems = refs[6:]
    copies = [pltpu.make_async_copy(s, t, sems.at[i]) for i, (s, t) in enumerate(zip(sources, landed))]
    for copy in copies:
        copy.start()
    tiles = (before_ref, after_ref, own_ref, other_ref)
    blocks = own_ref.shape[1] // rows
    side = 2
    north = rows_of(*tiles, lev_share, rows)
    east = rows_of(*tiles, lev_share + 1, rows)
    faces = [
        jnp.where(lax.axis_index("cols") == side - i // rows, f32(0), n) if i % rows == 0 and i <= side * rows else n
        for i, n in enumerate(north)
    ]
    for i in range(len(north)):
        inner = 0 < i < len(north) - 1
        coef_ref[0, i] = 1.0 - north[i] - faces[i + 1] - east[i] - western(east[i]) if inner else jnp.zeros_like(east[i])
        coef_ref[1, i] = faces[i]
        coef_ref[2, i] = east[i]

    def body(level, carry):
        final = diffuse_rows(tiles, level, coef_ref, rows)
        for r in range(rows):
            out_ref[level, pl.ds(r, blocks, stride=rows), :] = final[r]
        return carry

    lax.fori_loop(0, lev_share, body, 0)
    for copy in copies:
        copy.wait()
    list_cells(rows, blocks * LANES, *landed, row_ref, lane_ref)


def second_diffusion_kernel(rows, coef_ref, before_ref, after_ref, own_ref, other_ref, out_ref):
    tiles = (before_ref, after_ref, own_ref, other_ref)
    lev_share = out_ref.shape[0]
    blocks = own_ref.shape[1] // rows

    def body(level, carry):
        final = diffuse_rows(tiles, level, coef_ref, rows)
        for r in range(rows):
            out_ref[level, pl.ds(r, blocks, stride=rows), :] = final[r]
        return carry

    lax.fori_loop(0, lev_share, body, 0)


def scatter_kernel(cap_rows, row_ref, lane_ref, slots_ref, *refs):
    sources, out_ref, kept, acc_ref, sems = refs[:3], refs[3], refs[4:7], refs[7], refs[8]
    copies = [pltpu.make_async_copy(s, t, sems.at[i]) for i, (s, t) in enumerate(zip(sources, kept))]
    for copy in copies:
        copy.start()
    own = out_ref.shape[1]
    lists = row_ref.shape[0] // cap_rows
    first = lax.axis_index("ens") * own
    acc_ref[...] = jnp.zeros_like(acc_ref)

    def step(q, carry):
        at = pl.ds(pl.multiple_of(q * cap_rows, cap_rows), cap_rows)
        rows = row_ref[at, :] - first
        lanes = lane_ref[at, :]
        terms = []
        for t in range(2):
            total = functools.reduce(
                jnp.add, [slots_ref[e * lists + q, t] for e in range(slots_ref.shape[0] // lists)]
            )
            terms += [h.astype(f32) for h in halves(total)]
        left, right = [], []
        for c in range(cap_rows):
            left.append(placed_at(rows[c : c + 1, :], own))
            mask = matches(lanes[c : c + 1, :], LANES)
            right.append(
                jnp.concatenate(
                    [
                        jnp.where(mask, spread(t[c : c + 1, :], bf16)[None], bf16(0)).reshape(LANES, LANES)
                        for t in terms
                    ],
                    axis=0,
                )
            )
        acc_ref[...] += product_nt(jnp.concatenate(right, axis=1), jnp.concatenate(left, axis=1))
        return carry

    lax.fori_loop(0, lists, step, 0)
    for t in range(2):
        at = 2 * t * LANES
        out_ref[t] = (acc_ref[at : at + LANES, :] + acc_ref[at + LANES : at + 2 * LANES, :]).T
    for copy in copies:
        copy.wait()


def matrices_kernel(scale, local_ref, root_ref, to_members_ref, to_static_ref):
    to_members_ref[...] = level_product(local_ref[...] * f32(scale), True)
    to_static_ref[...] = level_product(root_ref[...], True)


def static_kernel(matrix_ref, static_ref, *refs):
    parts, (out_ref, smooth_ref) = refs[:-2], refs[-2:]
    levels, per_level, _ = static_ref.shape
    gather_levels(parts, smooth_ref)
    for j in range(0, per_level, 32):
        terms = [three_terms(smooth_ref[:, j + i : j + i + 16, :].reshape(levels * 16, LANES)) for i in (0, 16)]
        change = jnp.dot(matrix_ref[...], jnp.concatenate(terms, axis=1), preferred_element_type=f32)
        for i, part in ((0, change[:, :LANES]), (16, change[:, LANES:])):
            at = slice(j + i, j + i + 16)
            out_ref[:, at, :] = static_ref[:, at, :] + part.reshape(levels, 16, LANES)


def shifted(x):
    count = lax.axis_size("cols")
    return [lax.ppermute(x, "cols", [(i, (i + by) % count) for i in range(count)]) for by in (2, -2)]


def from_peers(x):
    count = lax.axis_size("ens")
    return [lax.ppermute(x, "ens", [(peer(i, d, count), i) for i in range(count)]) for d in range(count - 1, 0, -1)]


def swapped(own, before, after):
    pack = jnp.stack([own, jnp.where(lax.axis_index("cols") % 2 == 1, before, after)])
    return lax.ppermute(pack, "cols", [(i, i ^ 1) for i in range(lax.axis_size("cols"))])


def local(
    static_control,
    ensemble_control,
    perturbations,
    vertical_root,
    vertical_local,
    face_north,
    face_east,
    innovation,
    obs_weight,
    obs_slot,
    send_index,
    send_count,
):
    n_ens = lax.axis_size("ens")
    n_cols = lax.axis_size("cols")
    members, levels, rows, lon = ensemble_control.shape
    per_level = rows * lon // LANES
    cells = levels * per_level
    lev_share = levels // n_ens
    own = lev_share * per_level
    lists, capacity = send_index.shape
    cap_rows = capacity // LANES
    entry_rows = lists * cap_rows
    member_scale = 1.0 / math.sqrt(members * n_ens - 1)

    static = in_hbm(tiled(static_control))
    control = in_hbm(tiled(ensemble_control))
    pert = in_hbm(tiled(perturbations))

    def whole(*shape):
        return pl.BlockSpec(shape, lambda i: (0,) * len(shape))

    obs_rows = obs_slot.shape[0] // LANES
    share_rows = obs_rows // n_ens
    coarse = n_cols * capacity // FINE
    size = levels * 16
    slots, packed, *parts = pl.pallas_call(
        functools.partial(observe_kernel, n_cols, cap_rows, member_scale),
        grid=(1,),
        in_specs=[pl.BlockSpec(memory_space=pl.ANY)] * 10,
        out_specs=[whole(n_ens * n_cols, 2, cap_rows, LANES)] + [VMEM] * (1 + n_ens),
        out_shape=[
            pltpu.HBM((n_ens * n_cols, 2, cap_rows, LANES), f32),
            pltpu.VMEM((lev_share + 2, per_level, LANES), f32),
        ]
        + [pltpu.VMEM((lev_share, per_level, LANES), f32)] * n_ens,
        scratch_shapes=[
            pltpu.VMEM((4 * FINE, coarse), f32),
            pltpu.VMEM((2, coarse, LANES), f32),
            pltpu.VMEM((size, 3 * size), bf16),
            pltpu.VMEM((levels, per_level, LANES), f32),
            pltpu.VMEM((share_rows, LANES), jnp.int32),
            pltpu.VMEM((share_rows, LANES), f32),
            pltpu.VMEM((share_rows, LANES), f32),
            pltpu.VMEM((levels, levels), f32),
            pltpu.VMEM(control.shape, f32),
            pltpu.VMEM(pert.shape, bf16),
            pltpu.SMEM((levels, levels), f32),
            pltpu.VMEM((levels, per_level, LANES), f32),
            pltpu.VMEM((per_level, LANES), f32),
            pltpu.VMEM((per_level, LANES), f32),
            pltpu.SemaphoreType.DMA((10,)),
        ]
        + [pltpu.VMEM((coarse, 8 * LANES), bf16), pltpu.VMEM((4 * FINE, 8 * LANES), bf16)] * 2,
        compiler_params=params(24),
        name="slot_sums_and_members",
    )(
        in_hbm(obs_slot.reshape(obs_rows, LANES)),
        in_hbm(obs_weight.reshape(obs_rows, LANES)),
        in_hbm(innovation.reshape(obs_rows, LANES)),
        in_hbm(vertical_local),
        control,
        pert,
        in_hbm(vertical_root),
        static,
        in_hbm(tiled(face_north)),
        in_hbm(tiled(face_east)),
    )
    slots = lax.all_to_all(slots, ("ens", "cols"), split_axis=0, concat_axis=0, tiled=True)
    before, after = shifted(packed)
    sums = [parts[0]] + [
        lax.ppermute(parts[back(d, n_ens)], "ens", [(peer(i, d, n_ens), i) for i in range(n_ens)])
        for d in range(n_ens - 1, 0, -1)
    ]
    other = swapped(packed, before, after)

    increment, coefs, entry_row, entry_lane = pl.pallas_call(
        functools.partial(first_diffusion_kernel, lev_share, rows),
        in_specs=[VMEM] * 4 + [pl.BlockSpec(memory_space=pl.ANY)] * 2,
        out_specs=[VMEM] * 4,
        out_shape=[
            pltpu.VMEM((lev_share, per_level, LANES), f32),
            pltpu.VMEM((3, 5 * rows, per_level // rows, LANES), f32),
            pltpu.VMEM((entry_rows, LANES), jnp.int32),
            pltpu.VMEM((entry_rows, LANES), jnp.int32),
        ],
        scratch_shapes=[
            pltpu.VMEM((lists, capacity), jnp.int32),
            pltpu.SMEM((lists,), jnp.int32),
            pltpu.SemaphoreType.DMA((2,)),
        ],
        compiler_params=params(8),
        cost_estimate=pl.CostEstimate(flops=1 << 26, bytes_accessed=1 << 22, transcendentals=0),
        name="diffuse_forward",
    )(before, after, packed, other, in_hbm(send_index), in_hbm(send_count))

    increment, coefs, slots = lax.optimization_barrier((increment, coefs, slots))
    slot_sums, static_here, control_here, pert_here = pl.pallas_call(
        functools.partial(scatter_kernel, cap_rows),
        in_specs=[VMEM] * 3 + [pl.BlockSpec(memory_space=pl.ANY)] * 3,
        out_specs=[VMEM] * 4,
        out_shape=[
            pltpu.VMEM((2, own, LANES), f32),
            pltpu.VMEM(static.shape, f32),
            pltpu.VMEM(control.shape, f32),
            pltpu.VMEM(pert.shape, bf16),
        ],
        scratch_shapes=[pltpu.VMEM((4 * LANES, own), f32), pltpu.SemaphoreType.DMA((3,))],
        compiler_params=params(16),
        cost_estimate=pl.CostEstimate(flops=8 * own * LANES * lists * capacity, bytes_accessed=1 << 23, transcendentals=0),
        name="scatter",
    )(entry_row, entry_lane, slots, static, control, pert)

    slot_sums = slot_sums.reshape(2, lev_share, per_level, LANES)
    tile = functools.reduce(jnp.add, sums) + increment
    tile = tile * slot_sums[0] - slot_sums[1]
    tile_before, tile_after = shifted(tile)
    adjoints = [tile] + from_peers(tile)
    tile, vertical_local, vertical_root = lax.optimization_barrier((tile, vertical_local, vertical_root))
    from_local, from_root = pl.pallas_call(
        functools.partial(matrices_kernel, member_scale),
        grid=(1,),
        in_specs=[whole(levels, levels)] * 2,
        out_specs=[VMEM] * 2,
        out_shape=[pltpu.VMEM((size, 3 * size), bf16)] * 2,
        compiler_params=params(8),
        name="level_matrices",
    )(in_hbm(vertical_local), in_hbm(vertical_root))
    tile_before, tile_after, from_local, from_root = lax.optimization_barrier(
        (tile_before, tile_after, from_local, from_root)
    )
    tile_other = swapped(tile, tile_before, tile_after)

    smooth = pl.pallas_call(
        functools.partial(second_diffusion_kernel, rows),
        in_specs=[VMEM] * 5,
        out_specs=VMEM,
        out_shape=pltpu.VMEM((lev_share, per_level, LANES), f32),
        compiler_params=params(8),
        name="diffuse_adjoint",
    )(coefs, tile_before, tile_after, tile, tile_other)
    smooth, from_local = lax.optimization_barrier((smooth, from_local))
    smooths = [smooth] + from_peers(smooth)

    group = 2 - members % 2
    ensemble_grad = pl.pallas_call(
        member_kernel,
        grid=(members // group,),
        in_specs=[VMEM] * (3 + n_ens),
        out_specs=pl.BlockSpec((group, levels, per_level, LANES), lambda k: (k, 0, 0, 0)),
        out_shape=jax.ShapeDtypeStruct((members, levels, per_level, LANES), f32),
        scratch_shapes=[pltpu.VMEM((levels, per_level, LANES), f32)],
        compiler_params=params(16),
        name="members_gradient",
    )(from_local, control_here, pert_here, *adjoints)

    static_grad = pl.pallas_call(
        static_kernel,
        grid=(1,),
        in_specs=[VMEM] * (2 + n_ens),
        out_specs=whole(levels, per_level, LANES),
        out_shape=jax.ShapeDtypeStruct((levels, per_level, LANES), f32),
        scratch_shapes=[pltpu.VMEM((levels, per_level, LANES), f32)],
        compiler_params=params(8),
        name="static_gradient",
    )(from_root, static_here, *smooths)
    return (untiled(static_grad, rows), untiled(ensemble_grad, rows))


def solution(mesh):
    placed = (
        P(None, "cols", None),
        P("ens", None, "cols", None),
        P("ens", None, "cols", None),
        P(),
        P(),
        P("cols", None),
        P("cols", None),
        P("cols"),
        P("cols"),
        P("cols"),
        P("cols", None),
        P("cols"),
    )
    return jax.shard_map(
        local,
        mesh=mesh,
        in_specs=placed,
        out_specs=(P(None, "cols", None), P("ens", None, "cols", None)),
        check_vma=False,
    )
```

```python
import functools
import math

import jax
import jax.numpy as jnp
from jax import lax
from jax.experimental import pallas as pl
from jax.experimental.pallas import tpu as pltpu
from jax.sharding import PartitionSpec as P

NDIFF = 4
LANES = 128
FINE = 64
MIB = 1 << 20

f32 = jnp.float32
bf16 = jnp.bfloat16
SMEM = pl.BlockSpec(memory_space=pltpu.SMEM)
VMEM = pl.BlockSpec(memory_space=pltpu.VMEM)


def tiled(field):
    *lead, rows, lon = field.shape
    field = field.reshape(*lead, rows, lon // LANES, LANES)
    return jnp.swapaxes(field, -3, -2).reshape(*lead, rows * lon // LANES, LANES)


def untiled(field, rows):
    *lead, count, lanes = field.shape
    field = field.reshape(*lead, count // rows, rows, lanes)
    return jnp.swapaxes(field, -3, -2).reshape(*lead, rows, count // rows * lanes)


def params(limit, **more):
    return pltpu.CompilerParams(vmem_limit_bytes=limit * MIB, **more)


def halves(x):
    high = x.astype(bf16)
    return high, (x - high.astype(f32)).astype(bf16)


def in_hbm(x):
    return pltpu.with_memory_space_constraint(x, pltpu.HBM)


def spread(row, dtype):
    return jnp.broadcast_to(row, (16, row.shape[1])).astype(dtype)


def matches(index, count):
    ids = lax.broadcasted_iota(jnp.int32, (count, index.shape[1]), 0).astype(jnp.int16)
    return ids.reshape(count // 16, 16, index.shape[1]) == spread(index, jnp.int16)[None]


def placed_at(index, count, amount=None):
    where = matches(index, count)
    amount = bf16(1) if amount is None else spread(amount, bf16)[None]
    return jnp.where(where, amount, bf16(0)).reshape(count, index.shape[1])


def in_turns(count, build, use, slots):
    build(0, slots[0])

    def step(i, carry):
        use(2 * i, slots[0])
        build(2 * i + 1, slots[1])
        use(2 * i + 1, slots[1])
        build(jnp.minimum(2 * i + 2, count - 1), slots[0])
        return carry

    lax.fori_loop(0, count // 2, step, 0)
    if count % 2:
        use(count - 1, slots[0])


def product_nt(left, right):
    return lax.dot_general(left, right, (((1,), (1,)), ((), ())), preferred_element_type=f32)


def over(x, size):
    if size & (size - 1):
        return lax.div(x, jnp.int32(size)), lax.rem(x, jnp.int32(size))
    return lax.shift_right_logical(x, jnp.int32(size.bit_length() - 1)), x & (size - 1)


def peer(i, d, count):
    return (i + d) % count if count & (count - 1) else i ^ d


def back(d, count):
    return count - d if count & (count - 1) else d


def prepare(root_ref, static_ref, north_ref, east_ref, out_ref):
    levels = static_ref.shape[0]
    lev_share = out_ref.shape[0] - 2
    first = lax.axis_index("ens") * lev_share
    for j in range(lev_share):
        total = root_ref[first + j, 0] * static_ref[0]
        for m in range(1, levels):
            total = total + root_ref[first + j, m] * static_ref[m]
        out_ref[j] = total
    out_ref[lev_share] = north_ref[...]
    out_ref[lev_share + 1] = east_ref[...]


def list_cells(rows, lon, index_ref, count_ref, row_ref, lane_ref):
    lists, capacity = index_ref.shape
    pieces = capacity // LANES
    slot = lax.broadcasted_iota(jnp.int32, (1, capacity), 1)
    for q in range(lists):
        rest, lane = over(index_ref[q : q + 1, :], LANES)
        rest, block = over(rest, lon // LANES)
        level, row = over(rest, rows)
        grid_row = (level * (lon // LANES) + block) * rows + row
        grid_row = jnp.where(slot < count_ref[q], grid_row, -1)
        for c in range(pieces):
            at = q * pieces + c
            row_ref[at : at + 1, :] = grid_row[:, c * LANES : (c + 1) * LANES]
            lane_ref[at : at + 1, :] = lane[:, c * LANES : (c + 1) * LANES]


def level_product(matrix, transpose):
    levels = matrix.shape[0]
    size = levels * 16
    pick = lax.broadcasted_iota(jnp.int32, (size, levels), 0) // 16
    pick = jnp.where(pick == lax.broadcasted_iota(jnp.int32, (size, levels), 1), f32(1), f32(0)).astype(bf16)
    same = (
        lax.broadcasted_iota(jnp.int32, (size, size), 0) % 16 == lax.broadcasted_iota(jnp.int32, (size, size), 1) % 16
    )
    out = []
    for half in halves(matrix):
        if transpose:
            wide = product_nt(pick, half)
        else:
            wide = jnp.dot(pick, half, preferred_element_type=f32)
        wide = product_nt(wide.astype(bf16), pick)
        out.append(jnp.where(same, wide, f32(0)).astype(bf16))
    return jnp.concatenate([out[0], out[0], out[1]], axis=1)


def three_terms(x):
    high, low = halves(x)
    return jnp.concatenate([high, low, high], axis=0)


def observe_kernel(n_cols, cap_rows, scale, *refs):
    n_ens = len(refs) - 32
    sources, (out_ref, packed_ref), parts = refs[:10], refs[10:12], refs[12 : 12 + n_ens]
    refs = refs[12 + n_ens :]
    (acc_ref, fold_ref, matrix_ref, part_ref), landed, sems, slots, sums_ref = (
        refs[:4],
        refs[4:14],
        refs[14],
        (refs[15:17], refs[17:19]),
        refs[19],
    )
    slot_ref, weight_ref, innov_ref, local_ref, control_ref, pert_ref, *static_refs = landed
    coarse = acc_ref.shape[1]
    obs_rows = slot_ref.shape[0]
    group = min(8, obs_rows)
    here = pl.ds(pl.multiple_of(lax.axis_index("ens") * obs_rows, obs_rows), obs_rows)
    copies = [
        pltpu.make_async_copy(s.at[here, :] if i < 3 else s, t, sems.at[i])
        for i, (s, t) in enumerate(zip(sources, landed))
    ]
    for copy in copies:
        copy.start()
    acc_ref[...] = jnp.zeros_like(acc_ref)
    for copy in copies[:3]:
        copy.wait()

    def build(i, to):
        at = pl.ds(pl.multiple_of(i * group, group), group)
        weight = weight_ref[at, :]
        amount = weight * innov_ref[at, :]
        upper, lower = over(slot_ref[at, :], FINE)
        terms = [t.astype(f32) for t in halves(weight) + halves(amount)]
        for r in range(group):
            here = slice(r * LANES, (r + 1) * LANES)
            to[0][:, here] = placed_at(upper[r : r + 1, :], coarse)
            mask = matches(lower[r : r + 1, :], FINE)
            for t, term in enumerate(terms):
                term = spread(term[r : r + 1, :], bf16)[None]
                to[1][t * FINE : (t + 1) * FINE, here] = jnp.where(mask, term, bf16(0)).reshape(FINE, LANES)

    def use(i, of):
        acc_ref[...] += product_nt(of[1][...], of[0][...])

    in_turns(obs_rows // group, build, use, slots)
    for t in range(2):
        at = 2 * t * FINE
        terms = acc_ref[at : at + FINE, :] + acc_ref[at + FINE : at + 2 * FINE, :]
        fold_ref[t] = jnp.concatenate([terms] * (LANES // FINE), axis=0).T
    per_row = LANES // FINE
    lane = lax.broadcasted_iota(jnp.int32, (coarse // per_row, LANES), 1)
    weights, amounts = (
        jnp.where(
            lane < FINE,
            fold_ref[t, pl.ds(0, coarse // per_row, stride=per_row), :],
            fold_ref[t, pl.ds(1, coarse // per_row, stride=per_row), :],
        )
        for t in range(2)
    )
    for p in range(n_cols):
        sums_ref[p, 0] = weights[p * cap_rows : (p + 1) * cap_rows]
        sums_ref[p, 1] = amounts[p * cap_rows : (p + 1) * cap_rows]
    writes = [
        pltpu.make_async_copy(sums_ref, out_ref.at[pl.ds(e * n_cols, n_cols)], sems.at[len(copies) + e])
        for e in range(n_ens)
    ]
    for write in writes:
        write.start()
    for copy in copies[3:]:
        copy.wait()
    prepare(*static_refs, packed_ref)
    matrix_ref[...] = level_product(local_ref[...] * f32(scale), False)
    sum_members(matrix_ref, control_ref, pert_ref, part_ref)
    share = part_ref.shape[0] // n_ens
    for d, part in enumerate(parts):
        at = peer(lax.axis_index("ens"), d, n_ens) * share
        part[...] = part_ref[pl.ds(at, share)]
    for write in writes:
        write.wait()


def sum_members(matrix_ref, control_ref, pert_ref, out_ref):
    members, levels, per_level, _ = control_ref.shape
    group = 2 - members % 2

    def chunk(j, carry):
        at = pl.ds(pl.multiple_of(j * 16, 16), 16)
        total = jnp.zeros((levels * 16, LANES), f32)
        for k in range(0, members, group):
            terms = [three_terms(control_ref[k + i, :, at, :].reshape(levels * 16, LANES)) for i in range(group)]
            local = jnp.dot(matrix_ref[...], jnp.concatenate(terms, axis=1), preferred_element_type=f32)
            for i in range(group):
                pert = pert_ref[k + i, :, at, :].astype(f32).reshape(levels * 16, LANES)
                total = total + pert * local[:, i * LANES : (i + 1) * LANES]
        out_ref[:, at, :] = total.reshape(levels, 16, LANES)
        return carry

    lax.fori_loop(0, per_level // 16, chunk, 0)


def gather_levels(parts, to_ref):
    share = to_ref.shape[0] // len(parts)
    for i, part in enumerate(parts):
        at = peer(lax.axis_index("ens"), (len(parts) - i) % len(parts), len(parts))
        to_ref[pl.ds(at * share, share)] = part[...]


def member_kernel(matrix_ref, control_ref, pert_ref, *refs):
    parts, out_ref, adjoint_ref = refs[:-2], refs[-2], refs[-1]
    group, levels, per_level, _ = out_ref.shape
    first = pl.program_id(0) * group

    @pl.when(pl.program_id(0) == 0)
    def _():
        gather_levels(parts, adjoint_ref)

    def chunk(j, carry):
        at = pl.ds(pl.multiple_of(j * 16, 16), 16)
        adjoint = adjoint_ref[:, at, :]
        terms = [
            three_terms((pert_ref[first + i, :, at, :].astype(f32) * adjoint).reshape(levels * 16, LANES))
            for i in range(group)
        ]
        change = jnp.dot(matrix_ref[...], jnp.concatenate(terms, axis=1), preferred_element_type=f32)
        for i in range(group):
            part = change[:, i * LANES : (i + 1) * LANES].reshape(levels, 16, LANES)
            out_ref[i, :, at, :] = control_ref[first + i, :, at, :] + part
        return carry

    lax.fori_loop(0, per_level // 16, chunk, 0)


def eastern(x):
    lane = lax.broadcasted_iota(jnp.int32, x.shape, 1)
    near = pltpu.roll(x, LANES - 1, 1)
    return jnp.where(lane == LANES - 1, pltpu.roll(near, x.shape[0] - 1, 0), near)


def western(x):
    lane = lax.broadcasted_iota(jnp.int32, x.shape, 1)
    near = pltpu.roll(x, 1, 1)
    return jnp.where(lane == 0, pltpu.roll(near, 1, 0), near)


def rows_of(second_ref, first_ref, own_ref, other_ref, plane, rows):
    at = lax.axis_index("cols")
    count = lax.axis_size("cols")
    core, chip = at % 2, at // 2 % 2
    reads = [pl.ds(r, own_ref.shape[1] // rows, stride=rows) for r in range(rows)]
    first = [first_ref[plane, r, :] for r in reads]
    second = [second_ref[plane, r, :] for r in reads]
    out = [jnp.where(jnp.logical_and(chip == 1, at >= 2), f, f32(0)) for f in first]
    out = [jnp.where(jnp.logical_and(chip == 0, at >= 2), s, o) for s, o in zip(second, out)]
    out += [jnp.where(at >= 1, other_ref[1 - core, plane, r, :], f32(0)) for r in reads]
    out += [own_ref[plane, r, :] for r in reads]
    out += [jnp.where(at < count - 1, other_ref[core, plane, r, :], f32(0)) for r in reads]
    last = [jnp.where(jnp.logical_and(chip == 0, at < count - 2), f, f32(0)) for f in first]
    return out + [jnp.where(jnp.logical_and(chip == 1, at < count - 2), s, o) for s, o in zip(second, last)]


def diffuse_rows(tiles, level, coef_ref, rows):
    field = rows_of(*tiles, level, rows)
    for step in range(NDIFF):
        field = [
            coef_ref[0, i + step] * field[i]
            + coef_ref[1, i + step] * field[i - 1]
            + coef_ref[1, i + step + 1] * field[i + 1]
            + coef_ref[2, i + step] * eastern(field[i])
            + western(coef_ref[2, i + step] * field[i])
            for i in range(1, len(field) - 1)
        ]
    return field


def first_diffusion_kernel(lev_share, rows, *refs):
    second_ref, first_ref, own_ref, other_ref, *sources = refs[:6]
    out_ref, coef_ref, row_ref, lane_ref, *landed, sems = refs[6:]
    copies = [pltpu.make_async_copy(s, t, sems.at[i]) for i, (s, t) in enumerate(zip(sources, landed))]
    for copy in copies:
        copy.start()
    tiles = (second_ref, first_ref, own_ref, other_ref)
    blocks = own_ref.shape[1] // rows
    side = 2
    north = rows_of(*tiles, lev_share, rows)
    east = rows_of(*tiles, lev_share + 1, rows)
    faces = [
        jnp.where(lax.axis_index("cols") == side - i // rows, f32(0), n) if i % rows == 0 and i <= side * rows else n
        for i, n in enumerate(north)
    ]
    for i in range(len(north)):
        inner = 0 < i < len(north) - 1
        coef_ref[0, i] = 1.0 - north[i] - faces[i + 1] - east[i] - western(east[i]) if inner else jnp.zeros_like(east[i])
        coef_ref[1, i] = faces[i]
        coef_ref[2, i] = east[i]

    def body(level, carry):
        final = diffuse_rows(tiles, level, coef_ref, rows)
        for r in range(rows):
            out_ref[level, pl.ds(r, blocks, stride=rows), :] = final[r]
        return carry

    lax.fori_loop(0, lev_share, body, 0)
    for copy in copies:
        copy.wait()
    list_cells(rows, blocks * LANES, *landed, row_ref, lane_ref)


def second_diffusion_kernel(rows, coef_ref, second_ref, first_ref, own_ref, other_ref, out_ref):
    tiles = (second_ref, first_ref, own_ref, other_ref)
    lev_share = out_ref.shape[0]
    blocks = own_ref.shape[1] // rows

    def body(level, carry):
        final = diffuse_rows(tiles, level, coef_ref, rows)
        for r in range(rows):
            out_ref[level, pl.ds(r, blocks, stride=rows), :] = final[r]
        return carry

    lax.fori_loop(0, lev_share, body, 0)


def scatter_kernel(cap_rows, row_ref, lane_ref, slots_ref, *refs):
    sources, out_ref, kept, acc_ref, sems = refs[:3], refs[3], refs[4:7], refs[7], refs[8]
    copies = [pltpu.make_async_copy(s, t, sems.at[i]) for i, (s, t) in enumerate(zip(sources, kept))]
    for copy in copies:
        copy.start()
    own = out_ref.shape[1]
    lists = row_ref.shape[0] // cap_rows
    first = lax.axis_index("ens") * own
    acc_ref[...] = jnp.zeros_like(acc_ref)

    def step(q, carry):
        at = pl.ds(pl.multiple_of(q * cap_rows, cap_rows), cap_rows)
        rows = row_ref[at, :] - first
        lanes = lane_ref[at, :]
        terms = []
        for t in range(2):
            total = functools.reduce(
                jnp.add, [slots_ref[e * lists + q, t] for e in range(slots_ref.shape[0] // lists)]
            )
            terms += [h.astype(f32) for h in halves(total)]
        left, right = [], []
        for c in range(cap_rows):
            left.append(placed_at(rows[c : c + 1, :], own))
            mask = matches(lanes[c : c + 1, :], LANES)
            right.append(
                jnp.concatenate(
                    [
                        jnp.where(mask, spread(t[c : c + 1, :], bf16)[None], bf16(0)).reshape(LANES, LANES)
                        for t in terms
                    ],
                    axis=0,
                )
            )
        acc_ref[...] += product_nt(jnp.concatenate(right, axis=1), jnp.concatenate(left, axis=1))
        return carry

    lax.fori_loop(0, lists, step, 0)
    for t in range(2):
        at = 2 * t * LANES
        out_ref[t] = (acc_ref[at : at + LANES, :] + acc_ref[at + LANES : at + 2 * LANES, :]).T
    for copy in copies:
        copy.wait()


def matrices_kernel(scale, local_ref, root_ref, to_members_ref, to_static_ref):
    to_members_ref[...] = level_product(local_ref[...] * f32(scale), True)
    to_static_ref[...] = level_product(root_ref[...], True)


def static_kernel(matrix_ref, static_ref, *refs):
    parts, (out_ref, smooth_ref) = refs[:-2], refs[-2:]
    levels, per_level, _ = static_ref.shape
    gather_levels(parts, smooth_ref)
    for j in range(0, per_level, 32):
        terms = [three_terms(smooth_ref[:, j + i : j + i + 16, :].reshape(levels * 16, LANES)) for i in (0, 16)]
        change = jnp.dot(matrix_ref[...], jnp.concatenate(terms, axis=1), preferred_element_type=f32)
        for i, part in ((0, change[:, :LANES]), (16, change[:, LANES:])):
            at = slice(j + i, j + i + 16)
            out_ref[:, at, :] = static_ref[:, at, :] + part.reshape(levels, 16, LANES)


def exchanged(x, starts):
    count = lax.axis_size("cols")
    out = []
    for start in starts:
        pairs = []
        for i in range(count):
            chip, core = divmod(i, 2)
            partner = (chip + start ^ 1) - start
            pairs.append((i, 2 * partner + core if 0 <= 2 * partner + core < count else i))
        out.append(lax.ppermute(x, "cols", pairs))
    return out


def from_peers(x):
    count = lax.axis_size("ens")
    return [lax.ppermute(x, "ens", [(peer(i, d, count), i) for i in range(count)]) for d in range(count - 1, 0, -1)]


def swapped(own, first, second):
    at = lax.axis_index("cols")
    pack = jnp.stack([own, jnp.where(at % 2 == at // 2 % 2, first, second)])
    return lax.ppermute(pack, "cols", [(i, i ^ 1) for i in range(lax.axis_size("cols"))])


def local(
    static_control,
    ensemble_control,
    perturbations,
    vertical_root,
    vertical_local,
    face_north,
    face_east,
    innovation,
    obs_weight,
    obs_slot,
    send_index,
    send_count,
):
    n_ens = lax.axis_size("ens")
    n_cols = lax.axis_size("cols")
    members, levels, rows, lon = ensemble_control.shape
    per_level = rows * lon // LANES
    cells = levels * per_level
    lev_share = levels // n_ens
    own = lev_share * per_level
    lists, capacity = send_index.shape
    cap_rows = capacity // LANES
    entry_rows = lists * cap_rows
    member_scale = 1.0 / math.sqrt(members * n_ens - 1)

    static = in_hbm(tiled(static_control))
    control = in_hbm(tiled(ensemble_control))
    pert = in_hbm(tiled(perturbations))

    def whole(*shape):
        return pl.BlockSpec(shape, lambda i: (0,) * len(shape))

    obs_rows = obs_slot.shape[0] // LANES
    share_rows = obs_rows // n_ens
    coarse = n_cols * capacity // FINE
    size = levels * 16
    slots, packed, *parts = pl.pallas_call(
        functools.partial(observe_kernel, n_cols, cap_rows, member_scale),
        grid=(1,),
        in_specs=[pl.BlockSpec(memory_space=pl.ANY)] * 10,
        out_specs=[pl.BlockSpec(memory_space=pl.ANY)] + [VMEM] * (1 + n_ens),
        out_shape=[
            pltpu.HBM((n_ens * n_cols, 2, cap_rows, LANES), f32),
            pltpu.VMEM((lev_share + 2, per_level, LANES), f32),
        ]
        + [pltpu.VMEM((lev_share, per_level, LANES), f32)] * n_ens,
        scratch_shapes=[
            pltpu.VMEM((4 * FINE, coarse), f32),
            pltpu.VMEM((2, coarse, LANES), f32),
            pltpu.VMEM((size, 3 * size), bf16),
            pltpu.VMEM((levels, per_level, LANES), f32),
            pltpu.VMEM((share_rows, LANES), jnp.int32),
            pltpu.VMEM((share_rows, LANES), f32),
            pltpu.VMEM((share_rows, LANES), f32),
            pltpu.VMEM((levels, levels), f32),
            pltpu.VMEM(control.shape, f32),
            pltpu.VMEM(pert.shape, bf16),
            pltpu.SMEM((levels, levels), f32),
            pltpu.VMEM((levels, per_level, LANES), f32),
            pltpu.VMEM((per_level, LANES), f32),
            pltpu.VMEM((per_level, LANES), f32),
            pltpu.SemaphoreType.DMA((10 + n_ens,)),
        ]
        + [pltpu.VMEM((coarse, 8 * LANES), bf16), pltpu.VMEM((4 * FINE, 8 * LANES), bf16)] * 2
        + [pltpu.VMEM((n_cols, 2, cap_rows, LANES), f32)],
        compiler_params=params(24),
        name="slot_sums_and_members",
    )(
        in_hbm(obs_slot.reshape(obs_rows, LANES)),
        in_hbm(obs_weight.reshape(obs_rows, LANES)),
        in_hbm(innovation.reshape(obs_rows, LANES)),
        in_hbm(vertical_local),
        control,
        pert,
        in_hbm(vertical_root),
        static,
        in_hbm(tiled(face_north)),
        in_hbm(tiled(face_east)),
    )
    slots = lax.all_to_all(slots, ("ens", "cols"), split_axis=0, concat_axis=0, tiled=True)
    second, first = exchanged(packed, (1, 0))
    sums = [parts[0]] + [
        lax.ppermute(parts[back(d, n_ens)], "ens", [(peer(i, d, n_ens), i) for i in range(n_ens)])
        for d in range(n_ens - 1, 0, -1)
    ]
    other = swapped(packed, first, second)

    increment, coefs, entry_row, entry_lane = pl.pallas_call(
        functools.partial(first_diffusion_kernel, lev_share, rows),
        in_specs=[VMEM] * 4 + [pl.BlockSpec(memory_space=pl.ANY)] * 2,
        out_specs=[VMEM] * 4,
        out_shape=[
            pltpu.VMEM((lev_share, per_level, LANES), f32),
            pltpu.VMEM((3, 5 * rows, per_level // rows, LANES), f32),
            pltpu.VMEM((entry_rows, LANES), jnp.int32),
            pltpu.VMEM((entry_rows, LANES), jnp.int32),
        ],
        scratch_shapes=[
            pltpu.VMEM((lists, capacity), jnp.int32),
            pltpu.SMEM((lists,), jnp.int32),
            pltpu.SemaphoreType.DMA((2,)),
        ],
        compiler_params=params(8),
        cost_estimate=pl.CostEstimate(flops=1 << 26, bytes_accessed=1 << 22, transcendentals=0),
        name="diffuse_forward",
    )(second, first, packed, other, in_hbm(send_index), in_hbm(send_count))

    increment, coefs, slots = lax.optimization_barrier((increment, coefs, slots))
    slot_sums, static_here, control_here, pert_here = pl.pallas_call(
        functools.partial(scatter_kernel, cap_rows),
        in_specs=[VMEM] * 3 + [pl.BlockSpec(memory_space=pl.ANY)] * 3,
        out_specs=[VMEM] * 4,
        out_shape=[
            pltpu.VMEM((2, own, LANES), f32),
            pltpu.VMEM(static.shape, f32),
            pltpu.VMEM(control.shape, f32),
            pltpu.VMEM(pert.shape, bf16),
        ],
        scratch_shapes=[pltpu.VMEM((4 * LANES, own), f32), pltpu.SemaphoreType.DMA((3,))],
        compiler_params=params(16),
        cost_estimate=pl.CostEstimate(flops=8 * own * LANES * lists * capacity, bytes_accessed=1 << 23, transcendentals=0),
        name="scatter",
    )(entry_row, entry_lane, slots, static, control, pert)

    slot_sums = slot_sums.reshape(2, lev_share, per_level, LANES)
    tile = functools.reduce(jnp.add, sums) + increment
    tile = tile * slot_sums[0] - slot_sums[1]
    tile_first, tile_second = exchanged(tile, (0, 1))
    adjoints = [tile] + from_peers(tile)
    tile, vertical_local, vertical_root = lax.optimization_barrier((tile, vertical_local, vertical_root))
    from_local, from_root = pl.pallas_call(
        functools.partial(matrices_kernel, member_scale),
        grid=(1,),
        in_specs=[whole(levels, levels)] * 2,
        out_specs=[VMEM] * 2,
        out_shape=[pltpu.VMEM((size, 3 * size), bf16)] * 2,
        compiler_params=params(8),
        name="level_matrices",
    )(in_hbm(vertical_local), in_hbm(vertical_root))
    tile_first, tile_second, from_local, from_root = lax.optimization_barrier(
        (tile_first, tile_second, from_local, from_root)
    )
    tile_other = swapped(tile, tile_first, tile_second)

    smooth = pl.pallas_call(
        functools.partial(second_diffusion_kernel, rows),
        in_specs=[VMEM] * 5,
        out_specs=VMEM,
        out_shape=pltpu.VMEM((lev_share, per_level, LANES), f32),
        compiler_params=params(8),
        name="diffuse_adjoint",
    )(coefs, tile_second, tile_first, tile, tile_other)
    smooth, from_local = lax.optimization_barrier((smooth, from_local))
    smooths = [smooth] + from_peers(smooth)

    group = 2 - members % 2
    ensemble_grad = pl.pallas_call(
        member_kernel,
        grid=(members // group,),
        in_specs=[VMEM] * (3 + n_ens),
        out_specs=pl.BlockSpec((group, levels, per_level, LANES), lambda k: (k, 0, 0, 0)),
        out_shape=jax.ShapeDtypeStruct((members, levels, per_level, LANES), f32),
        scratch_shapes=[pltpu.VMEM((levels, per_level, LANES), f32)],
        compiler_params=params(16),
        name="members_gradient",
    )(from_local, control_here, pert_here, *adjoints)

    static_grad = pl.pallas_call(
        static_kernel,
        grid=(1,),
        in_specs=[VMEM] * (2 + n_ens),
        out_specs=whole(levels, per_level, LANES),
        out_shape=jax.ShapeDtypeStruct((levels, per_level, LANES), f32),
        scratch_shapes=[pltpu.VMEM((levels, per_level, LANES), f32)],
        compiler_params=params(8),
        name="static_gradient",
    )(from_root, static_here, *smooths)
    return (untiled(static_grad, rows), untiled(ensemble_grad, rows))


def solution(mesh):
    placed = (
        P(None, "cols", None),
        P("ens", None, "cols", None),
        P("ens", None, "cols", None),
        P(),
        P(),
        P("cols", None),
        P("cols", None),
        P("cols"),
        P("cols"),
        P("cols"),
        P("cols", None),
        P("cols"),
    )
    return jax.shard_map(
        local,
        mesh=mesh,
        in_specs=placed,
        out_specs=(P(None, "cols", None), P("ens", None, "cols", None)),
        check_vma=False,
    )
```

```python
import functools
import math

import jax
import jax.numpy as jnp
from jax import lax
from jax.experimental import pallas as pl
from jax.experimental.pallas import tpu as pltpu
from jax.sharding import PartitionSpec as P

NDIFF = 4
LANES = 128
FINE = 64
MIB = 1 << 20

f32 = jnp.float32
bf16 = jnp.bfloat16
SMEM = pl.BlockSpec(memory_space=pltpu.SMEM)
VMEM = pl.BlockSpec(memory_space=pltpu.VMEM)


def tiled(field):
    *lead, rows, lon = field.shape
    field = field.reshape(*lead, rows, lon // LANES, LANES)
    return jnp.swapaxes(field, -3, -2).reshape(*lead, rows * lon // LANES, LANES)


def untiled(field, rows):
    *lead, count, lanes = field.shape
    field = field.reshape(*lead, count // rows, rows, lanes)
    return jnp.swapaxes(field, -3, -2).reshape(*lead, rows, count // rows * lanes)


def params(limit, **more):
    return pltpu.CompilerParams(vmem_limit_bytes=limit * MIB, **more)


def halves(x):
    high = x.astype(bf16)
    return high, (x - high.astype(f32)).astype(bf16)


def in_hbm(x):
    return pltpu.with_memory_space_constraint(x, pltpu.HBM)


def spread(row, dtype):
    return jnp.broadcast_to(row, (16, row.shape[1])).astype(dtype)


def matches(index, count):
    ids = lax.broadcasted_iota(jnp.int32, (count, index.shape[1]), 0).astype(jnp.int16)
    return ids.reshape(count // 16, 16, index.shape[1]) == spread(index, jnp.int16)[None]


def placed_at(index, count, amount=None):
    where = matches(index, count)
    amount = bf16(1) if amount is None else spread(amount, bf16)[None]
    return jnp.where(where, amount, bf16(0)).reshape(count, index.shape[1])


def in_turns(count, build, use, slots, between, beside, chunks):
    build(0, slots[0])

    def step(i, carry):
        use(2 * i, slots[0])
        build(2 * i + 1, slots[1])
        use(2 * i + 1, slots[1])
        build(jnp.minimum(2 * i + 2, count - 1), slots[0])
        return carry

    def last_step(i, carry):
        beside(i - first)
        return step(i, carry)

    first = max(count // 2 - chunks, 0)
    lax.fori_loop(0, first, step, 0)
    between()
    lax.fori_loop(first, count // 2, last_step, 0)
    if count % 2:
        use(count - 1, slots[0])
    for j in range(count // 2 - first, chunks):
        beside(j)


def product_nt(left, right):
    return lax.dot_general(left, right, (((1,), (1,)), ((), ())), preferred_element_type=f32)


def over(x, size):
    if size & (size - 1):
        return lax.div(x, jnp.int32(size)), lax.rem(x, jnp.int32(size))
    return lax.shift_right_logical(x, jnp.int32(size.bit_length() - 1)), x & (size - 1)


def peer(i, d, count):
    return (i + d) % count if count & (count - 1) else i ^ d


def back(d, count):
    return count - d if count & (count - 1) else d


def prepare(root_ref, static_ref, north_ref, east_ref, out_ref):
    levels = static_ref.shape[0]
    lev_share = out_ref.shape[0] - 2
    first = lax.axis_index("ens") * lev_share
    for j in range(lev_share):
        total = root_ref[first + j, 0] * static_ref[0]
        for m in range(1, levels):
            total = total + root_ref[first + j, m] * static_ref[m]
        out_ref[j] = total
    out_ref[lev_share] = north_ref[...]
    out_ref[lev_share + 1] = east_ref[...]


def list_cells(rows, lon, index_ref, count_ref, row_ref, lane_ref):
    lists, capacity = index_ref.shape
    pieces = capacity // LANES
    slot = lax.broadcasted_iota(jnp.int32, (1, capacity), 1)
    for q in range(lists):
        rest, lane = over(index_ref[q : q + 1, :], LANES)
        rest, block = over(rest, lon // LANES)
        level, row = over(rest, rows)
        grid_row = (level * (lon // LANES) + block) * rows + row
        grid_row = jnp.where(slot < count_ref[q], grid_row, -1)
        for c in range(pieces):
            at = q * pieces + c
            row_ref[at : at + 1, :] = grid_row[:, c * LANES : (c + 1) * LANES]
            lane_ref[at : at + 1, :] = lane[:, c * LANES : (c + 1) * LANES]


def level_product(matrix, transpose):
    levels = matrix.shape[0]
    size = levels * 16
    pick = lax.broadcasted_iota(jnp.int32, (size, levels), 0) // 16
    pick = jnp.where(pick == lax.broadcasted_iota(jnp.int32, (size, levels), 1), f32(1), f32(0)).astype(bf16)
    same = (
        lax.broadcasted_iota(jnp.int32, (size, size), 0) % 16 == lax.broadcasted_iota(jnp.int32, (size, size), 1) % 16
    )
    out = []
    for half in halves(matrix):
        if transpose:
            wide = product_nt(pick, half)
        else:
            wide = jnp.dot(pick, half, preferred_element_type=f32)
        wide = product_nt(wide.astype(bf16), pick)
        out.append(jnp.where(same, wide, f32(0)).astype(bf16))
    return jnp.concatenate([out[0], out[0], out[1]], axis=1)


def three_terms(x):
    high, low = halves(x)
    return jnp.concatenate([high, low, high], axis=0)


def observe_kernel(n_cols, cap_rows, scale, *refs):
    n_ens = len(refs) - 32
    sources, (out_ref, packed_ref), parts = refs[:10], refs[10:12], refs[12 : 12 + n_ens]
    refs = refs[12 + n_ens :]
    (acc_ref, fold_ref, matrix_ref, part_ref), landed, sems, slots, sums_ref = (
        refs[:4],
        refs[4:14],
        refs[14],
        (refs[15:17], refs[17:19]),
        refs[19],
    )
    slot_ref, weight_ref, innov_ref, local_ref, control_ref, pert_ref, *static_refs = landed
    coarse = acc_ref.shape[1]
    obs_rows = slot_ref.shape[0]
    group = min(8, obs_rows)
    here = pl.ds(pl.multiple_of(lax.axis_index("ens") * obs_rows, obs_rows), obs_rows)
    copies = [
        pltpu.make_async_copy(s.at[here, :] if i < 3 else s, t, sems.at[i])
        for i, (s, t) in enumerate(zip(sources, landed))
    ]
    for copy in copies:
        copy.start()
    acc_ref[...] = jnp.zeros_like(acc_ref)
    for copy in copies[:3]:
        copy.wait()

    def build(i, to):
        at = pl.ds(pl.multiple_of(i * group, group), group)
        weight = weight_ref[at, :]
        amount = weight * innov_ref[at, :]
        upper, lower = over(slot_ref[at, :], FINE)
        terms = [t.astype(f32) for t in halves(weight) + halves(amount)]
        for r in range(group):
            here = slice(r * LANES, (r + 1) * LANES)
            to[0][:, here] = placed_at(upper[r : r + 1, :], coarse)
            mask = matches(lower[r : r + 1, :], FINE)
            for t, term in enumerate(terms):
                term = spread(term[r : r + 1, :], bf16)[None]
                to[1][t * FINE : (t + 1) * FINE, here] = jnp.where(mask, term, bf16(0)).reshape(FINE, LANES)

    def use(i, of):
        acc_ref[...] += product_nt(of[1][...], of[0][...])

    def fields():
        for copy in copies[3:]:
            copy.wait()
        matrix_ref[...] = level_product(local_ref[...] * f32(scale), False)

    def members(j):
        sum_members(j, matrix_ref, control_ref, pert_ref, part_ref)

    in_turns(obs_rows // group, build, use, slots, fields, members, part_ref.shape[1] // 16)
    for t in range(2):
        at = 2 * t * FINE
        terms = acc_ref[at : at + FINE, :] + acc_ref[at + FINE : at + 2 * FINE, :]
        fold_ref[t] = jnp.concatenate([terms] * (LANES // FINE), axis=0).T
    per_row = LANES // FINE
    lane = lax.broadcasted_iota(jnp.int32, (coarse // per_row, LANES), 1)
    weights, amounts = (
        jnp.where(
            lane < FINE,
            fold_ref[t, pl.ds(0, coarse // per_row, stride=per_row), :],
            fold_ref[t, pl.ds(1, coarse // per_row, stride=per_row), :],
        )
        for t in range(2)
    )
    for p in range(n_cols):
        sums_ref[p, 0] = weights[p * cap_rows : (p + 1) * cap_rows]
        sums_ref[p, 1] = amounts[p * cap_rows : (p + 1) * cap_rows]
    writes = [
        pltpu.make_async_copy(sums_ref, out_ref.at[pl.ds(e * n_cols, n_cols)], sems.at[len(copies) + e])
        for e in range(n_ens)
    ]
    for write in writes:
        write.start()
    prepare(*static_refs, packed_ref)
    share = part_ref.shape[0] // n_ens
    for d, part in enumerate(parts):
        at = peer(lax.axis_index("ens"), d, n_ens) * share
        part[...] = part_ref[pl.ds(at, share)]
    for write in writes:
        write.wait()


def sum_members(j, matrix_ref, control_ref, pert_ref, out_ref):
    members, levels, _, _ = control_ref.shape
    group = 2 - members % 2
    at = pl.ds(pl.multiple_of(j * 16, 16), 16)
    total = jnp.zeros((levels * 16, LANES), f32)
    for k in range(0, members, group):
        terms = [three_terms(control_ref[k + i, :, at, :].reshape(levels * 16, LANES)) for i in range(group)]
        local = jnp.dot(matrix_ref[...], jnp.concatenate(terms, axis=1), preferred_element_type=f32)
        for i in range(group):
            pert = pert_ref[k + i, :, at, :].astype(f32).reshape(levels * 16, LANES)
            total = total + pert * local[:, i * LANES : (i + 1) * LANES]
    out_ref[:, at, :] = total.reshape(levels, 16, LANES)


def gather_levels(parts, to_ref):
    share = to_ref.shape[0] // len(parts)
    for i, part in enumerate(parts):
        at = peer(lax.axis_index("ens"), (len(parts) - i) % len(parts), len(parts))
        to_ref[pl.ds(at * share, share)] = part[...]


def member_kernel(matrix_ref, control_ref, pert_ref, *refs):
    parts, out_ref, adjoint_ref = refs[:-2], refs[-2], refs[-1]
    group, levels, per_level, _ = out_ref.shape
    first = pl.program_id(0) * group

    @pl.when(pl.program_id(0) == 0)
    def _():
        gather_levels(parts, adjoint_ref)

    def chunk(j, carry):
        at = pl.ds(pl.multiple_of(j * 16, 16), 16)
        adjoint = adjoint_ref[:, at, :]
        terms = [
            three_terms((pert_ref[first + i, :, at, :].astype(f32) * adjoint).reshape(levels * 16, LANES))
            for i in range(group)
        ]
        change = jnp.dot(matrix_ref[...], jnp.concatenate(terms, axis=1), preferred_element_type=f32)
        for i in range(group):
            part = change[:, i * LANES : (i + 1) * LANES].reshape(levels, 16, LANES)
            out_ref[i, :, at, :] = control_ref[first + i, :, at, :] + part
        return carry

    lax.fori_loop(0, per_level // 16, chunk, 0)


def eastern(x):
    lane = lax.broadcasted_iota(jnp.int32, x.shape, 1)
    near = pltpu.roll(x, LANES - 1, 1)
    return jnp.where(lane == LANES - 1, pltpu.roll(near, x.shape[0] - 1, 0), near)


def western(x):
    lane = lax.broadcasted_iota(jnp.int32, x.shape, 1)
    near = pltpu.roll(x, 1, 1)
    return jnp.where(lane == 0, pltpu.roll(near, 1, 0), near)


def rows_of(second_ref, first_ref, own_ref, other_ref, plane, rows):
    at = lax.axis_index("cols")
    count = lax.axis_size("cols")
    core, chip = at % 2, at // 2 % 2
    reads = [pl.ds(r, own_ref.shape[1] // rows, stride=rows) for r in range(rows)]
    first = [first_ref[plane, r, :] for r in reads]
    second = [second_ref[plane, r, :] for r in reads]
    out = [jnp.where(jnp.logical_and(chip == 1, at >= 2), f, f32(0)) for f in first]
    out = [jnp.where(jnp.logical_and(chip == 0, at >= 2), s, o) for s, o in zip(second, out)]
    out += [jnp.where(at >= 1, other_ref[1 - core, plane, r, :], f32(0)) for r in reads]
    out += [own_ref[plane, r, :] for r in reads]
    out += [jnp.where(at < count - 1, other_ref[core, plane, r, :], f32(0)) for r in reads]
    last = [jnp.where(jnp.logical_and(chip == 0, at < count - 2), f, f32(0)) for f in first]
    return out + [jnp.where(jnp.logical_and(chip == 1, at < count - 2), s, o) for s, o in zip(second, last)]


def diffuse_rows(tiles, level, coef_ref, rows):
    field = rows_of(*tiles, level, rows)
    for step in range(NDIFF):
        field = [
            coef_ref[0, i + step] * field[i]
            + coef_ref[1, i + step] * field[i - 1]
            + coef_ref[1, i + step + 1] * field[i + 1]
            + coef_ref[2, i + step] * eastern(field[i])
            + western(coef_ref[2, i + step] * field[i])
            for i in range(1, len(field) - 1)
        ]
    return field


def first_diffusion_kernel(lev_share, rows, *refs):
    second_ref, first_ref, own_ref, other_ref, *sources = refs[:6]
    out_ref, coef_ref, row_ref, lane_ref, *landed, sems = refs[6:]
    copies = [pltpu.make_async_copy(s, t, sems.at[i]) for i, (s, t) in enumerate(zip(sources, landed))]
    for copy in copies:
        copy.start()
    tiles = (second_ref, first_ref, own_ref, other_ref)
    blocks = own_ref.shape[1] // rows
    side = 2
    north = rows_of(*tiles, lev_share, rows)
    east = rows_of(*tiles, lev_share + 1, rows)
    faces = [
        jnp.where(lax.axis_index("cols") == side - i // rows, f32(0), n) if i % rows == 0 and i <= side * rows else n
        for i, n in enumerate(north)
    ]
    for i in range(len(north)):
        inner = 0 < i < len(north) - 1
        coef_ref[0, i] = 1.0 - north[i] - faces[i + 1] - east[i] - western(east[i]) if inner else jnp.zeros_like(east[i])
        coef_ref[1, i] = faces[i]
        coef_ref[2, i] = east[i]

    def body(level, carry):
        final = diffuse_rows(tiles, level, coef_ref, rows)
        for r in range(rows):
            out_ref[level, pl.ds(r, blocks, stride=rows), :] = final[r]
        return carry

    lax.fori_loop(0, lev_share, body, 0)
    for copy in copies:
        copy.wait()
    list_cells(rows, blocks * LANES, *landed, row_ref, lane_ref)


def second_diffusion_kernel(rows, coef_ref, second_ref, first_ref, own_ref, other_ref, out_ref):
    tiles = (second_ref, first_ref, own_ref, other_ref)
    lev_share = out_ref.shape[0]
    blocks = own_ref.shape[1] // rows

    def body(level, carry):
        final = diffuse_rows(tiles, level, coef_ref, rows)
        for r in range(rows):
            out_ref[level, pl.ds(r, blocks, stride=rows), :] = final[r]
        return carry

    lax.fori_loop(0, lev_share, body, 0)


def scatter_kernel(cap_rows, row_ref, lane_ref, slots_ref, *refs):
    sources, out_ref, kept, acc_ref, sems = refs[:3], refs[3], refs[4:7], refs[7], refs[8]
    copies = [pltpu.make_async_copy(s, t, sems.at[i]) for i, (s, t) in enumerate(zip(sources, kept))]
    for copy in copies:
        copy.start()
    own = out_ref.shape[1]
    lists = row_ref.shape[0] // cap_rows
    first = lax.axis_index("ens") * own
    acc_ref[...] = jnp.zeros_like(acc_ref)

    def step(q, carry):
        at = pl.ds(pl.multiple_of(q * cap_rows, cap_rows), cap_rows)
        rows = row_ref[at, :] - first
        lanes = lane_ref[at, :]
        terms = []
        for t in range(2):
            total = functools.reduce(
                jnp.add, [slots_ref[e * lists + q, t] for e in range(slots_ref.shape[0] // lists)]
            )
            terms += [h.astype(f32) for h in halves(total)]
        left, right = [], []
        for c in range(cap_rows):
            left.append(placed_at(rows[c : c + 1, :], own))
            mask = matches(lanes[c : c + 1, :], LANES)
            right.append(
                jnp.concatenate(
                    [
                        jnp.where(mask, spread(t[c : c + 1, :], bf16)[None], bf16(0)).reshape(LANES, LANES)
                        for t in terms
                    ],
                    axis=0,
                )
            )
        acc_ref[...] += product_nt(jnp.concatenate(right, axis=1), jnp.concatenate(left, axis=1))
        return carry

    lax.fori_loop(0, lists, step, 0)
    for t in range(2):
        at = 2 * t * LANES
        out_ref[t] = (acc_ref[at : at + LANES, :] + acc_ref[at + LANES : at + 2 * LANES, :]).T
    for copy in copies:
        copy.wait()


def matrices_kernel(scale, local_ref, root_ref, to_members_ref, to_static_ref):
    to_members_ref[...] = level_product(local_ref[...] * f32(scale), True)
    to_static_ref[...] = level_product(root_ref[...], True)


def static_kernel(matrix_ref, static_ref, *refs):
    parts, (out_ref, smooth_ref) = refs[:-2], refs[-2:]
    levels, per_level, _ = static_ref.shape
    gather_levels(parts, smooth_ref)
    for j in range(0, per_level, 32):
        terms = [three_terms(smooth_ref[:, j + i : j + i + 16, :].reshape(levels * 16, LANES)) for i in (0, 16)]
        change = jnp.dot(matrix_ref[...], jnp.concatenate(terms, axis=1), preferred_element_type=f32)
        for i, part in ((0, change[:, :LANES]), (16, change[:, LANES:])):
            at = slice(j + i, j + i + 16)
            out_ref[:, at, :] = static_ref[:, at, :] + part.reshape(levels, 16, LANES)


def exchanged(x, starts):
    count = lax.axis_size("cols")
    out = []
    for start in starts:
        pairs = []
        for i in range(count):
            chip, core = divmod(i, 2)
            partner = (chip + start ^ 1) - start
            pairs.append((i, 2 * partner + core if 0 <= 2 * partner + core < count else i))
        out.append(lax.ppermute(x, "cols", pairs))
    return out


def from_peers(x):
    count = lax.axis_size("ens")
    return [lax.ppermute(x, "ens", [(peer(i, d, count), i) for i in range(count)]) for d in range(count - 1, 0, -1)]


def swapped(own, first, second):
    at = lax.axis_index("cols")
    pack = jnp.stack([own, jnp.where(at % 2 == at // 2 % 2, first, second)])
    return lax.ppermute(pack, "cols", [(i, i ^ 1) for i in range(lax.axis_size("cols"))])


def local(
    static_control,
    ensemble_control,
    perturbations,
    vertical_root,
    vertical_local,
    face_north,
    face_east,
    innovation,
    obs_weight,
    obs_slot,
    send_index,
    send_count,
):
    n_ens = lax.axis_size("ens")
    n_cols = lax.axis_size("cols")
    members, levels, rows, lon = ensemble_control.shape
    per_level = rows * lon // LANES
    cells = levels * per_level
    lev_share = levels // n_ens
    own = lev_share * per_level
    lists, capacity = send_index.shape
    cap_rows = capacity // LANES
    entry_rows = lists * cap_rows
    member_scale = 1.0 / math.sqrt(members * n_ens - 1)

    static = in_hbm(tiled(static_control))
    control = in_hbm(tiled(ensemble_control))
    pert = in_hbm(tiled(perturbations))

    def whole(*shape):
        return pl.BlockSpec(shape, lambda i: (0,) * len(shape))

    obs_rows = obs_slot.shape[0] // LANES
    share_rows = obs_rows // n_ens
    coarse = n_cols * capacity // FINE
    size = levels * 16
    slots, packed, *parts = pl.pallas_call(
        functools.partial(observe_kernel, n_cols, cap_rows, member_scale),
        grid=(1,),
        in_specs=[pl.BlockSpec(memory_space=pl.ANY)] * 10,
        out_specs=[pl.BlockSpec(memory_space=pl.ANY)] + [VMEM] * (1 + n_ens),
        out_shape=[
            pltpu.HBM((n_ens * n_cols, 2, cap_rows, LANES), f32),
            pltpu.VMEM((lev_share + 2, per_level, LANES), f32),
        ]
        + [pltpu.VMEM((lev_share, per_level, LANES), f32)] * n_ens,
        scratch_shapes=[
            pltpu.VMEM((4 * FINE, coarse), f32),
            pltpu.VMEM((2, coarse, LANES), f32),
            pltpu.VMEM((size, 3 * size), bf16),
            pltpu.VMEM((levels, per_level, LANES), f32),
            pltpu.VMEM((share_rows, LANES), jnp.int32),
            pltpu.VMEM((share_rows, LANES), f32),
            pltpu.VMEM((share_rows, LANES), f32),
            pltpu.VMEM((levels, levels), f32),
            pltpu.VMEM(control.shape, f32),
            pltpu.VMEM(pert.shape, bf16),
            pltpu.SMEM((levels, levels), f32),
            pltpu.VMEM((levels, per_level, LANES), f32),
            pltpu.VMEM((per_level, LANES), f32),
            pltpu.VMEM((per_level, LANES), f32),
            pltpu.SemaphoreType.DMA((10 + n_ens,)),
        ]
        + [pltpu.VMEM((coarse, 8 * LANES), bf16), pltpu.VMEM((4 * FINE, 8 * LANES), bf16)] * 2
        + [pltpu.VMEM((n_cols, 2, cap_rows, LANES), f32)],
        compiler_params=params(24),
        name="slot_sums_and_members",
    )(
        in_hbm(obs_slot.reshape(obs_rows, LANES)),
        in_hbm(obs_weight.reshape(obs_rows, LANES)),
        in_hbm(innovation.reshape(obs_rows, LANES)),
        in_hbm(vertical_local),
        control,
        pert,
        in_hbm(vertical_root),
        static,
        in_hbm(tiled(face_north)),
        in_hbm(tiled(face_east)),
    )
    slots = lax.all_to_all(slots, ("ens", "cols"), split_axis=0, concat_axis=0, tiled=True)
    second, first = exchanged(packed, (1, 0))
    sums = [parts[0]] + [
        lax.ppermute(parts[back(d, n_ens)], "ens", [(peer(i, d, n_ens), i) for i in range(n_ens)])
        for d in range(n_ens - 1, 0, -1)
    ]
    other = swapped(packed, first, second)

    increment, coefs, entry_row, entry_lane = pl.pallas_call(
        functools.partial(first_diffusion_kernel, lev_share, rows),
        in_specs=[VMEM] * 4 + [pl.BlockSpec(memory_space=pl.ANY)] * 2,
        out_specs=[VMEM] * 4,
        out_shape=[
            pltpu.VMEM((lev_share, per_level, LANES), f32),
            pltpu.VMEM((3, 5 * rows, per_level // rows, LANES), f32),
            pltpu.VMEM((entry_rows, LANES), jnp.int32),
            pltpu.VMEM((entry_rows, LANES), jnp.int32),
        ],
        scratch_shapes=[
            pltpu.VMEM((lists, capacity), jnp.int32),
            pltpu.SMEM((lists,), jnp.int32),
            pltpu.SemaphoreType.DMA((2,)),
        ],
        compiler_params=params(8),
        cost_estimate=pl.CostEstimate(flops=1 << 26, bytes_accessed=1 << 22, transcendentals=0),
        name="diffuse_forward",
    )(second, first, packed, other, in_hbm(send_index), in_hbm(send_count))

    increment, coefs, slots = lax.optimization_barrier((increment, coefs, slots))
    slot_sums, static_here, control_here, pert_here = pl.pallas_call(
        functools.partial(scatter_kernel, cap_rows),
        in_specs=[VMEM] * 3 + [pl.BlockSpec(memory_space=pl.ANY)] * 3,
        out_specs=[VMEM] * 4,
        out_shape=[
            pltpu.VMEM((2, own, LANES), f32),
            pltpu.VMEM(static.shape, f32),
            pltpu.VMEM(control.shape, f32),
            pltpu.VMEM(pert.shape, bf16),
        ],
        scratch_shapes=[pltpu.VMEM((4 * LANES, own), f32), pltpu.SemaphoreType.DMA((3,))],
        compiler_params=params(16),
        cost_estimate=pl.CostEstimate(flops=8 * own * LANES * lists * capacity, bytes_accessed=1 << 23, transcendentals=0),
        name="scatter",
    )(entry_row, entry_lane, slots, static, control, pert)

    slot_sums = slot_sums.reshape(2, lev_share, per_level, LANES)
    tile = functools.reduce(jnp.add, sums) + increment
    tile = tile * slot_sums[0] - slot_sums[1]
    tile_first, tile_second = exchanged(tile, (0, 1))
    adjoints = [tile] + from_peers(tile)
    tile, vertical_local, vertical_root = lax.optimization_barrier((tile, vertical_local, vertical_root))
    from_local, from_root = pl.pallas_call(
        functools.partial(matrices_kernel, member_scale),
        grid=(1,),
        in_specs=[whole(levels, levels)] * 2,
        out_specs=[VMEM] * 2,
        out_shape=[pltpu.VMEM((size, 3 * size), bf16)] * 2,
        compiler_params=params(8),
        name="level_matrices",
    )(in_hbm(vertical_local), in_hbm(vertical_root))
    tile_first, tile_second, from_local, from_root = lax.optimization_barrier(
        (tile_first, tile_second, from_local, from_root)
    )
    tile_other = swapped(tile, tile_first, tile_second)

    smooth = pl.pallas_call(
        functools.partial(second_diffusion_kernel, rows),
        in_specs=[VMEM] * 5,
        out_specs=VMEM,
        out_shape=pltpu.VMEM((lev_share, per_level, LANES), f32),
        compiler_params=params(8),
        name="diffuse_adjoint",
    )(coefs, tile_second, tile_first, tile, tile_other)
    smooth, from_local = lax.optimization_barrier((smooth, from_local))
    smooths = [smooth] + from_peers(smooth)

    group = 2 - members % 2
    ensemble_grad = pl.pallas_call(
        member_kernel,
        grid=(members // group,),
        in_specs=[VMEM] * (3 + n_ens),
        out_specs=pl.BlockSpec((group, levels, per_level, LANES), lambda k: (k, 0, 0, 0)),
        out_shape=jax.ShapeDtypeStruct((members, levels, per_level, LANES), f32),
        scratch_shapes=[pltpu.VMEM((levels, per_level, LANES), f32)],
        compiler_params=params(16),
        name="members_gradient",
    )(from_local, control_here, pert_here, *adjoints)

    static_grad = pl.pallas_call(
        static_kernel,
        grid=(1,),
        in_specs=[VMEM] * (2 + n_ens),
        out_specs=whole(levels, per_level, LANES),
        out_shape=jax.ShapeDtypeStruct((levels, per_level, LANES), f32),
        scratch_shapes=[pltpu.VMEM((levels, per_level, LANES), f32)],
        compiler_params=params(8),
        name="static_gradient",
    )(from_root, static_here, *smooths)
    return (untiled(static_grad, rows), untiled(ensemble_grad, rows))


def solution(mesh):
    placed = (
        P(None, "cols", None),
        P("ens", None, "cols", None),
        P("ens", None, "cols", None),
        P(),
        P(),
        P("cols", None),
        P("cols", None),
        P("cols"),
        P("cols"),
        P("cols"),
        P("cols", None),
        P("cols"),
    )
    return jax.shard_map(
        local,
        mesh=mesh,
        in_specs=placed,
        out_specs=(P(None, "cols", None), P("ens", None, "cols", None)),
        check_vma=False,
    )
```

```python
import functools
import math

import jax
import jax.numpy as jnp
from jax import lax
from jax.experimental import pallas as pl
from jax.experimental.pallas import tpu as pltpu
from jax.sharding import PartitionSpec as P

NDIFF = 4
LANES = 128
FINE = 64
MIB = 1 << 20

f32 = jnp.float32
bf16 = jnp.bfloat16
SMEM = pl.BlockSpec(memory_space=pltpu.SMEM)
VMEM = pl.BlockSpec(memory_space=pltpu.VMEM)


def tiled(field):
    *lead, rows, lon = field.shape
    field = field.reshape(*lead, rows, lon // LANES, LANES)
    return jnp.swapaxes(field, -3, -2).reshape(*lead, rows * lon // LANES, LANES)


def untiled(field, rows):
    *lead, count, lanes = field.shape
    field = field.reshape(*lead, count // rows, rows, lanes)
    return jnp.swapaxes(field, -3, -2).reshape(*lead, rows, count // rows * lanes)


def params(limit, **more):
    return pltpu.CompilerParams(vmem_limit_bytes=limit * MIB, **more)


def halves(x):
    high = x.astype(bf16)
    return high, (x - high.astype(f32)).astype(bf16)


def in_hbm(x):
    return pltpu.with_memory_space_constraint(x, pltpu.HBM)


def spread(row, dtype):
    return jnp.broadcast_to(row, (16, row.shape[1])).astype(dtype)


def matches(index, count):
    ids = lax.broadcasted_iota(jnp.int32, (count, index.shape[1]), 0).astype(jnp.int16)
    return ids.reshape(count // 16, 16, index.shape[1]) == spread(index, jnp.int16)[None]


def placed_at(index, count, amount=None):
    where = matches(index, count)
    amount = bf16(1) if amount is None else spread(amount, bf16)[None]
    return jnp.where(where, amount, bf16(0)).reshape(count, index.shape[1])


def in_turns(count, build, use, slots, between, beside, chunks):
    build(0, slots[0])

    def step(i, carry):
        use(2 * i, slots[0])
        build(2 * i + 1, slots[1])
        use(2 * i + 1, slots[1])
        build(jnp.minimum(2 * i + 2, count - 1), slots[0])
        return carry

    def last_step(i, carry):
        beside(i - first)
        return step(i, carry)

    first = max(count // 2 - chunks, 0)
    lax.fori_loop(0, first, step, 0)
    between()
    lax.fori_loop(first, count // 2, last_step, 0)
    if count % 2:
        use(count - 1, slots[0])
    for j in range(count // 2 - first, chunks):
        beside(j)


def product_nt(left, right):
    return lax.dot_general(left, right, (((1,), (1,)), ((), ())), preferred_element_type=f32)


def over(x, size):
    if size & (size - 1):
        return lax.div(x, jnp.int32(size)), lax.rem(x, jnp.int32(size))
    return lax.shift_right_logical(x, jnp.int32(size.bit_length() - 1)), x & (size - 1)


def peer(i, d, count):
    return (i + d) % count if count & (count - 1) else i ^ d


def back(d, count):
    return count - d if count & (count - 1) else d


def prepare(root_ref, static_ref, north_ref, east_ref, out_ref):
    levels = static_ref.shape[0]
    lev_share = out_ref.shape[0] - 2
    first = lax.axis_index("ens") * lev_share
    for j in range(lev_share):
        total = root_ref[first + j, 0] * static_ref[0]
        for m in range(1, levels):
            total = total + root_ref[first + j, m] * static_ref[m]
        out_ref[j] = total
    out_ref[lev_share] = north_ref[...]
    out_ref[lev_share + 1] = east_ref[...]


def list_cells(rows, lon, index_ref, count_ref, row_ref, lane_ref):
    lists, capacity = index_ref.shape
    pieces = capacity // LANES
    slot = lax.broadcasted_iota(jnp.int32, (1, capacity), 1)
    for q in range(lists):
        rest, lane = over(index_ref[q : q + 1, :], LANES)
        rest, block = over(rest, lon // LANES)
        level, row = over(rest, rows)
        grid_row = (level * (lon // LANES) + block) * rows + row
        grid_row = jnp.where(slot < count_ref[q], grid_row, -1)
        for c in range(pieces):
            at = q * pieces + c
            row_ref[at : at + 1, :] = grid_row[:, c * LANES : (c + 1) * LANES]
            lane_ref[at : at + 1, :] = lane[:, c * LANES : (c + 1) * LANES]


def level_product(matrix, transpose):
    levels = matrix.shape[0]
    size = levels * 16
    pick = lax.broadcasted_iota(jnp.int32, (size, levels), 0) // 16
    pick = jnp.where(pick == lax.broadcasted_iota(jnp.int32, (size, levels), 1), f32(1), f32(0)).astype(bf16)
    same = (
        lax.broadcasted_iota(jnp.int32, (size, size), 0) % 16 == lax.broadcasted_iota(jnp.int32, (size, size), 1) % 16
    )
    out = []
    for half in halves(matrix):
        if transpose:
            wide = product_nt(pick, half)
        else:
            wide = jnp.dot(pick, half, preferred_element_type=f32)
        wide = product_nt(wide.astype(bf16), pick)
        out.append(jnp.where(same, wide, f32(0)).astype(bf16))
    return jnp.concatenate([out[0], out[0], out[1]], axis=1)


def three_terms(x):
    high, low = halves(x)
    return jnp.concatenate([high, low, high], axis=0)


def observe_kernel(n_cols, cap_rows, scale, *refs):
    n_ens = len(refs) - 32
    sources, (out_ref, packed_ref), parts = refs[:10], refs[10:12], refs[12 : 12 + n_ens]
    refs = refs[12 + n_ens :]
    (acc_ref, fold_ref, matrix_ref, part_ref), landed, sems, slots, sums_ref = (
        refs[:4],
        refs[4:14],
        refs[14],
        (refs[15:17], refs[17:19]),
        refs[19],
    )
    slot_ref, weight_ref, innov_ref, local_ref, control_ref, pert_ref, *static_refs = landed
    coarse = acc_ref.shape[1]
    obs_rows = slot_ref.shape[0]
    group = min(8, obs_rows)
    here = pl.ds(pl.multiple_of(lax.axis_index("ens") * obs_rows, obs_rows), obs_rows)
    copies = [
        pltpu.make_async_copy(s.at[here, :] if i < 3 else s, t, sems.at[i])
        for i, (s, t) in enumerate(zip(sources, landed))
    ]
    for copy in copies:
        copy.start()
    acc_ref[...] = jnp.zeros_like(acc_ref)
    for copy in copies[:3]:
        copy.wait()

    def build(i, to):
        at = pl.ds(pl.multiple_of(i * group, group), group)
        weight = weight_ref[at, :]
        amount = weight * innov_ref[at, :]
        upper, lower = over(slot_ref[at, :], FINE)
        terms = [t.astype(f32) for t in halves(weight) + halves(amount)]
        for r in range(group):
            here = slice(r * LANES, (r + 1) * LANES)
            to[0][:, here] = placed_at(upper[r : r + 1, :], coarse)
            mask = matches(lower[r : r + 1, :], FINE)
            for t, term in enumerate(terms):
                term = spread(term[r : r + 1, :], bf16)[None]
                to[1][t * FINE : (t + 1) * FINE, here] = jnp.where(mask, term, bf16(0)).reshape(FINE, LANES)

    def use(i, of):
        acc_ref[...] += product_nt(of[1][...], of[0][...])

    def fields():
        for copy in copies[3:]:
            copy.wait()
        matrix_ref[...] = level_product(local_ref[...] * f32(scale), False)

    def members(j):
        sum_members(j, matrix_ref, control_ref, pert_ref, part_ref)

    in_turns(obs_rows // group, build, use, slots, fields, members, part_ref.shape[1] // 16)
    for t in range(2):
        at = 2 * t * FINE
        terms = acc_ref[at : at + FINE, :] + acc_ref[at + FINE : at + 2 * FINE, :]
        fold_ref[t] = jnp.concatenate([terms] * (LANES // FINE), axis=0).T
    per_row = LANES // FINE
    lane = lax.broadcasted_iota(jnp.int32, (coarse // per_row, LANES), 1)
    weights, amounts = (
        jnp.where(
            lane < FINE,
            fold_ref[t, pl.ds(0, coarse // per_row, stride=per_row), :],
            fold_ref[t, pl.ds(1, coarse // per_row, stride=per_row), :],
        )
        for t in range(2)
    )
    for p in range(n_cols):
        sums_ref[p, 0] = weights[p * cap_rows : (p + 1) * cap_rows]
        sums_ref[p, 1] = amounts[p * cap_rows : (p + 1) * cap_rows]
    writes = [
        pltpu.make_async_copy(sums_ref, out_ref.at[pl.ds(e * n_cols, n_cols)], sems.at[len(copies) + e])
        for e in range(n_ens)
    ]
    for write in writes:
        write.start()
    prepare(*static_refs, packed_ref)
    share = part_ref.shape[0] // n_ens
    for d, part in enumerate(parts):
        at = peer(lax.axis_index("ens"), d, n_ens) * share
        part[...] = part_ref[pl.ds(at, share)]
    for write in writes:
        write.wait()


def sum_members(j, matrix_ref, control_ref, pert_ref, out_ref):
    members, levels, _, _ = control_ref.shape
    group = 2 - members % 2
    at = pl.ds(pl.multiple_of(j * 16, 16), 16)
    total = jnp.zeros((levels * 16, LANES), f32)
    for k in range(0, members, group):
        terms = [three_terms(control_ref[k + i, :, at, :].reshape(levels * 16, LANES)) for i in range(group)]
        local = jnp.dot(matrix_ref[...], jnp.concatenate(terms, axis=1), preferred_element_type=f32)
        for i in range(group):
            pert = pert_ref[k + i, :, at, :].astype(f32).reshape(levels * 16, LANES)
            total = total + pert * local[:, i * LANES : (i + 1) * LANES]
    out_ref[:, at, :] = total.reshape(levels, 16, LANES)


def gather_levels(parts, to_ref):
    share = to_ref.shape[0] // len(parts)
    for i, part in enumerate(parts):
        at = peer(lax.axis_index("ens"), (len(parts) - i) % len(parts), len(parts))
        to_ref[pl.ds(at * share, share)] = part[...]


def member_kernel(matrix_ref, control_ref, pert_ref, *refs):
    parts, out_ref, adjoint_ref = refs[:-2], refs[-2], refs[-1]
    group, levels, per_level, _ = out_ref.shape
    first = pl.program_id(0) * group

    @pl.when(pl.program_id(0) == 0)
    def _():
        gather_levels(parts, adjoint_ref)

    def chunk(j, carry):
        at = pl.ds(pl.multiple_of(j * 16, 16), 16)
        adjoint = adjoint_ref[:, at, :]
        terms = [
            three_terms((pert_ref[first + i, :, at, :].astype(f32) * adjoint).reshape(levels * 16, LANES))
            for i in range(group)
        ]
        change = jnp.dot(matrix_ref[...], jnp.concatenate(terms, axis=1), preferred_element_type=f32)
        for i in range(group):
            part = change[:, i * LANES : (i + 1) * LANES].reshape(levels, 16, LANES)
            out_ref[i, :, at, :] = control_ref[first + i, :, at, :] + part
        return carry

    lax.fori_loop(0, per_level // 16, chunk, 0)


def eastern(x):
    lane = lax.broadcasted_iota(jnp.int32, x.shape, 1)
    near = pltpu.roll(x, LANES - 1, 1)
    return jnp.where(lane == LANES - 1, pltpu.roll(near, x.shape[0] - 1, 0), near)


def western(x):
    lane = lax.broadcasted_iota(jnp.int32, x.shape, 1)
    near = pltpu.roll(x, 1, 1)
    return jnp.where(lane == 0, pltpu.roll(near, 1, 0), near)


def rows_of(second_ref, first_ref, own_ref, other_ref, plane, rows):
    at = lax.axis_index("cols")
    count = lax.axis_size("cols")
    core, chip = at % 2, at // 2 % 2
    reads = [pl.ds(r, own_ref.shape[1] // rows, stride=rows) for r in range(rows)]
    first = [first_ref[plane, r, :] for r in reads]
    second = [second_ref[plane, r, :] for r in reads]
    out = [jnp.where(jnp.logical_and(chip == 1, at >= 2), f, f32(0)) for f in first]
    out = [jnp.where(jnp.logical_and(chip == 0, at >= 2), s, o) for s, o in zip(second, out)]
    out += [jnp.where(at >= 1, other_ref[1 - core, plane, r, :], f32(0)) for r in reads]
    out += [own_ref[plane, r, :] for r in reads]
    out += [jnp.where(at < count - 1, other_ref[core, plane, r, :], f32(0)) for r in reads]
    last = [jnp.where(jnp.logical_and(chip == 0, at < count - 2), f, f32(0)) for f in first]
    return out + [jnp.where(jnp.logical_and(chip == 1, at < count - 2), s, o) for s, o in zip(second, last)]


def diffuse_rows(tiles, level, coef_ref, rows):
    field = rows_of(*tiles, level, rows)
    for step in range(NDIFF):
        field = [
            coef_ref[0, i + step] * field[i]
            + coef_ref[1, i + step] * field[i - 1]
            + coef_ref[1, i + step + 1] * field[i + 1]
            + coef_ref[2, i + step] * eastern(field[i])
            + western(coef_ref[2, i + step] * field[i])
            for i in range(1, len(field) - 1)
        ]
    return field


def first_diffusion_kernel(lev_share, rows, *refs):
    second_ref, first_ref, own_ref, other_ref, *sources = refs[:6]
    out_ref, coef_ref, row_ref, lane_ref, *landed, sems = refs[6:]
    copies = [pltpu.make_async_copy(s, t, sems.at[i]) for i, (s, t) in enumerate(zip(sources, landed))]
    for copy in copies:
        copy.start()
    tiles = (second_ref, first_ref, own_ref, other_ref)
    blocks = own_ref.shape[1] // rows
    side = 2
    north = rows_of(*tiles, lev_share, rows)
    east = rows_of(*tiles, lev_share + 1, rows)
    faces = [
        jnp.where(lax.axis_index("cols") == side - i // rows, f32(0), n) if i % rows == 0 and i <= side * rows else n
        for i, n in enumerate(north)
    ]
    for i in range(len(north)):
        inner = 0 < i < len(north) - 1
        coef_ref[0, i] = 1.0 - north[i] - faces[i + 1] - east[i] - western(east[i]) if inner else jnp.zeros_like(east[i])
        coef_ref[1, i] = faces[i]
        coef_ref[2, i] = east[i]

    def body(level, carry):
        final = diffuse_rows(tiles, level, coef_ref, rows)
        for r in range(rows):
            out_ref[level, pl.ds(r, blocks, stride=rows), :] = final[r]
        return carry

    lax.fori_loop(0, lev_share, body, 0)
    for copy in copies:
        copy.wait()
    list_cells(rows, blocks * LANES, *landed, row_ref, lane_ref)


def second_diffusion_kernel(rows, coef_ref, second_ref, first_ref, own_ref, other_ref, out_ref):
    tiles = (second_ref, first_ref, own_ref, other_ref)
    lev_share = out_ref.shape[0]
    blocks = own_ref.shape[1] // rows

    def body(level, carry):
        final = diffuse_rows(tiles, level, coef_ref, rows)
        for r in range(rows):
            out_ref[level, pl.ds(r, blocks, stride=rows), :] = final[r]
        return carry

    lax.fori_loop(0, lev_share, body, 0)


def scatter_kernel(cap_rows, row_ref, lane_ref, slots_ref, *refs):
    sources, out_ref, kept, acc_ref, sems = refs[:3], refs[3], refs[4:7], refs[7], refs[8]
    copies = [pltpu.make_async_copy(s, t, sems.at[i]) for i, (s, t) in enumerate(zip(sources, kept))]
    for copy in copies:
        copy.start()
    own = out_ref.shape[1]
    lists = row_ref.shape[0] // cap_rows
    first = lax.axis_index("ens") * own
    acc_ref[...] = jnp.zeros_like(acc_ref)

    def step(q, carry):
        at = pl.ds(pl.multiple_of(q * cap_rows, cap_rows), cap_rows)
        rows = row_ref[at, :] - first
        lanes = lane_ref[at, :]
        terms = []
        for t in range(2):
            total = functools.reduce(
                jnp.add, [slots_ref[e * lists + q, t] for e in range(slots_ref.shape[0] // lists)]
            )
            terms += [h.astype(f32) for h in halves(total)]
        left, right = [], []
        for c in range(cap_rows):
            left.append(placed_at(rows[c : c + 1, :], own))
            mask = matches(lanes[c : c + 1, :], LANES)
            right.append(
                jnp.concatenate(
                    [
                        jnp.where(mask, spread(t[c : c + 1, :], bf16)[None], bf16(0)).reshape(LANES, LANES)
                        for t in terms
                    ],
                    axis=0,
                )
            )
        acc_ref[...] += product_nt(jnp.concatenate(right, axis=1), jnp.concatenate(left, axis=1))
        return carry

    lax.fori_loop(0, lists, step, 0)
    for t in range(2):
        at = 2 * t * LANES
        out_ref[t] = (acc_ref[at : at + LANES, :] + acc_ref[at + LANES : at + 2 * LANES, :]).T
    for copy in copies:
        copy.wait()


def matrices_kernel(scale, local_ref, root_ref, to_members_ref, to_static_ref):
    to_members_ref[...] = level_product(local_ref[...] * f32(scale), True)
    to_static_ref[...] = level_product(root_ref[...], True)


def static_kernel(matrix_ref, static_ref, *refs):
    parts, (out_ref, smooth_ref) = refs[:-2], refs[-2:]
    levels, per_level, _ = static_ref.shape
    gather_levels(parts, smooth_ref)
    for j in range(0, per_level, 32):
        terms = [three_terms(smooth_ref[:, j + i : j + i + 16, :].reshape(levels * 16, LANES)) for i in (0, 16)]
        change = jnp.dot(matrix_ref[...], jnp.concatenate(terms, axis=1), preferred_element_type=f32)
        for i, part in ((0, change[:, :LANES]), (16, change[:, LANES:])):
            at = slice(j + i, j + i + 16)
            out_ref[:, at, :] = static_ref[:, at, :] + part.reshape(levels, 16, LANES)


def exchanged(x, starts):
    count = lax.axis_size("cols")
    out = []
    for start in starts:
        pairs = []
        for i in range(count):
            chip, core = divmod(i, 2)
            partner = (chip + start ^ 1) - start
            pairs.append((i, 2 * partner + core if 0 <= 2 * partner + core < count else i))
        out.append(lax.ppermute(x, "cols", pairs))
    return out


def from_peers(x):
    count = lax.axis_size("ens")
    return [lax.ppermute(x, "ens", [(peer(i, d, count), i) for i in range(count)]) for d in range(count - 1, 0, -1)]


def swapped(own, first, second):
    at = lax.axis_index("cols")
    pack = jnp.stack([own, jnp.where(at % 2 == at // 2 % 2, first, second)])
    return lax.ppermute(pack, "cols", [(i, i ^ 1) for i in range(lax.axis_size("cols"))])


def local(
    static_control,
    ensemble_control,
    perturbations,
    vertical_root,
    vertical_local,
    face_north,
    face_east,
    innovation,
    obs_weight,
    obs_slot,
    send_index,
    send_count,
):
    n_ens = lax.axis_size("ens")
    n_cols = lax.axis_size("cols")
    members, levels, rows, lon = ensemble_control.shape
    per_level = rows * lon // LANES
    cells = levels * per_level
    lev_share = levels // n_ens
    own = lev_share * per_level
    lists, capacity = send_index.shape
    cap_rows = capacity // LANES
    entry_rows = lists * cap_rows
    member_scale = 1.0 / math.sqrt(members * n_ens - 1)

    static = in_hbm(tiled(static_control))
    control = in_hbm(tiled(ensemble_control))
    pert = in_hbm(tiled(perturbations))

    def whole(*shape):
        return pl.BlockSpec(shape, lambda i: (0,) * len(shape))

    obs_rows = obs_slot.shape[0] // LANES
    share_rows = obs_rows // n_ens
    coarse = n_cols * capacity // FINE
    size = levels * 16
    slots, packed, *parts = pl.pallas_call(
        functools.partial(observe_kernel, n_cols, cap_rows, member_scale),
        grid=(1,),
        in_specs=[pl.BlockSpec(memory_space=pl.ANY)] * 10,
        out_specs=[pl.BlockSpec(memory_space=pl.ANY)] + [VMEM] * (1 + n_ens),
        out_shape=[
            pltpu.HBM((n_ens * n_cols, 2, cap_rows, LANES), f32),
            pltpu.VMEM((lev_share + 2, per_level, LANES), f32),
        ]
        + [pltpu.VMEM((lev_share, per_level, LANES), f32)] * n_ens,
        scratch_shapes=[
            pltpu.VMEM((4 * FINE, coarse), f32),
            pltpu.VMEM((2, coarse, LANES), f32),
            pltpu.VMEM((size, 3 * size), bf16),
            pltpu.VMEM((levels, per_level, LANES), f32),
            pltpu.VMEM((share_rows, LANES), jnp.int32),
            pltpu.VMEM((share_rows, LANES), f32),
            pltpu.VMEM((share_rows, LANES), f32),
            pltpu.VMEM((levels, levels), f32),
            pltpu.VMEM(control.shape, f32),
            pltpu.VMEM(pert.shape, bf16),
            pltpu.SMEM((levels, levels), f32),
            pltpu.VMEM((levels, per_level, LANES), f32),
            pltpu.VMEM((per_level, LANES), f32),
            pltpu.VMEM((per_level, LANES), f32),
            pltpu.SemaphoreType.DMA((10 + n_ens,)),
        ]
        + [pltpu.VMEM((coarse, 8 * LANES), bf16), pltpu.VMEM((4 * FINE, 8 * LANES), bf16)] * 2
        + [pltpu.VMEM((n_cols, 2, cap_rows, LANES), f32)],
        compiler_params=params(24),
        name="slot_sums_and_members",
    )(
        in_hbm(obs_slot.reshape(obs_rows, LANES)),
        in_hbm(obs_weight.reshape(obs_rows, LANES)),
        in_hbm(innovation.reshape(obs_rows, LANES)),
        in_hbm(vertical_local),
        control,
        pert,
        in_hbm(vertical_root),
        static,
        in_hbm(tiled(face_north)),
        in_hbm(tiled(face_east)),
    )
    slots = lax.all_to_all(slots, ("ens", "cols"), split_axis=0, concat_axis=0, tiled=True)
    second, first = exchanged(packed, (1, 0))
    sums = [parts[0]] + [
        lax.ppermute(parts[back(d, n_ens)], "ens", [(peer(i, d, n_ens), i) for i in range(n_ens)])
        for d in range(n_ens - 1, 0, -1)
    ]
    other = swapped(packed, first, second)

    increment, coefs, entry_row, entry_lane = pl.pallas_call(
        functools.partial(first_diffusion_kernel, lev_share, rows),
        in_specs=[VMEM] * 4 + [pl.BlockSpec(memory_space=pl.ANY)] * 2,
        out_specs=[VMEM] * 4,
        out_shape=[
            pltpu.VMEM((lev_share, per_level, LANES), f32),
            pltpu.VMEM((3, 5 * rows, per_level // rows, LANES), f32),
            pltpu.VMEM((entry_rows, LANES), jnp.int32),
            pltpu.VMEM((entry_rows, LANES), jnp.int32),
        ],
        scratch_shapes=[
            pltpu.VMEM((lists, capacity), jnp.int32),
            pltpu.SMEM((lists,), jnp.int32),
            pltpu.SemaphoreType.DMA((2,)),
        ],
        compiler_params=params(8),
        cost_estimate=pl.CostEstimate(flops=1 << 26, bytes_accessed=1 << 22, transcendentals=0),
        name="diffuse_forward",
    )(second, first, packed, other, in_hbm(send_index), in_hbm(send_count))

    increment, coefs, slots = lax.optimization_barrier((increment, coefs, slots))
    slot_sums, static_here, control_here, pert_here = pl.pallas_call(
        functools.partial(scatter_kernel, cap_rows),
        in_specs=[VMEM] * 3 + [pl.BlockSpec(memory_space=pl.ANY)] * 3,
        out_specs=[VMEM] * 4,
        out_shape=[
            pltpu.VMEM((2, own, LANES), f32),
            pltpu.VMEM(static.shape, f32),
            pltpu.VMEM(control.shape, f32),
            pltpu.VMEM(pert.shape, bf16),
        ],
        scratch_shapes=[pltpu.VMEM((4 * LANES, own), f32), pltpu.SemaphoreType.DMA((3,))],
        compiler_params=params(16),
        cost_estimate=pl.CostEstimate(flops=8 * own * LANES * lists * capacity, bytes_accessed=1 << 23, transcendentals=0),
        name="scatter",
    )(entry_row, entry_lane, slots, static, control, pert)

    slot_sums = slot_sums.reshape(2, lev_share, per_level, LANES)
    tile = functools.reduce(jnp.add, sums) + increment
    tile = tile * slot_sums[0] - slot_sums[1]
    tile_first, tile_second = exchanged(tile, (0, 1))
    adjoints = [tile] + from_peers(tile)
    tile, vertical_local, vertical_root = lax.optimization_barrier((tile, vertical_local, vertical_root))
    from_local, from_root = pl.pallas_call(
        functools.partial(matrices_kernel, member_scale),
        grid=(1,),
        in_specs=[whole(levels, levels)] * 2,
        out_specs=[VMEM] * 2,
        out_shape=[pltpu.VMEM((size, 3 * size), bf16)] * 2,
        compiler_params=params(8),
        name="level_matrices",
    )(in_hbm(vertical_local), in_hbm(vertical_root))
    tile_first, tile_second, adjoints[-1], from_local, from_root = lax.optimization_barrier(
        (tile_first, tile_second, adjoints[-1], from_local, from_root)
    )
    tile_other = swapped(tile, tile_first, tile_second)

    smooth = pl.pallas_call(
        functools.partial(second_diffusion_kernel, rows),
        in_specs=[VMEM] * 5,
        out_specs=VMEM,
        out_shape=pltpu.VMEM((lev_share, per_level, LANES), f32),
        compiler_params=params(8),
        name="diffuse_adjoint",
    )(coefs, tile_second, tile_first, tile, tile_other)
    smooth, from_local = lax.optimization_barrier((smooth, from_local))
    smooths = [smooth] + from_peers(smooth)

    group = 2 - members % 2
    ensemble_grad = pl.pallas_call(
        member_kernel,
        grid=(members // group,),
        in_specs=[VMEM] * (3 + n_ens),
        out_specs=pl.BlockSpec((group, levels, per_level, LANES), lambda k: (k, 0, 0, 0)),
        out_shape=jax.ShapeDtypeStruct((members, levels, per_level, LANES), f32),
        scratch_shapes=[pltpu.VMEM((levels, per_level, LANES), f32)],
        compiler_params=params(16),
        name="members_gradient",
    )(from_local, control_here, pert_here, *adjoints)

    static_grad = pl.pallas_call(
        static_kernel,
        grid=(1,),
        in_specs=[VMEM] * (2 + n_ens),
        out_specs=whole(levels, per_level, LANES),
        out_shape=jax.ShapeDtypeStruct((levels, per_level, LANES), f32),
        scratch_shapes=[pltpu.VMEM((levels, per_level, LANES), f32)],
        compiler_params=params(8),
        name="static_gradient",
    )(from_root, static_here, *smooths)
    return (untiled(static_grad, rows), untiled(ensemble_grad, rows))


def solution(mesh):
    placed = (
        P(None, "cols", None),
        P("ens", None, "cols", None),
        P("ens", None, "cols", None),
        P(),
        P(),
        P("cols", None),
        P("cols", None),
        P("cols"),
        P("cols"),
        P("cols"),
        P("cols", None),
        P("cols"),
    )
    return jax.shard_map(
        local,
        mesh=mesh,
        in_specs=placed,
        out_specs=(P(None, "cols", None), P("ens", None, "cols", None)),
        check_vma=False,
    )
```

```python
import functools
import math

import jax
import jax.numpy as jnp
from jax import lax
from jax.experimental import pallas as pl
from jax.experimental.pallas import tpu as pltpu
from jax.sharding import PartitionSpec as P

NDIFF = 4
LANES = 128
FINE = 64
MIB = 1 << 20

f32 = jnp.float32
bf16 = jnp.bfloat16
SMEM = pl.BlockSpec(memory_space=pltpu.SMEM)
VMEM = pl.BlockSpec(memory_space=pltpu.VMEM)


def tiled(field):
    *lead, rows, lon = field.shape
    field = field.reshape(*lead, rows, lon // LANES, LANES)
    return jnp.swapaxes(field, -3, -2).reshape(*lead, rows * lon // LANES, LANES)


def untiled(field, rows):
    *lead, count, lanes = field.shape
    field = field.reshape(*lead, count // rows, rows, lanes)
    return jnp.swapaxes(field, -3, -2).reshape(*lead, rows, count // rows * lanes)


def params(limit, **more):
    return pltpu.CompilerParams(vmem_limit_bytes=limit * MIB, **more)


def halves(x):
    high = x.astype(bf16)
    return high, (x - high.astype(f32)).astype(bf16)


def in_hbm(x):
    return pltpu.with_memory_space_constraint(x, pltpu.HBM)


def spread(row, dtype):
    return jnp.broadcast_to(row, (16, row.shape[1])).astype(dtype)


def matches(index, count):
    ids = lax.broadcasted_iota(jnp.int32, (count, index.shape[1]), 0).astype(jnp.int16)
    return ids.reshape(count // 16, 16, index.shape[1]) == spread(index, jnp.int16)[None]


def placed_at(index, count, amount=None):
    where = matches(index, count)
    amount = bf16(1) if amount is None else spread(amount, bf16)[None]
    return jnp.where(where, amount, bf16(0)).reshape(count, index.shape[1])


def in_turns(count, build, use, slots, between, beside, chunks):
    build(0, slots[0])

    def step(i, carry):
        use(2 * i, slots[0])
        build(2 * i + 1, slots[1])
        use(2 * i + 1, slots[1])
        build(jnp.minimum(2 * i + 2, count - 1), slots[0])
        return carry

    def last_step(i, carry):
        beside(i - first)
        return step(i, carry)

    first = max(count // 2 - chunks, 0)
    lax.fori_loop(0, first, step, 0)
    between()
    lax.fori_loop(first, count // 2, last_step, 0)
    if count % 2:
        use(count - 1, slots[0])
    for j in range(count // 2 - first, chunks):
        beside(j)


def product_nt(left, right):
    return lax.dot_general(left, right, (((1,), (1,)), ((), ())), preferred_element_type=f32)


def over(x, size):
    if size & (size - 1):
        return lax.div(x, jnp.int32(size)), lax.rem(x, jnp.int32(size))
    return lax.shift_right_logical(x, jnp.int32(size.bit_length() - 1)), x & (size - 1)


def peer(i, d, count):
    return (i + d) % count if count & (count - 1) else i ^ d


def back(d, count):
    return count - d if count & (count - 1) else d


def prepare(root_ref, static_ref, north_ref, east_ref, out_ref):
    levels = static_ref.shape[0]
    lev_share = out_ref.shape[0] - 2
    first = lax.axis_index("ens") * lev_share
    for j in range(lev_share):
        total = root_ref[first + j, 0] * static_ref[0]
        for m in range(1, levels):
            total = total + root_ref[first + j, m] * static_ref[m]
        out_ref[j] = total
    out_ref[lev_share] = north_ref[...]
    out_ref[lev_share + 1] = east_ref[...]


def list_cells(rows, lon, index_ref, count_ref, row_ref, lane_ref):
    lists, capacity = index_ref.shape
    pieces = capacity // LANES
    slot = lax.broadcasted_iota(jnp.int32, (1, capacity), 1)
    for q in range(lists):
        rest, lane = over(index_ref[q : q + 1, :], LANES)
        rest, block = over(rest, lon // LANES)
        level, row = over(rest, rows)
        grid_row = (level * (lon // LANES) + block) * rows + row
        grid_row = jnp.where(slot < count_ref[q], grid_row, -1)
        for c in range(pieces):
            at = q * pieces + c
            row_ref[at : at + 1, :] = grid_row[:, c * LANES : (c + 1) * LANES]
            lane_ref[at : at + 1, :] = lane[:, c * LANES : (c + 1) * LANES]


def level_product(matrix, transpose):
    levels = matrix.shape[0]
    size = levels * 16
    pick = lax.broadcasted_iota(jnp.int32, (size, levels), 0) // 16
    pick = jnp.where(pick == lax.broadcasted_iota(jnp.int32, (size, levels), 1), f32(1), f32(0)).astype(bf16)
    same = (
        lax.broadcasted_iota(jnp.int32, (size, size), 0) % 16 == lax.broadcasted_iota(jnp.int32, (size, size), 1) % 16
    )
    out = []
    for half in halves(matrix):
        if transpose:
            wide = product_nt(pick, half)
        else:
            wide = jnp.dot(pick, half, preferred_element_type=f32)
        wide = product_nt(wide.astype(bf16), pick)
        out.append(jnp.where(same, wide, f32(0)).astype(bf16))
    return jnp.concatenate([out[0], out[0], out[1]], axis=1)


def three_terms(x):
    high, low = halves(x)
    return jnp.concatenate([high, low, high], axis=0)


def observe_kernel(n_cols, cap_rows, scale, *refs):
    n_ens = len(refs) - 32
    sources, (out_ref, packed_ref), parts = refs[:10], refs[10:12], refs[12 : 12 + n_ens]
    refs = refs[12 + n_ens :]
    (acc_ref, fold_ref, matrix_ref, part_ref), landed, sems, slots, sums_ref = (
        refs[:4],
        refs[4:14],
        refs[14],
        (refs[15:17], refs[17:19]),
        refs[19],
    )
    slot_ref, weight_ref, innov_ref, local_ref, control_ref, pert_ref, *static_refs = landed
    coarse = acc_ref.shape[1]
    obs_rows = slot_ref.shape[0]
    group = min(8, obs_rows)
    here = pl.ds(pl.multiple_of(lax.axis_index("ens") * obs_rows, obs_rows), obs_rows)
    copies = [
        pltpu.make_async_copy(s.at[here, :] if i < 3 else s, t, sems.at[i])
        for i, (s, t) in enumerate(zip(sources, landed))
    ]
    for copy in copies:
        copy.start()
    acc_ref[...] = jnp.zeros_like(acc_ref)
    for copy in copies[:3]:
        copy.wait()

    def build(i, to):
        at = pl.ds(pl.multiple_of(i * group, group), group)
        weight = weight_ref[at, :]
        amount = weight * innov_ref[at, :]
        upper, lower = over(slot_ref[at, :], FINE)
        terms = [t.astype(f32) for t in halves(weight) + halves(amount)]
        for r in range(group):
            here = slice(r * LANES, (r + 1) * LANES)
            to[0][:, here] = placed_at(upper[r : r + 1, :], coarse)
            mask = matches(lower[r : r + 1, :], FINE)
            for t, term in enumerate(terms):
                term = spread(term[r : r + 1, :], bf16)[None]
                to[1][t * FINE : (t + 1) * FINE, here] = jnp.where(mask, term, bf16(0)).reshape(FINE, LANES)

    def use(i, of):
        acc_ref[...] += product_nt(of[1][...], of[0][...])

    def fields():
        for copy in copies[3:]:
            copy.wait()
        matrix_ref[...] = level_product(local_ref[...] * f32(scale), False)

    def members(j):
        sum_members(j, matrix_ref, control_ref, pert_ref, part_ref)

    in_turns(obs_rows // group, build, use, slots, fields, members, part_ref.shape[1] // 16)
    for t in range(2):
        at = 2 * t * FINE
        terms = acc_ref[at : at + FINE, :] + acc_ref[at + FINE : at + 2 * FINE, :]
        fold_ref[t] = jnp.concatenate([terms] * (LANES // FINE), axis=0).T
    per_row = LANES // FINE
    lane = lax.broadcasted_iota(jnp.int32, (coarse // per_row, LANES), 1)
    weights, amounts = (
        jnp.where(
            lane < FINE,
            fold_ref[t, pl.ds(0, coarse // per_row, stride=per_row), :],
            fold_ref[t, pl.ds(1, coarse // per_row, stride=per_row), :],
        )
        for t in range(2)
    )
    for p in range(n_cols):
        sums_ref[p, 0] = weights[p * cap_rows : (p + 1) * cap_rows]
        sums_ref[p, 1] = amounts[p * cap_rows : (p + 1) * cap_rows]
    writes = [
        pltpu.make_async_copy(sums_ref, out_ref.at[pl.ds(e * n_cols, n_cols)], sems.at[len(copies) + e])
        for e in range(n_ens)
    ]
    for write in writes:
        write.start()
    prepare(*static_refs, packed_ref)
    share = part_ref.shape[0] // n_ens
    for d, part in enumerate(parts):
        at = peer(lax.axis_index("ens"), d, n_ens) * share
        part[...] = part_ref[pl.ds(at, share)]
    for write in writes:
        write.wait()


def sum_members(j, matrix_ref, control_ref, pert_ref, out_ref):
    members, levels, _, _ = control_ref.shape
    group = 2 - members % 2
    at = pl.ds(pl.multiple_of(j * 16, 16), 16)
    total = jnp.zeros((levels * 16, LANES), f32)
    for k in range(0, members, group):
        terms = [three_terms(control_ref[k + i, :, at, :].reshape(levels * 16, LANES)) for i in range(group)]
        local = jnp.dot(matrix_ref[...], jnp.concatenate(terms, axis=1), preferred_element_type=f32)
        for i in range(group):
            pert = pert_ref[k + i, :, at, :].astype(f32).reshape(levels * 16, LANES)
            total = total + pert * local[:, i * LANES : (i + 1) * LANES]
    out_ref[:, at, :] = total.reshape(levels, 16, LANES)


def gather_levels(parts, to_ref, far_first):
    share = to_ref.shape[0] // len(parts)
    for i, part in enumerate(parts):
        at = peer(lax.axis_index("ens"), (len(parts) - i) % len(parts) if far_first else i, len(parts))
        to_ref[pl.ds(at * share, share)] = part[...]


def member_kernel(matrix_ref, control_ref, pert_ref, *refs):
    parts, out_ref, adjoint_ref = refs[:-2], refs[-2], refs[-1]
    group, levels, per_level, _ = out_ref.shape
    first = pl.program_id(0) * group

    @pl.when(pl.program_id(0) == 0)
    def _():
        gather_levels(parts, adjoint_ref, True)

    def chunk(j, carry):
        at = pl.ds(pl.multiple_of(j * 16, 16), 16)
        adjoint = adjoint_ref[:, at, :]
        terms = [
            three_terms((pert_ref[first + i, :, at, :].astype(f32) * adjoint).reshape(levels * 16, LANES))
            for i in range(group)
        ]
        change = jnp.dot(matrix_ref[...], jnp.concatenate(terms, axis=1), preferred_element_type=f32)
        for i in range(group):
            part = change[:, i * LANES : (i + 1) * LANES].reshape(levels, 16, LANES)
            out_ref[i, :, at, :] = control_ref[first + i, :, at, :] + part
        return carry

    lax.fori_loop(0, per_level // 16, chunk, 0)


def eastern(x):
    lane = lax.broadcasted_iota(jnp.int32, x.shape, 1)
    near = pltpu.roll(x, LANES - 1, 1)
    return jnp.where(lane == LANES - 1, pltpu.roll(near, x.shape[0] - 1, 0), near)


def western(x):
    lane = lax.broadcasted_iota(jnp.int32, x.shape, 1)
    near = pltpu.roll(x, 1, 1)
    return jnp.where(lane == 0, pltpu.roll(near, 1, 0), near)


def rows_of(second_ref, first_ref, own_ref, other_ref, plane, rows):
    at = lax.axis_index("cols")
    count = lax.axis_size("cols")
    core, chip = at % 2, at // 2 % 2
    reads = [pl.ds(r, own_ref.shape[1] // rows, stride=rows) for r in range(rows)]
    first = [first_ref[plane, r, :] for r in reads]
    second = [second_ref[plane, r, :] for r in reads]
    out = [jnp.where(jnp.logical_and(chip == 1, at >= 2), f, f32(0)) for f in first]
    out = [jnp.where(jnp.logical_and(chip == 0, at >= 2), s, o) for s, o in zip(second, out)]
    out += [jnp.where(at >= 1, other_ref[1 - core, plane, r, :], f32(0)) for r in reads]
    out += [own_ref[plane, r, :] for r in reads]
    out += [jnp.where(at < count - 1, other_ref[core, plane, r, :], f32(0)) for r in reads]
    last = [jnp.where(jnp.logical_and(chip == 0, at < count - 2), f, f32(0)) for f in first]
    return out + [jnp.where(jnp.logical_and(chip == 1, at < count - 2), s, o) for s, o in zip(second, last)]


def diffuse_rows(tiles, level, coef_ref, rows):
    field = rows_of(*tiles, level, rows)
    for step in range(NDIFF):
        field = [
            coef_ref[0, i + step] * field[i]
            + coef_ref[1, i + step] * field[i - 1]
            + coef_ref[1, i + step + 1] * field[i + 1]
            + coef_ref[2, i + step] * eastern(field[i])
            + western(coef_ref[2, i + step] * field[i])
            for i in range(1, len(field) - 1)
        ]
    return field


def first_diffusion_kernel(lev_share, rows, *refs):
    second_ref, first_ref, own_ref, other_ref, *sources = refs[:6]
    out_ref, coef_ref, row_ref, lane_ref, *landed, sems = refs[6:]
    copies = [pltpu.make_async_copy(s, t, sems.at[i]) for i, (s, t) in enumerate(zip(sources, landed))]
    for copy in copies:
        copy.start()
    tiles = (second_ref, first_ref, own_ref, other_ref)
    blocks = own_ref.shape[1] // rows
    side = 2
    north = rows_of(*tiles, lev_share, rows)
    east = rows_of(*tiles, lev_share + 1, rows)
    faces = [
        jnp.where(lax.axis_index("cols") == side - i // rows, f32(0), n) if i % rows == 0 and i <= side * rows else n
        for i, n in enumerate(north)
    ]
    for i in range(len(north)):
        inner = 0 < i < len(north) - 1
        coef_ref[0, i] = 1.0 - north[i] - faces[i + 1] - east[i] - western(east[i]) if inner else jnp.zeros_like(east[i])
        coef_ref[1, i] = faces[i]
        coef_ref[2, i] = east[i]

    def body(level, carry):
        final = diffuse_rows(tiles, level, coef_ref, rows)
        for r in range(rows):
            out_ref[level, pl.ds(r, blocks, stride=rows), :] = final[r]
        return carry

    lax.fori_loop(0, lev_share, body, 0)
    for copy in copies:
        copy.wait()
    list_cells(rows, blocks * LANES, *landed, row_ref, lane_ref)


def second_diffusion_kernel(rows, coef_ref, second_ref, first_ref, own_ref, other_ref, out_ref):
    tiles = (second_ref, first_ref, own_ref, other_ref)
    lev_share = out_ref.shape[0]
    blocks = own_ref.shape[1] // rows

    def body(level, carry):
        final = diffuse_rows(tiles, level, coef_ref, rows)
        for r in range(rows):
            out_ref[level, pl.ds(r, blocks, stride=rows), :] = final[r]
        return carry

    lax.fori_loop(0, lev_share, body, 0)


def scatter_kernel(cap_rows, row_ref, lane_ref, slots_ref, *refs):
    sources, out_ref, kept, acc_ref, sems = refs[:3], refs[3], refs[4:7], refs[7], refs[8]
    copies = [pltpu.make_async_copy(s, t, sems.at[i]) for i, (s, t) in enumerate(zip(sources, kept))]
    for copy in copies:
        copy.start()
    own = out_ref.shape[1]
    lists = row_ref.shape[0] // cap_rows
    first = lax.axis_index("ens") * own
    acc_ref[...] = jnp.zeros_like(acc_ref)

    def step(q, carry):
        at = pl.ds(pl.multiple_of(q * cap_rows, cap_rows), cap_rows)
        rows = row_ref[at, :] - first
        lanes = lane_ref[at, :]
        terms = []
        for t in range(2):
            total = functools.reduce(
                jnp.add, [slots_ref[e * lists + q, t] for e in range(slots_ref.shape[0] // lists)]
            )
            terms += [h.astype(f32) for h in halves(total)]
        left, right = [], []
        for c in range(cap_rows):
            left.append(placed_at(rows[c : c + 1, :], own))
            mask = matches(lanes[c : c + 1, :], LANES)
            right.append(
                jnp.concatenate(
                    [
                        jnp.where(mask, spread(t[c : c + 1, :], bf16)[None], bf16(0)).reshape(LANES, LANES)
                        for t in terms
                    ],
                    axis=0,
                )
            )
        acc_ref[...] += product_nt(jnp.concatenate(right, axis=1), jnp.concatenate(left, axis=1))
        return carry

    lax.fori_loop(0, lists, step, 0)
    for t in range(2):
        at = 2 * t * LANES
        out_ref[t] = (acc_ref[at : at + LANES, :] + acc_ref[at + LANES : at + 2 * LANES, :]).T
    for copy in copies:
        copy.wait()


def matrices_kernel(scale, local_ref, root_ref, to_members_ref, to_static_ref):
    to_members_ref[...] = level_product(local_ref[...] * f32(scale), True)
    to_static_ref[...] = level_product(root_ref[...], True)


def static_kernel(matrix_ref, static_ref, *refs):
    parts, (out_ref, smooth_ref) = refs[:-2], refs[-2:]
    levels, per_level, _ = static_ref.shape
    gather_levels(parts, smooth_ref, False)
    for j in range(0, per_level, 32):
        terms = [three_terms(smooth_ref[:, j + i : j + i + 16, :].reshape(levels * 16, LANES)) for i in (0, 16)]
        change = jnp.dot(matrix_ref[...], jnp.concatenate(terms, axis=1), preferred_element_type=f32)
        for i, part in ((0, change[:, :LANES]), (16, change[:, LANES:])):
            at = slice(j + i, j + i + 16)
            out_ref[:, at, :] = static_ref[:, at, :] + part.reshape(levels, 16, LANES)


def exchanged(x, starts):
    count = lax.axis_size("cols")
    out = []
    for start in starts:
        pairs = []
        for i in range(count):
            chip, core = divmod(i, 2)
            partner = (chip + start ^ 1) - start
            pairs.append((i, 2 * partner + core if 0 <= 2 * partner + core < count else i))
        out.append(lax.ppermute(x, "cols", pairs))
    return out


def from_peers(x):
    count = lax.axis_size("ens")
    return [lax.ppermute(x, "ens", [(peer(i, d, count), i) for i in range(count)]) for d in range(count - 1, 0, -1)]


def swapped(own, first, second):
    at = lax.axis_index("cols")
    pack = jnp.stack([own, jnp.where(at % 2 == at // 2 % 2, first, second)])
    return lax.ppermute(pack, "cols", [(i, i ^ 1) for i in range(lax.axis_size("cols"))])


def local(
    static_control,
    ensemble_control,
    perturbations,
    vertical_root,
    vertical_local,
    face_north,
    face_east,
    innovation,
    obs_weight,
    obs_slot,
    send_index,
    send_count,
):
    n_ens = lax.axis_size("ens")
    n_cols = lax.axis_size("cols")
    members, levels, rows, lon = ensemble_control.shape
    per_level = rows * lon // LANES
    cells = levels * per_level
    lev_share = levels // n_ens
    own = lev_share * per_level
    lists, capacity = send_index.shape
    cap_rows = capacity // LANES
    entry_rows = lists * cap_rows
    member_scale = 1.0 / math.sqrt(members * n_ens - 1)

    static = in_hbm(tiled(static_control))
    control = in_hbm(tiled(ensemble_control))
    pert = in_hbm(tiled(perturbations))

    def whole(*shape):
        return pl.BlockSpec(shape, lambda i: (0,) * len(shape))

    obs_rows = obs_slot.shape[0] // LANES
    share_rows = obs_rows // n_ens
    coarse = n_cols * capacity // FINE
    size = levels * 16
    slots, packed, *parts = pl.pallas_call(
        functools.partial(observe_kernel, n_cols, cap_rows, member_scale),
        grid=(1,),
        in_specs=[pl.BlockSpec(memory_space=pl.ANY)] * 10,
        out_specs=[pl.BlockSpec(memory_space=pl.ANY)] + [VMEM] * (1 + n_ens),
        out_shape=[
            pltpu.HBM((n_ens * n_cols, 2, cap_rows, LANES), f32),
            pltpu.VMEM((lev_share + 2, per_level, LANES), f32),
        ]
        + [pltpu.VMEM((lev_share, per_level, LANES), f32)] * n_ens,
        scratch_shapes=[
            pltpu.VMEM((4 * FINE, coarse), f32),
            pltpu.VMEM((2, coarse, LANES), f32),
            pltpu.VMEM((size, 3 * size), bf16),
            pltpu.VMEM((levels, per_level, LANES), f32),
            pltpu.VMEM((share_rows, LANES), jnp.int32),
            pltpu.VMEM((share_rows, LANES), f32),
            pltpu.VMEM((share_rows, LANES), f32),
            pltpu.VMEM((levels, levels), f32),
            pltpu.VMEM(control.shape, f32),
            pltpu.VMEM(pert.shape, bf16),
            pltpu.SMEM((levels, levels), f32),
            pltpu.VMEM((levels, per_level, LANES), f32),
            pltpu.VMEM((per_level, LANES), f32),
            pltpu.VMEM((per_level, LANES), f32),
            pltpu.SemaphoreType.DMA((10 + n_ens,)),
        ]
        + [pltpu.VMEM((coarse, 8 * LANES), bf16), pltpu.VMEM((4 * FINE, 8 * LANES), bf16)] * 2
        + [pltpu.VMEM((n_cols, 2, cap_rows, LANES), f32)],
        compiler_params=params(24),
        name="slot_sums_and_members",
    )(
        in_hbm(obs_slot.reshape(obs_rows, LANES)),
        in_hbm(obs_weight.reshape(obs_rows, LANES)),
        in_hbm(innovation.reshape(obs_rows, LANES)),
        in_hbm(vertical_local),
        control,
        pert,
        in_hbm(vertical_root),
        static,
        in_hbm(tiled(face_north)),
        in_hbm(tiled(face_east)),
    )
    slots = lax.all_to_all(slots, ("ens", "cols"), split_axis=0, concat_axis=0, tiled=True)
    second, first = exchanged(packed, (1, 0))
    sums = [parts[0]] + [
        lax.ppermute(parts[back(d, n_ens)], "ens", [(peer(i, d, n_ens), i) for i in range(n_ens)])
        for d in range(n_ens - 1, 0, -1)
    ]
    other = swapped(packed, first, second)

    increment, coefs, entry_row, entry_lane = pl.pallas_call(
        functools.partial(first_diffusion_kernel, lev_share, rows),
        in_specs=[VMEM] * 4 + [pl.BlockSpec(memory_space=pl.ANY)] * 2,
        out_specs=[VMEM] * 4,
        out_shape=[
            pltpu.VMEM((lev_share, per_level, LANES), f32),
            pltpu.VMEM((3, 5 * rows, per_level // rows, LANES), f32),
            pltpu.VMEM((entry_rows, LANES), jnp.int32),
            pltpu.VMEM((entry_rows, LANES), jnp.int32),
        ],
        scratch_shapes=[
            pltpu.VMEM((lists, capacity), jnp.int32),
            pltpu.SMEM((lists,), jnp.int32),
            pltpu.SemaphoreType.DMA((2,)),
        ],
        compiler_params=params(8),
        cost_estimate=pl.CostEstimate(flops=1 << 26, bytes_accessed=1 << 22, transcendentals=0),
        name="diffuse_forward",
    )(second, first, packed, other, in_hbm(send_index), in_hbm(send_count))

    increment, coefs, slots = lax.optimization_barrier((increment, coefs, slots))
    slot_sums, static_here, control_here, pert_here = pl.pallas_call(
        functools.partial(scatter_kernel, cap_rows),
        in_specs=[VMEM] * 3 + [pl.BlockSpec(memory_space=pl.ANY)] * 3,
        out_specs=[VMEM] * 4,
        out_shape=[
            pltpu.VMEM((2, own, LANES), f32),
            pltpu.VMEM(static.shape, f32),
            pltpu.VMEM(control.shape, f32),
            pltpu.VMEM(pert.shape, bf16),
        ],
        scratch_shapes=[pltpu.VMEM((4 * LANES, own), f32), pltpu.SemaphoreType.DMA((3,))],
        compiler_params=params(16),
        cost_estimate=pl.CostEstimate(flops=8 * own * LANES * lists * capacity, bytes_accessed=1 << 23, transcendentals=0),
        name="scatter",
    )(entry_row, entry_lane, slots, static, control, pert)

    slot_sums = slot_sums.reshape(2, lev_share, per_level, LANES)
    tile = functools.reduce(jnp.add, sums) + increment
    tile = tile * slot_sums[0] - slot_sums[1]
    tile_first, tile_second = exchanged(tile, (0, 1))
    adjoints = [tile] + from_peers(tile)
    tile, vertical_local, vertical_root = lax.optimization_barrier((tile, vertical_local, vertical_root))
    from_local, from_root = pl.pallas_call(
        functools.partial(matrices_kernel, member_scale),
        grid=(1,),
        in_specs=[whole(levels, levels)] * 2,
        out_specs=[VMEM] * 2,
        out_shape=[pltpu.VMEM((size, 3 * size), bf16)] * 2,
        compiler_params=params(8),
        name="level_matrices",
    )(in_hbm(vertical_local), in_hbm(vertical_root))
    tile_first, tile_second, from_local, from_root = lax.optimization_barrier(
        (tile_first, tile_second, from_local, from_root)
    )
    tile_other = swapped(tile, tile_first, tile_second)

    smooth = pl.pallas_call(
        functools.partial(second_diffusion_kernel, rows),
        in_specs=[VMEM] * 5,
        out_specs=VMEM,
        out_shape=pltpu.VMEM((lev_share, per_level, LANES), f32),
        compiler_params=params(8),
        name="diffuse_adjoint",
    )(coefs, tile_second, tile_first, tile, tile_other)
    smooth, from_local = lax.optimization_barrier((smooth, from_local))
    smooths = [smooth] + from_peers(smooth)[::-1]

    group = 2 - members % 2
    ensemble_grad = pl.pallas_call(
        member_kernel,
        grid=(members // group,),
        in_specs=[VMEM] * (3 + n_ens),
        out_specs=pl.BlockSpec((group, levels, per_level, LANES), lambda k: (k, 0, 0, 0)),
        out_shape=jax.ShapeDtypeStruct((members, levels, per_level, LANES), f32),
        scratch_shapes=[pltpu.VMEM((levels, per_level, LANES), f32)],
        compiler_params=params(16),
        name="members_gradient",
    )(from_local, control_here, pert_here, *adjoints)

    static_grad = pl.pallas_call(
        static_kernel,
        grid=(1,),
        in_specs=[VMEM] * (2 + n_ens),
        out_specs=whole(levels, per_level, LANES),
        out_shape=jax.ShapeDtypeStruct((levels, per_level, LANES), f32),
        scratch_shapes=[pltpu.VMEM((levels, per_level, LANES), f32)],
        compiler_params=params(8),
        name="static_gradient",
    )(from_root, static_here, *smooths)
    return (untiled(static_grad, rows), untiled(ensemble_grad, rows))


def solution(mesh):
    placed = (
        P(None, "cols", None),
        P("ens", None, "cols", None),
        P("ens", None, "cols", None),
        P(),
        P(),
        P("cols", None),
        P("cols", None),
        P("cols"),
        P("cols"),
        P("cols"),
        P("cols", None),
        P("cols"),
    )
    return jax.shard_map(
        local,
        mesh=mesh,
        in_specs=placed,
        out_specs=(P(None, "cols", None), P("ens", None, "cols", None)),
        check_vma=False,
    )
```

```python
import functools
import math

import jax
import jax.numpy as jnp
from jax import lax
from jax.experimental import pallas as pl
from jax.experimental.pallas import tpu as pltpu
from jax.sharding import PartitionSpec as P

NDIFF = 4
LANES = 128
FINE = 64
MIB = 1 << 20

f32 = jnp.float32
bf16 = jnp.bfloat16
SMEM = pl.BlockSpec(memory_space=pltpu.SMEM)
VMEM = pl.BlockSpec(memory_space=pltpu.VMEM)


def tiled(field):
    *lead, rows, lon = field.shape
    field = field.reshape(*lead, rows, lon // LANES, LANES)
    return jnp.swapaxes(field, -3, -2).reshape(*lead, rows * lon // LANES, LANES)


def untiled(field, rows):
    *lead, count, lanes = field.shape
    field = field.reshape(*lead, count // rows, rows, lanes)
    return jnp.swapaxes(field, -3, -2).reshape(*lead, rows, count // rows * lanes)


def params(limit, **more):
    return pltpu.CompilerParams(vmem_limit_bytes=limit * MIB, **more)


def halves(x):
    high = x.astype(bf16)
    return high, (x - high.astype(f32)).astype(bf16)


def in_hbm(x):
    return pltpu.with_memory_space_constraint(x, pltpu.HBM)


def spread(row, dtype):
    return jnp.broadcast_to(row, (16, row.shape[1])).astype(dtype)


def matches(index, count):
    ids = lax.broadcasted_iota(jnp.int32, (count, index.shape[1]), 0).astype(jnp.int16)
    return ids.reshape(count // 16, 16, index.shape[1]) == spread(index, jnp.int16)[None]


def placed_at(index, count, amount=None):
    where = matches(index, count)
    amount = bf16(1) if amount is None else spread(amount, bf16)[None]
    return jnp.where(where, amount, bf16(0)).reshape(count, index.shape[1])


def in_turns(count, build, use, slots, between, beside, chunks):
    build(0, slots[0])

    def step(i, carry):
        use(2 * i, slots[0])
        build(2 * i + 1, slots[1])
        use(2 * i + 1, slots[1])
        build(jnp.minimum(2 * i + 2, count - 1), slots[0])
        return carry

    def last_step(i, carry):
        beside(i - first)
        return step(i, carry)

    first = max(count // 2 - chunks, 0)
    lax.fori_loop(0, first, step, 0)
    between()
    lax.fori_loop(first, count // 2, last_step, 0)
    if count % 2:
        use(count - 1, slots[0])
    for j in range(count // 2 - first, chunks):
        beside(j)


def product_nt(left, right):
    return lax.dot_general(left, right, (((1,), (1,)), ((), ())), preferred_element_type=f32)


def over(x, size):
    if size & (size - 1):
        return lax.div(x, jnp.int32(size)), lax.rem(x, jnp.int32(size))
    return lax.shift_right_logical(x, jnp.int32(size.bit_length() - 1)), x & (size - 1)


def peer(i, d, count):
    return (i + d) % count if count & (count - 1) else i ^ d


def back(d, count):
    return count - d if count & (count - 1) else d


def prepare(root_ref, static_ref, north_ref, east_ref, out_ref):
    levels = static_ref.shape[0]
    lev_share = out_ref.shape[0] - 2
    first = lax.axis_index("ens") * lev_share
    for j in range(lev_share):
        total = root_ref[first + j, 0] * static_ref[0]
        for m in range(1, levels):
            total = total + root_ref[first + j, m] * static_ref[m]
        out_ref[j] = total
    out_ref[lev_share] = north_ref[...]
    out_ref[lev_share + 1] = east_ref[...]


def list_cells(rows, lon, index_ref, count_ref, row_ref, lane_ref):
    lists, capacity = index_ref.shape
    pieces = capacity // LANES
    slot = lax.broadcasted_iota(jnp.int32, (1, capacity), 1)
    for q in range(lists):
        rest, lane = over(index_ref[q : q + 1, :], LANES)
        rest, block = over(rest, lon // LANES)
        level, row = over(rest, rows)
        grid_row = (level * (lon // LANES) + block) * rows + row
        grid_row = jnp.where(slot < count_ref[q], grid_row, -1)
        for c in range(pieces):
            at = q * pieces + c
            row_ref[at : at + 1, :] = grid_row[:, c * LANES : (c + 1) * LANES]
            lane_ref[at : at + 1, :] = lane[:, c * LANES : (c + 1) * LANES]


def level_product(matrix, transpose):
    levels = matrix.shape[0]
    size = levels * 16
    pick = lax.broadcasted_iota(jnp.int32, (size, levels), 0) // 16
    pick = jnp.where(pick == lax.broadcasted_iota(jnp.int32, (size, levels), 1), f32(1), f32(0)).astype(bf16)
    same = (
        lax.broadcasted_iota(jnp.int32, (size, size), 0) % 16 == lax.broadcasted_iota(jnp.int32, (size, size), 1) % 16
    )
    out = []
    for half in halves(matrix):
        if transpose:
            wide = product_nt(pick, half)
        else:
            wide = jnp.dot(pick, half, preferred_element_type=f32)
        wide = product_nt(wide.astype(bf16), pick)
        out.append(jnp.where(same, wide, f32(0)).astype(bf16))
    return jnp.concatenate([out[0], out[0], out[1]], axis=1)


def three_terms(x):
    high, low = halves(x)
    return jnp.concatenate([high, low, high], axis=0)


def observe_kernel(n_cols, cap_rows, scale, *refs):
    n_ens = len(refs) - 32
    sources, (out_ref, packed_ref), parts = refs[:10], refs[10:12], refs[12 : 12 + n_ens]
    refs = refs[12 + n_ens :]
    (acc_ref, fold_ref, matrix_ref, part_ref), landed, sems, slots, sums_ref = (
        refs[:4],
        refs[4:14],
        refs[14],
        (refs[15:17], refs[17:19]),
        refs[19],
    )
    slot_ref, weight_ref, innov_ref, local_ref, control_ref, pert_ref, *static_refs = landed
    coarse = acc_ref.shape[1]
    obs_rows = slot_ref.shape[0]
    group = min(8, obs_rows)
    here = pl.ds(pl.multiple_of(lax.axis_index("ens") * obs_rows, obs_rows), obs_rows)
    copies = [
        pltpu.make_async_copy(s.at[here, :] if i < 3 else s, t, sems.at[i])
        for i, (s, t) in enumerate(zip(sources, landed))
    ]
    for copy in copies:
        copy.start()
    acc_ref[...] = jnp.zeros_like(acc_ref)
    for copy in copies[:3]:
        copy.wait()

    def build(i, to):
        at = pl.ds(pl.multiple_of(i * group, group), group)
        weight = weight_ref[at, :]
        amount = weight * innov_ref[at, :]
        upper, lower = over(slot_ref[at, :], FINE)
        terms = [t.astype(f32) for t in halves(weight) + halves(amount)]
        for r in range(group):
            here = slice(r * LANES, (r + 1) * LANES)
            to[0][:, here] = placed_at(upper[r : r + 1, :], coarse)
            mask = matches(lower[r : r + 1, :], FINE)
            for t, term in enumerate(terms):
                term = spread(term[r : r + 1, :], bf16)[None]
                to[1][t * FINE : (t + 1) * FINE, here] = jnp.where(mask, term, bf16(0)).reshape(FINE, LANES)

    def use(i, of):
        acc_ref[...] += product_nt(of[1][...], of[0][...])

    def fields():
        for copy in copies[3:]:
            copy.wait()
        matrix_ref[...] = level_product(local_ref[...] * f32(scale), False)

    def members(j):
        sum_members(j, matrix_ref, control_ref, pert_ref, part_ref)

    in_turns(obs_rows // group, build, use, slots, fields, members, part_ref.shape[1] // 16)
    for t in range(2):
        at = 2 * t * FINE
        terms = acc_ref[at : at + FINE, :] + acc_ref[at + FINE : at + 2 * FINE, :]
        fold_ref[t] = jnp.concatenate([terms] * (LANES // FINE), axis=0).T
    per_row = LANES // FINE
    lane = lax.broadcasted_iota(jnp.int32, (coarse // per_row, LANES), 1)
    weights, amounts = (
        jnp.where(
            lane < FINE,
            fold_ref[t, pl.ds(0, coarse // per_row, stride=per_row), :],
            fold_ref[t, pl.ds(1, coarse // per_row, stride=per_row), :],
        )
        for t in range(2)
    )
    for p in range(n_cols):
        sums_ref[p, 0] = weights[p * cap_rows : (p + 1) * cap_rows]
        sums_ref[p, 1] = amounts[p * cap_rows : (p + 1) * cap_rows]
    writes = [
        pltpu.make_async_copy(sums_ref, out_ref.at[pl.ds(e * n_cols, n_cols)], sems.at[len(copies) + e])
        for e in range(n_ens)
    ]
    for write in writes:
        write.start()
    prepare(*static_refs, packed_ref)
    share = part_ref.shape[0] // n_ens
    for d, part in enumerate(parts):
        at = peer(lax.axis_index("ens"), d, n_ens) * share
        part[...] = part_ref[pl.ds(at, share)]
    for write in writes:
        write.wait()


def sum_members(j, matrix_ref, control_ref, pert_ref, out_ref):
    members, levels, _, _ = control_ref.shape
    group = 2 - members % 2
    at = pl.ds(pl.multiple_of(j * 16, 16), 16)
    total = jnp.zeros((levels * 16, LANES), f32)
    for k in range(0, members, group):
        terms = [three_terms(control_ref[k + i, :, at, :].reshape(levels * 16, LANES)) for i in range(group)]
        local = jnp.dot(matrix_ref[...], jnp.concatenate(terms, axis=1), preferred_element_type=f32)
        for i in range(group):
            pert = pert_ref[k + i, :, at, :].astype(f32).reshape(levels * 16, LANES)
            total = total + pert * local[:, i * LANES : (i + 1) * LANES]
    out_ref[:, at, :] = total.reshape(levels, 16, LANES)


def gather_levels(parts, to_ref, far_first):
    share = to_ref.shape[0] // len(parts)
    for i, part in enumerate(parts):
        at = peer(lax.axis_index("ens"), (len(parts) - i) % len(parts) if far_first else i, len(parts))
        to_ref[pl.ds(at * share, share)] = part[...]


def member_kernel(matrix_ref, control_ref, pert_ref, *refs):
    parts, out_ref, adjoint_ref = refs[:-2], refs[-2], refs[-1]
    group, levels, per_level, _ = out_ref.shape
    first = pl.program_id(0) * group

    @pl.when(pl.program_id(0) == 0)
    def _():
        gather_levels(parts, adjoint_ref, False)

    def chunk(j, carry):
        at = pl.ds(pl.multiple_of(j * 16, 16), 16)
        adjoint = adjoint_ref[:, at, :]
        terms = [
            three_terms((pert_ref[first + i, :, at, :].astype(f32) * adjoint).reshape(levels * 16, LANES))
            for i in range(group)
        ]
        change = jnp.dot(matrix_ref[...], jnp.concatenate(terms, axis=1), preferred_element_type=f32)
        for i in range(group):
            part = change[:, i * LANES : (i + 1) * LANES].reshape(levels, 16, LANES)
            out_ref[i, :, at, :] = control_ref[first + i, :, at, :] + part
        return carry

    lax.fori_loop(0, per_level // 16, chunk, 0)


def eastern(x):
    lane = lax.broadcasted_iota(jnp.int32, x.shape, 1)
    near = pltpu.roll(x, LANES - 1, 1)
    return jnp.where(lane == LANES - 1, pltpu.roll(near, x.shape[0] - 1, 0), near)


def western(x):
    lane = lax.broadcasted_iota(jnp.int32, x.shape, 1)
    near = pltpu.roll(x, 1, 1)
    return jnp.where(lane == 0, pltpu.roll(near, 1, 0), near)


def rows_of(second_ref, first_ref, own_ref, other_ref, plane, rows):
    at = lax.axis_index("cols")
    count = lax.axis_size("cols")
    core, chip = at % 2, at // 2 % 2
    reads = [pl.ds(r, own_ref.shape[1] // rows, stride=rows) for r in range(rows)]
    first = [first_ref[plane, r, :] for r in reads]
    second = [second_ref[plane, r, :] for r in reads]
    out = [jnp.where(jnp.logical_and(chip == 1, at >= 2), f, f32(0)) for f in first]
    out = [jnp.where(jnp.logical_and(chip == 0, at >= 2), s, o) for s, o in zip(second, out)]
    out += [jnp.where(at >= 1, other_ref[1 - core, plane, r, :], f32(0)) for r in reads]
    out += [own_ref[plane, r, :] for r in reads]
    out += [jnp.where(at < count - 1, other_ref[core, plane, r, :], f32(0)) for r in reads]
    last = [jnp.where(jnp.logical_and(chip == 0, at < count - 2), f, f32(0)) for f in first]
    return out + [jnp.where(jnp.logical_and(chip == 1, at < count - 2), s, o) for s, o in zip(second, last)]


def diffuse_rows(tiles, level, coef_ref, rows):
    field = rows_of(*tiles, level, rows)
    for step in range(NDIFF):
        field = [
            coef_ref[0, i + step] * field[i]
            + coef_ref[1, i + step] * field[i - 1]
            + coef_ref[1, i + step + 1] * field[i + 1]
            + coef_ref[2, i + step] * eastern(field[i])
            + western(coef_ref[2, i + step] * field[i])
            for i in range(1, len(field) - 1)
        ]
    return field


def first_diffusion_kernel(lev_share, rows, *refs):
    second_ref, first_ref, own_ref, other_ref, *sources = refs[:6]
    out_ref, coef_ref, row_ref, lane_ref, *landed, sems = refs[6:]
    copies = [pltpu.make_async_copy(s, t, sems.at[i]) for i, (s, t) in enumerate(zip(sources, landed))]
    for copy in copies:
        copy.start()
    tiles = (second_ref, first_ref, own_ref, other_ref)
    blocks = own_ref.shape[1] // rows
    side = 2
    north = rows_of(*tiles, lev_share, rows)
    east = rows_of(*tiles, lev_share + 1, rows)
    faces = [
        jnp.where(lax.axis_index("cols") == side - i // rows, f32(0), n) if i % rows == 0 and i <= side * rows else n
        for i, n in enumerate(north)
    ]
    for i in range(len(north)):
        inner = 0 < i < len(north) - 1
        coef_ref[0, i] = 1.0 - north[i] - faces[i + 1] - east[i] - western(east[i]) if inner else jnp.zeros_like(east[i])
        coef_ref[1, i] = faces[i]
        coef_ref[2, i] = east[i]

    def body(level, carry):
        final = diffuse_rows(tiles, level, coef_ref, rows)
        for r in range(rows):
            out_ref[level, pl.ds(r, blocks, stride=rows), :] = final[r]
        return carry

    lax.fori_loop(0, lev_share, body, 0)
    for copy in copies:
        copy.wait()
    list_cells(rows, blocks * LANES, *landed, row_ref, lane_ref)


def second_diffusion_kernel(rows, coef_ref, second_ref, first_ref, own_ref, other_ref, out_ref):
    tiles = (second_ref, first_ref, own_ref, other_ref)
    lev_share = out_ref.shape[0]
    blocks = own_ref.shape[1] // rows

    def body(level, carry):
        final = diffuse_rows(tiles, level, coef_ref, rows)
        for r in range(rows):
            out_ref[level, pl.ds(r, blocks, stride=rows), :] = final[r]
        return carry

    lax.fori_loop(0, lev_share, body, 0)


def scatter_kernel(cap_rows, row_ref, lane_ref, slots_ref, *refs):
    sources, out_ref, kept, acc_ref, sems = refs[:3], refs[3], refs[4:7], refs[7], refs[8]
    copies = [pltpu.make_async_copy(s, t, sems.at[i]) for i, (s, t) in enumerate(zip(sources, kept))]
    for copy in copies:
        copy.start()
    own = out_ref.shape[1]
    lists = row_ref.shape[0] // cap_rows
    first = lax.axis_index("ens") * own
    acc_ref[...] = jnp.zeros_like(acc_ref)

    def step(q, carry):
        at = pl.ds(pl.multiple_of(q * cap_rows, cap_rows), cap_rows)
        rows = row_ref[at, :] - first
        lanes = lane_ref[at, :]
        terms = []
        for t in range(2):
            total = functools.reduce(
                jnp.add, [slots_ref[e * lists + q, t] for e in range(slots_ref.shape[0] // lists)]
            )
            terms += [h.astype(f32) for h in halves(total)]
        left, right = [], []
        for c in range(cap_rows):
            left.append(placed_at(rows[c : c + 1, :], own))
            mask = matches(lanes[c : c + 1, :], LANES)
            right.append(
                jnp.concatenate(
                    [
                        jnp.where(mask, spread(t[c : c + 1, :], bf16)[None], bf16(0)).reshape(LANES, LANES)
                        for t in terms
                    ],
                    axis=0,
                )
            )
        acc_ref[...] += product_nt(jnp.concatenate(right, axis=1), jnp.concatenate(left, axis=1))
        return carry

    lax.fori_loop(0, lists, step, 0)
    for t in range(2):
        at = 2 * t * LANES
        out_ref[t] = (acc_ref[at : at + LANES, :] + acc_ref[at + LANES : at + 2 * LANES, :]).T
    for copy in copies:
        copy.wait()


def matrices_kernel(scale, local_ref, root_ref, to_members_ref, to_static_ref):
    to_members_ref[...] = level_product(local_ref[...] * f32(scale), True)
    to_static_ref[...] = level_product(root_ref[...], True)


def static_kernel(matrix_ref, static_ref, *refs):
    parts, (out_ref, smooth_ref) = refs[:-2], refs[-2:]
    levels, per_level, _ = static_ref.shape
    gather_levels(parts, smooth_ref, False)
    for j in range(0, per_level, 32):
        terms = [three_terms(smooth_ref[:, j + i : j + i + 16, :].reshape(levels * 16, LANES)) for i in (0, 16)]
        change = jnp.dot(matrix_ref[...], jnp.concatenate(terms, axis=1), preferred_element_type=f32)
        for i, part in ((0, change[:, :LANES]), (16, change[:, LANES:])):
            at = slice(j + i, j + i + 16)
            out_ref[:, at, :] = static_ref[:, at, :] + part.reshape(levels, 16, LANES)


def exchanged(x, starts):
    count = lax.axis_size("cols")
    out = []
    for start in starts:
        pairs = []
        for i in range(count):
            chip, core = divmod(i, 2)
            partner = (chip + start ^ 1) - start
            pairs.append((i, 2 * partner + core if 0 <= 2 * partner + core < count else i))
        out.append(lax.ppermute(x, "cols", pairs))
    return out


def from_peers(x):
    count = lax.axis_size("ens")
    return [lax.ppermute(x, "ens", [(peer(i, d, count), i) for i in range(count)]) for d in range(count - 1, 0, -1)]


def swapped(own, first, second):
    at = lax.axis_index("cols")
    pack = jnp.stack([own, jnp.where(at % 2 == at // 2 % 2, first, second)])
    return lax.ppermute(pack, "cols", [(i, i ^ 1) for i in range(lax.axis_size("cols"))])


def local(
    static_control,
    ensemble_control,
    perturbations,
    vertical_root,
    vertical_local,
    face_north,
    face_east,
    innovation,
    obs_weight,
    obs_slot,
    send_index,
    send_count,
):
    n_ens = lax.axis_size("ens")
    n_cols = lax.axis_size("cols")
    members, levels, rows, lon = ensemble_control.shape
    per_level = rows * lon // LANES
    cells = levels * per_level
    lev_share = levels // n_ens
    own = lev_share * per_level
    lists, capacity = send_index.shape
    cap_rows = capacity // LANES
    entry_rows = lists * cap_rows
    member_scale = 1.0 / math.sqrt(members * n_ens - 1)

    static = in_hbm(tiled(static_control))
    control = in_hbm(tiled(ensemble_control))
    pert = in_hbm(tiled(perturbations))

    def whole(*shape):
        return pl.BlockSpec(shape, lambda i: (0,) * len(shape))

    obs_rows = obs_slot.shape[0] // LANES
    share_rows = obs_rows // n_ens
    coarse = n_cols * capacity // FINE
    size = levels * 16
    slots, packed, *parts = pl.pallas_call(
        functools.partial(observe_kernel, n_cols, cap_rows, member_scale),
        grid=(1,),
        in_specs=[pl.BlockSpec(memory_space=pl.ANY)] * 10,
        out_specs=[pl.BlockSpec(memory_space=pl.ANY)] + [VMEM] * (1 + n_ens),
        out_shape=[
            pltpu.HBM((n_ens * n_cols, 2, cap_rows, LANES), f32),
            pltpu.VMEM((lev_share + 2, per_level, LANES), f32),
        ]
        + [pltpu.VMEM((lev_share, per_level, LANES), f32)] * n_ens,
        scratch_shapes=[
            pltpu.VMEM((4 * FINE, coarse), f32),
            pltpu.VMEM((2, coarse, LANES), f32),
            pltpu.VMEM((size, 3 * size), bf16),
            pltpu.VMEM((levels, per_level, LANES), f32),
            pltpu.VMEM((share_rows, LANES), jnp.int32),
            pltpu.VMEM((share_rows, LANES), f32),
            pltpu.VMEM((share_rows, LANES), f32),
            pltpu.VMEM((levels, levels), f32),
            pltpu.VMEM(control.shape, f32),
            pltpu.VMEM(pert.shape, bf16),
            pltpu.SMEM((levels, levels), f32),
            pltpu.VMEM((levels, per_level, LANES), f32),
            pltpu.VMEM((per_level, LANES), f32),
            pltpu.VMEM((per_level, LANES), f32),
            pltpu.SemaphoreType.DMA((10 + n_ens,)),
        ]
        + [pltpu.VMEM((coarse, 8 * LANES), bf16), pltpu.VMEM((4 * FINE, 8 * LANES), bf16)] * 2
        + [pltpu.VMEM((n_cols, 2, cap_rows, LANES), f32)],
        compiler_params=params(24),
        name="slot_sums_and_members",
    )(
        in_hbm(obs_slot.reshape(obs_rows, LANES)),
        in_hbm(obs_weight.reshape(obs_rows, LANES)),
        in_hbm(innovation.reshape(obs_rows, LANES)),
        in_hbm(vertical_local),
        control,
        pert,
        in_hbm(vertical_root),
        static,
        in_hbm(tiled(face_north)),
        in_hbm(tiled(face_east)),
    )
    slots = lax.all_to_all(slots, ("ens", "cols"), split_axis=0, concat_axis=0, tiled=True)
    second, first = exchanged(packed, (1, 0))
    sums = [parts[0]] + [
        lax.ppermute(parts[back(d, n_ens)], "ens", [(peer(i, d, n_ens), i) for i in range(n_ens)])
        for d in range(n_ens - 1, 0, -1)
    ]
    other = swapped(packed, first, second)

    increment, coefs, entry_row, entry_lane = pl.pallas_call(
        functools.partial(first_diffusion_kernel, lev_share, rows),
        in_specs=[VMEM] * 4 + [pl.BlockSpec(memory_space=pl.ANY)] * 2,
        out_specs=[VMEM] * 4,
        out_shape=[
            pltpu.VMEM((lev_share, per_level, LANES), f32),
            pltpu.VMEM((3, 5 * rows, per_level // rows, LANES), f32),
            pltpu.VMEM((entry_rows, LANES), jnp.int32),
            pltpu.VMEM((entry_rows, LANES), jnp.int32),
        ],
        scratch_shapes=[
            pltpu.VMEM((lists, capacity), jnp.int32),
            pltpu.SMEM((lists,), jnp.int32),
            pltpu.SemaphoreType.DMA((2,)),
        ],
        compiler_params=params(8),
        cost_estimate=pl.CostEstimate(flops=1 << 26, bytes_accessed=1 << 22, transcendentals=0),
        name="diffuse_forward",
    )(second, first, packed, other, in_hbm(send_index), in_hbm(send_count))

    increment, coefs, slots = lax.optimization_barrier((increment, coefs, slots))
    slot_sums, static_here, control_here, pert_here = pl.pallas_call(
        functools.partial(scatter_kernel, cap_rows),
        in_specs=[VMEM] * 3 + [pl.BlockSpec(memory_space=pl.ANY)] * 3,
        out_specs=[VMEM] * 4,
        out_shape=[
            pltpu.VMEM((2, own, LANES), f32),
            pltpu.VMEM(static.shape, f32),
            pltpu.VMEM(control.shape, f32),
            pltpu.VMEM(pert.shape, bf16),
        ],
        scratch_shapes=[pltpu.VMEM((4 * LANES, own), f32), pltpu.SemaphoreType.DMA((3,))],
        compiler_params=params(16),
        cost_estimate=pl.CostEstimate(flops=8 * own * LANES * lists * capacity, bytes_accessed=1 << 23, transcendentals=0),
        name="scatter",
    )(entry_row, entry_lane, slots, static, control, pert)

    slot_sums = slot_sums.reshape(2, lev_share, per_level, LANES)
    tile = functools.reduce(jnp.add, sums) + increment
    tile = tile * slot_sums[0] - slot_sums[1]
    tile_first, tile_second = exchanged(tile, (0, 1))
    adjoints = [tile] + from_peers(tile)[::-1]
    tile, vertical_local, vertical_root = lax.optimization_barrier((tile, vertical_local, vertical_root))
    from_local, from_root = pl.pallas_call(
        functools.partial(matrices_kernel, member_scale),
        grid=(1,),
        in_specs=[whole(levels, levels)] * 2,
        out_specs=[VMEM] * 2,
        out_shape=[pltpu.VMEM((size, 3 * size), bf16)] * 2,
        compiler_params=params(8),
        name="level_matrices",
    )(in_hbm(vertical_local), in_hbm(vertical_root))
    tile_first, tile_second, from_local, from_root = lax.optimization_barrier(
        (tile_first, tile_second, from_local, from_root)
    )
    tile_other = swapped(tile, tile_first, tile_second)

    smooth = pl.pallas_call(
        functools.partial(second_diffusion_kernel, rows),
        in_specs=[VMEM] * 5,
        out_specs=VMEM,
        out_shape=pltpu.VMEM((lev_share, per_level, LANES), f32),
        compiler_params=params(8),
        name="diffuse_adjoint",
    )(coefs, tile_second, tile_first, tile, tile_other)
    smooth, from_local = lax.optimization_barrier((smooth, from_local))
    smooths = [smooth] + from_peers(smooth)[::-1]

    group = 2 - members % 2
    ensemble_grad = pl.pallas_call(
        member_kernel,
        grid=(members // group,),
        in_specs=[VMEM] * (3 + n_ens),
        out_specs=pl.BlockSpec((group, levels, per_level, LANES), lambda k: (k, 0, 0, 0)),
        out_shape=jax.ShapeDtypeStruct((members, levels, per_level, LANES), f32),
        scratch_shapes=[pltpu.VMEM((levels, per_level, LANES), f32)],
        compiler_params=params(16),
        name="members_gradient",
    )(from_local, control_here, pert_here, *adjoints)

    static_grad = pl.pallas_call(
        static_kernel,
        grid=(1,),
        in_specs=[VMEM] * (2 + n_ens),
        out_specs=whole(levels, per_level, LANES),
        out_shape=jax.ShapeDtypeStruct((levels, per_level, LANES), f32),
        scratch_shapes=[pltpu.VMEM((levels, per_level, LANES), f32)],
        compiler_params=params(8),
        name="static_gradient",
    )(from_root, static_here, *smooths)
    return (untiled(static_grad, rows), untiled(ensemble_grad, rows))


def solution(mesh):
    placed = (
        P(None, "cols", None),
        P("ens", None, "cols", None),
        P("ens", None, "cols", None),
        P(),
        P(),
        P("cols", None),
        P("cols", None),
        P("cols"),
        P("cols"),
        P("cols"),
        P("cols", None),
        P("cols"),
    )
    return jax.shard_map(
        local,
        mesh=mesh,
        in_specs=placed,
        out_specs=(P(None, "cols", None), P("ens", None, "cols", None)),
        check_vma=False,
    )
```
